32 devices in a mesh: runs: 2 (over x), line: 16 (over z, y, core).
Axes of the slice: x: 2, y: 2, z: 4, core: 2. Of those that a mesh axis runs over, the one named last changes fastest.
Arguments:
- velocity: float32 [3, 64, 128, 128], P(None, ('runs', 'line')), parts along dimension 1, may hold values from -6 to 6
- stress: float32 [6, 64, 128, 128], P(None, ('runs', 'line')), parts along dimension 1, may hold values from -6 to 6
- memory: float32 [6, 64, 128, 128], P(None, ('runs', 'line')), parts along dimension 1, may hold values from -4 to 4
- truck_loads: float32 [512, 128], P(('runs', 'line')), parts along dimension 0, may hold values from -8 to 8
- pier_panels: float32 [16, 16, 1536], P('line', 'runs'), parts along dimension 1, may hold values from -8 to 8
- lame_lambda: float32 [8], replicated, may hold values from 0.3 to 1
- lame_mu: float32 [8], replicated, may hold values from 0.2 to 0.6
- buoyancy: float32 [8], replicated, may hold values from 0.5 to 1.5
- relax_rate: float32 [8], replicated, may hold values from 0.3 to 3
- defect_mu: float32 [8], replicated, may hold values from 0.05 to 0.4
- layer: int32 [128], replicated, may hold values from 0 to 7, never falling along the last dimension, each value on 1 to 32 neighbouring positions
- truck_entry: int32 [6, 512], P(None, ('runs', 'line')), parts along dimension 1, may hold values from -1 to 15
- truck_cell: int32 [6, 512], P(None, ('runs', 'line')), parts along dimension 1, may hold values from 0 to 1
- pier_cell: int32 [8], replicated, may hold values from 0 to 31
Outputs:
- velocity_out: float32 [3, 64, 128, 128], P(None, ('runs', 'line')), parts along dimension 1
- stress_out: float32 [6, 64, 128, 128], P(None, ('runs', 'line')), parts along dimension 1
- memory_out: float32 [6, 64, 128, 128], P(None, ('runs', 'line')), parts along dimension 1
The draws below stay inside these ranges and needn't reach their ends.
There are 2 independent parts, one for each index of `runs`. The reference program is written for one: setup_inputs(seed, part) draws one part's arguments, and reference() takes and returns one part's arrays. A program takes and returns all parts, laid end to end along the dimension named above; an argument that names none is the same for every part. Nothing has to cross between parts.
Inputs may be any that keep to these rules, and one draw needn't show every extreme that they name: `truck_entry`: -1 keeps a slot's own truck; k takes slot k of the tile behind. `truck_cell`: A cell within the tile. `layer`: never falls with depth.
All inputs are finite; a program needn't handle non-finite values.
Results may differ from the reference program's by a relative error of at most 0.0001.
Values sent between devices are 32-bit elements; how exact they have to be, the bound alone decides.
No kernel may reach another device: no remote copies, remote signals or barrier semaphores. Data moves between devices by JAX's collectives and lax.ppermute only.
A program may use at most 64 MiB of HBM per device.

```python
import math
import jax
import jax.numpy as jnp
import numpy as np
from jax import lax

CX = 2
CY = 128
NZ = 128
STEPS = 6
LAYERS = 8
CAP = 16
FY = 8
FZ = 64
NX = 32
PIERS = 8
RECORDS = 16
PANEL = 1536
N_LINE = 16


def set_ends(result, rng, low, largest):
    longest = result.shape.index(max(result.shape))
    spots = []
    for shift in (0, 1):
        where = [jax.random.randint(jax.random.fold_in(rng, axis), (), 0, length) for axis, length in enumerate(result.shape)]
        where[longest] = (where[longest] + shift) % result.shape[longest]
        spots.append(tuple(where))
    return result.at[spots[0]].set(low).at[spots[1]].set(largest)


def steps_of(key, shape, pieces, smallest, largest):
    def one(dim, shards_of):
        draws = jax.random.uniform(jax.random.fold_in(jax.random.fold_in(key, 6), dim), (shards_of,), jnp.float32, smallest / len(pieces), largest / len(pieces))
        return jnp.repeat(jnp.exp(draws), shape[dim] // shards_of).reshape((-1,) + (1,) * (len(shape) - dim - 1))

    factor_of = one(*pieces[0])
    for cut in pieces[1:]:
        factor_of = factor_of * one(*cut)
    return factor_of


def cumulative_ranks(number_of, skew):
    loads = [(1 << 20) // math.isqrt(grade ** skew) + 1 for grade in range(1, number_of + 1)]
    deviation = 1 + sum(loads) // (1 << 30)
    return np.cumsum(np.array([max(1, weight // deviation) for weight in loads]))


def ranked(key, extent, amount, lean):
    listing = cumulative_ranks(amount, lean)
    lot = jax.random.randint(jax.random.fold_in(key, 1), extent, 0, int(listing[amount - 1]))
    grade = jnp.searchsorted(jnp.asarray(listing, jnp.int32), lot, side="right")
    return jax.random.permutation(jax.random.fold_in(key, 2), amount)[grade].astype(jnp.int32)


def split_up(amount, total, limit, skew):
    weights = [(1 << 20) // math.isqrt(grade ** skew) + 1 for grade in range(2, amount + 1)]
    surplus, counts = total - limit - (amount - 1), [1] * (amount - 1)
    while surplus > 0:
        free = [i for i in range(amount - 1) if counts[i] < limit]
        mass, remaining = sum([weights[i] for i in free]), surplus
        for i in free:
            more = min(limit - counts[i], max(1, remaining * weights[i] // mass), surplus)
            counts[i] = counts[i] + more
            surplus = surplus - more
    return np.array([limit] + counts)


def ragged(own_key, number_of, total, limit, skew):
    if number_of == 2:
        one = jax.random.randint(own_key, (), max(1, total - limit), min(limit, total - 1) + 1)
        return jnp.stack([one, total - one])
    sizes = jnp.asarray(split_up(number_of, total, limit, skew), jnp.int32)
    pairs = (number_of - 1) // 2
    giver, receiver = sizes[1:1 + 2 * pairs:2], sizes[2:2 + 2 * pairs:2]
    margin = jnp.minimum(giver - 1, limit - receiver)
    passed = jax.random.randint(jax.random.fold_in(own_key, 1), (pairs,), 0, 1 << 20) % (margin + 1)
    sizes = sizes.at[1:1 + 2 * pairs:2].set(giver - passed).at[2:2 + 2 * pairs:2].set(receiver + passed)
    return sizes[jax.random.permutation(jax.random.fold_in(own_key, 2), number_of)]


def centred(rng, shape, spread, reach, pieces=(), kind=jnp.bfloat16):
    gain = steps_of(rng, shape, pieces, -0.22, 0.18) if pieces else 1.0
    result = jax.random.normal(rng, shape, jnp.float32) * spread * gain
    return jnp.minimum(jnp.maximum(result, -reach), reach).astype(kind)


def setup_inputs(seed: int = 0, part: int = 0) -> dict:
    seeds = jax.random.split(jax.random.key(seed), 15)
    part_splits = jax.random.split(jax.random.fold_in(seeds[14], part), 15)
    return {
        "velocity": centred(part_splits[0], (3, NX, CY, NZ), 1.0, 6.0, ((1, 16),), jnp.float32),
        "stress": centred(part_splits[1], (6, NX, CY, NZ), 1.0, 6.0, ((1, 16),), jnp.float32),
        "memory": centred(part_splits[2], (6, NX, CY, NZ), 0.5, 4.0, ((1, 16),), jnp.float32),
        "truck_loads": centred(part_splits[3], (N_LINE * CAP, CY), 2.0, 8.0, ((0, 16),), jnp.float32),
        "pier_panels": centred(part_splits[4], (RECORDS, PIERS, PANEL), 2.0, 8.0, ((0, 16),), jnp.float32),
        "lame_lambda": jnp.clip(jnp.exp(jax.random.uniform(seeds[5], (LAYERS,), jnp.float32, math.log(0.3), math.log(1.0))), 0.3, 1.0),
        "lame_mu": jnp.clip(jnp.exp(jax.random.uniform(seeds[6], (LAYERS,), jnp.float32, math.log(0.2), math.log(0.6))), 0.2, 0.6),
        "buoyancy": jnp.clip(jnp.exp(jax.random.uniform(seeds[7], (LAYERS,), jnp.float32, math.log(0.5), math.log(1.5))), 0.5, 1.5),
        "relax_rate": jnp.clip(jnp.exp(jax.random.uniform(seeds[8], (LAYERS,), jnp.float32, math.log(0.3), math.log(3.0))), 0.3, 3.0),
        "defect_mu": jnp.clip(jnp.exp(jax.random.uniform(seeds[9], (LAYERS,), jnp.float32, math.log(0.05), math.log(0.4))), 0.05, 0.4),
        "layer": jnp.searchsorted(jnp.cumsum(ragged(seeds[10], LAYERS, NZ, NZ // 4, 0)), jnp.arange(NZ), side="right").astype(jnp.int32),
        "truck_entry": set_ends(jax.random.randint(part_splits[11], (STEPS, N_LINE * CAP), -1, CAP), jax.random.fold_in(part_splits[11], 1), -1, CAP - 1).astype(jnp.int32),
        "truck_cell": set_ends(jax.random.randint(part_splits[12], (STEPS, N_LINE * CAP), 0, CX), jax.random.fold_in(part_splits[12], 1), 0, CX - 1).astype(jnp.int32),
        "pier_cell": set_ends(ranked(seeds[13], (PIERS,), NX, 2), jax.random.fold_in(seeds[13], 3), 0, NX - 1).astype(jnp.int32),
    }


time_step = 0.25


def behind(field, axis):
    size = field.shape[axis]
    head = jnp.zeros_like(lax.slice_in_dim(field, 0, 1, axis=axis))
    return jnp.concatenate([head, lax.slice_in_dim(field, 0, size - 1, axis=axis)], axis=axis)


def ahead(field, axis):
    size = field.shape[axis]
    tail = jnp.zeros_like(lax.slice_in_dim(field, 0, 1, axis=axis))
    return jnp.concatenate([lax.slice_in_dim(field, 1, size, axis=axis), tail], axis=axis)


def per_depth(layer, table):
    levels = jnp.arange(table.shape[0], dtype=jnp.int32)
    return jnp.sum(jnp.where(layer[:, None] == levels[None, :], table[None, :], jnp.float32(0.0)), axis=1)


def velocity_rates(stresses, ahead_xx, behind_xy, behind_xz):
    s_xx, s_yy, s_zz, s_xy, s_xz, s_yz = stresses
    rate_x = (ahead_xx - s_xx) + (s_xy - behind(s_xy, 1)) + (s_xz - behind(s_xz, 2))
    rate_y = (s_xy - behind_xy) + (ahead(s_yy, 1) - s_yy) + (s_yz - behind(s_yz, 2))
    rate_z = (s_xz - behind_xz) + (s_yz - behind(s_yz, 1)) + (ahead(s_zz, 2) - s_zz)
    return (rate_x, rate_y, rate_z)


def strain_rates(speeds, behind_ux, ahead_uy, ahead_uz):
    u_x, u_y, u_z = speeds
    e_xx = u_x - behind_ux
    e_yy = u_y - behind(u_y, 1)
    e_zz = u_z - behind(u_z, 2)
    e_xy = 0.5 * ((ahead(u_x, 1) - u_x) + (ahead_uy - u_y))
    e_xz = 0.5 * ((ahead(u_x, 2) - u_x) + (ahead_uz - u_z))
    e_yz = 0.5 * ((ahead(u_y, 2) - u_y) + (ahead(u_z, 1) - u_z))
    return (e_xx, e_yy, e_zz, e_xy, e_xz, e_yz)


def relax(stresses, memories, strains, lambda_z, shear_z, decay_z, defect_z):
    trace = strains[0] + strains[1] + strains[2]
    new_stress = []
    new_memory = []
    for comp in range(6):
        drive = 2.0 * shear_z * strains[comp] + memories[comp]
        if comp < 3:
            drive = drive + lambda_z * trace
        new_stress.append(stresses[comp] + time_step * drive)
        new_memory.append(memories[comp] * (1.0 - time_step * decay_z) - time_step * decay_z * 2.0 * defect_z * strains[comp])
    return new_stress, new_memory


def reference(velocity, stress, memory, truck_loads, pier_panels, lame_lambda, lame_mu, buoyancy, relax_rate, defect_mu, layer, truck_entry, truck_cell, pier_cell):
    lambda_z = per_depth(layer, lame_lambda)
    shear_z = per_depth(layer, lame_mu)
    buoy_z = per_depth(layer, buoyancy)
    decay_z = per_depth(layer, relax_rate)
    defect_z = per_depth(layer, defect_mu)
    speeds = [velocity[0], velocity[1], velocity[2]]
    stresses = [stress[comp] for comp in range(6)]
    memories = [memory[comp] for comp in range(6)]
    truck_rows = truck_loads.reshape(N_LINE, CAP, CY)
    slot_ids = jnp.arange(CAP, dtype=jnp.int32)
    cells_x = jnp.arange(NX, dtype=jnp.int32)
    pier_hit = (pier_cell[None, :] == cells_x[:, None]).astype(jnp.float32)
    tile_start = (jnp.arange(N_LINE, dtype=jnp.int32) * CX)[:, None]
    corner = (CY - FY) // 2
    for step_index in range(STEPS):
        entry = truck_entry[step_index].reshape(N_LINE, CAP)
        incoming = jnp.concatenate([jnp.zeros((1, CAP, CY), jnp.float32), truck_rows[:-1]], axis=0)
        match = entry[:, :, None] == slot_ids[None, None, :]
        picked = jnp.sum(jnp.where(match[:, :, :, None], incoming[:, None, :, :], jnp.float32(0.0)), axis=2)
        truck_rows = jnp.where((entry >= 0)[:, :, None], picked, truck_rows)
        rates = velocity_rates(stresses, ahead(stresses[0], 0), behind(stresses[3], 0), behind(stresses[4], 0))
        pier_force = jnp.dot(pier_hit, pier_panels[step_index], precision=lax.Precision.HIGHEST).reshape(NX, 3, FY, FZ)
        for comp in range(3):
            moved = speeds[comp] + time_step * buoy_z * rates[comp]
            speeds[comp] = moved.at[:, corner:corner + FY, 0:FZ].add(time_step * pier_force[:, comp])
        strains = strain_rates(speeds, behind(speeds[0], 0), ahead(speeds[1], 0), ahead(speeds[2], 0))
        stresses, memories = relax(stresses, memories, strains, lambda_z, shear_z, decay_z, defect_z)
        global_cell = (truck_cell[step_index].reshape(N_LINE, CAP) + tile_start).reshape(N_LINE * CAP)
        truck_hit = (global_cell[None, :] == cells_x[:, None]).astype(jnp.float32)
        surface = jnp.dot(truck_hit, truck_rows.reshape(N_LINE * CAP, CY), precision=lax.Precision.HIGHEST)
        stresses[2] = stresses[2].at[:, :, 0].add(time_step * surface)
    return jnp.stack(speeds), jnp.stack(stresses), jnp.stack(memories)
```

```python
import functools

import jax
import jax.numpy as jnp
from jax import lax
from jax.experimental import pallas as pl
from jax.experimental.pallas import tpu as pltpu
from jax.sharding import PartitionSpec as P

STEPS = 6
FY = 8
FZ = 64
DT = 0.25
PAD = 8
ROWS = 16
VMEM_LIMIT = 32 * 1024 * 1024

C_B, C_B0, C_B1, C_M0, C_M1, C_LAM, C_MU2, C_MU, C_K1, C_K2, C_K2H, C_L0 = range(12)
N_COEF = 16

VX, VY, VZ = range(3)
XX, YY, ZZ, XY, XZ, YZ = range(6)


def lane_roll(x, shift):
    return pltpu.roll(x, shift % x.shape[-1], x.ndim - 1)


def before(x):
    return lane_roll(x, 1)


def after(x):
    return lane_roll(x, -1)


def over_rows(count, work):
    def step(i, carry):
        work(pl.multiple_of(i * ROWS, ROWS))
        return carry

    lax.fori_loop(0, count // ROWS, step, 0)


def coefs(coef_ref, ids):
    return [coef_ref[i : i + 1, :] for i in ids]


def place():
    index = lax.axis_index("line")
    return lax.rem(index, 2) == 0, index > 0, index < lax.axis_size("line") - 1


def pre_ahead(V, S, coef_ref, msg):
    b, b0 = coefs(coef_ref, (C_B, C_B0))

    def work(r):
        here, up = pl.ds(PAD + r, ROWS), pl.ds(PAD + r - 1, ROWS)
        sxy, sxz = S[XY, 1, here], S[XZ, 1, here]
        px = V[VX, 1, here] + b * (sxy - S[XY, 1, up] + sxz - S[XX, 1, here]) - b0 * before(sxz)
        V[VX, 1, here] = px
        out = pl.ds(r, ROWS)
        msg[0, out] = sxy
        msg[1, out] = sxz
        msg[2, out] = px

    over_rows(msg.shape[1], work)


def pre_behind(V, S, coef_ref, msg):
    b, b0, b1 = coefs(coef_ref, (C_B, C_B0, C_B1))

    def work(r):
        here, up, down = pl.ds(PAD + r, ROWS), pl.ds(PAD + r - 1, ROWS), pl.ds(PAD + r + 1, ROWS)
        syz, szz = S[YZ, 0, here], S[ZZ, 0, here]
        qy = V[VY, 0, here] + b * (S[XY, 0, here] + S[YY, 0, down] - S[YY, 0, here] + syz) - b0 * before(syz)
        qz = V[VZ, 0, here] + b * (S[XZ, 0, here] + syz - S[YZ, 0, up] - szz) + b1 * after(szz)
        V[VY, 0, here] = qy
        V[VZ, 0, here] = qz
        out = pl.ds(r, ROWS)
        msg[0, out] = S[XX, 0, here]
        msg[1, out] = qy
        msg[2, out] = qz

    over_rows(msg.shape[1], work)


def add_force(ref, index, force, which, corner_rows):
    rows = pl.ds(corner_rows, 16)
    ref[(*index, rows)] = ref[(*index, rows)] + force[which]


def inner(V, S, coef_ref, force, window, depth_rows):
    b, b0, b1 = coefs(coef_ref, (C_B, C_B0, C_B1))

    def work(r):
        here, up, down = pl.ds(PAD + r, ROWS), pl.ds(PAD + r - 1, ROWS), pl.ds(PAD + r + 1, ROWS)
        sxy, sxz = S[XY, 0, here], S[XZ, 0, here]
        V[VX, 0, here] = (
            V[VX, 0, here]
            + b * (S[XX, 1, here] - S[XX, 0, here] + sxy - S[XY, 0, up] + sxz)
            - b0 * before(sxz)
        )
        syz, szz = S[YZ, 1, here], S[ZZ, 1, here]
        V[VY, 1, here] = (
            V[VY, 1, here]
            + b * (S[XY, 1, here] - sxy + S[YY, 1, down] - S[YY, 1, here] + syz)
            - b0 * before(syz)
        )
        V[VZ, 1, here] = (
            V[VZ, 1, here]
            + b * (S[XZ, 1, here] - sxz + syz - S[YZ, 1, up] - szz)
            + b1 * after(szz)
        )

    over_rows(depth_rows, work)
    add_force(V, (VX, 0), force, (VX, 1), PAD + window)
    add_force(V, (VY, 1), force, (VY, 1), PAD + window)
    add_force(V, (VZ, 1), force, (VZ, 1), PAD + window)


def post(V, S, R, coef_ref, surface, cell, column, behind_x, ahead_y, ahead_z):
    m0, m1, lam, mu2, mu, k1, k2, k2h, l0 = coefs(
        coef_ref, (C_M0, C_M1, C_LAM, C_MU2, C_MU, C_K1, C_K2, C_K2H, C_L0)
    )

    def work(r):
        here, up, down = pl.ds(PAD + r, ROWS), pl.ds(PAD + r - 1, ROWS), pl.ds(PAD + r + 1, ROWS)
        out = pl.ds(r, ROWS)
        vx, vy, vz = V[VX, cell, here], V[VY, cell, here], V[VZ, cell, here]
        exx = vx - behind_x(r)
        eyy = vy - V[VY, cell, up]
        ezz = vz - m0 * before(vz)
        exy = V[VX, cell, down] - vx + (ahead_y(r) - vy)
        exz = m1 * after(vx) - vx + (ahead_z(r) - vz)
        eyz = m1 * after(vy) - vy + (V[VZ, cell, down] - vz)
        volume = lam * (exx + eyy + ezz)
        for comp, e in ((XX, exx), (YY, eyy), (ZZ, ezz)):
            old = R[comp, cell, out]
            new = S[comp, cell, here] + (volume + mu2 * e) + DT * old
            if comp == ZZ:
                new = new + l0 * lane_roll(surface[out, :], -column)
            S[comp, cell, here] = new
            R[comp, cell, out] = k1 * old - k2 * e
        for comp, e in ((XY, exy), (XZ, exz), (YZ, eyz)):
            old = R[comp, cell, out]
            S[comp, cell, here] = S[comp, cell, here] + mu * e + DT * old
            R[comp, cell, out] = k1 * old - k2h * e

    over_rows(R.shape[2], work)


def ahead_bond(V, S, R, coef_ref, force, surface, msg, G, step, window, has_ahead):
    (b,) = coefs(coef_ref, (C_B,))
    keep = jnp.where(has_ahead, 1.0, 0.0).astype(jnp.float32)

    def work(r):
        here, out = pl.ds(PAD + r, ROWS), pl.ds(r, ROWS)
        V[VX, 1, here] = V[VX, 1, here] + b * msg[0, out]
        G[0, out] = keep * (msg[1, out] - b * S[XY, 1, here])
        G[1, out] = keep * (msg[2, out] - b * S[XZ, 1, here])

    over_rows(R.shape[2], work)
    add_force(V, (VX, 1), force, (VX, 2), PAD + window)
    add_force(G, (0,), force, (VY, 2), window)
    add_force(G, (1,), force, (VZ, 2), window)
    post(
        V, S, R, coef_ref, surface, 1, 2 * step + 1,
        lambda r: V[VX, 0, pl.ds(PAD + r, ROWS)],
        lambda r: G[0, pl.ds(r, ROWS)],
        lambda r: G[1, pl.ds(r, ROWS)],
    )


def behind_bond(V, S, R, coef_ref, force, surface, msg, G, step, window, has_behind):
    (b,) = coefs(coef_ref, (C_B,))
    keep = jnp.where(has_behind, 1.0, 0.0).astype(jnp.float32)

    def work(r):
        here, out = pl.ds(PAD + r, ROWS), pl.ds(r, ROWS)
        V[VY, 0, here] = V[VY, 0, here] - b * msg[0, out]
        V[VZ, 0, here] = V[VZ, 0, here] - b * msg[1, out]
        G[0, out] = keep * (msg[2, out] + b * S[XX, 0, here])

    over_rows(R.shape[2], work)
    add_force(V, (VY, 0), force, (VY, 0), PAD + window)
    add_force(V, (VZ, 0), force, (VZ, 0), PAD + window)
    add_force(G, (0,), force, (VX, 0), window)
    post(
        V, S, R, coef_ref, surface, 0, 2 * step,
        lambda r: G[0, pl.ds(r, ROWS)],
        lambda r: V[VY, 1, pl.ds(PAD + r, ROWS)],
        lambda r: V[VZ, 1, pl.ds(PAD + r, ROWS)],
    )


def start_kernel(
    velocity, stress, layer_ref, lam, mu, buoy, rate, defect,
    V, S, coef_ref, msg_near, msg_far, sems,
):
    across = velocity.shape[2]
    inside = pl.ds(PAD, across)
    load_v = pltpu.make_async_copy(velocity, V.at[:, :, inside], sems.at[0])
    load_s = pltpu.make_async_copy(stress, S.at[:, :, inside], sems.at[1])
    load_v.start()
    load_s.start()
    edge = jnp.zeros((PAD, V.shape[3]), jnp.float32)
    for ref in (V, S):
        for comp in range(ref.shape[0]):
            for cell in range(ref.shape[1]):
                ref[comp, cell, pl.ds(0, PAD)] = edge
                ref[comp, cell, pl.ds(PAD + across, PAD)] = edge
    layer = layer_ref[...]

    def per_depth(table):
        row = jnp.zeros(layer.shape, jnp.float32)
        for level in range(table.shape[0]):
            row = jnp.where(layer == level, table[level], row)
        return row

    lane = lax.broadcasted_iota(jnp.int32, layer.shape, 1)
    not_first = jnp.where(lane > 0, 1.0, 0.0).astype(jnp.float32)
    not_last = jnp.where(lane < layer.shape[1] - 1, 1.0, 0.0).astype(jnp.float32)
    b = DT * per_depth(buoy)
    two_mu = (2.0 * DT) * per_depth(mu)
    decay = DT * per_depth(rate)
    drop = 2.0 * decay * per_depth(defect)
    for row, value in (
        (C_B, b),
        (C_B0, b * not_first),
        (C_B1, b * not_last),
        (C_M0, not_first),
        (C_M1, not_last),
        (C_LAM, DT * per_depth(lam)),
        (C_MU2, two_mu),
        (C_MU, 0.5 * two_mu),
        (C_K1, 1.0 - decay),
        (C_K2, drop),
        (C_K2H, 0.5 * drop),
        (C_L0, DT * (1.0 - not_first)),
    ):
        coef_ref[row : row + 1, :] = value
    coef_ref[12:16, :] = jnp.zeros((4, layer.shape[1]), jnp.float32)
    load_v.wait()
    load_s.wait()
    even, _, _ = place()

    @pl.when(even)
    def _():
        pre_ahead(V, S, coef_ref, msg_near)
        pre_behind(V, S, coef_ref, msg_far)

    @pl.when(jnp.logical_not(even))
    def _():
        pre_behind(V, S, coef_ref, msg_near)
        pre_ahead(V, S, coef_ref, msg_far)


def near_kernel(step, window, V0, S0, R0, coef_ref, force, surface, msg, V, S, R, *rest):
    G = rest[-1]
    even, has_behind, has_ahead = place()
    here = force.at[step]
    inner(V, S, coef_ref, here, window, R.shape[2])

    @pl.when(even)
    def _():
        ahead_bond(V, S, R, coef_ref, here, surface, msg, G, step, window, has_ahead)
        if step < STEPS - 1:
            pre_ahead(V, S, coef_ref, rest[0])

    @pl.when(jnp.logical_not(even))
    def _():
        behind_bond(V, S, R, coef_ref, here, surface, msg, G, step, window, has_behind)
        if step < STEPS - 1:
            pre_behind(V, S, coef_ref, rest[0])


def far_kernel(step, window, V0, S0, R0, coef_ref, force, surface, msg, V, S, R, *rest):
    G = rest[-1]
    even, has_behind, has_ahead = place()
    here = force.at[step]

    @pl.when(even)
    def _():
        behind_bond(V, S, R, coef_ref, here, surface, msg, G, step, window, has_behind)
        if step < STEPS - 1:
            pre_behind(V, S, coef_ref, rest[0])

    @pl.when(jnp.logical_not(even))
    def _():
        ahead_bond(V, S, R, coef_ref, here, surface, msg, G, step, window, has_ahead)
        if step < STEPS - 1:
            pre_ahead(V, S, coef_ref, rest[0])


def last_kernel(
    step, window, V0, S0, R0, coef_ref, force, surface, msg, V, S, R, v_out, s_out, r_out, G, sems
):
    even, has_behind, has_ahead = place()
    here = force.at[step]

    @pl.when(even)
    def _():
        behind_bond(V, S, R, coef_ref, here, surface, msg, G, step, window, has_behind)

    @pl.when(jnp.logical_not(even))
    def _():
        ahead_bond(V, S, R, coef_ref, here, surface, msg, G, step, window, has_ahead)

    inside = pl.ds(PAD, R.shape[2])
    copies = [
        pltpu.make_async_copy(V.at[:, :, inside], v_out, sems.at[0]),
        pltpu.make_async_copy(S.at[:, :, inside], s_out, sems.at[1]),
        pltpu.make_async_copy(R, r_out, sems.at[2]),
    ]
    for copy in copies:
        copy.start()
    for copy in copies:
        copy.wait()


def split_kernel(record, cells, out):
    tiles = out.shape[0]
    lanes = out.shape[2]
    pieces = record.shape[1] // lanes
    third = pieces // 3
    cell_of = cells[...]
    row = lax.broadcasted_iota(jnp.int32, (3 * tiles, cell_of.shape[1]), 0)
    first = lax.div(row, 3) * 2 + lax.rem(row, 3)
    hit_x = jnp.where(first - 1 == cell_of, 1.0, 0.0).astype(jnp.float32)
    hit_yz = jnp.where(first == cell_of, 1.0, 0.0).astype(jnp.float32)
    for m in range(pieces):
        panel = record[:, m * lanes : (m + 1) * lanes]
        part = jnp.dot(
            hit_x if m < third else hit_yz, panel,
            precision=lax.Precision.HIGHEST, preferred_element_type=jnp.float32,
        )
        for tile in range(tiles):
            out[tile, 3 * m : 3 * m + 3, :] = part[3 * tile : 3 * tile + 3, :]


def force_kernel(parts, force):
    steps, comps, cells = force.shape[:3]
    force[...] = jnp.zeros(force.shape, jnp.float32)
    per = parts.shape[1] // (comps * cells)
    lane = lax.broadcasted_iota(jnp.int32, (per, parts.shape[2]), 1)
    scale = jnp.where(lane < FZ, DT, 0.0).astype(jnp.float32)
    for s in range(steps):
        for comp in range(comps):
            for cell in range(cells):
                panel = parts[s, pl.ds(comp * per * cells + cell, per, stride=cells), :]
                force[s, comp, cell, pl.ds(4, per, stride=2), :] = scale * panel
                force[s, comp, cell, pl.ds(5, per, stride=2), :] = scale * lane_roll(panel, FZ)


def truck_kernel(slots, own, one, two, four, cells, out, table, rows_out):
    table[...] = jnp.zeros(table.shape, jnp.float32)
    rows = []
    for k in range(STEPS + 1):
        source, at = ((own, 0), (one, 0), (two, 0), (two, 1), (four, 0), (four, 1), (four, 2))[k]
        base = at * (slots + 8)
        rows.append(source[base : base + slots, :])
        table[8 * k : 8 * k + 8, :] = source[base + slots : base + slots + 8, :]
    table[8 * (STEPS + 1) : 8 * (STEPS + 1) + 8, :] = cells[...]
    columns = table[...].T
    rows_out[...] = jnp.zeros(rows_out.shape, jnp.float32)
    for s in range(STEPS):
        moved = []
        for k in range(STEPS - s):
            at = 8 * k + s
            entry = jnp.broadcast_to(columns[0:slots, at : at + 1], rows[k].shape)
            new = rows[k]
            for slot in range(slots):
                new = jnp.where(entry == float(slot), rows[k + 1][slot : slot + 1, :], new)
            moved.append(new)
        rows = moved
        at = 8 * (STEPS + 1) + s
        cell = jnp.broadcast_to(columns[0:slots, at : at + 1], rows[0].shape)
        for c in range(2):
            load = jnp.sum(jnp.where(cell == float(c), rows[0], 0.0), axis=0, keepdims=True)
            rows_out[2 * s + c : 2 * s + c + 1, :] = load
    out[...] = rows_out[...].T


def in_vmem(x):
    return pltpu.with_memory_space_constraint(x, pltpu.VMEM)


WHOLE = pl.BlockSpec(memory_space=pltpu.VMEM)
SCALARS = pl.BlockSpec(memory_space=pltpu.SMEM)
ANYWHERE = pl.BlockSpec(memory_space=pl.ANY)


def call(kernel, ins, specs, outs, out_specs, scratch=(), aliases=None, name=None):
    return pl.pallas_call(
        kernel,
        out_shape=outs,
        in_specs=specs,
        out_specs=out_specs,
        scratch_shapes=list(scratch),
        input_output_aliases=aliases or {},
        compiler_params=pltpu.CompilerParams(vmem_limit_bytes=VMEM_LIMIT),
        name=name,
    )(*ins)


def body(
    velocity, stress, memory, truck_loads, pier_panels,
    lame_lambda, lame_mu, buoyancy, relax_rate, defect_mu, layer,
    truck_entry, truck_cell, pier_cell,
):
    tiles = lax.axis_size("line")
    width_x, across, depth = velocity.shape[1:]
    slots = truck_loads.shape[0]
    window = (across - FY) // 2 - 4
    f32 = jnp.float32

    near = [(i, i ^ 1) for i in range(tiles) if (i ^ 1) < tiles]
    far = [(i, i + 1) for i in range(1, tiles - 1, 2)] + [(i + 1, i) for i in range(1, tiles - 1, 2)]

    def ahead_by(x, distance):
        return lax.ppermute(x, "line", [(i, i + distance) for i in range(tiles - distance)])

    padded = across + 2 * PAD
    v_type = pltpu.VMEM((3, width_x, padded, depth), f32)
    s_type = pltpu.VMEM((6, width_x, padded, depth), f32)
    r_type = pltpu.VMEM((6, width_x, across, depth), f32)
    c_type = pltpu.VMEM((N_COEF, depth), f32)
    m_type = pltpu.VMEM((3, across, depth), f32)

    V, S, coef, msg_near, msg_far = call(
        start_kernel,
        (velocity, stress, layer[None, :], lame_lambda, lame_mu, buoyancy, relax_rate, defect_mu),
        (ANYWHERE, ANYWHERE, WHOLE, SCALARS, SCALARS, SCALARS, SCALARS, SCALARS),
        (v_type, s_type, c_type, m_type, m_type),
        (WHOLE,) * 5,
        scratch=(pltpu.SemaphoreType.DMA((2,)),),
        name="start",
    )
    msg_far = lax.ppermute(msg_far, "line", far)
    msg_near = lax.ppermute(msg_near, "line", near)

    pieces = pier_panels.shape[2] // depth
    parts = call(
        split_kernel,
        (pier_panels[0], pier_cell[None, :]),
        (WHOLE, WHOLE),
        jax.ShapeDtypeStruct((tiles, 3 * pieces, depth), f32),
        WHOLE,
        name="split",
    )
    parts = lax.all_to_all(parts, "line", 0, 0, tiled=True)
    force = call(
        force_kernel,
        (parts[:STEPS],),
        (WHOLE,),
        pltpu.VMEM((STEPS, 3, 3, 16, depth), f32),
        WHOLE,
        name="force",
    )

    entries = jnp.pad(truck_entry.astype(f32), ((0, 8 - STEPS), (0, depth - slots)))
    cells = jnp.pad(truck_cell.astype(f32), ((0, 8 - STEPS), (0, depth - slots)))
    own = jnp.concatenate([truck_loads, entries], axis=0)
    one = ahead_by(own, 1)
    pair = jnp.concatenate([own, one], axis=0)
    two = ahead_by(pair, 2)
    four = ahead_by(jnp.concatenate([pair, two[: slots + 8]], axis=0), 4)
    surface = call(
        functools.partial(truck_kernel, slots),
        (own, one, two, four, cells),
        (WHOLE,) * 5,
        pltpu.VMEM((across, depth), f32),
        WHOLE,
        scratch=(pltpu.VMEM((depth, depth), f32), pltpu.VMEM((depth, across), f32)),
        name="trucks",
    )

    R = memory
    ghost = pltpu.VMEM((2, across, depth), f32)
    for step in range(STEPS):
        for far_side in (False, True):
            final = far_side and step == STEPS - 1
            sends = step < STEPS - 1
            ins = (V, S, R, coef, force, surface, msg_far if far_side else msg_near)
            ins = tuple(in_vmem(x) for x in ins)
            if final:
                return call(
                    functools.partial(last_kernel, step, window),
                    ins,
                    (WHOLE,) * len(ins),
                    (
                        v_type,
                        s_type,
                        r_type,
                        jax.ShapeDtypeStruct(velocity.shape, f32),
                        jax.ShapeDtypeStruct(stress.shape, f32),
                        jax.ShapeDtypeStruct(memory.shape, f32),
                    ),
                    (WHOLE,) * 3 + (ANYWHERE,) * 3,
                    scratch=(ghost, pltpu.SemaphoreType.DMA((3,))),
                    aliases={0: 0, 1: 1, 2: 2},
                    name="last",
                )[3:]
            outs = (v_type, s_type, r_type) + ((m_type,) if sends else ())
            kernel = far_kernel if far_side else near_kernel
            V, S, R, *msg = call(
                functools.partial(kernel, step, window),
                ins,
                (WHOLE,) * len(ins),
                outs,
                (WHOLE,) * len(outs),
                scratch=(ghost,),
                aliases={0: 0, 1: 1, 2: 2},
                name=("far" if far_side else "near") + str(step),
            )
            if sends and far_side:
                msg_far = lax.ppermute(msg[0], "line", far)
            elif sends:
                msg_near = lax.ppermute(msg[0], "line", near)


def solution(mesh):
    placed = (
        P(None, ("runs", "line"), None, None),
        P(None, ("runs", "line"), None, None),
        P(None, ("runs", "line"), None, None),
        P(("runs", "line"), None),
        P("line", "runs", None),
        P(),
        P(),
        P(),
        P(),
        P(),
        P(),
        P(None, ("runs", "line")),
        P(None, ("runs", "line")),
        P(),
    )
    return jax.shard_map(
        body,
        mesh=mesh,
        in_specs=placed,
        out_specs=(
            P(None, ("runs", "line"), None, None),
            P(None, ("runs", "line"), None, None),
            P(None, ("runs", "line"), None, None),
        ),
        check_vma=False,
    )
```

```python
import functools

import jax
import jax.numpy as jnp
import numpy as np
from jax import lax
from jax.experimental import pallas as pl
from jax.experimental.pallas import tpu as pltpu
from jax.sharding import PartitionSpec as P

STEPS = 6
FY = 8
FZ = 64
DT = 0.25
PAD = 8
ROWS = 16
UNROLL = 4
VMEM_LIMIT = 32 * 1024 * 1024

C_B, C_B0, C_B1, C_M0, C_M1, C_LAM, C_MU2, C_MU, C_K1, C_K2, C_K2H, C_L0 = range(12)
N_COEF = 16

VX, VY, VZ = range(3)
XX, YY, ZZ, XY, XZ, YZ = range(6)


def lane_roll(x, shift):
    return pltpu.roll(x, shift % x.shape[-1], x.ndim - 1)


def before(x):
    return lane_roll(x, 1)


def after(x):
    return lane_roll(x, -1)


def over_rows(count, work):
    def step(i, carry):
        work(pl.multiple_of(i * ROWS, ROWS))
        return carry

    lax.fori_loop(0, count // ROWS, step, 0, unroll=UNROLL)


def coefs(coef_ref, ids):
    return [coef_ref[i : i + 1, :] for i in ids]


def place():
    index = lax.axis_index("line")
    return lax.rem(index, 2) == 0, index > 0, index < lax.axis_size("line") - 1


def spans(r):
    return pl.ds(PAD + r, ROWS), pl.ds(PAD + r - 1, ROWS), pl.ds(PAD + r + 1, ROWS), pl.ds(r, ROWS)


def zero_edges(ref):
    across = ref.shape[-2] - 2 * PAD
    edge = jnp.zeros((PAD, ref.shape[-1]), jnp.float32)
    for where in np.ndindex(*ref.shape[:-2]):
        ref[(*where, pl.ds(0, PAD))] = edge
        ref[(*where, pl.ds(PAD + across, PAD))] = edge


def add_force(ref, index, force, which, first_row):
    rows = pl.ds(first_row, 16)
    ref[(*index, rows)] = ref[(*index, rows)] + force[which]


def pre_ahead(V, S, coef_ref, msg, force, window):
    b, b0 = coefs(coef_ref, (C_B, C_B0))

    def work(r):
        here, up, _, out = spans(r)
        sxy, sxz = S[XY, 1, here], S[XZ, 1, here]
        px = V[VX, 1, here] + b * (sxy - S[XY, 1, up] + sxz - S[XX, 1, here]) - b0 * before(sxz)
        V[VX, 1, here] = px
        if msg is not None:
            msg[0, out] = sxy
            msg[1, out] = sxz
            msg[2, out] = px

    over_rows(V.shape[2] - 2 * PAD, work)
    if force is not None:
        add_force(V, (VX, 1), force, (VX, 2), PAD + window)
        if msg is not None:
            add_force(msg, (2,), force, (VX, 2), window)


def pre_behind(V, S, coef_ref, msg, force, window):
    b, b0, b1 = coefs(coef_ref, (C_B, C_B0, C_B1))

    def work(r):
        here, up, down, out = spans(r)
        syz, szz = S[YZ, 0, here], S[ZZ, 0, here]
        qy = V[VY, 0, here] + b * (S[XY, 0, here] + S[YY, 0, down] - S[YY, 0, here] + syz) - b0 * before(syz)
        qz = V[VZ, 0, here] + b * (S[XZ, 0, here] + syz - S[YZ, 0, up] - szz) + b1 * after(szz)
        V[VY, 0, here] = qy
        V[VZ, 0, here] = qz
        if msg is not None:
            msg[0, out] = S[XX, 0, here]
            msg[1, out] = qy
            msg[2, out] = qz

    over_rows(V.shape[2] - 2 * PAD, work)
    if force is not None:
        add_force(V, (VY, 0), force, (VY, 0), PAD + window)
        add_force(V, (VZ, 0), force, (VZ, 0), PAD + window)
        if msg is not None:
            add_force(msg, (1,), force, (VY, 0), window)
            add_force(msg, (2,), force, (VZ, 0), window)


def inner(V, S, coef_ref, force, window):
    b, b0, b1 = coefs(coef_ref, (C_B, C_B0, C_B1))

    def work(r):
        here, up, down, _ = spans(r)
        sxy, sxz = S[XY, 0, here], S[XZ, 0, here]
        V[VX, 0, here] = (
            V[VX, 0, here]
            + b * (S[XX, 1, here] - S[XX, 0, here] + sxy - S[XY, 0, up] + sxz)
            - b0 * before(sxz)
        )
        syz, szz = S[YZ, 1, here], S[ZZ, 1, here]
        V[VY, 1, here] = (
            V[VY, 1, here]
            + b * (S[XY, 1, here] - sxy + S[YY, 1, down] - S[YY, 1, here] + syz)
            - b0 * before(syz)
        )
        V[VZ, 1, here] = (
            V[VZ, 1, here]
            + b * (S[XZ, 1, here] - sxz + syz - S[YZ, 1, up] - szz)
            + b1 * after(szz)
        )

    over_rows(V.shape[2] - 2 * PAD, work)
    add_force(V, (VX, 0), force, (VX, 1), PAD + window)
    add_force(V, (VY, 1), force, (VY, 1), PAD + window)
    add_force(V, (VZ, 1), force, (VZ, 1), PAD + window)


def post(V, S, R, coef_ref, surface, cell, column, behind_x, ahead_y, ahead_z):
    m0, m1, lam, mu2, mu, k1, k2, k2h, l0 = coefs(
        coef_ref, (C_M0, C_M1, C_LAM, C_MU2, C_MU, C_K1, C_K2, C_K2H, C_L0)
    )

    def work(r):
        here, up, down, out = spans(r)
        vx, vy, vz = V[VX, cell, here], V[VY, cell, here], V[VZ, cell, here]
        exx = vx - behind_x(r)
        eyy = vy - V[VY, cell, up]
        ezz = vz - m0 * before(vz)
        exy = V[VX, cell, down] - vx + (ahead_y(r) - vy)
        exz = m1 * after(vx) - vx + (ahead_z(r) - vz)
        eyz = m1 * after(vy) - vy + (V[VZ, cell, down] - vz)
        volume = lam * (exx + eyy + ezz)
        for comp, e in ((XX, exx), (YY, eyy), (ZZ, ezz)):
            old = R[comp, cell, out]
            new = S[comp, cell, here] + (volume + mu2 * e) + DT * old
            if comp == ZZ:
                new = new + l0 * lane_roll(surface[out, :], -column)
            S[comp, cell, here] = new
            R[comp, cell, out] = k1 * old - k2 * e
        for comp, e in ((XY, exy), (XZ, exz), (YZ, eyz)):
            old = R[comp, cell, out]
            S[comp, cell, here] = S[comp, cell, here] + mu * e + DT * old
            R[comp, cell, out] = k1 * old - k2h * e

    over_rows(R.shape[2], work)


def response_behind(V, S, coef_ref, D, W):
    b, b0, b1, m0, m1, lam, mu2, mu = coefs(coef_ref, (C_B, C_B0, C_B1, C_M0, C_M1, C_LAM, C_MU2, C_MU))

    def work(r):
        here, up, down, out = spans(r)
        sxy = S[XY, 1, here]
        vy, vz = -b * sxy, -b * S[XZ, 1, here]
        exx = -V[VX, 1, here]
        eyy = b * (S[XY, 1, up] - sxy)
        ezz = vz - m0 * before(vz)
        volume = lam * (exx + eyy + ezz)
        dyy, dzz = volume + mu2 * eyy, volume + mu2 * ezz
        dyz = mu * (m1 * after(vy) - vy - b * S[XZ, 1, down] - vz)
        W[0, here] = dyy
        W[1, here] = dyz
        D[0, out] = volume + mu2 * exx
        D[1, out] = vy + b * (dyz - mu * vy - dyy) - b0 * before(dyz)
        D[2, out] = vz + b * (dyz - mu * vz - dzz) + b1 * after(dzz)

    over_rows(D.shape[1], work)

    def rest(r):
        _, up, down, out = spans(r)
        D[1, out] = D[1, out] + b * W[0, down]
        D[2, out] = D[2, out] - b * W[1, up]

    over_rows(D.shape[1], rest)


def response_ahead(V, S, coef_ref, D, W):
    b, b0, m1, lam, mu2, mu = coefs(coef_ref, (C_B, C_B0, C_M1, C_LAM, C_MU2, C_MU))

    def work(r):
        here, _, down, out = spans(r)
        vx = b * S[XX, 0, here]
        dxy = mu * (b * S[XX, 0, down] - vx + V[VY, 0, here])
        dxz = mu * (m1 * after(vx) - vx + V[VZ, 0, here])
        W[0, here] = dxy
        D[0, out] = dxy
        D[1, out] = dxz
        D[2, out] = vx + b * (dxy + dxz - (lam + mu2) * vx) - b0 * before(dxz)

    over_rows(D.shape[1], work)

    def rest(r):
        _, up, _, out = spans(r)
        D[2, out] = D[2, out] - b * W[0, up]

    over_rows(D.shape[1], rest)


def early_ahead(V, S, R, coef_ref, msg, W, force, window):
    b, b0, m0, m1, lam, mu2, mu = coefs(coef_ref, (C_B, C_B0, C_M0, C_M1, C_LAM, C_MU2, C_MU))

    def work(r):
        here, up, down, out = spans(r)
        vx, vy, vz = V[VX, 1, here], V[VY, 1, here], V[VZ, 1, here]
        exx = vx - V[VX, 0, here]
        volume = lam * (exx + (vy - V[VY, 1, up]) + (vz - m0 * before(vz)))
        sxx = S[XX, 1, here] + (volume + mu2 * exx) + DT * R[XX, 1, out]
        sxy = S[XY, 1, here] + mu * (V[VX, 1, down] - vx - vy) + DT * R[XY, 1, out]
        sxz = S[XZ, 1, here] + mu * (m1 * after(vx) - vx - vz) + DT * R[XZ, 1, out]
        W[0, here] = sxy
        msg[0, out] = sxy
        msg[1, out] = sxz
        msg[2, out] = vx + b * (sxy + sxz - sxx) - b0 * before(sxz)

    over_rows(msg.shape[1], work)

    def rest(r):
        _, up, _, out = spans(r)
        msg[2, out] = msg[2, out] - b * W[0, up]

    over_rows(msg.shape[1], rest)
    add_force(msg, (2,), force, (VX, 2), window)


def early_behind(V, S, R, coef_ref, surface, column, msg, W, force, window):
    b, b0, b1, m0, m1, lam, mu2, mu, l0 = coefs(
        coef_ref, (C_B, C_B0, C_B1, C_M0, C_M1, C_LAM, C_MU2, C_MU, C_L0)
    )

    def work(r):
        here, up, down, out = spans(r)
        vx, vy, vz = V[VX, 0, here], V[VY, 0, here], V[VZ, 0, here]
        eyy = vy - V[VY, 0, up]
        ezz = vz - m0 * before(vz)
        volume = lam * (vx + eyy + ezz)
        sxx = S[XX, 0, here] + (volume + mu2 * vx) + DT * R[XX, 0, out]
        syy = S[YY, 0, here] + (volume + mu2 * eyy) + DT * R[YY, 0, out]
        szz = S[ZZ, 0, here] + (volume + mu2 * ezz) + DT * R[ZZ, 0, out]
        szz = szz + l0 * lane_roll(surface[out, :], -column)
        sxy = S[XY, 0, here] + mu * (V[VX, 0, down] - vx + (V[VY, 1, here] - vy)) + DT * R[XY, 0, out]
        sxz = S[XZ, 0, here] + mu * (m1 * after(vx) - vx + (V[VZ, 1, here] - vz)) + DT * R[XZ, 0, out]
        syz = S[YZ, 0, here] + mu * (m1 * after(vy) - vy + (V[VZ, 0, down] - vz)) + DT * R[YZ, 0, out]
        W[0, here] = syy
        W[1, here] = syz
        msg[0, out] = sxx
        msg[1, out] = vy + b * (sxy - syy + syz) - b0 * before(syz)
        msg[2, out] = vz + b * (sxz + syz - szz) + b1 * after(szz)

    over_rows(msg.shape[1], work)

    def rest(r):
        _, up, down, out = spans(r)
        msg[1, out] = msg[1, out] + b * W[0, down]
        msg[2, out] = msg[2, out] - b * W[1, up]

    over_rows(msg.shape[1], rest)
    add_force(msg, (1,), force, (VY, 0), window)
    add_force(msg, (2,), force, (VZ, 0), window)


def ahead_bond(V, S, R, coef_ref, force, surface, msg, missing, G, step, window, respond=None):
    (b,) = coefs(coef_ref, (C_B,))
    _, _, has_ahead = place()
    keep = jnp.where(has_ahead, 1.0, 0.0).astype(jnp.float32)

    def got(i, out):
        return msg[i, out] if missing is None else msg[i, out] + missing[i, out]

    def work(r):
        here, _, _, out = spans(r)
        V[VX, 1, here] = V[VX, 1, here] + (keep * b) * got(0, out)
        G[0, out] = keep * (got(1, out) - b * S[XY, 1, here])
        G[1, out] = keep * (got(2, out) - b * S[XZ, 1, here])

    over_rows(R.shape[2], work)
    if step == 0:
        add_force(G, (0,), force, (VY, 2), window)
        add_force(G, (1,), force, (VZ, 2), window)
    if respond is not None:
        respond()
    post(
        V, S, R, coef_ref, surface, 1, 2 * step + 1,
        lambda r: V[VX, 0, pl.ds(PAD + r, ROWS)],
        lambda r: G[0, pl.ds(r, ROWS)],
        lambda r: G[1, pl.ds(r, ROWS)],
    )


def behind_bond(V, S, R, coef_ref, force, surface, msg, missing, G, step, window, respond=None):
    (b,) = coefs(coef_ref, (C_B,))
    _, has_behind, _ = place()
    keep = jnp.where(has_behind, 1.0, 0.0).astype(jnp.float32)

    def got(i, out):
        return msg[i, out] if missing is None else msg[i, out] + missing[i, out]

    def work(r):
        here, _, _, out = spans(r)
        V[VY, 0, here] = V[VY, 0, here] - (keep * b) * got(0, out)
        V[VZ, 0, here] = V[VZ, 0, here] - (keep * b) * got(1, out)
        G[0, out] = keep * (got(2, out) + b * S[XX, 0, here])

    over_rows(R.shape[2], work)
    if step == 0:
        add_force(G, (0,), force, (VX, 0), window)
    if respond is not None:
        respond()
    post(
        V, S, R, coef_ref, surface, 0, 2 * step,
        lambda r: G[0, pl.ds(r, ROWS)],
        lambda r: V[VY, 1, pl.ds(PAD + r, ROWS)],
        lambda r: V[VZ, 1, pl.ds(PAD + r, ROWS)],
    )


def start_kernel(
    velocity, stress, memory, layer_ref, lam, mu, buoy, rate, defect,
    V, S, R, coef_ref, msg_near, msg_far, sems,
):
    across = velocity.shape[2]
    inside = pl.ds(PAD, across)
    copies = [pltpu.make_async_copy(stress.at[i], S.at[i, :, inside], sems.at[i]) for i in range(6)]
    copies += [pltpu.make_async_copy(velocity.at[i], V.at[i, :, inside], sems.at[6 + i]) for i in range(3)]
    late = [pltpu.make_async_copy(memory.at[i], R.at[i], sems.at[9 + i]) for i in range(6)]
    for copy in copies + late:
        copy.start()
    zero_edges(V)
    zero_edges(S)
    layer = layer_ref[...]

    def per_depth(table):
        row = jnp.zeros(layer.shape, jnp.float32)
        for level in range(table.shape[0]):
            row = jnp.where(layer == level, table[level], row)
        return row

    lane = lax.broadcasted_iota(jnp.int32, layer.shape, 1)
    not_first = jnp.where(lane > 0, 1.0, 0.0).astype(jnp.float32)
    not_last = jnp.where(lane < layer.shape[1] - 1, 1.0, 0.0).astype(jnp.float32)
    b = DT * per_depth(buoy)
    two_mu = (2.0 * DT) * per_depth(mu)
    decay = DT * per_depth(rate)
    drop = 2.0 * decay * per_depth(defect)
    for row, value in (
        (C_B, b),
        (C_B0, b * not_first),
        (C_B1, b * not_last),
        (C_M0, not_first),
        (C_M1, not_last),
        (C_LAM, DT * per_depth(lam)),
        (C_MU2, two_mu),
        (C_MU, 0.5 * two_mu),
        (C_K1, 1.0 - decay),
        (C_K2, drop),
        (C_K2H, 0.5 * drop),
        (C_L0, DT * (1.0 - not_first)),
    ):
        coef_ref[row : row + 1, :] = value
    coef_ref[12:16, :] = jnp.zeros((4, layer.shape[1]), jnp.float32)
    for copy in copies:
        copy.wait()
    even, _, _ = place()

    @pl.when(even)
    def _():
        pre_ahead(V, S, coef_ref, msg_near, None, 0)
        pre_behind(V, S, coef_ref, msg_far, None, 0)

    @pl.when(jnp.logical_not(even))
    def _():
        pre_behind(V, S, coef_ref, msg_near, None, 0)
        pre_ahead(V, S, coef_ref, msg_far, None, 0)

    for copy in late:
        copy.wait()


def first_kernel(window, V0, S, R, coef_ref, force, surface, V, msg, W):
    even, _, _ = place()
    zero_edges(W)
    now, then = force.at[0], force.at[1]
    add_force(V, (VX, 1), now, (VX, 2), PAD + window)
    add_force(V, (VY, 0), now, (VY, 0), PAD + window)
    add_force(V, (VZ, 0), now, (VZ, 0), PAD + window)
    inner(V, S, coef_ref, now, window)

    @pl.when(even)
    def _():
        early_behind(V, S, R, coef_ref, surface, 0, msg, W, then, window)

    @pl.when(jnp.logical_not(even))
    def _():
        early_ahead(V, S, R, coef_ref, msg, W, then, window)


def near_kernel(step, window, V0, S0, R0, coef_ref, force, surface, msg, V, S, R, *rest):
    G = rest[-1]
    even, _, _ = place()
    more = step < STEPS - 1

    @pl.when(even)
    def _():
        ahead_bond(V, S, R, coef_ref, force.at[step], surface, msg, None, G, step, window)
        if more:
            pre_ahead(V, S, coef_ref, rest[0], force.at[step + 1], window)

    @pl.when(jnp.logical_not(even))
    def _():
        behind_bond(V, S, R, coef_ref, force.at[step], surface, msg, None, G, step, window)
        if more:
            pre_behind(V, S, coef_ref, rest[0], force.at[step + 1], window)


def far_kernel(step, window, V0, S0, R0, coef_ref, force, surface, msg, *rest):
    rest = list(rest)
    missing = rest.pop(0) if step > 0 else None
    V, S, R, D = rest[:4]
    G, W = rest[-2:]
    early = rest[4] if step < STEPS - 2 else None
    even, _, _ = place()
    zero_edges(W)
    here, then = force.at[step], force.at[step + 1]

    @pl.when(even)
    def _():
        behind_bond(
            V, S, R, coef_ref, here, surface, msg, missing, G, step, window,
            lambda: response_ahead(V, S, coef_ref, D, W),
        )
        pre_behind(V, S, coef_ref, None, then, window)

    @pl.when(jnp.logical_not(even))
    def _():
        ahead_bond(
            V, S, R, coef_ref, here, surface, msg, missing, G, step, window,
            lambda: response_behind(V, S, coef_ref, D, W),
        )
        pre_ahead(V, S, coef_ref, None, then, window)

    inner(V, S, coef_ref, then, window)
    if early is not None:
        later = force.at[step + 2]

        @pl.when(even)
        def _():
            early_behind(V, S, R, coef_ref, surface, 2 * (step + 1), early, W, later, window)

        @pl.when(jnp.logical_not(even))
        def _():
            early_ahead(V, S, R, coef_ref, early, W, later, window)


def last_kernel(
    step, window, V0, S0, R0, coef_ref, force, surface, msg, missing, V, S, R, v_out, s_out, r_out, G, sems
):
    even, _, _ = place()
    here = force.at[step]
    inside = pl.ds(PAD, R.shape[2])

    def copies(cell):
        return [
            pltpu.make_async_copy(V.at[:, cell, inside], v_out.at[:, cell], sems.at[cell, 0]),
            pltpu.make_async_copy(S.at[:, cell, inside], s_out.at[:, cell], sems.at[cell, 1]),
            pltpu.make_async_copy(R.at[:, cell], r_out.at[:, cell], sems.at[cell, 2]),
        ]

    def finish(cell, bond):
        done, other = copies(1 - cell), copies(cell)
        for copy in done:
            copy.start()
        bond(V, S, R, coef_ref, here, surface, msg, missing, G, step, window)
        for copy in other:
            copy.start()
        for copy in done + other:
            copy.wait()

    @pl.when(even)
    def _():
        finish(0, behind_bond)

    @pl.when(jnp.logical_not(even))
    def _():
        finish(1, ahead_bond)


ENTRY_ROW, TRUCK_ROW = 36, 40


def lane_blocks(table, width):
    return sum(lane_roll(table[s : s + 1, :], s * width) for s in range(STEPS))


def split_kernel(record, cells, loads, entries, out):
    tiles, _, lanes = out.shape
    slots = loads.shape[0]
    pieces = record.shape[1] // lanes
    third = pieces // 3
    cell_of = cells[...]
    row = lax.broadcasted_iota(jnp.int32, (3 * tiles, cell_of.shape[1]), 0)
    first = lax.div(row, 3) * 2 + lax.rem(row, 3)

    def share(cell, columns):
        hit = jnp.where(cell == cell_of, 1.0, 0.0).astype(jnp.float32)
        return jnp.dot(
            hit, record[:, columns], precision=lax.Precision.HIGHEST, preferred_element_type=jnp.float32
        )

    part_x = share(first - 1, slice(0, third * lanes))
    part_yz = share(first, slice(third * lanes, pieces * lanes))
    rows, entry = loads[...], lane_blocks(entries[...], slots)
    for tile in range(tiles):
        mine = slice(3 * tile, 3 * tile + 3)
        for m in range(pieces):
            part, at = (part_x, m) if m < third else (part_yz, m - third)
            out[tile, 3 * m : 3 * m + 3, :] = part[mine, at * lanes : (at + 1) * lanes]
        out[tile, ENTRY_ROW : ENTRY_ROW + 1, :] = entry
        out[tile, TRUCK_ROW : TRUCK_ROW + slots, :] = rows


def prepare_kernel(parts, loads, entries, cells, force, surface, table, rows_out):
    steps, comps, width = force.shape[:3]
    lanes = parts.shape[2]
    force[...] = jnp.zeros(force.shape, jnp.float32)
    per = ENTRY_ROW // (comps * width)
    lane = lax.broadcasted_iota(jnp.int32, (per, lanes), 1)
    scale = jnp.where(lane < FZ, DT, 0.0).astype(jnp.float32)
    for s in range(steps):
        for comp in range(comps):
            for cell in range(width):
                panel = parts[s, pl.ds(comp * per * width + cell, per, stride=width), :]
                force[s, comp, cell, pl.ds(4, per, stride=2), :] = scale * panel
                force[s, comp, cell, pl.ds(5, per, stride=2), :] = scale * lane_roll(panel, FZ)

    slots = loads.shape[0]
    me = lax.axis_index("line")
    table[...] = jnp.zeros(table.shape, jnp.float32)
    table[0:1, :] = lane_blocks(entries[...], slots)
    table[STEPS + 1 : STEPS + 2, :] = lane_blocks(cells[...], slots)
    rows = [loads[...]]
    for k in range(1, STEPS + 1):
        source = jnp.maximum(me - k, 0)
        there = jnp.where(me >= k, 1.0, 0.0).astype(jnp.float32)
        rows.append(there * parts[source, TRUCK_ROW : TRUCK_ROW + slots, :])
        table[k : k + 1, :] = parts[source, ENTRY_ROW : ENTRY_ROW + 1, :]
    columns = table[...].T
    rows_out[...] = jnp.zeros(rows_out.shape, jnp.float32)
    for s in range(STEPS):
        block = slice(s * slots, (s + 1) * slots)
        moved = []
        for k in range(STEPS - s):
            entry = jnp.broadcast_to(columns[block, k : k + 1], rows[k].shape)
            new = rows[k]
            for slot in range(slots):
                new = jnp.where(entry == float(slot), rows[k + 1][slot : slot + 1, :], new)
            moved.append(new)
        rows = moved
        cell = jnp.broadcast_to(columns[block, STEPS + 1 : STEPS + 2], rows[0].shape)
        for c in range(2):
            load = jnp.sum(jnp.where(cell == float(c), rows[0], 0.0), axis=0, keepdims=True)
            rows_out[2 * s + c : 2 * s + c + 1, :] = load
    surface[...] = rows_out[...].T


def in_vmem(x):
    return pltpu.with_memory_space_constraint(x, pltpu.VMEM)


WHOLE = pl.BlockSpec(memory_space=pltpu.VMEM)
SCALARS = pl.BlockSpec(memory_space=pltpu.SMEM)
ANYWHERE = pl.BlockSpec(memory_space=pl.ANY)


def call(kernel, ins, specs, outs, out_specs, scratch=(), aliases=None, name=None):
    size = sum(x.size * 4 for x in ins)
    return pl.pallas_call(
        kernel,
        out_shape=outs,
        in_specs=specs,
        out_specs=out_specs,
        scratch_shapes=list(scratch),
        input_output_aliases=aliases or {},
        compiler_params=pltpu.CompilerParams(vmem_limit_bytes=VMEM_LIMIT),
        cost_estimate=pl.CostEstimate(flops=8 * size, bytes_accessed=2 * size, transcendentals=0),
        name=name,
    )(*ins)


def body(
    velocity, stress, memory, truck_loads, pier_panels,
    lame_lambda, lame_mu, buoyancy, relax_rate, defect_mu, layer,
    truck_entry, truck_cell, pier_cell,
):
    tiles = lax.axis_size("line")
    width_x, across, depth = velocity.shape[1:]
    slots = truck_loads.shape[0]
    window = (across - FY) // 2 - 4
    f32 = jnp.float32

    near = [(i, i ^ 1) for i in range(tiles) if (i ^ 1) < tiles]
    far = [(i, i + 1) for i in range(1, tiles - 1, 2)] + [(i + 1, i) for i in range(1, tiles - 1, 2)]

    padded = across + 2 * PAD
    v_type = pltpu.VMEM((3, width_x, padded, depth), f32)
    s_type = pltpu.VMEM((6, width_x, padded, depth), f32)
    r_type = pltpu.VMEM((6, width_x, across, depth), f32)
    c_type = pltpu.VMEM((N_COEF, depth), f32)
    m_type = pltpu.VMEM((3, across, depth), f32)
    ghost = pltpu.VMEM((2, across, depth), f32)
    work = pltpu.VMEM((2, padded, depth), f32)

    def as_rows(table):
        return jnp.pad(table.astype(f32), ((0, 8 - STEPS), (0, depth - slots)))

    entries, cells = as_rows(truck_entry), as_rows(truck_cell)
    parts = call(
        split_kernel,
        (pier_panels[0], pier_cell[None, :], truck_loads, entries),
        (WHOLE,) * 4,
        jax.ShapeDtypeStruct((tiles, TRUCK_ROW + slots, depth), f32),
        WHOLE,
        name="split",
    )
    parts = lax.all_to_all(parts, "line", 0, 0, tiled=True)

    V, S, R, coef, msg_near, msg_far = call(
        start_kernel,
        (
            *(pltpu.with_memory_space_constraint(x, pltpu.HBM) for x in (velocity, stress, memory)),
            layer[None, :], lame_lambda, lame_mu, buoyancy, relax_rate, defect_mu,
        ),
        (ANYWHERE,) * 3 + (WHOLE,) + (SCALARS,) * 5,
        (v_type, s_type, r_type, c_type, m_type, m_type),
        (WHOLE,) * 6,
        scratch=(pltpu.SemaphoreType.DMA((15,)),),
        name="start",
    )
    msg_far = lax.ppermute(msg_far, "line", far)
    msg_near = lax.ppermute(msg_near, "line", near)

    force, surface = call(
        prepare_kernel,
        (parts, truck_loads, entries, cells),
        (WHOLE,) * 4,
        (pltpu.VMEM((STEPS, 3, 3, 16, depth), f32), pltpu.VMEM((across, depth), f32)),
        (WHOLE,) * 2,
        scratch=(pltpu.VMEM((depth, depth), f32), pltpu.VMEM((depth, across), f32)),
        name="prepare",
    )
    V, early = call(
        functools.partial(first_kernel, window),
        tuple(in_vmem(x) for x in (V, S, R, coef, force, surface)),
        (WHOLE,) * 6,
        (v_type, m_type),
        (WHOLE,) * 2,
        scratch=(work,),
        aliases={0: 0},
        name="first",
    )
    early = lax.ppermute(early, "line", far)
    state = (v_type, s_type, r_type)
    same = {0: 0, 1: 1, 2: 2}
    missing = None
    for step in range(STEPS):
        more = step < STEPS - 1
        ins = tuple(in_vmem(x) for x in (V, S, R, coef, force, surface, msg_near))
        outs = state + ((m_type,) if more else ())
        V, S, R, *msg = call(
            functools.partial(near_kernel, step, window),
            ins,
            (WHOLE,) * len(ins),
            outs,
            (WHOLE,) * len(outs),
            scratch=(ghost,),
            aliases=same,
            name="near" + str(step),
        )
        if more:
            msg_near = lax.ppermute(msg[0], "line", near)
        ins = (V, S, R, coef, force, surface, msg_far) + ((missing,) if step else ())
        ins = tuple(in_vmem(x) for x in ins)
        if more:
            outs = state + (m_type,) + ((m_type,) if step < STEPS - 2 else ())
            V, S, R, missing, *msg = call(
                functools.partial(far_kernel, step, window),
                ins,
                (WHOLE,) * len(ins),
                outs,
                (WHOLE,) * len(outs),
                scratch=(ghost, work),
                aliases=same,
                name="far" + str(step),
            )
            msg_far = early
            if msg:
                early = lax.ppermute(msg[0], "line", far)
    results = call(
        functools.partial(last_kernel, STEPS - 1, window),
        ins,
        (WHOLE,) * len(ins),
        state + tuple(jax.ShapeDtypeStruct(x.shape, f32) for x in (velocity, stress, memory)),
        (WHOLE,) * 3 + (ANYWHERE,) * 3,
        scratch=(ghost, pltpu.SemaphoreType.DMA((2, 3))),
        aliases=same,
        name="last",
    )
    return results[3:]


def solution(mesh):
    placed = (
        P(None, ("runs", "line"), None, None),
        P(None, ("runs", "line"), None, None),
        P(None, ("runs", "line"), None, None),
        P(("runs", "line"), None),
        P("line", "runs", None),
        P(),
        P(),
        P(),
        P(),
        P(),
        P(),
        P(None, ("runs", "line")),
        P(None, ("runs", "line")),
        P(),
    )
    return jax.shard_map(
        body,
        mesh=mesh,
        in_specs=placed,
        out_specs=(
            P(None, ("runs", "line"), None, None),
            P(None, ("runs", "line"), None, None),
            P(None, ("runs", "line"), None, None),
        ),
        check_vma=False,
    )
```

```python
import functools

import jax
import jax.numpy as jnp
import numpy as np
from jax import lax
from jax.experimental import pallas as pl
from jax.experimental.pallas import tpu as pltpu
from jax.sharding import PartitionSpec as P

STEPS = 6
FY = 8
FZ = 64
DT = 0.25
PAD = 8
ROWS = 16
UNROLL = 4
VMEM_LIMIT = 32 * 1024 * 1024

C_B, C_B0, C_B1, C_M0, C_M1, C_LAM, C_MU2, C_MU, C_K1, C_K2, C_K2H, C_L0 = range(12)
N_COEF = 16

VX, VY, VZ = range(3)
XX, YY, ZZ, XY, XZ, YZ = range(6)


def lane_roll(x, shift):
    return pltpu.roll(x, shift % x.shape[-1], x.ndim - 1)


def before(x):
    return lane_roll(x, 1)


def after(x):
    return lane_roll(x, -1)


def over_rows(count, work):
    def step(i, carry):
        work(pl.multiple_of(i * ROWS, ROWS))
        return carry

    lax.fori_loop(0, count // ROWS, step, 0, unroll=UNROLL)


def coefs(coef_ref, ids):
    return [coef_ref[i : i + 1, :] for i in ids]


def place():
    index = lax.axis_index("line")
    return lax.rem(index, 2) == 0, index > 0, index < lax.axis_size("line") - 1


def spans(r):
    return pl.ds(PAD + r, ROWS), pl.ds(PAD + r - 1, ROWS), pl.ds(PAD + r + 1, ROWS), pl.ds(r, ROWS)


def zero_edges(ref):
    across = ref.shape[-2] - 2 * PAD
    edge = jnp.zeros((PAD, ref.shape[-1]), jnp.float32)
    for where in np.ndindex(*ref.shape[:-2]):
        ref[(*where, pl.ds(0, PAD))] = edge
        ref[(*where, pl.ds(PAD + across, PAD))] = edge


def add_force(ref, index, force, which, first_row):
    rows = pl.ds(first_row, 16)
    ref[(*index, rows)] = ref[(*index, rows)] + force[which]


def pre_ahead(V, S, coef_ref, msg, force, window):
    b, b0 = coefs(coef_ref, (C_B, C_B0))

    def work(r):
        here, up, _, out = spans(r)
        sxy, sxz = S[XY, 1, here], S[XZ, 1, here]
        px = V[VX, 1, here] + b * (sxy - S[XY, 1, up] + sxz - S[XX, 1, here]) - b0 * before(sxz)
        V[VX, 1, here] = px
        if msg is not None:
            msg[0, out] = sxy
            msg[1, out] = sxz
            msg[2, out] = px

    over_rows(V.shape[2] - 2 * PAD, work)
    if force is not None:
        add_force(V, (VX, 1), force, (VX, 2), PAD + window)
        if msg is not None:
            add_force(msg, (2,), force, (VX, 2), window)


def pre_behind(V, S, coef_ref, msg, force, window):
    b, b0, b1 = coefs(coef_ref, (C_B, C_B0, C_B1))

    def work(r):
        here, up, down, out = spans(r)
        syz, szz = S[YZ, 0, here], S[ZZ, 0, here]
        qy = V[VY, 0, here] + b * (S[XY, 0, here] + S[YY, 0, down] - S[YY, 0, here] + syz) - b0 * before(syz)
        qz = V[VZ, 0, here] + b * (S[XZ, 0, here] + syz - S[YZ, 0, up] - szz) + b1 * after(szz)
        V[VY, 0, here] = qy
        V[VZ, 0, here] = qz
        if msg is not None:
            msg[0, out] = S[XX, 0, here]
            msg[1, out] = qy
            msg[2, out] = qz

    over_rows(V.shape[2] - 2 * PAD, work)
    if force is not None:
        add_force(V, (VY, 0), force, (VY, 0), PAD + window)
        add_force(V, (VZ, 0), force, (VZ, 0), PAD + window)
        if msg is not None:
            add_force(msg, (1,), force, (VY, 0), window)
            add_force(msg, (2,), force, (VZ, 0), window)


def inner(V, S, coef_ref, force, window):
    b, b0, b1 = coefs(coef_ref, (C_B, C_B0, C_B1))

    def work(r):
        here, up, down, _ = spans(r)
        sxy, sxz = S[XY, 0, here], S[XZ, 0, here]
        V[VX, 0, here] = (
            V[VX, 0, here]
            + b * (S[XX, 1, here] - S[XX, 0, here] + sxy - S[XY, 0, up] + sxz)
            - b0 * before(sxz)
        )
        syz, szz = S[YZ, 1, here], S[ZZ, 1, here]
        V[VY, 1, here] = (
            V[VY, 1, here]
            + b * (S[XY, 1, here] - sxy + S[YY, 1, down] - S[YY, 1, here] + syz)
            - b0 * before(syz)
        )
        V[VZ, 1, here] = (
            V[VZ, 1, here]
            + b * (S[XZ, 1, here] - sxz + syz - S[YZ, 1, up] - szz)
            + b1 * after(szz)
        )

    over_rows(V.shape[2] - 2 * PAD, work)
    add_force(V, (VX, 0), force, (VX, 1), PAD + window)
    add_force(V, (VY, 1), force, (VY, 1), PAD + window)
    add_force(V, (VZ, 1), force, (VZ, 1), PAD + window)


def post(V, S, R, old_r, coef_ref, surface, cell, column, behind_x, ahead_y, ahead_z):
    m0, m1, lam, mu2, mu, k1, k2, k2h, l0 = coefs(
        coef_ref, (C_M0, C_M1, C_LAM, C_MU2, C_MU, C_K1, C_K2, C_K2H, C_L0)
    )

    def work(r):
        here, up, down, out = spans(r)
        vx, vy, vz = V[VX, cell, here], V[VY, cell, here], V[VZ, cell, here]
        exx = vx - behind_x(r)
        eyy = vy - V[VY, cell, up]
        ezz = vz - m0 * before(vz)
        exy = V[VX, cell, down] - vx + (ahead_y(r) - vy)
        exz = m1 * after(vx) - vx + (ahead_z(r) - vz)
        eyz = m1 * after(vy) - vy + (V[VZ, cell, down] - vz)
        volume = lam * (exx + eyy + ezz)
        for comp, e in ((XX, exx), (YY, eyy), (ZZ, ezz)):
            old = old_r[comp, cell, out]
            new = S[comp, cell, here] + (volume + mu2 * e) + DT * old
            if comp == ZZ:
                new = new + l0 * lane_roll(surface[out, :], -column)
            S[comp, cell, here] = new
            R[comp, cell, out] = k1 * old - k2 * e
        for comp, e in ((XY, exy), (XZ, exz), (YZ, eyz)):
            old = old_r[comp, cell, out]
            S[comp, cell, here] = S[comp, cell, here] + mu * e + DT * old
            R[comp, cell, out] = k1 * old - k2h * e

    over_rows(R.shape[2], work)


def response_behind(V, S, coef_ref, D, W):
    b, b0, b1, m0, m1, lam, mu2, mu = coefs(coef_ref, (C_B, C_B0, C_B1, C_M0, C_M1, C_LAM, C_MU2, C_MU))

    def work(r):
        here, up, down, out = spans(r)
        sxy = S[XY, 1, here]
        vy, vz = -b * sxy, -b * S[XZ, 1, here]
        exx = -V[VX, 1, here]
        eyy = b * (S[XY, 1, up] - sxy)
        ezz = vz - m0 * before(vz)
        volume = lam * (exx + eyy + ezz)
        dyy, dzz = volume + mu2 * eyy, volume + mu2 * ezz
        dyz = mu * (m1 * after(vy) - vy - b * S[XZ, 1, down] - vz)
        W[0, here] = dyy
        W[1, here] = dyz
        D[0, out] = volume + mu2 * exx
        D[1, out] = vy + b * (dyz - mu * vy - dyy) - b0 * before(dyz)
        D[2, out] = vz + b * (dyz - mu * vz - dzz) + b1 * after(dzz)

    over_rows(D.shape[1], work)

    def rest(r):
        _, up, down, out = spans(r)
        D[1, out] = D[1, out] + b * W[0, down]
        D[2, out] = D[2, out] - b * W[1, up]

    over_rows(D.shape[1], rest)


def response_ahead(V, S, coef_ref, D, W):
    b, b0, m1, lam, mu2, mu = coefs(coef_ref, (C_B, C_B0, C_M1, C_LAM, C_MU2, C_MU))

    def work(r):
        here, _, down, out = spans(r)
        vx = b * S[XX, 0, here]
        dxy = mu * (b * S[XX, 0, down] - vx + V[VY, 0, here])
        dxz = mu * (m1 * after(vx) - vx + V[VZ, 0, here])
        W[0, here] = dxy
        D[0, out] = dxy
        D[1, out] = dxz
        D[2, out] = vx + b * (dxy + dxz - (lam + mu2) * vx) - b0 * before(dxz)

    over_rows(D.shape[1], work)

    def rest(r):
        _, up, _, out = spans(r)
        D[2, out] = D[2, out] - b * W[0, up]

    over_rows(D.shape[1], rest)


def early_ahead(V, S, R, coef_ref, msg, W, force, window):
    b, b0, m0, m1, lam, mu2, mu = coefs(coef_ref, (C_B, C_B0, C_M0, C_M1, C_LAM, C_MU2, C_MU))

    def work(r):
        here, up, down, out = spans(r)
        vx, vy, vz = V[VX, 1, here], V[VY, 1, here], V[VZ, 1, here]
        exx = vx - V[VX, 0, here]
        volume = lam * (exx + (vy - V[VY, 1, up]) + (vz - m0 * before(vz)))
        sxx = S[XX, 1, here] + (volume + mu2 * exx) + DT * R[XX, 1, out]
        sxy = S[XY, 1, here] + mu * (V[VX, 1, down] - vx - vy) + DT * R[XY, 1, out]
        sxz = S[XZ, 1, here] + mu * (m1 * after(vx) - vx - vz) + DT * R[XZ, 1, out]
        W[0, here] = sxy
        msg[0, out] = sxy
        msg[1, out] = sxz
        msg[2, out] = vx + b * (sxy + sxz - sxx) - b0 * before(sxz)

    over_rows(msg.shape[1], work)

    def rest(r):
        _, up, _, out = spans(r)
        msg[2, out] = msg[2, out] - b * W[0, up]

    over_rows(msg.shape[1], rest)
    add_force(msg, (2,), force, (VX, 2), window)


def early_behind(V, S, R, coef_ref, surface, column, msg, W, force, window):
    b, b0, b1, m0, m1, lam, mu2, mu, l0 = coefs(
        coef_ref, (C_B, C_B0, C_B1, C_M0, C_M1, C_LAM, C_MU2, C_MU, C_L0)
    )

    def work(r):
        here, up, down, out = spans(r)
        vx, vy, vz = V[VX, 0, here], V[VY, 0, here], V[VZ, 0, here]
        eyy = vy - V[VY, 0, up]
        ezz = vz - m0 * before(vz)
        volume = lam * (vx + eyy + ezz)
        sxx = S[XX, 0, here] + (volume + mu2 * vx) + DT * R[XX, 0, out]
        syy = S[YY, 0, here] + (volume + mu2 * eyy) + DT * R[YY, 0, out]
        szz = S[ZZ, 0, here] + (volume + mu2 * ezz) + DT * R[ZZ, 0, out]
        szz = szz + l0 * lane_roll(surface[out, :], -column)
        sxy = S[XY, 0, here] + mu * (V[VX, 0, down] - vx + (V[VY, 1, here] - vy)) + DT * R[XY, 0, out]
        sxz = S[XZ, 0, here] + mu * (m1 * after(vx) - vx + (V[VZ, 1, here] - vz)) + DT * R[XZ, 0, out]
        syz = S[YZ, 0, here] + mu * (m1 * after(vy) - vy + (V[VZ, 0, down] - vz)) + DT * R[YZ, 0, out]
        W[0, here] = syy
        W[1, here] = syz
        msg[0, out] = sxx
        msg[1, out] = vy + b * (sxy - syy + syz) - b0 * before(syz)
        msg[2, out] = vz + b * (sxz + syz - szz) + b1 * after(szz)

    over_rows(msg.shape[1], work)

    def rest(r):
        _, up, down, out = spans(r)
        msg[1, out] = msg[1, out] + b * W[0, down]
        msg[2, out] = msg[2, out] - b * W[1, up]

    over_rows(msg.shape[1], rest)
    add_force(msg, (1,), force, (VY, 0), window)
    add_force(msg, (2,), force, (VZ, 0), window)


def ahead_bond(V, S, R, old_r, coef_ref, force, surface, msg, missing, G, step, window, respond=None):
    (b,) = coefs(coef_ref, (C_B,))
    _, _, has_ahead = place()
    keep = jnp.where(has_ahead, 1.0, 0.0).astype(jnp.float32)

    def got(i, out):
        return msg[i, out] if missing is None else msg[i, out] + missing[i, out]

    def work(r):
        here, _, _, out = spans(r)
        V[VX, 1, here] = V[VX, 1, here] + (keep * b) * got(0, out)
        G[0, out] = keep * (got(1, out) - b * S[XY, 1, here])
        G[1, out] = keep * (got(2, out) - b * S[XZ, 1, here])

    over_rows(R.shape[2], work)
    if step == 0:
        add_force(G, (0,), force, (VY, 2), window)
        add_force(G, (1,), force, (VZ, 2), window)
    if respond is not None:
        respond()
    post(
        V, S, R, old_r, coef_ref, surface, 1, 2 * step + 1,
        lambda r: V[VX, 0, pl.ds(PAD + r, ROWS)],
        lambda r: G[0, pl.ds(r, ROWS)],
        lambda r: G[1, pl.ds(r, ROWS)],
    )


def behind_bond(V, S, R, old_r, coef_ref, force, surface, msg, missing, G, step, window, respond=None):
    (b,) = coefs(coef_ref, (C_B,))
    _, has_behind, _ = place()
    keep = jnp.where(has_behind, 1.0, 0.0).astype(jnp.float32)

    def got(i, out):
        return msg[i, out] if missing is None else msg[i, out] + missing[i, out]

    def work(r):
        here, _, _, out = spans(r)
        V[VY, 0, here] = V[VY, 0, here] - (keep * b) * got(0, out)
        V[VZ, 0, here] = V[VZ, 0, here] - (keep * b) * got(1, out)
        G[0, out] = keep * (got(2, out) + b * S[XX, 0, here])

    over_rows(R.shape[2], work)
    if step == 0:
        add_force(G, (0,), force, (VX, 0), window)
    if respond is not None:
        respond()
    post(
        V, S, R, old_r, coef_ref, surface, 0, 2 * step,
        lambda r: G[0, pl.ds(r, ROWS)],
        lambda r: V[VY, 1, pl.ds(PAD + r, ROWS)],
        lambda r: V[VZ, 1, pl.ds(PAD + r, ROWS)],
    )


def start_kernel(
    velocity, stress, layer_ref, lam, mu, buoy, rate, defect, after_this, V, S, coef_ref, msg_near, msg_far
):
    del after_this
    zero_edges(V)
    zero_edges(S)

    def load(r):
        here, _, _, out = spans(r)
        for ref, source in ((V, velocity), (S, stress)):
            for where in np.ndindex(*source.shape[:2]):
                ref[(*where, here)] = source[(*where, out)]

    over_rows(velocity.shape[2], load)
    layer = layer_ref[...]

    def per_depth(table):
        row = jnp.zeros(layer.shape, jnp.float32)
        for level in range(table.shape[0]):
            row = jnp.where(layer == level, table[level], row)
        return row

    lane = lax.broadcasted_iota(jnp.int32, layer.shape, 1)
    not_first = jnp.where(lane > 0, 1.0, 0.0).astype(jnp.float32)
    not_last = jnp.where(lane < layer.shape[1] - 1, 1.0, 0.0).astype(jnp.float32)
    b = DT * per_depth(buoy)
    two_mu = (2.0 * DT) * per_depth(mu)
    decay = DT * per_depth(rate)
    drop = 2.0 * decay * per_depth(defect)
    for row, value in (
        (C_B, b),
        (C_B0, b * not_first),
        (C_B1, b * not_last),
        (C_M0, not_first),
        (C_M1, not_last),
        (C_LAM, DT * per_depth(lam)),
        (C_MU2, two_mu),
        (C_MU, 0.5 * two_mu),
        (C_K1, 1.0 - decay),
        (C_K2, drop),
        (C_K2H, 0.5 * drop),
        (C_L0, DT * (1.0 - not_first)),
    ):
        coef_ref[row : row + 1, :] = value
    coef_ref[12:16, :] = jnp.zeros((4, layer.shape[1]), jnp.float32)
    even, _, _ = place()

    @pl.when(even)
    def _():
        pre_ahead(V, S, coef_ref, msg_near, None, 0)
        pre_behind(V, S, coef_ref, msg_far, None, 0)

    @pl.when(jnp.logical_not(even))
    def _():
        pre_behind(V, S, coef_ref, msg_near, None, 0)
        pre_ahead(V, S, coef_ref, msg_far, None, 0)


def first_kernel(window, V0, S, R, coef_ref, force, surface, V, msg, W):
    even, _, _ = place()
    zero_edges(W)
    now, then = force.at[0], force.at[1]
    add_force(V, (VX, 1), now, (VX, 2), PAD + window)
    add_force(V, (VY, 0), now, (VY, 0), PAD + window)
    add_force(V, (VZ, 0), now, (VZ, 0), PAD + window)
    inner(V, S, coef_ref, now, window)

    @pl.when(even)
    def _():
        early_behind(V, S, R, coef_ref, surface, 0, msg, W, then, window)

    @pl.when(jnp.logical_not(even))
    def _():
        early_ahead(V, S, R, coef_ref, msg, W, then, window)


def near_kernel(step, window, V0, S0, R0, coef_ref, force, surface, msg, V, S, R, *rest):
    G = rest[-1]
    R0 = R0 if step == 0 else R
    even, _, _ = place()
    more = step < STEPS - 1

    @pl.when(even)
    def _():
        ahead_bond(V, S, R, R0, coef_ref, force.at[step], surface, msg, None, G, step, window)
        if more:
            pre_ahead(V, S, coef_ref, rest[0], force.at[step + 1], window)

    @pl.when(jnp.logical_not(even))
    def _():
        behind_bond(V, S, R, R0, coef_ref, force.at[step], surface, msg, None, G, step, window)
        if more:
            pre_behind(V, S, coef_ref, rest[0], force.at[step + 1], window)


def far_kernel(step, window, V0, S0, R0, coef_ref, force, surface, msg, other, *rest):
    V, S, R, D = rest[:4]
    missing, old_r = (other, R) if step > 0 else (None, other)
    G, W = rest[-2:]
    early = rest[4] if step < STEPS - 2 else None
    even, _, _ = place()
    zero_edges(W)
    here, then = force.at[step], force.at[step + 1]

    @pl.when(even)
    def _():
        behind_bond(
            V, S, R, old_r, coef_ref, here, surface, msg, missing, G, step, window,
            lambda: response_ahead(V, S, coef_ref, D, W),
        )
        pre_behind(V, S, coef_ref, None, then, window)

    @pl.when(jnp.logical_not(even))
    def _():
        ahead_bond(
            V, S, R, old_r, coef_ref, here, surface, msg, missing, G, step, window,
            lambda: response_behind(V, S, coef_ref, D, W),
        )
        pre_ahead(V, S, coef_ref, None, then, window)

    inner(V, S, coef_ref, then, window)
    if early is not None:
        later = force.at[step + 2]

        @pl.when(even)
        def _():
            early_behind(V, S, R, coef_ref, surface, 2 * (step + 1), early, W, later, window)

        @pl.when(jnp.logical_not(even))
        def _():
            early_ahead(V, S, R, coef_ref, early, W, later, window)


def last_kernel(
    step, window, V0, S0, R0, coef_ref, force, surface, msg, missing, V, S, R, v_out, s_out, r_out, G, sems
):
    even, _, _ = place()
    here = force.at[step]
    inside = pl.ds(PAD, R.shape[2])

    def copies(cell):
        return [
            pltpu.make_async_copy(V.at[:, cell, inside], v_out.at[:, cell], sems.at[cell, 0]),
            pltpu.make_async_copy(S.at[:, cell, inside], s_out.at[:, cell], sems.at[cell, 1]),
            pltpu.make_async_copy(R.at[:, cell], r_out.at[:, cell], sems.at[cell, 2]),
        ]

    def finish(cell, bond):
        done, other = copies(1 - cell), copies(cell)
        for copy in done:
            copy.start()
        bond(V, S, R, R, coef_ref, here, surface, msg, missing, G, step, window)
        for copy in other:
            copy.start()
        for copy in done + other:
            copy.wait()

    @pl.when(even)
    def _():
        finish(0, behind_bond)

    @pl.when(jnp.logical_not(even))
    def _():
        finish(1, ahead_bond)


ENTRY_ROW, TRUCK_ROW = 36, 40
GROUP = 8


def lane_blocks(table, width):
    return sum(lane_roll(table[s : s + 1, :], s * width) for s in range(STEPS))


def split_kernel(panel, slots, own, behind, cells, out):
    tiles, _, lanes = out.shape
    pieces = panel // lanes
    third = pieces // 3
    cell_of = cells[...]
    me = lax.axis_index("line")
    group, mine = lax.div(me, tiles), lax.rem(me, tiles)
    row = lax.broadcasted_iota(jnp.int32, (3 * tiles, cell_of.shape[1]), 0)
    first = (lax.div(row, 3) + group * tiles) * 2 + lax.rem(row, 3)
    record = jnp.where(group == 0, own[:, :panel], behind[:, :panel])

    def share(cell, columns):
        hit = jnp.where(cell == cell_of, 1.0, 0.0).astype(jnp.float32)
        return jnp.dot(
            hit, record[:, columns], precision=lax.Precision.HIGHEST, preferred_element_type=jnp.float32
        )

    part_x = share(first - 1, slice(0, third * lanes))
    part_yz = share(first, slice(third * lanes, panel))

    def trucks(source):
        blocks = [source[0:8, panel + i * lanes : panel + (i + 1) * lanes] for i in range(slots // 8 + 1)]
        return blocks[:-1], lane_blocks(blocks[-1], slots)

    own_rows, own_entry = trucks(own)
    far_rows, far_entry = trucks(behind)
    for tile in range(tiles):
        these = slice(3 * tile, 3 * tile + 3)
        for m in range(pieces):
            part, at = (part_x, m) if m < third else (part_yz, m - third)
            out[tile, 3 * m : 3 * m + 3, :] = part[these, at * lanes : (at + 1) * lanes]
        passed = mine < tile
        out[tile, ENTRY_ROW : ENTRY_ROW + 1, :] = jnp.where(passed, own_entry, far_entry)
        for i in range(slots // 8):
            at = TRUCK_ROW + 8 * i
            out[tile, at : at + 8, :] = jnp.where(passed, own_rows[i], far_rows[i])


def prepare_kernel(parts, loads, entries, cells, force, surface, table, rows_out):
    steps, comps, width = force.shape[:3]
    lanes = parts.shape[2]
    force[...] = jnp.zeros(force.shape, jnp.float32)
    per = ENTRY_ROW // (comps * width)
    lane = lax.broadcasted_iota(jnp.int32, (per, lanes), 1)
    scale = jnp.where(lane < FZ, DT, 0.0).astype(jnp.float32)
    for s in range(steps):
        for comp in range(comps):
            for cell in range(width):
                panel = parts[s, pl.ds(comp * per * width + cell, per, stride=width), :]
                force[s, comp, cell, pl.ds(4, per, stride=2), :] = scale * panel
                force[s, comp, cell, pl.ds(5, per, stride=2), :] = scale * lane_roll(panel, FZ)

    slots = loads.shape[0]
    tiles = parts.shape[0]
    mine = lax.rem(lax.axis_index("line"), tiles)
    table[...] = jnp.zeros(table.shape, jnp.float32)
    table[0:1, :] = lane_blocks(entries[...], slots)
    table[STEPS + 1 : STEPS + 2, :] = lane_blocks(cells[...], slots)
    rows = [loads[...]]
    for k in range(1, STEPS + 1):
        source = lax.rem(mine + (tiles - k), tiles)
        rows.append(parts[source, TRUCK_ROW : TRUCK_ROW + slots, :])
        table[k : k + 1, :] = parts[source, ENTRY_ROW : ENTRY_ROW + 1, :]
    columns = table[...].T
    rows_out[...] = jnp.zeros(rows_out.shape, jnp.float32)
    for s in range(STEPS):
        block = slice(s * slots, (s + 1) * slots)
        moved = []
        for k in range(STEPS - s):
            entry = jnp.broadcast_to(columns[block, k : k + 1], rows[k].shape)
            new = rows[k]
            for slot in range(slots):
                new = jnp.where(entry == float(slot), rows[k + 1][slot : slot + 1, :], new)
            moved.append(new)
        rows = moved
        cell = jnp.broadcast_to(columns[block, STEPS + 1 : STEPS + 2], rows[0].shape)
        for c in range(2):
            load = jnp.sum(jnp.where(cell == float(c), rows[0], 0.0), axis=0, keepdims=True)
            rows_out[2 * s + c : 2 * s + c + 1, :] = load
    surface[...] = rows_out[...].T


def in_vmem(x):
    return pltpu.with_memory_space_constraint(x, pltpu.VMEM)


WHOLE = pl.BlockSpec(memory_space=pltpu.VMEM)
SCALARS = pl.BlockSpec(memory_space=pltpu.SMEM)
ANYWHERE = pl.BlockSpec(memory_space=pl.ANY)


def call(kernel, ins, specs, outs, out_specs, scratch=(), aliases=None, name=None):
    size = sum(x.size * 4 for x in ins)
    return pl.pallas_call(
        kernel,
        out_shape=outs,
        in_specs=specs,
        out_specs=out_specs,
        scratch_shapes=list(scratch),
        input_output_aliases=aliases or {},
        compiler_params=pltpu.CompilerParams(vmem_limit_bytes=VMEM_LIMIT),
        cost_estimate=pl.CostEstimate(flops=8 * size, bytes_accessed=2 * size, transcendentals=0),
        name=name,
    )(*ins)


def body(
    velocity, stress, memory, truck_loads, pier_panels,
    lame_lambda, lame_mu, buoyancy, relax_rate, defect_mu, layer,
    truck_entry, truck_cell, pier_cell,
):
    tiles = lax.axis_size("line")
    width_x, across, depth = velocity.shape[1:]
    slots = truck_loads.shape[0]
    window = (across - FY) // 2 - 4
    f32 = jnp.float32

    near = [(i, i ^ 1) for i in range(tiles) if (i ^ 1) < tiles]
    far = [(i, i + 1) for i in range(1, tiles - 1, 2)] + [(i + 1, i) for i in range(1, tiles - 1, 2)]

    padded = across + 2 * PAD
    v_type = pltpu.VMEM((3, width_x, padded, depth), f32)
    s_type = pltpu.VMEM((6, width_x, padded, depth), f32)
    r_type = pltpu.VMEM((6, width_x, across, depth), f32)
    c_type = pltpu.VMEM((N_COEF, depth), f32)
    m_type = pltpu.VMEM((3, across, depth), f32)
    ghost = pltpu.VMEM((2, across, depth), f32)
    work = pltpu.VMEM((2, padded, depth), f32)

    def as_rows(table):
        return jnp.pad(table.astype(f32), ((0, 8 - STEPS), (0, depth - slots)))

    def ahead_by(x, distance):
        return lax.ppermute(x, "line", [(i, i + distance) for i in range(tiles - distance)])

    entries, cells = as_rows(truck_entry), as_rows(truck_cell)
    piers, panel = pier_panels.shape[1:]
    blocks = [truck_loads[at : at + 8] for at in range(0, slots, 8)] + [entries]
    blocks = [jnp.pad(block, ((0, piers - 8), (0, 0))) for block in blocks]
    own = jnp.concatenate([pier_panels[0], *blocks], axis=1)
    behind = ahead_by(own, GROUP)
    reach = 2 * GROUP
    index = lax.axis_index("line")
    while reach < tiles:
        record = jnp.where(index < GROUP, own, behind)[:, :panel]
        record = jnp.where(index < reach, record, ahead_by(record, reach))
        behind = jnp.concatenate([record, behind[:, panel:]], axis=1)
        reach *= 2
    parts = call(
        functools.partial(split_kernel, panel, slots),
        (own, behind, pier_cell[None, :]),
        (WHOLE,) * 3,
        jax.ShapeDtypeStruct((GROUP, TRUCK_ROW + slots, depth), f32),
        WHOLE,
        name="split",
    )

    V, S, coef, msg_near, msg_far = call(
        start_kernel,
        (
            velocity, stress, layer[None, :], lame_lambda, lame_mu, buoyancy, relax_rate, defect_mu,
            parts,
        ),
        (WHOLE,) * 3 + (SCALARS,) * 5 + (ANYWHERE,),
        (v_type, s_type, c_type, m_type, m_type),
        (WHOLE,) * 5,
        name="start",
    )
    groups = [list(range(at, at + GROUP)) for at in range(0, tiles, GROUP)]
    parts = lax.all_to_all(parts, "line", 0, 0, axis_index_groups=groups, tiled=True)
    msg_far = lax.ppermute(msg_far, "line", far)
    msg_near = lax.ppermute(msg_near, "line", near)

    force, surface = call(
        prepare_kernel,
        (parts, truck_loads, entries, cells),
        (WHOLE,) * 4,
        (pltpu.VMEM((STEPS, 3, 3, 16, depth), f32), pltpu.VMEM((across, depth), f32)),
        (WHOLE,) * 2,
        scratch=(pltpu.VMEM((depth, depth), f32), pltpu.VMEM((depth, across), f32)),
        name="prepare",
    )
    V, early = call(
        functools.partial(first_kernel, window),
        tuple(in_vmem(x) for x in (V, S)) + (memory,) + tuple(in_vmem(x) for x in (coef, force, surface)),
        (WHOLE,) * 6,
        (v_type, m_type),
        (WHOLE,) * 2,
        scratch=(work,),
        aliases={0: 0},
        name="first",
    )
    early = lax.ppermute(early, "line", far)
    state = (v_type, s_type, r_type)
    same = {0: 0, 1: 1, 2: 2}
    R = missing = None
    for step in range(STEPS):
        more = step < STEPS - 1
        ins = [in_vmem(x) for x in (V, S, R if step else memory, coef, force, surface, msg_near)]
        if step == 0:
            ins[2] = memory
        outs = state + ((m_type,) if more else ())
        V, S, R, *msg = call(
            functools.partial(near_kernel, step, window),
            ins,
            (WHOLE,) * len(ins),
            outs,
            (WHOLE,) * len(outs),
            scratch=(ghost,),
            aliases=same if step else {0: 0, 1: 1},
            name="near" + str(step),
        )
        if more:
            msg_near = lax.ppermute(msg[0], "line", near)
        ins = tuple(in_vmem(x) for x in (V, S, R, coef, force, surface, msg_far))
        ins += (in_vmem(missing) if step else memory,)
        if more:
            outs = state + (m_type,) + ((m_type,) if step < STEPS - 2 else ())
            V, S, R, missing, *msg = call(
                functools.partial(far_kernel, step, window),
                ins,
                (WHOLE,) * len(ins),
                outs,
                (WHOLE,) * len(outs),
                scratch=(ghost, work),
                aliases=same,
                name="far" + str(step),
            )
            msg_far = early
            if msg:
                early = lax.ppermute(msg[0], "line", far)
    results = call(
        functools.partial(last_kernel, STEPS - 1, window),
        ins,
        (WHOLE,) * len(ins),
        state + tuple(jax.ShapeDtypeStruct(x.shape, f32) for x in (velocity, stress, memory)),
        (WHOLE,) * 3 + (ANYWHERE,) * 3,
        scratch=(ghost, pltpu.SemaphoreType.DMA((2, 3))),
        aliases=same,
        name="last",
    )
    return results[3:]


def solution(mesh):
    placed = (
        P(None, ("runs", "line"), None, None),
        P(None, ("runs", "line"), None, None),
        P(None, ("runs", "line"), None, None),
        P(("runs", "line"), None),
        P("line", "runs", None),
        P(),
        P(),
        P(),
        P(),
        P(),
        P(),
        P(None, ("runs", "line")),
        P(None, ("runs", "line")),
        P(),
    )
    return jax.shard_map(
        body,
        mesh=mesh,
        in_specs=placed,
        out_specs=(
            P(None, ("runs", "line"), None, None),
            P(None, ("runs", "line"), None, None),
            P(None, ("runs", "line"), None, None),
        ),
        check_vma=False,
    )
```

```python
import functools

import jax
import jax.numpy as jnp
import numpy as np
from jax import lax
from jax.experimental import pallas as pl
from jax.experimental.pallas import tpu as pltpu
from jax.sharding import PartitionSpec as P

STEPS = 6
FY = 8
FZ = 64
DT = 0.25
PAD = 8
ROWS = 16
UNROLL = 4
VMEM_LIMIT = 32 * 1024 * 1024

C_B, C_B0, C_B1, C_M0, C_M1, C_LAM, C_MU2, C_MU, C_K1, C_K2, C_K2H, C_L0 = range(12)
N_COEF = 16

VX, VY, VZ = range(3)
XX, YY, ZZ, XY, XZ, YZ = range(6)


def lane_roll(x, shift):
    return pltpu.roll(x, shift % x.shape[-1], x.ndim - 1)


def before(x):
    return lane_roll(x, 1)


def after(x):
    return lane_roll(x, -1)


def over_rows(count, work):
    def step(i, carry):
        work(pl.multiple_of(i * ROWS, ROWS))
        return carry

    lax.fori_loop(0, count // ROWS, step, 0, unroll=UNROLL)


class Planes:
    def __init__(self, ref, first, across):
        self.ref, self.first, self.shape = ref, first, (3, across, ref.shape[1])

    def rows(self, at):
        plane, out = at
        return pl.ds((self.first + plane) * self.shape[1] + out.start, out.size)

    def __getitem__(self, at):
        return self.ref[self.rows(at)]

    def __setitem__(self, at, value):
        self.ref[self.rows(at)] = value


def coefs(coef_ref, ids):
    return [coef_ref[i : i + 1, :] for i in ids]


def place():
    index = lax.axis_index("line")
    return lax.rem(index, 2) == 0, index > 0, index < lax.axis_size("line") - 1


def spans(r):
    return pl.ds(PAD + r, ROWS), pl.ds(PAD + r - 1, ROWS), pl.ds(PAD + r + 1, ROWS), pl.ds(r, ROWS)


def zero_edges(ref):
    across = ref.shape[-2] - 2 * PAD
    edge = jnp.zeros((PAD, ref.shape[-1]), jnp.float32)
    for where in np.ndindex(*ref.shape[:-2]):
        ref[(*where, pl.ds(0, PAD))] = edge
        ref[(*where, pl.ds(PAD + across, PAD))] = edge


def add_force(ref, index, force, which, first_row):
    rows = pl.ds(first_row, 16)
    ref[(*index, rows)] = ref[(*index, rows)] + force[which]


def pre_ahead(V, S, coef_ref, msg, force, window):
    b, b0 = coefs(coef_ref, (C_B, C_B0))

    def work(r):
        here, up, _, out = spans(r)
        sxy, sxz = S[XY, 1, here], S[XZ, 1, here]
        px = V[VX, 1, here] + b * (sxy - S[XY, 1, up] + sxz - S[XX, 1, here]) - b0 * before(sxz)
        V[VX, 1, here] = px
        if msg is not None:
            msg[0, out] = sxy
            msg[1, out] = sxz
            msg[2, out] = px

    over_rows(V.shape[2] - 2 * PAD, work)
    if force is not None:
        add_force(V, (VX, 1), force, (VX, 1), PAD + window)
        if msg is not None:
            add_force(msg, (2,), force, (VX, 1), window)


def pre_behind(V, S, coef_ref, msg, force, window):
    b, b0, b1 = coefs(coef_ref, (C_B, C_B0, C_B1))

    def work(r):
        here, up, down, out = spans(r)
        syz, szz = S[YZ, 0, here], S[ZZ, 0, here]
        qy = V[VY, 0, here] + b * (S[XY, 0, here] + S[YY, 0, down] - S[YY, 0, here] + syz) - b0 * before(syz)
        qz = V[VZ, 0, here] + b * (S[XZ, 0, here] + syz - S[YZ, 0, up] - szz) + b1 * after(szz)
        V[VY, 0, here] = qy
        V[VZ, 0, here] = qz
        if msg is not None:
            msg[0, out] = S[XX, 0, here]
            msg[1, out] = qy
            msg[2, out] = qz

    over_rows(V.shape[2] - 2 * PAD, work)
    if force is not None:
        add_force(V, (VY, 0), force, (VY, 0), PAD + window)
        add_force(V, (VZ, 0), force, (VZ, 0), PAD + window)
        if msg is not None:
            add_force(msg, (1,), force, (VY, 0), window)
            add_force(msg, (2,), force, (VZ, 0), window)


def inner(V, S, coef_ref, force, window):
    b, b0, b1 = coefs(coef_ref, (C_B, C_B0, C_B1))

    def work(r):
        here, up, down, _ = spans(r)
        sxy, sxz = S[XY, 0, here], S[XZ, 0, here]
        V[VX, 0, here] = (
            V[VX, 0, here]
            + b * (S[XX, 1, here] - S[XX, 0, here] + sxy - S[XY, 0, up] + sxz)
            - b0 * before(sxz)
        )
        syz, szz = S[YZ, 1, here], S[ZZ, 1, here]
        V[VY, 1, here] = (
            V[VY, 1, here]
            + b * (S[XY, 1, here] - sxy + S[YY, 1, down] - S[YY, 1, here] + syz)
            - b0 * before(syz)
        )
        V[VZ, 1, here] = (
            V[VZ, 1, here]
            + b * (S[XZ, 1, here] - sxz + syz - S[YZ, 1, up] - szz)
            + b1 * after(szz)
        )

    over_rows(V.shape[2] - 2 * PAD, work)
    if force is not None:
        add_force(V, (VX, 0), force, (VX, 0), PAD + window)
        add_force(V, (VY, 1), force, (VY, 1), PAD + window)
        add_force(V, (VZ, 1), force, (VZ, 1), PAD + window)


def post(V, S, R, old_r, coef_ref, surface, cell, column, behind_x, ahead_y, ahead_z):
    m0, m1, lam, mu2, mu, k1, k2, k2h, l0 = coefs(
        coef_ref, (C_M0, C_M1, C_LAM, C_MU2, C_MU, C_K1, C_K2, C_K2H, C_L0)
    )

    def work(r):
        here, up, down, out = spans(r)
        vx, vy, vz = V[VX, cell, here], V[VY, cell, here], V[VZ, cell, here]
        exx = vx - behind_x(r)
        eyy = vy - V[VY, cell, up]
        ezz = vz - m0 * before(vz)
        exy = V[VX, cell, down] - vx + (ahead_y(r) - vy)
        exz = m1 * after(vx) - vx + (ahead_z(r) - vz)
        eyz = m1 * after(vy) - vy + (V[VZ, cell, down] - vz)
        volume = lam * (exx + eyy + ezz)
        for comp, e in ((XX, exx), (YY, eyy), (ZZ, ezz)):
            old = old_r[comp, cell, out]
            new = S[comp, cell, here] + (volume + mu2 * e) + DT * old
            if comp == ZZ:
                new = new + l0 * lane_roll(surface[out, :], -column)
            S[comp, cell, here] = new
            R[comp, cell, out] = k1 * old - k2 * e
        for comp, e in ((XY, exy), (XZ, exz), (YZ, eyz)):
            old = old_r[comp, cell, out]
            S[comp, cell, here] = S[comp, cell, here] + mu * e + DT * old
            R[comp, cell, out] = k1 * old - k2h * e

    over_rows(R.shape[2], work)


def response_behind(V, S, coef_ref, D, W):
    b, b0, b1, m0, m1, lam, mu2, mu = coefs(coef_ref, (C_B, C_B0, C_B1, C_M0, C_M1, C_LAM, C_MU2, C_MU))

    def work(r):
        here, up, down, out = spans(r)
        sxy = S[XY, 1, here]
        vy, vz = -b * sxy, -b * S[XZ, 1, here]
        exx = -V[VX, 1, here]
        eyy = b * (S[XY, 1, up] - sxy)
        ezz = vz - m0 * before(vz)
        volume = lam * (exx + eyy + ezz)
        dyy, dzz = volume + mu2 * eyy, volume + mu2 * ezz
        dyz = mu * (m1 * after(vy) - vy - b * S[XZ, 1, down] - vz)
        W[0, here] = dyy
        W[1, here] = dyz
        D[0, out] = volume + mu2 * exx
        D[1, out] = vy + b * (dyz - mu * vy - dyy) - b0 * before(dyz)
        D[2, out] = vz + b * (dyz - mu * vz - dzz) + b1 * after(dzz)

    over_rows(D.shape[1], work)

    def rest(r):
        _, up, down, out = spans(r)
        D[1, out] = D[1, out] + b * W[0, down]
        D[2, out] = D[2, out] - b * W[1, up]

    over_rows(D.shape[1], rest)


def response_ahead(V, S, coef_ref, D, W):
    b, b0, m1, lam, mu2, mu = coefs(coef_ref, (C_B, C_B0, C_M1, C_LAM, C_MU2, C_MU))

    def work(r):
        here, _, down, out = spans(r)
        vx = b * S[XX, 0, here]
        dxy = mu * (b * S[XX, 0, down] - vx + V[VY, 0, here])
        dxz = mu * (m1 * after(vx) - vx + V[VZ, 0, here])
        W[0, here] = dxy
        D[0, out] = dxy
        D[1, out] = dxz
        D[2, out] = vx + b * (dxy + dxz - (lam + mu2) * vx) - b0 * before(dxz)

    over_rows(D.shape[1], work)

    def rest(r):
        _, up, _, out = spans(r)
        D[2, out] = D[2, out] - b * W[0, up]

    over_rows(D.shape[1], rest)


def first_response_behind(V, S, coef_ref, force, load, D, W, A, window):
    b, b0, b1, m0, m1, lam, mu2, mu, l0 = coefs(
        coef_ref, (C_B, C_B0, C_B1, C_M0, C_M1, C_LAM, C_MU2, C_MU, C_L0)
    )
    A[...] = jnp.zeros(A.shape, jnp.float32)

    def given(r):
        here, _, _, _ = spans(r)
        A[1, here] = -b * S[XY, 1, here]
        A[2, here] = -b * S[XZ, 1, here]

    over_rows(D.shape[1], given)
    for i, which in enumerate(((VX, 3), (VY, 2), (VZ, 2), (VY, 3), (VZ, 3))):
        add_force(A, (i,), force, which, PAD + window)

    def work(r):
        here, up, down, out = spans(r)
        vx, vy, vz = A[0, here], A[1, here], A[2, here]
        exx = vx - V[VX, 1, here]
        eyy = vy - A[1, up]
        ezz = vz - m0 * before(vz)
        volume = lam * (exx + eyy + ezz)
        dyy = volume + mu2 * eyy
        dzz = volume + mu2 * ezz + l0 * load[out, :]
        dxy = mu * (A[0, down] - vx + (A[3, here] - vy))
        dxz = mu * (m1 * after(vx) - vx + (A[4, here] - vz))
        dyz = mu * (m1 * after(vy) - vy + (A[2, down] - vz))
        W[0, here] = dyy
        W[1, here] = dyz
        D[0, out] = volume + mu2 * exx
        D[1, out] = vy + b * (dxy - dyy + dyz) - b0 * before(dyz)
        D[2, out] = vz + b * (dxz + dyz - dzz) + b1 * after(dzz)

    over_rows(D.shape[1], work)

    def rest(r):
        _, up, down, out = spans(r)
        D[1, out] = D[1, out] + b * W[0, down]
        D[2, out] = D[2, out] - b * W[1, up]

    over_rows(D.shape[1], rest)


def first_response_ahead(V, S, coef_ref, force, D, W, A, window):
    b, b0, m0, m1, lam, mu2, mu = coefs(coef_ref, (C_B, C_B0, C_M0, C_M1, C_LAM, C_MU2, C_MU))
    A[...] = jnp.zeros(A.shape, jnp.float32)

    def given(r):
        here, _, _, _ = spans(r)
        A[0, here] = b * S[XX, 0, here]

    over_rows(D.shape[1], given)
    for i, which in enumerate(((VX, 2), (VY, 3), (VZ, 3), (VX, 3))):
        add_force(A, (i,), force, which, PAD + window)

    def work(r):
        here, up, down, out = spans(r)
        vx, vy, vz = A[0, here], A[1, here], A[2, here]
        exx = vx - A[3, here]
        dxx = lam * (exx + (vy - A[1, up]) + (vz - m0 * before(vz))) + mu2 * exx
        dxy = mu * (A[0, down] - vx + (V[VY, 0, here] - vy))
        dxz = mu * (m1 * after(vx) - vx + (V[VZ, 0, here] - vz))
        W[0, here] = dxy
        D[0, out] = dxy
        D[1, out] = dxz
        D[2, out] = vx + b * (dxy + dxz - dxx) - b0 * before(dxz)

    over_rows(D.shape[1], work)

    def rest(r):
        _, up, _, out = spans(r)
        D[2, out] = D[2, out] - b * W[0, up]

    over_rows(D.shape[1], rest)


def early_ahead(V, S, R, coef_ref, msg, W, force, window):
    b, b0, m0, m1, lam, mu2, mu = coefs(coef_ref, (C_B, C_B0, C_M0, C_M1, C_LAM, C_MU2, C_MU))

    def work(r):
        here, up, down, out = spans(r)
        vx, vy, vz = V[VX, 1, here], V[VY, 1, here], V[VZ, 1, here]
        exx = vx - V[VX, 0, here]
        volume = lam * (exx + (vy - V[VY, 1, up]) + (vz - m0 * before(vz)))
        sxx = S[XX, 1, here] + (volume + mu2 * exx) + DT * R[XX, 1, out]
        sxy = S[XY, 1, here] + mu * (V[VX, 1, down] - vx - vy) + DT * R[XY, 1, out]
        sxz = S[XZ, 1, here] + mu * (m1 * after(vx) - vx - vz) + DT * R[XZ, 1, out]
        W[0, here] = sxy
        msg[0, out] = sxy
        msg[1, out] = sxz
        msg[2, out] = vx + b * (sxy + sxz - sxx) - b0 * before(sxz)

    over_rows(msg.shape[1], work)

    def rest(r):
        _, up, _, out = spans(r)
        msg[2, out] = msg[2, out] - b * W[0, up]

    over_rows(msg.shape[1], rest)
    if force is not None:
        add_force(msg, (2,), force, (VX, 1), window)


def early_behind(V, S, R, coef_ref, surface, column, msg, W, force, window):
    b, b0, b1, m0, m1, lam, mu2, mu, l0 = coefs(
        coef_ref, (C_B, C_B0, C_B1, C_M0, C_M1, C_LAM, C_MU2, C_MU, C_L0)
    )

    def work(r):
        here, up, down, out = spans(r)
        vx, vy, vz = V[VX, 0, here], V[VY, 0, here], V[VZ, 0, here]
        eyy = vy - V[VY, 0, up]
        ezz = vz - m0 * before(vz)
        volume = lam * (vx + eyy + ezz)
        sxx = S[XX, 0, here] + (volume + mu2 * vx) + DT * R[XX, 0, out]
        syy = S[YY, 0, here] + (volume + mu2 * eyy) + DT * R[YY, 0, out]
        szz = S[ZZ, 0, here] + (volume + mu2 * ezz) + DT * R[ZZ, 0, out]
        if surface is not None:
            szz = szz + l0 * lane_roll(surface[out, :], -column)
        sxy = S[XY, 0, here] + mu * (V[VX, 0, down] - vx + (V[VY, 1, here] - vy)) + DT * R[XY, 0, out]
        sxz = S[XZ, 0, here] + mu * (m1 * after(vx) - vx + (V[VZ, 1, here] - vz)) + DT * R[XZ, 0, out]
        syz = S[YZ, 0, here] + mu * (m1 * after(vy) - vy + (V[VZ, 0, down] - vz)) + DT * R[YZ, 0, out]
        W[0, here] = syy
        W[1, here] = syz
        msg[0, out] = sxx
        msg[1, out] = vy + b * (sxy - syy + syz) - b0 * before(syz)
        msg[2, out] = vz + b * (sxz + syz - szz) + b1 * after(szz)

    over_rows(msg.shape[1], work)

    def rest(r):
        _, up, down, out = spans(r)
        msg[1, out] = msg[1, out] + b * W[0, down]
        msg[2, out] = msg[2, out] - b * W[1, up]

    over_rows(msg.shape[1], rest)
    if force is not None:
        add_force(msg, (1,), force, (VY, 0), window)
        add_force(msg, (2,), force, (VZ, 0), window)


def ahead_bond(V, S, R, old_r, coef_ref, force, surface, msg, missing, G, step, window, unforced=0, respond=None):
    (b,) = coefs(coef_ref, (C_B,))
    _, _, has_ahead = place()
    keep = jnp.where(has_ahead, 1.0, 0.0).astype(jnp.float32)

    def got(i, out):
        return msg[i, out] if missing is None else msg[i, out] + missing[i, out]

    def work(r):
        here, _, _, out = spans(r)
        V[VX, 1, here] = V[VX, 1, here] + (keep * b) * got(0, out)
        G[0, out] = keep * (got(1, out) - b * S[XY, 1, here])
        G[1, out] = keep * (got(2, out) - b * S[XZ, 1, here])

    over_rows(R.shape[2], work)
    if step < unforced:
        add_force(G, (0,), force, (VY, 2), window)
        add_force(G, (1,), force, (VZ, 2), window)
    if respond is not None:
        respond()
    post(
        V, S, R, old_r, coef_ref, surface, 1, 2 * step + 1,
        lambda r: V[VX, 0, pl.ds(PAD + r, ROWS)],
        lambda r: G[0, pl.ds(r, ROWS)],
        lambda r: G[1, pl.ds(r, ROWS)],
    )


def behind_bond(V, S, R, old_r, coef_ref, force, surface, msg, missing, G, step, window, unforced=0, respond=None):
    (b,) = coefs(coef_ref, (C_B,))
    _, has_behind, _ = place()
    keep = jnp.where(has_behind, 1.0, 0.0).astype(jnp.float32)

    def got(i, out):
        return msg[i, out] if missing is None else msg[i, out] + missing[i, out]

    def work(r):
        here, _, _, out = spans(r)
        V[VY, 0, here] = V[VY, 0, here] - (keep * b) * got(0, out)
        V[VZ, 0, here] = V[VZ, 0, here] - (keep * b) * got(1, out)
        G[0, out] = keep * (got(2, out) + b * S[XX, 0, here])

    over_rows(R.shape[2], work)
    if step < unforced:
        add_force(G, (0,), force, (VX, 2), window)
    if respond is not None:
        respond()
    post(
        V, S, R, old_r, coef_ref, surface, 0, 2 * step,
        lambda r: G[0, pl.ds(r, ROWS)],
        lambda r: V[VY, 1, pl.ds(PAD + r, ROWS)],
        lambda r: V[VZ, 1, pl.ds(PAD + r, ROWS)],
    )


def step_table(table, entries, cells):
    table[...] = jnp.zeros(table.shape, jnp.float32)
    steps, slots = entries.shape
    table[0:steps, 0:slots] = entries[...].astype(jnp.float32)
    table[8 : 8 + steps, 0:slots] = cells[...].astype(jnp.float32)


def start_kernel(
    velocity, stress, memory, layer_ref, lam, mu, buoy, rate, defect, loads, entries, cells,
    V, S, coef_ref, msg_near, msg_far, W, table,
):
    across = velocity.shape[2]
    slots = loads.shape[0]
    zero_edges(V)
    zero_edges(S)
    zero_edges(W)
    step_table(table, entries, cells)
    columns = table[...].T
    trucks = 6 * across
    msg_far[trucks : trucks + slots, :] = loads[...]
    for i, at in enumerate((0, 8)):
        first_row = trucks + (1 + i) * slots
        column = columns[0:slots, at : at + 1]
        msg_far[first_row : first_row + slots, :] = jnp.broadcast_to(column, loads.shape)

    def load(r):
        here, _, _, out = spans(r)
        for ref, source in ((V, velocity), (S, stress)):
            for where in np.ndindex(*source.shape[:2]):
                ref[(*where, here)] = source[(*where, out)]

    over_rows(velocity.shape[2], load)
    layer = layer_ref[...]

    def per_depth(table):
        row = jnp.zeros(layer.shape, jnp.float32)
        for level in range(table.shape[0]):
            row = jnp.where(layer == level, table[level], row)
        return row

    lane = lax.broadcasted_iota(jnp.int32, layer.shape, 1)
    not_first = jnp.where(lane > 0, 1.0, 0.0).astype(jnp.float32)
    not_last = jnp.where(lane < layer.shape[1] - 1, 1.0, 0.0).astype(jnp.float32)
    b = DT * per_depth(buoy)
    two_mu = (2.0 * DT) * per_depth(mu)
    decay = DT * per_depth(rate)
    drop = 2.0 * decay * per_depth(defect)
    for row, value in (
        (C_B, b),
        (C_B0, b * not_first),
        (C_B1, b * not_last),
        (C_M0, not_first),
        (C_M1, not_last),
        (C_LAM, DT * per_depth(lam)),
        (C_MU2, two_mu),
        (C_MU, 0.5 * two_mu),
        (C_K1, 1.0 - decay),
        (C_K2, drop),
        (C_K2H, 0.5 * drop),
        (C_L0, DT * (1.0 - not_first)),
    ):
        coef_ref[row : row + 1, :] = value
    coef_ref[12:16, :] = jnp.zeros((4, layer.shape[1]), jnp.float32)
    even, _, _ = place()
    now, then = Planes(msg_far, 0, across), Planes(msg_far, 3, across)

    @pl.when(even)
    def _():
        pre_ahead(V, S, coef_ref, msg_near, None, 0)
        pre_behind(V, S, coef_ref, now, None, 0)

    @pl.when(jnp.logical_not(even))
    def _():
        pre_behind(V, S, coef_ref, msg_near, None, 0)
        pre_ahead(V, S, coef_ref, now, None, 0)

    inner(V, S, coef_ref, None, 0)

    @pl.when(even)
    def _():
        early_behind(V, S, memory, coef_ref, None, 0, then, W, None, 0)

    @pl.when(jnp.logical_not(even))
    def _():
        early_ahead(V, S, memory, coef_ref, then, W, None, 0)


def near_kernel(step, window, V0, S0, R0, coef_ref, force, surface, msg, V, S, R, *rest):
    G = rest[-1]
    R0 = R0 if step == 0 else R
    if step == 0:
        for comp in range(3):
            for cell in range(2):
                add_force(V, (comp, cell), force, (0, comp, cell), PAD + window)
    even, _, _ = place()
    more = step < STEPS - 1

    @pl.when(even)
    def _():
        ahead_bond(V, S, R, R0, coef_ref, force.at[step], surface, msg, None, G, step, window, 1)
        if more:
            pre_ahead(V, S, coef_ref, rest[0], force.at[step + 1], window)

    @pl.when(jnp.logical_not(even))
    def _():
        behind_bond(V, S, R, R0, coef_ref, force.at[step], surface, msg, None, G, step, window, 1)
        if more:
            pre_behind(V, S, coef_ref, rest[0], force.at[step + 1], window)


def load_ahead(msg, loads, across, rows_out, load):
    slots = loads.shape[0]
    rows, entry, cell = (msg[6 * across + i * slots : 6 * across + (i + 1) * slots, :] for i in range(3))
    for slot in range(slots):
        rows = jnp.where(entry == float(slot), loads[slot : slot + 1, :], rows)
    rows_out[...] = jnp.zeros(rows_out.shape, jnp.float32)
    rows_out[0:1, :] = jnp.sum(jnp.where(cell == 0.0, rows, 0.0), axis=0, keepdims=True)
    load[...] = rows_out[...].T


def far_kernel(step, window, V0, S0, R0, coef_ref, force, surface, msg, *rest):
    rest = list(rest)
    extra = [rest.pop(0) for _ in range(2 if step == 0 else 1)]
    V, S, R, D = rest[:4]
    early = rest[4] if step < STEPS - 2 else None
    across = R.shape[2]
    even, _, _ = place()
    here, then = force.at[step], force.at[step + 1]
    got = Planes(msg, 3 * step, across) if step < 2 else msg
    if step == 0:
        memory, loads = extra
        missing, old_r = None, memory
        G, W, A, load, rows_out = rest[-5:]
    else:
        missing, old_r = extra[0], R
        G, W = rest[-2:]
    zero_edges(W)

    @pl.when(even)
    def _():
        if step == 0:
            respond = lambda: first_response_ahead(V, S, coef_ref, here, D, W, A, window)
        else:
            respond = lambda: response_ahead(V, S, coef_ref, D, W)
        behind_bond(
            V, S, R, old_r, coef_ref, here, surface, got, missing, G, step, window, 2, respond
        )
        pre_behind(V, S, coef_ref, None, then, window)

    @pl.when(jnp.logical_not(even))
    def _():
        if step == 0:
            load_ahead(msg, loads, across, rows_out, load)
            respond = lambda: first_response_behind(V, S, coef_ref, here, load, D, W, A, window)
        else:
            respond = lambda: response_behind(V, S, coef_ref, D, W)
        ahead_bond(
            V, S, R, old_r, coef_ref, here, surface, got, missing, G, step, window, 2, respond
        )
        pre_ahead(V, S, coef_ref, None, then, window)

    inner(V, S, coef_ref, then, window)
    if early is not None:
        later = force.at[step + 2]

        @pl.when(even)
        def _():
            early_behind(V, S, R, coef_ref, surface, 2 * (step + 1), early, W, later, window)

        @pl.when(jnp.logical_not(even))
        def _():
            early_ahead(V, S, R, coef_ref, early, W, later, window)


def last_kernel(
    step, window, V0, S0, R0, coef_ref, force, surface, msg, missing, V, S, R, v_out, s_out, r_out, G, sems
):
    even, _, _ = place()
    here = force.at[step]
    inside = pl.ds(PAD, R.shape[2])

    def copies(cell):
        return [
            pltpu.make_async_copy(V.at[:, cell, inside], v_out.at[:, cell], sems.at[cell, 0]),
            pltpu.make_async_copy(S.at[:, cell, inside], s_out.at[:, cell], sems.at[cell, 1]),
            pltpu.make_async_copy(R.at[:, cell], r_out.at[:, cell], sems.at[cell, 2]),
        ]

    def finish(cell, bond):
        done, other = copies(1 - cell), copies(cell)
        for copy in done:
            copy.start()
        bond(V, S, R, R, coef_ref, here, surface, msg, missing, G, step, window)
        for copy in other:
            copy.start()
        for copy in done + other:
            copy.wait()

    @pl.when(even)
    def _():
        finish(0, behind_bond)

    @pl.when(jnp.logical_not(even))
    def _():
        finish(1, ahead_bond)


ENTRY_ROW, TRUCK_ROW = 48, 56
GROUP = 8


def pack_kernel(record, loads, entries, own):
    panel = record.shape[1]
    slots, lanes = loads.shape
    steps = entries.shape[0]
    own[...] = jnp.zeros(own.shape, jnp.float32)
    own[:, 0:panel] = record[...]
    for i in range(slots // 8):
        own[0:8, panel + i * lanes : panel + (i + 1) * lanes] = loads[8 * i : 8 * i + 8, :]
    at = panel + slots // 8 * lanes
    own[0:steps, at : at + slots] = entries[...].astype(jnp.float32)


def lane_blocks(table, width):
    return sum(lane_roll(table[s : s + 1, :], s * width) for s in range(STEPS))


def split_kernel(panel, slots, own, behind, cells, out):
    tiles, _, lanes = out.shape
    pieces = panel // lanes
    third = pieces // 3
    cell_of = cells[...]
    me = lax.axis_index("line")
    group, mine = lax.div(me, tiles), lax.rem(me, tiles)
    row = lax.broadcasted_iota(jnp.int32, (4 * tiles, cell_of.shape[1]), 0)
    tile, j = lax.div(row, 4), lax.rem(row, 4)
    odd = lax.rem(tile, 2)
    first = (tile + group * tiles) * 2
    cell_x = first + jnp.where(j == 2, -1, jnp.where(j == 3, 4 * odd - 2, j))
    cell_yz = first + jnp.where(j == 3, 4 * odd - 1, j)
    record = jnp.where(group == 0, own[:, :panel], behind[:, :panel])

    def share(cell, columns):
        hit = jnp.where(cell == cell_of, 1.0, 0.0).astype(jnp.float32)
        return jnp.dot(
            hit, record[:, columns], precision=lax.Precision.HIGHEST, preferred_element_type=jnp.float32
        )

    part_x = share(cell_x, slice(0, third * lanes))
    part_yz = share(cell_yz, slice(third * lanes, panel))

    def trucks(source):
        blocks = [source[0:8, panel + i * lanes : panel + (i + 1) * lanes] for i in range(slots // 8 + 1)]
        return blocks[:-1], lane_blocks(blocks[-1], slots)

    own_rows, own_entry = trucks(own)
    far_rows, far_entry = trucks(behind)
    for tile in range(tiles):
        these = slice(4 * tile, 4 * tile + 4)
        for m in range(pieces):
            part, at = (part_x, m) if m < third else (part_yz, m - third)
            out[tile, 4 * m : 4 * m + 4, :] = part[these, at * lanes : (at + 1) * lanes]
        passed = mine < tile
        out[tile, ENTRY_ROW : ENTRY_ROW + 1, :] = jnp.where(passed, own_entry, far_entry)
        for i in range(slots // 8):
            at = TRUCK_ROW + 8 * i
            out[tile, at : at + 8, :] = jnp.where(passed, own_rows[i], far_rows[i])


def prepare_kernel(parts, loads, entries, cells, force, surface, table, rows_out):
    steps, comps, width = force.shape[:3]
    lanes = parts.shape[2]
    force[...] = jnp.zeros(force.shape, jnp.float32)
    per = ENTRY_ROW // (comps * width)
    lane = lax.broadcasted_iota(jnp.int32, (per, lanes), 1)
    scale = jnp.where(lane < FZ, DT, 0.0).astype(jnp.float32)
    for s in range(steps):
        for comp in range(comps):
            for cell in range(width):
                panel = parts[s, pl.ds(comp * per * width + cell, per, stride=width), :]
                force[s, comp, cell, pl.ds(4, per, stride=2), :] = scale * panel
                force[s, comp, cell, pl.ds(5, per, stride=2), :] = scale * lane_roll(panel, FZ)

    slots = loads.shape[0]
    tiles = parts.shape[0]
    mine = lax.rem(lax.axis_index("line"), tiles)
    step_table(table, entries, cells)
    own_entry, own_cell = lane_blocks(table[0:8, :], slots), lane_blocks(table[8:16, :], slots)
    table[0:1, :] = own_entry
    table[STEPS + 1 : STEPS + 2, :] = own_cell
    rows = [loads[...]]
    for k in range(1, STEPS + 1):
        source = lax.rem(mine + (tiles - k), tiles)
        rows.append(parts[source, TRUCK_ROW : TRUCK_ROW + slots, :])
        table[k : k + 1, :] = parts[source, ENTRY_ROW : ENTRY_ROW + 1, :]
    columns = table[...].T
    rows_out[...] = jnp.zeros(rows_out.shape, jnp.float32)
    for s in range(STEPS):
        block = slice(s * slots, (s + 1) * slots)
        moved = []
        for k in range(STEPS - s):
            entry = jnp.broadcast_to(columns[block, k : k + 1], rows[k].shape)
            new = rows[k]
            for slot in range(slots):
                new = jnp.where(entry == float(slot), rows[k + 1][slot : slot + 1, :], new)
            moved.append(new)
        rows = moved
        cell = jnp.broadcast_to(columns[block, STEPS + 1 : STEPS + 2], rows[0].shape)
        for c in range(2):
            load = jnp.sum(jnp.where(cell == float(c), rows[0], 0.0), axis=0, keepdims=True)
            rows_out[2 * s + c : 2 * s + c + 1, :] = load
    surface[...] = rows_out[...].T


def in_vmem(x):
    return pltpu.with_memory_space_constraint(x, pltpu.VMEM)


WHOLE = pl.BlockSpec(memory_space=pltpu.VMEM)
SCALARS = pl.BlockSpec(memory_space=pltpu.SMEM)
ANYWHERE = pl.BlockSpec(memory_space=pl.ANY)


def call(kernel, ins, specs, outs, out_specs, scratch=(), aliases=None, name=None):
    size = sum(x.size * 4 for x in ins)
    return pl.pallas_call(
        kernel,
        out_shape=outs,
        in_specs=specs,
        out_specs=out_specs,
        scratch_shapes=list(scratch),
        input_output_aliases=aliases or {},
        compiler_params=pltpu.CompilerParams(vmem_limit_bytes=VMEM_LIMIT),
        cost_estimate=pl.CostEstimate(flops=8 * size, bytes_accessed=2 * size, transcendentals=0),
        name=name,
    )(*ins)


def body(
    velocity, stress, memory, truck_loads, pier_panels,
    lame_lambda, lame_mu, buoyancy, relax_rate, defect_mu, layer,
    truck_entry, truck_cell, pier_cell,
):
    tiles = lax.axis_size("line")
    width_x, across, depth = velocity.shape[1:]
    slots = truck_loads.shape[0]
    window = (across - FY) // 2 - 4
    f32 = jnp.float32

    near = [(i, i ^ 1) for i in range(tiles) if (i ^ 1) < tiles]
    far = [(i, i + 1) for i in range(1, tiles - 1, 2)] + [(i + 1, i) for i in range(1, tiles - 1, 2)]

    padded = across + 2 * PAD
    v_type = pltpu.VMEM((3, width_x, padded, depth), f32)
    s_type = pltpu.VMEM((6, width_x, padded, depth), f32)
    r_type = pltpu.VMEM((6, width_x, across, depth), f32)
    c_type = pltpu.VMEM((N_COEF, depth), f32)
    m_type = pltpu.VMEM((3, across, depth), f32)
    ghost = pltpu.VMEM((2, across, depth), f32)
    work = pltpu.VMEM((2, padded, depth), f32)
    square = pltpu.VMEM((across, depth), f32)

    def ahead_by(x, distance):
        return lax.ppermute(x, "line", [(i, i + distance) for i in range(tiles - distance)])

    piers, panel = pier_panels.shape[1:]
    own = call(
        pack_kernel,
        (pier_panels[0], truck_loads, truck_entry),
        (WHOLE,) * 3,
        jax.ShapeDtypeStruct((piers, panel + (slots // 8 + 1) * depth), f32),
        WHOLE,
        name="pack",
    )
    behind = ahead_by(own, GROUP)
    reach = 2 * GROUP
    index = lax.axis_index("line")
    while reach < tiles:
        record = jnp.where(index < GROUP, own, behind)[:, :panel]
        record = jnp.where(index < reach, record, ahead_by(record, reach))
        behind = jnp.concatenate([record, behind[:, panel:]], axis=1)
        reach *= 2
    parts = call(
        functools.partial(split_kernel, panel, slots),
        (own, behind, pier_cell[None, :]),
        (WHOLE,) * 3,
        jax.ShapeDtypeStruct((GROUP, TRUCK_ROW + slots, depth), f32),
        WHOLE,
        name="split",
    )

    V, S, coef, msg_near, msg_far = call(
        start_kernel,
        (
            velocity, stress, memory, layer[None, :], lame_lambda, lame_mu, buoyancy, relax_rate, defect_mu,
            truck_loads, truck_entry, truck_cell,
        ),
        (WHOLE,) * 4 + (SCALARS,) * 5 + (WHOLE,) * 3,
        (v_type, s_type, c_type, m_type, pltpu.VMEM((6 * across + 3 * slots, depth), f32)),
        (WHOLE,) * 5,
        scratch=(work, pltpu.VMEM((depth, depth), f32)),
        name="start",
    )
    groups = [list(range(at, at + GROUP)) for at in range(0, tiles, GROUP)]
    parts = lax.all_to_all(parts, "line", 0, 0, axis_index_groups=groups, tiled=True)
    msg_far = lax.ppermute(msg_far, "line", far)
    msg_near = lax.ppermute(msg_near, "line", near)

    force, surface = call(
        prepare_kernel,
        (parts, truck_loads, truck_entry, truck_cell),
        (WHOLE,) * 4,
        (pltpu.VMEM((STEPS, 3, 4, 16, depth), f32), pltpu.VMEM((across, depth), f32)),
        (WHOLE,) * 2,
        scratch=(pltpu.VMEM((depth, depth), f32), pltpu.VMEM((depth, across), f32)),
        name="prepare",
    )
    state = (v_type, s_type, r_type)
    same = {0: 0, 1: 1, 2: 2}
    R = missing = None
    for step in range(STEPS):
        more = step < STEPS - 1
        ins = [in_vmem(x) for x in (V, S, R if step else memory, coef, force, surface, msg_near)]
        if step == 0:
            ins[2] = memory
        outs = state + ((m_type,) if more else ())
        V, S, R, *msg = call(
            functools.partial(near_kernel, step, window),
            ins,
            (WHOLE,) * len(ins),
            outs,
            (WHOLE,) * len(outs),
            scratch=(ghost,),
            aliases=same if step else {0: 0, 1: 1},
            name="near" + str(step),
        )
        if more:
            msg_near = lax.ppermute(msg[0], "line", near)
        ins = tuple(in_vmem(x) for x in (V, S, R, coef, force, surface, msg_far))
        ins += (in_vmem(missing),) if step else (memory, truck_loads)
        if more:
            outs = state + (m_type,) + ((m_type,) if step < STEPS - 2 else ())
            V, S, R, missing, *msg = call(
                functools.partial(far_kernel, step, window),
                ins,
                (WHOLE,) * len(ins),
                outs,
                (WHOLE,) * len(outs),
                scratch=(ghost, work) + (() if step else (pltpu.VMEM((5, padded, depth), f32),) + (square,) * 2),
                aliases=same,
                name="far" + str(step),
            )
            if step > 0:
                msg_far = early
            if msg:
                early = lax.ppermute(msg[0], "line", far)
    results = call(
        functools.partial(last_kernel, STEPS - 1, window),
        ins,
        (WHOLE,) * len(ins),
        state + tuple(jax.ShapeDtypeStruct(x.shape, f32) for x in (velocity, stress, memory)),
        (WHOLE,) * 3 + (ANYWHERE,) * 3,
        scratch=(ghost, pltpu.SemaphoreType.DMA((2, 3))),
        aliases=same,
        name="last",
    )
    return results[3:]


def solution(mesh):
    placed = (
        P(None, ("runs", "line"), None, None),
        P(None, ("runs", "line"), None, None),
        P(None, ("runs", "line"), None, None),
        P(("runs", "line"), None),
        P("line", "runs", None),
        P(),
        P(),
        P(),
        P(),
        P(),
        P(),
        P(None, ("runs", "line")),
        P(None, ("runs", "line")),
        P(),
    )
    return jax.shard_map(
        body,
        mesh=mesh,
        in_specs=placed,
        out_specs=(
            P(None, ("runs", "line"), None, None),
            P(None, ("runs", "line"), None, None),
            P(None, ("runs", "line"), None, None),
        ),
        check_vma=False,
    )
```

```python
import functools

import jax
import jax.numpy as jnp
import numpy as np
from jax import lax
from jax.experimental import pallas as pl
from jax.experimental.pallas import tpu as pltpu
from jax.sharding import PartitionSpec as P

STEPS = 6
FY = 8
FZ = 64
DT = 0.25
PAD = 8
ROWS = 16
UNROLL = 4
VMEM_LIMIT = 32 * 1024 * 1024

C_B, C_B0, C_B1, C_M0, C_M1, C_LAM, C_MU2, C_MU, C_K1, C_K2, C_K2H, C_L0 = range(12)
N_COEF = 16

VX, VY, VZ = range(3)
XX, YY, ZZ, XY, XZ, YZ = range(6)


def lane_roll(x, shift):
    return pltpu.roll(x, shift % x.shape[-1], x.ndim - 1)


def before(x):
    return lane_roll(x, 1)


def after(x):
    return lane_roll(x, -1)


def over_rows(count, work):
    def step(i, carry):
        work(pl.multiple_of(i * ROWS, ROWS))
        return carry

    lax.fori_loop(0, count // ROWS, step, 0, unroll=UNROLL)


class Planes:
    def __init__(self, ref, first, across):
        self.ref, self.first, self.shape = ref, first, (3, across, ref.shape[1])

    def rows(self, at):
        plane, out = at
        return pl.ds((self.first + plane) * self.shape[1] + out.start, out.size)

    def __getitem__(self, at):
        return self.ref[self.rows(at)]

    def __setitem__(self, at, value):
        self.ref[self.rows(at)] = value


def coefs(coef_ref, ids):
    return [coef_ref[i : i + 1, :] for i in ids]


def place():
    index = lax.axis_index("line")
    return lax.rem(index, 2) == 0, index > 0, index < lax.axis_size("line") - 1


def spans(r):
    return pl.ds(PAD + r, ROWS), pl.ds(PAD + r - 1, ROWS), pl.ds(PAD + r + 1, ROWS), pl.ds(r, ROWS)


def zero_edges(ref):
    across = ref.shape[-2] - 2 * PAD
    edge = jnp.zeros((PAD, ref.shape[-1]), jnp.float32)
    for where in np.ndindex(*ref.shape[:-2]):
        ref[(*where, pl.ds(0, PAD))] = edge
        ref[(*where, pl.ds(PAD + across, PAD))] = edge


def add_force(ref, index, force, which, first_row):
    rows = pl.ds(first_row, 16)
    ref[(*index, rows)] = ref[(*index, rows)] + force[which]


def pre_ahead(V, S, coef_ref, msg, force, window):
    b, b0 = coefs(coef_ref, (C_B, C_B0))

    def work(r):
        here, up, _, out = spans(r)
        sxy, sxz = S[XY, 1, here], S[XZ, 1, here]
        px = V[VX, 1, here] + b * (sxy - S[XY, 1, up] + sxz - S[XX, 1, here]) - b0 * before(sxz)
        V[VX, 1, here] = px
        if msg is not None:
            msg[0, out] = sxy
            msg[1, out] = sxz
            msg[2, out] = px

    over_rows(V.shape[2] - 2 * PAD, work)
    if force is not None:
        add_force(V, (VX, 1), force, (VX, 1), PAD + window)
        if msg is not None:
            add_force(msg, (2,), force, (VX, 1), window)


def pre_behind(V, S, coef_ref, msg, force, window):
    b, b0, b1 = coefs(coef_ref, (C_B, C_B0, C_B1))

    def work(r):
        here, up, down, out = spans(r)
        syz, szz = S[YZ, 0, here], S[ZZ, 0, here]
        qy = V[VY, 0, here] + b * (S[XY, 0, here] + S[YY, 0, down] - S[YY, 0, here] + syz) - b0 * before(syz)
        qz = V[VZ, 0, here] + b * (S[XZ, 0, here] + syz - S[YZ, 0, up] - szz) + b1 * after(szz)
        V[VY, 0, here] = qy
        V[VZ, 0, here] = qz
        if msg is not None:
            msg[0, out] = S[XX, 0, here]
            msg[1, out] = qy
            msg[2, out] = qz

    over_rows(V.shape[2] - 2 * PAD, work)
    if force is not None:
        add_force(V, (VY, 0), force, (VY, 0), PAD + window)
        add_force(V, (VZ, 0), force, (VZ, 0), PAD + window)
        if msg is not None:
            add_force(msg, (1,), force, (VY, 0), window)
            add_force(msg, (2,), force, (VZ, 0), window)


def inner(V, S, coef_ref, force, window):
    b, b0, b1 = coefs(coef_ref, (C_B, C_B0, C_B1))

    def work(r):
        here, up, down, _ = spans(r)
        sxy, sxz = S[XY, 0, here], S[XZ, 0, here]
        V[VX, 0, here] = (
            V[VX, 0, here]
            + b * (S[XX, 1, here] - S[XX, 0, here] + sxy - S[XY, 0, up] + sxz)
            - b0 * before(sxz)
        )
        syz, szz = S[YZ, 1, here], S[ZZ, 1, here]
        V[VY, 1, here] = (
            V[VY, 1, here]
            + b * (S[XY, 1, here] - sxy + S[YY, 1, down] - S[YY, 1, here] + syz)
            - b0 * before(syz)
        )
        V[VZ, 1, here] = (
            V[VZ, 1, here]
            + b * (S[XZ, 1, here] - sxz + syz - S[YZ, 1, up] - szz)
            + b1 * after(szz)
        )

    over_rows(V.shape[2] - 2 * PAD, work)
    if force is not None:
        add_force(V, (VX, 0), force, (VX, 0), PAD + window)
        add_force(V, (VY, 1), force, (VY, 1), PAD + window)
        add_force(V, (VZ, 1), force, (VZ, 1), PAD + window)


def post(V, S, R, coef_ref, surface, cell, column, behind_x, ahead_y, ahead_z):
    m0, m1, lam, mu2, mu, k1, k2, k2h, l0 = coefs(
        coef_ref, (C_M0, C_M1, C_LAM, C_MU2, C_MU, C_K1, C_K2, C_K2H, C_L0)
    )

    def work(r):
        here, up, down, out = spans(r)
        vx, vy, vz = V[VX, cell, here], V[VY, cell, here], V[VZ, cell, here]
        exx = vx - behind_x(r)
        eyy = vy - V[VY, cell, up]
        ezz = vz - m0 * before(vz)
        exy = V[VX, cell, down] - vx + (ahead_y(r) - vy)
        exz = m1 * after(vx) - vx + (ahead_z(r) - vz)
        eyz = m1 * after(vy) - vy + (V[VZ, cell, down] - vz)
        volume = lam * (exx + eyy + ezz)
        for comp, e in ((XX, exx), (YY, eyy), (ZZ, ezz)):
            old = R[comp, cell, out]
            new = S[comp, cell, here] + (volume + mu2 * e) + DT * old
            if comp == ZZ:
                new = new + l0 * lane_roll(surface[out, :], -column)
            S[comp, cell, here] = new
            R[comp, cell, out] = k1 * old - k2 * e
        for comp, e in ((XY, exy), (XZ, exz), (YZ, eyz)):
            old = R[comp, cell, out]
            S[comp, cell, here] = S[comp, cell, here] + mu * e + DT * old
            R[comp, cell, out] = k1 * old - k2h * e

    over_rows(R.shape[2], work)


def response_behind(V, S, coef_ref, D, W):
    b, b0, b1, m0, m1, lam, mu2, mu = coefs(coef_ref, (C_B, C_B0, C_B1, C_M0, C_M1, C_LAM, C_MU2, C_MU))

    def work(r):
        here, up, down, out = spans(r)
        sxy = S[XY, 1, here]
        vy, vz = -b * sxy, -b * S[XZ, 1, here]
        exx = -V[VX, 1, here]
        eyy = b * (S[XY, 1, up] - sxy)
        ezz = vz - m0 * before(vz)
        volume = lam * (exx + eyy + ezz)
        dyy, dzz = volume + mu2 * eyy, volume + mu2 * ezz
        dyz = mu * (m1 * after(vy) - vy - b * S[XZ, 1, down] - vz)
        W[0, here] = dyy
        W[1, here] = dyz
        D[0, out] = volume + mu2 * exx
        D[1, out] = vy + b * (dyz - mu * vy - dyy) - b0 * before(dyz)
        D[2, out] = vz + b * (dyz - mu * vz - dzz) + b1 * after(dzz)

    over_rows(D.shape[1], work)

    def rest(r):
        _, up, down, out = spans(r)
        D[1, out] = D[1, out] + b * W[0, down]
        D[2, out] = D[2, out] - b * W[1, up]

    over_rows(D.shape[1], rest)


def response_ahead(V, S, coef_ref, D, W):
    b, b0, m1, lam, mu2, mu = coefs(coef_ref, (C_B, C_B0, C_M1, C_LAM, C_MU2, C_MU))

    def work(r):
        here, _, down, out = spans(r)
        vx = b * S[XX, 0, here]
        dxy = mu * (b * S[XX, 0, down] - vx + V[VY, 0, here])
        dxz = mu * (m1 * after(vx) - vx + V[VZ, 0, here])
        W[0, here] = dxy
        D[0, out] = dxy
        D[1, out] = dxz
        D[2, out] = vx + b * (dxy + dxz - (lam + mu2) * vx) - b0 * before(dxz)

    over_rows(D.shape[1], work)

    def rest(r):
        _, up, _, out = spans(r)
        D[2, out] = D[2, out] - b * W[0, up]

    over_rows(D.shape[1], rest)


def first_response_behind(V, S, coef_ref, force, load, D, W, A, window):
    b, b0, b1, m0, m1, lam, mu2, mu, l0 = coefs(
        coef_ref, (C_B, C_B0, C_B1, C_M0, C_M1, C_LAM, C_MU2, C_MU, C_L0)
    )
    A[...] = jnp.zeros(A.shape, jnp.float32)

    def given(r):
        here, _, _, _ = spans(r)
        A[1, here] = -b * S[XY, 1, here]
        A[2, here] = -b * S[XZ, 1, here]

    over_rows(D.shape[1], given)
    for i, which in enumerate(((VX, 3), (VY, 2), (VZ, 2), (VY, 3), (VZ, 3))):
        add_force(A, (i,), force, which, PAD + window)

    def work(r):
        here, up, down, out = spans(r)
        vx, vy, vz = A[0, here], A[1, here], A[2, here]
        exx = vx - V[VX, 1, here]
        eyy = vy - A[1, up]
        ezz = vz - m0 * before(vz)
        volume = lam * (exx + eyy + ezz)
        dyy = volume + mu2 * eyy
        dzz = volume + mu2 * ezz + l0 * load[out, :]
        dxy = mu * (A[0, down] - vx + (A[3, here] - vy))
        dxz = mu * (m1 * after(vx) - vx + (A[4, here] - vz))
        dyz = mu * (m1 * after(vy) - vy + (A[2, down] - vz))
        W[0, here] = dyy
        W[1, here] = dyz
        D[0, out] = volume + mu2 * exx
        D[1, out] = vy + b * (dxy - dyy + dyz) - b0 * before(dyz)
        D[2, out] = vz + b * (dxz + dyz - dzz) + b1 * after(dzz)

    over_rows(D.shape[1], work)

    def rest(r):
        _, up, down, out = spans(r)
        D[1, out] = D[1, out] + b * W[0, down]
        D[2, out] = D[2, out] - b * W[1, up]

    over_rows(D.shape[1], rest)


def first_response_ahead(V, S, coef_ref, force, D, W, A, window):
    b, b0, m0, m1, lam, mu2, mu = coefs(coef_ref, (C_B, C_B0, C_M0, C_M1, C_LAM, C_MU2, C_MU))
    A[...] = jnp.zeros(A.shape, jnp.float32)

    def given(r):
        here, _, _, _ = spans(r)
        A[0, here] = b * S[XX, 0, here]

    over_rows(D.shape[1], given)
    for i, which in enumerate(((VX, 2), (VY, 3), (VZ, 3), (VX, 3))):
        add_force(A, (i,), force, which, PAD + window)

    def work(r):
        here, up, down, out = spans(r)
        vx, vy, vz = A[0, here], A[1, here], A[2, here]
        exx = vx - A[3, here]
        dxx = lam * (exx + (vy - A[1, up]) + (vz - m0 * before(vz))) + mu2 * exx
        dxy = mu * (A[0, down] - vx + (V[VY, 0, here] - vy))
        dxz = mu * (m1 * after(vx) - vx + (V[VZ, 0, here] - vz))
        W[0, here] = dxy
        D[0, out] = dxy
        D[1, out] = dxz
        D[2, out] = vx + b * (dxy + dxz - dxx) - b0 * before(dxz)

    over_rows(D.shape[1], work)

    def rest(r):
        _, up, _, out = spans(r)
        D[2, out] = D[2, out] - b * W[0, up]

    over_rows(D.shape[1], rest)


def early_ahead(V, S, R, coef_ref, msg, W, force, window):
    b, b0, m0, m1, lam, mu2, mu = coefs(coef_ref, (C_B, C_B0, C_M0, C_M1, C_LAM, C_MU2, C_MU))

    def work(r):
        here, up, down, out = spans(r)
        vx, vy, vz = V[VX, 1, here], V[VY, 1, here], V[VZ, 1, here]
        exx = vx - V[VX, 0, here]
        volume = lam * (exx + (vy - V[VY, 1, up]) + (vz - m0 * before(vz)))
        sxx = S[XX, 1, here] + (volume + mu2 * exx) + DT * R[XX, 1, out]
        sxy = S[XY, 1, here] + mu * (V[VX, 1, down] - vx - vy) + DT * R[XY, 1, out]
        sxz = S[XZ, 1, here] + mu * (m1 * after(vx) - vx - vz) + DT * R[XZ, 1, out]
        W[0, here] = sxy
        msg[0, out] = sxy
        msg[1, out] = sxz
        msg[2, out] = vx + b * (sxy + sxz - sxx) - b0 * before(sxz)

    over_rows(msg.shape[1], work)

    def rest(r):
        _, up, _, out = spans(r)
        msg[2, out] = msg[2, out] - b * W[0, up]

    over_rows(msg.shape[1], rest)
    if force is not None:
        add_force(msg, (2,), force, (VX, 1), window)


def early_behind(V, S, R, coef_ref, surface, column, msg, W, force, window):
    b, b0, b1, m0, m1, lam, mu2, mu, l0 = coefs(
        coef_ref, (C_B, C_B0, C_B1, C_M0, C_M1, C_LAM, C_MU2, C_MU, C_L0)
    )

    def work(r):
        here, up, down, out = spans(r)
        vx, vy, vz = V[VX, 0, here], V[VY, 0, here], V[VZ, 0, here]
        eyy = vy - V[VY, 0, up]
        ezz = vz - m0 * before(vz)
        volume = lam * (vx + eyy + ezz)
        sxx = S[XX, 0, here] + (volume + mu2 * vx) + DT * R[XX, 0, out]
        syy = S[YY, 0, here] + (volume + mu2 * eyy) + DT * R[YY, 0, out]
        szz = S[ZZ, 0, here] + (volume + mu2 * ezz) + DT * R[ZZ, 0, out]
        if surface is not None:
            szz = szz + l0 * lane_roll(surface[out, :], -column)
        sxy = S[XY, 0, here] + mu * (V[VX, 0, down] - vx + (V[VY, 1, here] - vy)) + DT * R[XY, 0, out]
        sxz = S[XZ, 0, here] + mu * (m1 * after(vx) - vx + (V[VZ, 1, here] - vz)) + DT * R[XZ, 0, out]
        syz = S[YZ, 0, here] + mu * (m1 * after(vy) - vy + (V[VZ, 0, down] - vz)) + DT * R[YZ, 0, out]
        W[0, here] = syy
        W[1, here] = syz
        msg[0, out] = sxx
        msg[1, out] = vy + b * (sxy - syy + syz) - b0 * before(syz)
        msg[2, out] = vz + b * (sxz + syz - szz) + b1 * after(szz)

    over_rows(msg.shape[1], work)

    def rest(r):
        _, up, down, out = spans(r)
        msg[1, out] = msg[1, out] + b * W[0, down]
        msg[2, out] = msg[2, out] - b * W[1, up]

    over_rows(msg.shape[1], rest)
    if force is not None:
        add_force(msg, (1,), force, (VY, 0), window)
        add_force(msg, (2,), force, (VZ, 0), window)


def ahead_bond(V, S, R, coef_ref, force, surface, msg, missing, G, step, window, unforced=0, respond=None):
    (b,) = coefs(coef_ref, (C_B,))
    _, _, has_ahead = place()
    keep = jnp.where(has_ahead, 1.0, 0.0).astype(jnp.float32)

    def got(i, out):
        return msg[i, out] if missing is None else msg[i, out] + missing[i, out]

    def work(r):
        here, _, _, out = spans(r)
        V[VX, 1, here] = V[VX, 1, here] + (keep * b) * got(0, out)
        G[0, out] = keep * (got(1, out) - b * S[XY, 1, here])
        G[1, out] = keep * (got(2, out) - b * S[XZ, 1, here])

    over_rows(R.shape[2], work)
    if step < unforced:
        add_force(G, (0,), force, (VY, 2), window)
        add_force(G, (1,), force, (VZ, 2), window)
    if respond is not None:
        respond()
    post(
        V, S, R, coef_ref, surface, 1, 2 * step + 1,
        lambda r: V[VX, 0, pl.ds(PAD + r, ROWS)],
        lambda r: G[0, pl.ds(r, ROWS)],
        lambda r: G[1, pl.ds(r, ROWS)],
    )


def behind_bond(V, S, R, coef_ref, force, surface, msg, missing, G, step, window, unforced=0, respond=None):
    (b,) = coefs(coef_ref, (C_B,))
    _, has_behind, _ = place()
    keep = jnp.where(has_behind, 1.0, 0.0).astype(jnp.float32)

    def got(i, out):
        return msg[i, out] if missing is None else msg[i, out] + missing[i, out]

    def work(r):
        here, _, _, out = spans(r)
        V[VY, 0, here] = V[VY, 0, here] - (keep * b) * got(0, out)
        V[VZ, 0, here] = V[VZ, 0, here] - (keep * b) * got(1, out)
        G[0, out] = keep * (got(2, out) + b * S[XX, 0, here])

    over_rows(R.shape[2], work)
    if step < unforced:
        add_force(G, (0,), force, (VX, 2), window)
    if respond is not None:
        respond()
    post(
        V, S, R, coef_ref, surface, 0, 2 * step,
        lambda r: G[0, pl.ds(r, ROWS)],
        lambda r: V[VY, 1, pl.ds(PAD + r, ROWS)],
        lambda r: V[VZ, 1, pl.ds(PAD + r, ROWS)],
    )


def start_kernel(
    velocity, stress, memory, layer_in, lam_in, mu_in, buoy_in, rate_in, defect_in, loads, steps_table,
    V, S, R, coef_ref, msg_near, msg_far, W, table, layer_ref, lam, mu, buoy, rate, defect, sems,
):
    across = velocity.shape[2]
    inside = pl.ds(PAD, across)
    pairs = [
        (layer_in, layer_ref), (lam_in, lam), (mu_in, mu), (buoy_in, buoy), (rate_in, rate), (defect_in, defect),
    ]
    pairs += [(stress.at[i], S.at[i, :, inside]) for i in range(6)]
    pairs += [(velocity.at[i], V.at[i, :, inside]) for i in range(3)]
    pairs += [(memory.at[i], R.at[i]) for i in range(6)]
    copies = [pltpu.make_async_copy(*pair, sems.at[i]) for i, pair in enumerate(pairs)]
    for copy in copies:
        copy.start()
    slots = loads.shape[0]
    zero_edges(V)
    zero_edges(S)
    zero_edges(W)
    table[...] = jnp.zeros(table.shape, jnp.float32)
    table[0:16, :] = steps_table[...]
    columns = table[...].T
    trucks = 6 * across
    msg_far[trucks : trucks + slots, :] = loads[...]
    for i, at in enumerate((0, 8)):
        first_row = trucks + (1 + i) * slots
        column = columns[0:slots, at : at + 1]
        msg_far[first_row : first_row + slots, :] = jnp.broadcast_to(column, loads.shape)
    for copy in copies[:6]:
        copy.wait()
    layer = layer_ref[...]

    def per_depth(table):
        row = jnp.zeros(layer.shape, jnp.float32)
        for level in range(table.shape[0]):
            row = jnp.where(layer == level, table[level], row)
        return row

    lane = lax.broadcasted_iota(jnp.int32, layer.shape, 1)
    not_first = jnp.where(lane > 0, 1.0, 0.0).astype(jnp.float32)
    not_last = jnp.where(lane < layer.shape[1] - 1, 1.0, 0.0).astype(jnp.float32)
    b = DT * per_depth(buoy)
    two_mu = (2.0 * DT) * per_depth(mu)
    decay = DT * per_depth(rate)
    drop = 2.0 * decay * per_depth(defect)
    for row, value in (
        (C_B, b),
        (C_B0, b * not_first),
        (C_B1, b * not_last),
        (C_M0, not_first),
        (C_M1, not_last),
        (C_LAM, DT * per_depth(lam)),
        (C_MU2, two_mu),
        (C_MU, 0.5 * two_mu),
        (C_K1, 1.0 - decay),
        (C_K2, drop),
        (C_K2H, 0.5 * drop),
        (C_L0, DT * (1.0 - not_first)),
    ):
        coef_ref[row : row + 1, :] = value
    coef_ref[12:16, :] = jnp.zeros((4, layer.shape[1]), jnp.float32)
    for copy in copies[6:15]:
        copy.wait()
    even, _, _ = place()
    now, then = Planes(msg_far, 0, across), Planes(msg_far, 3, across)

    @pl.when(even)
    def _():
        pre_ahead(V, S, coef_ref, msg_near, None, 0)
        pre_behind(V, S, coef_ref, now, None, 0)

    @pl.when(jnp.logical_not(even))
    def _():
        pre_behind(V, S, coef_ref, msg_near, None, 0)
        pre_ahead(V, S, coef_ref, now, None, 0)

    inner(V, S, coef_ref, None, 0)
    for copy in copies[15:]:
        copy.wait()

    @pl.when(even)
    def _():
        early_behind(V, S, R, coef_ref, None, 0, then, W, None, 0)

    @pl.when(jnp.logical_not(even))
    def _():
        early_ahead(V, S, R, coef_ref, then, W, None, 0)


def near_kernel(step, window, V0, S0, R0, coef_ref, force, surface, msg, V, S, R, *rest):
    G = rest[-1]
    if step == 0:
        for comp in range(3):
            for cell in range(2):
                add_force(V, (comp, cell), force, (0, comp, cell), PAD + window)
    even, _, _ = place()
    more = step < STEPS - 1

    @pl.when(even)
    def _():
        ahead_bond(V, S, R, coef_ref, force.at[step], surface, msg, None, G, step, window, 1)
        if more:
            pre_ahead(V, S, coef_ref, rest[0], force.at[step + 1], window)

    @pl.when(jnp.logical_not(even))
    def _():
        behind_bond(V, S, R, coef_ref, force.at[step], surface, msg, None, G, step, window, 1)
        if more:
            pre_behind(V, S, coef_ref, rest[0], force.at[step + 1], window)


def load_ahead(msg, loads, across, rows_out, load):
    slots = loads.shape[0]
    rows, entry, cell = (msg[6 * across + i * slots : 6 * across + (i + 1) * slots, :] for i in range(3))
    for slot in range(slots):
        rows = jnp.where(entry == float(slot), loads[slot : slot + 1, :], rows)
    rows_out[...] = jnp.zeros(rows_out.shape, jnp.float32)
    rows_out[0:1, :] = jnp.sum(jnp.where(cell == 0.0, rows, 0.0), axis=0, keepdims=True)
    load[...] = rows_out[...].T


def far_kernel(step, window, V0, S0, R0, coef_ref, force, surface, msg, *rest):
    rest = list(rest)
    other = rest.pop(0)
    V, S, R, D = rest[:4]
    early = rest[4] if step < STEPS - 2 else None
    across = R.shape[2]
    even, _, _ = place()
    here, then = force.at[step], force.at[step + 1]
    got = Planes(msg, 3 * step, across) if step < 2 else msg
    if step == 0:
        missing, loads = None, other
        G, W, A, load, rows_out = rest[-5:]
    else:
        missing = other
        G, W = rest[-2:]
    zero_edges(W)

    @pl.when(even)
    def _():
        if step == 0:
            respond = lambda: first_response_ahead(V, S, coef_ref, here, D, W, A, window)
        else:
            respond = lambda: response_ahead(V, S, coef_ref, D, W)
        behind_bond(
            V, S, R, coef_ref, here, surface, got, missing, G, step, window, 2, respond
        )
        pre_behind(V, S, coef_ref, None, then, window)

    @pl.when(jnp.logical_not(even))
    def _():
        if step == 0:
            load_ahead(msg, loads, across, rows_out, load)
            respond = lambda: first_response_behind(V, S, coef_ref, here, load, D, W, A, window)
        else:
            respond = lambda: response_behind(V, S, coef_ref, D, W)
        ahead_bond(
            V, S, R, coef_ref, here, surface, got, missing, G, step, window, 2, respond
        )
        pre_ahead(V, S, coef_ref, None, then, window)

    inner(V, S, coef_ref, then, window)
    if early is not None:
        later = force.at[step + 2]

        @pl.when(even)
        def _():
            early_behind(V, S, R, coef_ref, surface, 2 * (step + 1), early, W, later, window)

        @pl.when(jnp.logical_not(even))
        def _():
            early_ahead(V, S, R, coef_ref, early, W, later, window)


def last_kernel(
    step, window, V0, S0, R0, coef_ref, force, surface, msg, missing, V, S, R, v_out, s_out, r_out, G, sems
):
    even, _, _ = place()
    here = force.at[step]
    inside = pl.ds(PAD, R.shape[2])

    def copies(cell):
        return [
            pltpu.make_async_copy(V.at[:, cell, inside], v_out.at[:, cell], sems.at[cell, 0]),
            pltpu.make_async_copy(S.at[:, cell, inside], s_out.at[:, cell], sems.at[cell, 1]),
            pltpu.make_async_copy(R.at[:, cell], r_out.at[:, cell], sems.at[cell, 2]),
        ]

    def finish(cell, bond):
        done, other = copies(1 - cell), copies(cell)
        for copy in done:
            copy.start()
        bond(V, S, R, coef_ref, here, surface, msg, missing, G, step, window)
        for copy in other:
            copy.start()
        for copy in done + other:
            copy.wait()

    @pl.when(even)
    def _():
        finish(0, behind_bond)

    @pl.when(jnp.logical_not(even))
    def _():
        finish(1, ahead_bond)


ENTRY_ROW, TRUCK_ROW = 48, 56
GROUP = 8


def pack_kernel(
    record, loads_in, entries_in, cells_in, piers_in, own, loads, steps_table, piers, entries, cells, sems
):
    panel = record.shape[1]
    slots, lanes = loads.shape
    steps = entries.shape[0]
    pairs = [(record, own.at[:, pl.ds(0, panel)]), (loads_in, loads), (entries_in, entries), (cells_in, cells)]
    pairs.append((piers_in, piers))
    copies = [pltpu.make_async_copy(*pair, sems.at[i]) for i, pair in enumerate(pairs)]
    for copy in copies:
        copy.start()
    own[:, panel:] = jnp.zeros((own.shape[0], own.shape[1] - panel), jnp.float32)
    steps_table[...] = jnp.zeros(steps_table.shape, jnp.float32)
    for copy in copies:
        copy.wait()
    steps_table[0:steps, 0:slots] = entries[...].astype(jnp.float32)
    steps_table[8 : 8 + steps, 0:slots] = cells[...].astype(jnp.float32)
    blocks = [loads[8 * i : 8 * i + 8, :] for i in range(slots // 8)] + [steps_table[0:8, :]]
    for i, block in enumerate(blocks):
        own[0:8, panel + i * lanes : panel + (i + 1) * lanes] = block


def lane_blocks(table, width):
    return sum(lane_roll(table[s : s + 1, :], s * width) for s in range(STEPS))


def split_kernel(panel, slots, own, behind, cells, after_this, out):
    del after_this
    tiles, _, lanes = out.shape
    pieces = panel // lanes
    third = pieces // 3
    cell_of = cells[...]
    me = lax.axis_index("line")
    group, mine = lax.div(me, tiles), lax.rem(me, tiles)
    row = lax.broadcasted_iota(jnp.int32, (4 * tiles, cell_of.shape[1]), 0)
    tile, j = lax.div(row, 4), lax.rem(row, 4)
    odd = lax.rem(tile, 2)
    first = (tile + group * tiles) * 2
    cell_x = first + jnp.where(j == 2, -1, jnp.where(j == 3, 4 * odd - 2, j))
    cell_yz = first + jnp.where(j == 3, 4 * odd - 1, j)
    record = jnp.where(group == 0, own[:, :panel], behind[:, :panel])

    def share(cell, columns):
        hit = jnp.where(cell == cell_of, 1.0, 0.0).astype(jnp.float32)
        return jnp.dot(
            hit, record[:, columns], precision=lax.Precision.HIGHEST, preferred_element_type=jnp.float32
        )

    part_x = share(cell_x, slice(0, third * lanes))
    part_yz = share(cell_yz, slice(third * lanes, panel))

    def trucks(source):
        blocks = [source[0:8, panel + i * lanes : panel + (i + 1) * lanes] for i in range(slots // 8 + 1)]
        return blocks[:-1], lane_blocks(blocks[-1], slots)

    own_rows, own_entry = trucks(own)
    far_rows, far_entry = trucks(behind)
    for tile in range(tiles):
        these = slice(4 * tile, 4 * tile + 4)
        for m in range(pieces):
            part, at = (part_x, m) if m < third else (part_yz, m - third)
            out[tile, 4 * m : 4 * m + 4, :] = part[these, at * lanes : (at + 1) * lanes]
        passed = mine < tile
        out[tile, ENTRY_ROW : ENTRY_ROW + 1, :] = jnp.where(passed, own_entry, far_entry)
        for i in range(slots // 8):
            at = TRUCK_ROW + 8 * i
            out[tile, at : at + 8, :] = jnp.where(passed, own_rows[i], far_rows[i])


def prepare_kernel(parts, loads, steps_table, force, surface, table, rows_out):
    steps, comps, width = force.shape[:3]
    lanes = parts.shape[2]
    force[...] = jnp.zeros(force.shape, jnp.float32)
    per = ENTRY_ROW // (comps * width)
    lane = lax.broadcasted_iota(jnp.int32, (per, lanes), 1)
    scale = jnp.where(lane < FZ, DT, 0.0).astype(jnp.float32)
    for s in range(steps):
        for comp in range(comps):
            for cell in range(width):
                panel = parts[s, pl.ds(comp * per * width + cell, per, stride=width), :]
                force[s, comp, cell, pl.ds(4, per, stride=2), :] = scale * panel
                force[s, comp, cell, pl.ds(5, per, stride=2), :] = scale * lane_roll(panel, FZ)

    slots = loads.shape[0]
    tiles = parts.shape[0]
    mine = lax.rem(lax.axis_index("line"), tiles)
    table[...] = jnp.zeros(table.shape, jnp.float32)
    table[0:1, :] = lane_blocks(steps_table[0:8, :], slots)
    table[STEPS + 1 : STEPS + 2, :] = lane_blocks(steps_table[8:16, :], slots)
    rows = [loads[...]]
    for k in range(1, STEPS + 1):
        source = lax.rem(mine + (tiles - k), tiles)
        rows.append(parts[source, TRUCK_ROW : TRUCK_ROW + slots, :])
        table[k : k + 1, :] = parts[source, ENTRY_ROW : ENTRY_ROW + 1, :]
    columns = table[...].T
    rows_out[...] = jnp.zeros(rows_out.shape, jnp.float32)
    for s in range(STEPS):
        block = slice(s * slots, (s + 1) * slots)
        moved = []
        for k in range(STEPS - s):
            entry = jnp.broadcast_to(columns[block, k : k + 1], rows[k].shape)
            new = rows[k]
            for slot in range(slots):
                new = jnp.where(entry == float(slot), rows[k + 1][slot : slot + 1, :], new)
            moved.append(new)
        rows = moved
        cell = jnp.broadcast_to(columns[block, STEPS + 1 : STEPS + 2], rows[0].shape)
        for c in range(2):
            load = jnp.sum(jnp.where(cell == float(c), rows[0], 0.0), axis=0, keepdims=True)
            rows_out[2 * s + c : 2 * s + c + 1, :] = load
    surface[...] = rows_out[...].T


def in_vmem(x):
    return pltpu.with_memory_space_constraint(x, pltpu.VMEM)


WHOLE = pl.BlockSpec(memory_space=pltpu.VMEM)
SCALARS = pl.BlockSpec(memory_space=pltpu.SMEM)
ANYWHERE = pl.BlockSpec(memory_space=pl.ANY)


def call(kernel, ins, specs, outs, out_specs, scratch=(), aliases=None, name=None):
    return pl.pallas_call(
        kernel,
        out_shape=outs,
        in_specs=specs,
        out_specs=out_specs,
        scratch_shapes=list(scratch),
        input_output_aliases=aliases or {},
        compiler_params=pltpu.CompilerParams(vmem_limit_bytes=VMEM_LIMIT),
        name=name,
    )(*ins)


def body(
    velocity, stress, memory, truck_loads, pier_panels,
    lame_lambda, lame_mu, buoyancy, relax_rate, defect_mu, layer,
    truck_entry, truck_cell, pier_cell,
):
    tiles = lax.axis_size("line")
    width_x, across, depth = velocity.shape[1:]
    slots = truck_loads.shape[0]
    window = (across - FY) // 2 - 4
    f32 = jnp.float32

    near = [(i, i ^ 1) for i in range(tiles) if (i ^ 1) < tiles]
    far = [(i, i + 1) for i in range(1, tiles - 1, 2)] + [(i + 1, i) for i in range(1, tiles - 1, 2)]

    padded = across + 2 * PAD
    v_type = pltpu.VMEM((3, width_x, padded, depth), f32)
    s_type = pltpu.VMEM((6, width_x, padded, depth), f32)
    r_type = pltpu.VMEM((6, width_x, across, depth), f32)
    c_type = pltpu.VMEM((N_COEF, depth), f32)
    m_type = pltpu.VMEM((3, across, depth), f32)
    ghost = pltpu.VMEM((2, across, depth), f32)
    work = pltpu.VMEM((2, padded, depth), f32)
    square = pltpu.VMEM((across, depth), f32)

    def ahead_by(x, distance):
        return lax.ppermute(x, "line", [(i, i + distance) for i in range(tiles - distance)])

    def in_hbm(*arrays):
        return tuple(pltpu.with_memory_space_constraint(x, pltpu.HBM) for x in arrays)

    dma = pltpu.SemaphoreType.DMA
    piers, panel = pier_panels.shape[1:]
    own, loads, steps_table, pier_row = call(
        pack_kernel,
        in_hbm(pier_panels[0], truck_loads, truck_entry, truck_cell, pier_cell[None, :]),
        (ANYWHERE,) * 5,
        (
            pltpu.VMEM((piers, panel + (slots // 8 + 1) * depth), f32),
            pltpu.VMEM((slots, depth), f32),
            pltpu.VMEM((16, depth), f32),
            pltpu.VMEM((1, piers), jnp.int32),
        ),
        (WHOLE,) * 4,
        scratch=(pltpu.VMEM(truck_entry.shape, jnp.int32), pltpu.VMEM(truck_cell.shape, jnp.int32), dma((5,))),
        name="pack",
    )
    behind = ahead_by(own, GROUP)
    reach = 2 * GROUP
    index = lax.axis_index("line")
    while reach < tiles:
        record = jnp.where(index < GROUP, own, behind)[:, :panel]
        record = jnp.where(index < reach, record, ahead_by(record, reach))
        behind = jnp.concatenate([record, behind[:, panel:]], axis=1)
        reach *= 2
    tables = (lame_lambda, lame_mu, buoyancy, relax_rate, defect_mu)
    V, S, R, coef, msg_near, msg_far = call(
        start_kernel,
        in_hbm(velocity, stress, memory, layer[None, :], *tables) + (in_vmem(loads), in_vmem(steps_table)),
        (ANYWHERE,) * 9 + (WHOLE,) * 2,
        (v_type, s_type, r_type, c_type, m_type, pltpu.VMEM((6 * across + 3 * slots, depth), f32)),
        (WHOLE,) * 6,
        scratch=(
            work, pltpu.VMEM((depth, depth), f32), pltpu.VMEM((1, depth), jnp.int32),
            *(pltpu.SMEM(table.shape, f32) for table in tables), dma((21,)),
        ),
        name="start",
    )
    msg_far = lax.ppermute(msg_far, "line", far)
    msg_near = lax.ppermute(msg_near, "line", near)
    parts = call(
        functools.partial(split_kernel, panel, slots),
        (own, behind, in_vmem(pier_row), msg_near),
        (WHOLE,) * 3 + (ANYWHERE,),
        jax.ShapeDtypeStruct((GROUP, TRUCK_ROW + slots, depth), f32),
        WHOLE,
        name="split",
    )
    groups = [list(range(at, at + GROUP)) for at in range(0, tiles, GROUP)]
    parts = lax.all_to_all(parts, "line", 0, 0, axis_index_groups=groups, tiled=True)
    force, surface = call(
        prepare_kernel,
        (parts, in_vmem(loads), in_vmem(steps_table)),
        (WHOLE,) * 3,
        (pltpu.VMEM((STEPS, 3, 4, 16, depth), f32), pltpu.VMEM((across, depth), f32)),
        (WHOLE,) * 2,
        scratch=(pltpu.VMEM((depth, depth), f32), pltpu.VMEM((depth, across), f32)),
        name="prepare",
    )
    state = (v_type, s_type, r_type)
    same = {0: 0, 1: 1, 2: 2}
    missing = None
    for step in range(STEPS):
        more = step < STEPS - 1
        ins = tuple(in_vmem(x) for x in (V, S, R, coef, force, surface, msg_near))
        outs = state + ((m_type,) if more else ())
        V, S, R, *msg = call(
            functools.partial(near_kernel, step, window),
            ins,
            (WHOLE,) * len(ins),
            outs,
            (WHOLE,) * len(outs),
            scratch=(ghost,),
            aliases=same,
            name="near" + str(step),
        )
        if more:
            msg_near = lax.ppermute(msg[0], "line", near)
        ins = (V, S, R, coef, force, surface, msg_far, missing if step else loads)
        ins = tuple(in_vmem(x) for x in ins)
        if more:
            outs = state + (m_type,) + ((m_type,) if step < STEPS - 2 else ())
            V, S, R, missing, *msg = call(
                functools.partial(far_kernel, step, window),
                ins,
                (WHOLE,) * len(ins),
                outs,
                (WHOLE,) * len(outs),
                scratch=(ghost, work) + (() if step else (pltpu.VMEM((5, padded, depth), f32),) + (square,) * 2),
                aliases=same,
                name="far" + str(step),
            )
            if step > 0:
                msg_far = early
            if msg:
                early = lax.ppermute(msg[0], "line", far)
    results = call(
        functools.partial(last_kernel, STEPS - 1, window),
        ins,
        (WHOLE,) * len(ins),
        state + tuple(jax.ShapeDtypeStruct(x.shape, f32) for x in (velocity, stress, memory)),
        (WHOLE,) * 3 + (ANYWHERE,) * 3,
        scratch=(ghost, pltpu.SemaphoreType.DMA((2, 3))),
        aliases=same,
        name="last",
    )
    return results[3:]


def solution(mesh):
    placed = (
        P(None, ("runs", "line"), None, None),
        P(None, ("runs", "line"), None, None),
        P(None, ("runs", "line"), None, None),
        P(("runs", "line"), None),
        P("line", "runs", None),
        P(),
        P(),
        P(),
        P(),
        P(),
        P(),
        P(None, ("runs", "line")),
        P(None, ("runs", "line")),
        P(),
    )
    return jax.shard_map(
        body,
        mesh=mesh,
        in_specs=placed,
        out_specs=(
            P(None, ("runs", "line"), None, None),
            P(None, ("runs", "line"), None, None),
            P(None, ("runs", "line"), None, None),
        ),
        check_vma=False,
    )
```

```python
import functools

import jax
import jax.numpy as jnp
import numpy as np
from jax import lax
from jax.experimental import pallas as pl
from jax.experimental.pallas import tpu as pltpu
from jax.sharding import PartitionSpec as P

STEPS = 6
FY = 8
FZ = 64
DT = 0.25
PAD = 8
ROWS = 16
UNROLL = 4
VMEM_LIMIT = 32 * 1024 * 1024

C_B, C_B0, C_B1, C_M0, C_M1, C_LAM, C_MU2, C_MU, C_K1, C_K2, C_K2H, C_L0 = range(12)
N_COEF = 16

VX, VY, VZ = range(3)
XX, YY, ZZ, XY, XZ, YZ = range(6)


def lane_roll(x, shift):
    return pltpu.roll(x, shift % x.shape[-1], x.ndim - 1)


def before(x):
    return lane_roll(x, 1)


def after(x):
    return lane_roll(x, -1)


def over_rows(count, work):
    def step(i, carry):
        work(pl.multiple_of(i * ROWS, ROWS))
        return carry

    lax.fori_loop(0, count // ROWS, step, 0, unroll=UNROLL)


class Planes:
    def __init__(self, ref, first, across):
        self.ref, self.first, self.shape = ref, first, (3, across, ref.shape[1])

    def rows(self, at):
        plane, out = at
        return pl.ds((self.first + plane) * self.shape[1] + out.start, out.size)

    def __getitem__(self, at):
        return self.ref[self.rows(at)]

    def __setitem__(self, at, value):
        self.ref[self.rows(at)] = value


def coefs(coef_ref, ids):
    return [coef_ref[i : i + 1, :] for i in ids]


def place():
    index = lax.axis_index("line")
    return lax.rem(index, 2) == 0, index > 0, index < lax.axis_size("line") - 1


def spans(r):
    return pl.ds(PAD + r, ROWS), pl.ds(PAD + r - 1, ROWS), pl.ds(PAD + r + 1, ROWS), pl.ds(r, ROWS)


def zero_edges(ref):
    across = ref.shape[-2] - 2 * PAD
    edge = jnp.zeros((PAD, ref.shape[-1]), jnp.float32)
    for where in np.ndindex(*ref.shape[:-2]):
        ref[(*where, pl.ds(0, PAD))] = edge
        ref[(*where, pl.ds(PAD + across, PAD))] = edge


def add_force(ref, index, force, which, first_row):
    rows = pl.ds(first_row, 16)
    ref[(*index, rows)] = ref[(*index, rows)] + force[which]


def pre_ahead(V, S, coef_ref, msg, force, window):
    b, b0 = coefs(coef_ref, (C_B, C_B0))

    def work(r):
        here, up, _, out = spans(r)
        sxy, sxz = S[XY, 1, here], S[XZ, 1, here]
        px = V[VX, 1, here] + b * (sxy - S[XY, 1, up] + sxz - S[XX, 1, here]) - b0 * before(sxz)
        V[VX, 1, here] = px
        if msg is not None:
            msg[0, out] = sxy
            msg[1, out] = sxz
            msg[2, out] = px

    over_rows(V.shape[2] - 2 * PAD, work)
    if force is not None:
        add_force(V, (VX, 1), force, (VX, 1), PAD + window)
        if msg is not None:
            add_force(msg, (2,), force, (VX, 1), window)


def pre_behind(V, S, coef_ref, msg, force, window):
    b, b0, b1 = coefs(coef_ref, (C_B, C_B0, C_B1))

    def work(r):
        here, up, down, out = spans(r)
        syz, szz = S[YZ, 0, here], S[ZZ, 0, here]
        qy = V[VY, 0, here] + b * (S[XY, 0, here] + S[YY, 0, down] - S[YY, 0, here] + syz) - b0 * before(syz)
        qz = V[VZ, 0, here] + b * (S[XZ, 0, here] + syz - S[YZ, 0, up] - szz) + b1 * after(szz)
        V[VY, 0, here] = qy
        V[VZ, 0, here] = qz
        if msg is not None:
            msg[0, out] = S[XX, 0, here]
            msg[1, out] = qy
            msg[2, out] = qz

    over_rows(V.shape[2] - 2 * PAD, work)
    if force is not None:
        add_force(V, (VY, 0), force, (VY, 0), PAD + window)
        add_force(V, (VZ, 0), force, (VZ, 0), PAD + window)
        if msg is not None:
            add_force(msg, (1,), force, (VY, 0), window)
            add_force(msg, (2,), force, (VZ, 0), window)


def inner(V, S, coef_ref, force, window):
    b, b0, b1 = coefs(coef_ref, (C_B, C_B0, C_B1))

    def work(r):
        here, up, down, _ = spans(r)
        sxy, sxz = S[XY, 0, here], S[XZ, 0, here]
        V[VX, 0, here] = (
            V[VX, 0, here]
            + b * (S[XX, 1, here] - S[XX, 0, here] + sxy - S[XY, 0, up] + sxz)
            - b0 * before(sxz)
        )
        syz, szz = S[YZ, 1, here], S[ZZ, 1, here]
        V[VY, 1, here] = (
            V[VY, 1, here]
            + b * (S[XY, 1, here] - sxy + S[YY, 1, down] - S[YY, 1, here] + syz)
            - b0 * before(syz)
        )
        V[VZ, 1, here] = (
            V[VZ, 1, here]
            + b * (S[XZ, 1, here] - sxz + syz - S[YZ, 1, up] - szz)
            + b1 * after(szz)
        )

    over_rows(V.shape[2] - 2 * PAD, work)
    if force is not None:
        add_force(V, (VX, 0), force, (VX, 0), PAD + window)
        add_force(V, (VY, 1), force, (VY, 1), PAD + window)
        add_force(V, (VZ, 1), force, (VZ, 1), PAD + window)


def post(V, S, R, coef_ref, surface, cell, column, behind_x, ahead_y, ahead_z):
    m0, m1, lam, mu2, mu, k1, k2, k2h, l0 = coefs(
        coef_ref, (C_M0, C_M1, C_LAM, C_MU2, C_MU, C_K1, C_K2, C_K2H, C_L0)
    )

    def work(r):
        here, up, down, out = spans(r)
        vx, vy, vz = V[VX, cell, here], V[VY, cell, here], V[VZ, cell, here]
        exx = vx - behind_x(r)
        eyy = vy - V[VY, cell, up]
        ezz = vz - m0 * before(vz)
        exy = V[VX, cell, down] - vx + (ahead_y(r) - vy)
        exz = m1 * after(vx) - vx + (ahead_z(r) - vz)
        eyz = m1 * after(vy) - vy + (V[VZ, cell, down] - vz)
        volume = lam * (exx + eyy + ezz)
        for comp, e in ((XX, exx), (YY, eyy), (ZZ, ezz)):
            old = R[comp, cell, out]
            new = S[comp, cell, here] + (volume + mu2 * e) + DT * old
            if comp == ZZ:
                new = new + l0 * lane_roll(surface[out, :], -column)
            S[comp, cell, here] = new
            R[comp, cell, out] = k1 * old - k2 * e
        for comp, e in ((XY, exy), (XZ, exz), (YZ, eyz)):
            old = R[comp, cell, out]
            S[comp, cell, here] = S[comp, cell, here] + mu * e + DT * old
            R[comp, cell, out] = k1 * old - k2h * e

    over_rows(R.shape[2], work)


def response_behind(V, S, coef_ref, D, W):
    b, b0, b1, m0, m1, lam, mu2, mu = coefs(coef_ref, (C_B, C_B0, C_B1, C_M0, C_M1, C_LAM, C_MU2, C_MU))

    def work(r):
        here, up, down, out = spans(r)
        sxy = S[XY, 1, here]
        vy, vz = -b * sxy, -b * S[XZ, 1, here]
        exx = -V[VX, 1, here]
        eyy = b * (S[XY, 1, up] - sxy)
        ezz = vz - m0 * before(vz)
        volume = lam * (exx + eyy + ezz)
        dyy, dzz = volume + mu2 * eyy, volume + mu2 * ezz
        dyz = mu * (m1 * after(vy) - vy - b * S[XZ, 1, down] - vz)
        W[0, here] = dyy
        W[1, here] = dyz
        D[0, out] = volume + mu2 * exx
        D[1, out] = vy + b * (dyz - mu * vy - dyy) - b0 * before(dyz)
        D[2, out] = vz + b * (dyz - mu * vz - dzz) + b1 * after(dzz)

    over_rows(D.shape[1], work)

    def rest(r):
        _, up, down, out = spans(r)
        D[1, out] = D[1, out] + b * W[0, down]
        D[2, out] = D[2, out] - b * W[1, up]

    over_rows(D.shape[1], rest)


def response_ahead(V, S, coef_ref, D, W):
    b, b0, m1, lam, mu2, mu = coefs(coef_ref, (C_B, C_B0, C_M1, C_LAM, C_MU2, C_MU))

    def work(r):
        here, _, down, out = spans(r)
        vx = b * S[XX, 0, here]
        dxy = mu * (b * S[XX, 0, down] - vx + V[VY, 0, here])
        dxz = mu * (m1 * after(vx) - vx + V[VZ, 0, here])
        W[0, here] = dxy
        D[0, out] = dxy
        D[1, out] = dxz
        D[2, out] = vx + b * (dxy + dxz - (lam + mu2) * vx) - b0 * before(dxz)

    over_rows(D.shape[1], work)

    def rest(r):
        _, up, _, out = spans(r)
        D[2, out] = D[2, out] - b * W[0, up]

    over_rows(D.shape[1], rest)


def first_response_behind(V, S, coef_ref, force, load, D, W, A, window):
    b, b0, b1, m0, m1, lam, mu2, mu, l0 = coefs(
        coef_ref, (C_B, C_B0, C_B1, C_M0, C_M1, C_LAM, C_MU2, C_MU, C_L0)
    )
    A[...] = jnp.zeros(A.shape, jnp.float32)

    def given(r):
        here, _, _, _ = spans(r)
        A[1, here] = -b * S[XY, 1, here]
        A[2, here] = -b * S[XZ, 1, here]

    over_rows(D.shape[1], given)
    for i, which in enumerate(((VX, 3), (VY, 2), (VZ, 2), (VY, 3), (VZ, 3))):
        add_force(A, (i,), force, which, PAD + window)

    def work(r):
        here, up, down, out = spans(r)
        vx, vy, vz = A[0, here], A[1, here], A[2, here]
        exx = vx - V[VX, 1, here]
        eyy = vy - A[1, up]
        ezz = vz - m0 * before(vz)
        volume = lam * (exx + eyy + ezz)
        dyy = volume + mu2 * eyy
        dzz = volume + mu2 * ezz + l0 * load[out, :]
        dxy = mu * (A[0, down] - vx + (A[3, here] - vy))
        dxz = mu * (m1 * after(vx) - vx + (A[4, here] - vz))
        dyz = mu * (m1 * after(vy) - vy + (A[2, down] - vz))
        W[0, here] = dyy
        W[1, here] = dyz
        D[0, out] = volume + mu2 * exx
        D[1, out] = vy + b * (dxy - dyy + dyz) - b0 * before(dyz)
        D[2, out] = vz + b * (dxz + dyz - dzz) + b1 * after(dzz)

    over_rows(D.shape[1], work)

    def rest(r):
        _, up, down, out = spans(r)
        D[1, out] = D[1, out] + b * W[0, down]
        D[2, out] = D[2, out] - b * W[1, up]

    over_rows(D.shape[1], rest)


def first_response_ahead(V, S, coef_ref, force, D, W, A, window):
    b, b0, m0, m1, lam, mu2, mu = coefs(coef_ref, (C_B, C_B0, C_M0, C_M1, C_LAM, C_MU2, C_MU))
    A[...] = jnp.zeros(A.shape, jnp.float32)

    def given(r):
        here, _, _, _ = spans(r)
        A[0, here] = b * S[XX, 0, here]

    over_rows(D.shape[1], given)
    for i, which in enumerate(((VX, 2), (VY, 3), (VZ, 3), (VX, 3))):
        add_force(A, (i,), force, which, PAD + window)

    def work(r):
        here, up, down, out = spans(r)
        vx, vy, vz = A[0, here], A[1, here], A[2, here]
        exx = vx - A[3, here]
        dxx = lam * (exx + (vy - A[1, up]) + (vz - m0 * before(vz))) + mu2 * exx
        dxy = mu * (A[0, down] - vx + (V[VY, 0, here] - vy))
        dxz = mu * (m1 * after(vx) - vx + (V[VZ, 0, here] - vz))
        W[0, here] = dxy
        D[0, out] = dxy
        D[1, out] = dxz
        D[2, out] = vx + b * (dxy + dxz - dxx) - b0 * before(dxz)

    over_rows(D.shape[1], work)

    def rest(r):
        _, up, _, out = spans(r)
        D[2, out] = D[2, out] - b * W[0, up]

    over_rows(D.shape[1], rest)


def early_ahead(V, S, R, coef_ref, msg, W, force, window):
    b, b0, m0, m1, lam, mu2, mu = coefs(coef_ref, (C_B, C_B0, C_M0, C_M1, C_LAM, C_MU2, C_MU))

    def work(r):
        here, up, down, out = spans(r)
        vx, vy, vz = V[VX, 1, here], V[VY, 1, here], V[VZ, 1, here]
        exx = vx - V[VX, 0, here]
        volume = lam * (exx + (vy - V[VY, 1, up]) + (vz - m0 * before(vz)))
        sxx = S[XX, 1, here] + (volume + mu2 * exx) + DT * R[XX, 1, out]
        sxy = S[XY, 1, here] + mu * (V[VX, 1, down] - vx - vy) + DT * R[XY, 1, out]
        sxz = S[XZ, 1, here] + mu * (m1 * after(vx) - vx - vz) + DT * R[XZ, 1, out]
        W[0, here] = sxy
        msg[0, out] = sxy
        msg[1, out] = sxz
        msg[2, out] = vx + b * (sxy + sxz - sxx) - b0 * before(sxz)

    over_rows(msg.shape[1], work)

    def rest(r):
        _, up, _, out = spans(r)
        msg[2, out] = msg[2, out] - b * W[0, up]

    over_rows(msg.shape[1], rest)
    if force is not None:
        add_force(msg, (2,), force, (VX, 1), window)


def early_behind(V, S, R, coef_ref, surface, column, msg, W, force, window):
    b, b0, b1, m0, m1, lam, mu2, mu, l0 = coefs(
        coef_ref, (C_B, C_B0, C_B1, C_M0, C_M1, C_LAM, C_MU2, C_MU, C_L0)
    )

    def work(r):
        here, up, down, out = spans(r)
        vx, vy, vz = V[VX, 0, here], V[VY, 0, here], V[VZ, 0, here]
        eyy = vy - V[VY, 0, up]
        ezz = vz - m0 * before(vz)
        volume = lam * (vx + eyy + ezz)
        sxx = S[XX, 0, here] + (volume + mu2 * vx) + DT * R[XX, 0, out]
        syy = S[YY, 0, here] + (volume + mu2 * eyy) + DT * R[YY, 0, out]
        szz = S[ZZ, 0, here] + (volume + mu2 * ezz) + DT * R[ZZ, 0, out]
        if surface is not None:
            szz = szz + l0 * lane_roll(surface[out, :], -column)
        sxy = S[XY, 0, here] + mu * (V[VX, 0, down] - vx + (V[VY, 1, here] - vy)) + DT * R[XY, 0, out]
        sxz = S[XZ, 0, here] + mu * (m1 * after(vx) - vx + (V[VZ, 1, here] - vz)) + DT * R[XZ, 0, out]
        syz = S[YZ, 0, here] + mu * (m1 * after(vy) - vy + (V[VZ, 0, down] - vz)) + DT * R[YZ, 0, out]
        W[0, here] = syy
        W[1, here] = syz
        msg[0, out] = sxx
        msg[1, out] = vy + b * (sxy - syy + syz) - b0 * before(syz)
        msg[2, out] = vz + b * (sxz + syz - szz) + b1 * after(szz)

    over_rows(msg.shape[1], work)

    def rest(r):
        _, up, down, out = spans(r)
        msg[1, out] = msg[1, out] + b * W[0, down]
        msg[2, out] = msg[2, out] - b * W[1, up]

    over_rows(msg.shape[1], rest)
    if force is not None:
        add_force(msg, (1,), force, (VY, 0), window)
        add_force(msg, (2,), force, (VZ, 0), window)


def ahead_bond(V, S, R, coef_ref, force, surface, msg, missing, G, step, window, unforced=0, respond=None):
    (b,) = coefs(coef_ref, (C_B,))
    _, _, has_ahead = place()
    keep = jnp.where(has_ahead, 1.0, 0.0).astype(jnp.float32)

    def got(i, out):
        return msg[i, out] if missing is None else msg[i, out] + missing[i, out]

    def work(r):
        here, _, _, out = spans(r)
        V[VX, 1, here] = V[VX, 1, here] + (keep * b) * got(0, out)
        G[0, out] = keep * (got(1, out) - b * S[XY, 1, here])
        G[1, out] = keep * (got(2, out) - b * S[XZ, 1, here])

    over_rows(R.shape[2], work)
    if step < unforced:
        add_force(G, (0,), force, (VY, 2), window)
        add_force(G, (1,), force, (VZ, 2), window)
    if respond is not None:
        respond()
    post(
        V, S, R, coef_ref, surface, 1, 2 * step + 1,
        lambda r: V[VX, 0, pl.ds(PAD + r, ROWS)],
        lambda r: G[0, pl.ds(r, ROWS)],
        lambda r: G[1, pl.ds(r, ROWS)],
    )


def behind_bond(V, S, R, coef_ref, force, surface, msg, missing, G, step, window, unforced=0, respond=None):
    (b,) = coefs(coef_ref, (C_B,))
    _, has_behind, _ = place()
    keep = jnp.where(has_behind, 1.0, 0.0).astype(jnp.float32)

    def got(i, out):
        return msg[i, out] if missing is None else msg[i, out] + missing[i, out]

    def work(r):
        here, _, _, out = spans(r)
        V[VY, 0, here] = V[VY, 0, here] - (keep * b) * got(0, out)
        V[VZ, 0, here] = V[VZ, 0, here] - (keep * b) * got(1, out)
        G[0, out] = keep * (got(2, out) + b * S[XX, 0, here])

    over_rows(R.shape[2], work)
    if step < unforced:
        add_force(G, (0,), force, (VX, 2), window)
    if respond is not None:
        respond()
    post(
        V, S, R, coef_ref, surface, 0, 2 * step,
        lambda r: G[0, pl.ds(r, ROWS)],
        lambda r: V[VY, 1, pl.ds(PAD + r, ROWS)],
        lambda r: V[VZ, 1, pl.ds(PAD + r, ROWS)],
    )


def start_kernel(
    velocity, stress, memory, layer_in, lam_in, mu_in, buoy_in, rate_in, defect_in, loads, steps_table,
    V, S, R, coef_ref, msg_near, msg_far, W, table, layer_ref, lam, mu, buoy, rate, defect, sems,
):
    across = velocity.shape[2]
    inside = pl.ds(PAD, across)
    pairs = [
        (layer_in, layer_ref), (lam_in, lam), (mu_in, mu), (buoy_in, buoy), (rate_in, rate), (defect_in, defect),
    ]
    pairs += [(stress.at[i], S.at[i, :, inside]) for i in range(6)]
    pairs += [(velocity.at[i], V.at[i, :, inside]) for i in range(3)]
    pairs += [(memory.at[i], R.at[i]) for i in range(6)]
    copies = [pltpu.make_async_copy(*pair, sems.at[i]) for i, pair in enumerate(pairs)]
    for copy in copies:
        copy.start()
    slots = loads.shape[0]
    zero_edges(V)
    zero_edges(S)
    zero_edges(W)
    table[...] = jnp.zeros(table.shape, jnp.float32)
    table[0:16, :] = steps_table[...]
    columns = table[...].T
    trucks = 6 * across
    msg_far[trucks : trucks + slots, :] = loads[...]
    for i, at in enumerate((0, 8)):
        first_row = trucks + (1 + i) * slots
        column = columns[0:slots, at : at + 1]
        msg_far[first_row : first_row + slots, :] = jnp.broadcast_to(column, loads.shape)
    for copy in copies[:6]:
        copy.wait()
    layer = layer_ref[...]

    def per_depth(table):
        row = jnp.zeros(layer.shape, jnp.float32)
        for level in range(table.shape[0]):
            row = jnp.where(layer == level, table[level], row)
        return row

    lane = lax.broadcasted_iota(jnp.int32, layer.shape, 1)
    not_first = jnp.where(lane > 0, 1.0, 0.0).astype(jnp.float32)
    not_last = jnp.where(lane < layer.shape[1] - 1, 1.0, 0.0).astype(jnp.float32)
    b = DT * per_depth(buoy)
    two_mu = (2.0 * DT) * per_depth(mu)
    decay = DT * per_depth(rate)
    drop = 2.0 * decay * per_depth(defect)
    for row, value in (
        (C_B, b),
        (C_B0, b * not_first),
        (C_B1, b * not_last),
        (C_M0, not_first),
        (C_M1, not_last),
        (C_LAM, DT * per_depth(lam)),
        (C_MU2, two_mu),
        (C_MU, 0.5 * two_mu),
        (C_K1, 1.0 - decay),
        (C_K2, drop),
        (C_K2H, 0.5 * drop),
        (C_L0, DT * (1.0 - not_first)),
    ):
        coef_ref[row : row + 1, :] = value
    coef_ref[12:16, :] = jnp.zeros((4, layer.shape[1]), jnp.float32)
    for copy in copies[6:15]:
        copy.wait()
    even, _, _ = place()
    now, then = Planes(msg_far, 0, across), Planes(msg_far, 3, across)

    @pl.when(even)
    def _():
        pre_ahead(V, S, coef_ref, msg_near, None, 0)
        pre_behind(V, S, coef_ref, now, None, 0)

    @pl.when(jnp.logical_not(even))
    def _():
        pre_behind(V, S, coef_ref, msg_near, None, 0)
        pre_ahead(V, S, coef_ref, now, None, 0)

    inner(V, S, coef_ref, None, 0)
    for copy in copies[15:]:
        copy.wait()

    @pl.when(even)
    def _():
        early_behind(V, S, R, coef_ref, None, 0, then, W, None, 0)

    @pl.when(jnp.logical_not(even))
    def _():
        early_ahead(V, S, R, coef_ref, then, W, None, 0)


def near_kernel(step, window, V0, S0, R0, coef_ref, force, surface, msg, V, S, R, *rest):
    G = rest[-1]
    if step == 0:
        for comp in range(3):
            for cell in range(2):
                add_force(V, (comp, cell), force, (0, comp, cell), PAD + window)
    even, _, _ = place()
    more = step < STEPS - 1

    @pl.when(even)
    def _():
        ahead_bond(V, S, R, coef_ref, force.at[step], surface, msg, None, G, step, window, 1)
        if more:
            pre_ahead(V, S, coef_ref, rest[0], force.at[step + 1], window)

    @pl.when(jnp.logical_not(even))
    def _():
        behind_bond(V, S, R, coef_ref, force.at[step], surface, msg, None, G, step, window, 1)
        if more:
            pre_behind(V, S, coef_ref, rest[0], force.at[step + 1], window)


def load_ahead(msg, loads, across, rows_out, load):
    slots = loads.shape[0]
    rows, entry, cell = (msg[6 * across + i * slots : 6 * across + (i + 1) * slots, :] for i in range(3))
    for slot in range(slots):
        rows = jnp.where(entry == float(slot), loads[slot : slot + 1, :], rows)
    rows_out[...] = jnp.zeros(rows_out.shape, jnp.float32)
    rows_out[0:1, :] = jnp.sum(jnp.where(cell == 0.0, rows, 0.0), axis=0, keepdims=True)
    load[...] = rows_out[...].T


def far_kernel(step, window, V0, S0, R0, coef_ref, force, surface, msg, *rest):
    rest = list(rest)
    other = rest.pop(0)
    V, S, R, D = rest[:4]
    early = rest[4] if step < STEPS - 2 else None
    across = R.shape[2]
    even, _, _ = place()
    here, then = force.at[step], force.at[step + 1]
    got = Planes(msg, 3 * step, across) if step < 2 else msg
    if step == 0:
        missing, loads = None, other
        G, W, A, load, rows_out = rest[-5:]
    else:
        missing = other
        G, W = rest[-2:]
    zero_edges(W)

    @pl.when(even)
    def _():
        if step == 0:
            respond = lambda: first_response_ahead(V, S, coef_ref, here, D, W, A, window)
        else:
            respond = lambda: response_ahead(V, S, coef_ref, D, W)
        behind_bond(
            V, S, R, coef_ref, here, surface, got, missing, G, step, window, 2, respond
        )
        pre_behind(V, S, coef_ref, None, then, window)

    @pl.when(jnp.logical_not(even))
    def _():
        if step == 0:
            load_ahead(msg, loads, across, rows_out, load)
            respond = lambda: first_response_behind(V, S, coef_ref, here, load, D, W, A, window)
        else:
            respond = lambda: response_behind(V, S, coef_ref, D, W)
        ahead_bond(
            V, S, R, coef_ref, here, surface, got, missing, G, step, window, 2, respond
        )
        pre_ahead(V, S, coef_ref, None, then, window)

    inner(V, S, coef_ref, then, window)
    if early is not None:
        later = force.at[step + 2]

        @pl.when(even)
        def _():
            early_behind(V, S, R, coef_ref, surface, 2 * (step + 1), early, W, later, window)

        @pl.when(jnp.logical_not(even))
        def _():
            early_ahead(V, S, R, coef_ref, early, W, later, window)


def last_kernel(
    step, window, V0, S0, R0, coef_ref, force, surface, msg, missing, V, S, R, v_out, s_out, r_out, G, sems
):
    even, _, _ = place()
    here = force.at[step]
    inside = pl.ds(PAD, R.shape[2])

    def copies(cell):
        return [
            pltpu.make_async_copy(V.at[:, cell, inside], v_out.at[:, cell], sems.at[cell, 0]),
            pltpu.make_async_copy(S.at[:, cell, inside], s_out.at[:, cell], sems.at[cell, 1]),
            pltpu.make_async_copy(R.at[:, cell], r_out.at[:, cell], sems.at[cell, 2]),
        ]

    def finish(cell, bond):
        done, other = copies(1 - cell), copies(cell)
        for copy in done:
            copy.start()
        bond(V, S, R, coef_ref, here, surface, msg, missing, G, step, window)
        for copy in other:
            copy.start()
        for copy in done + other:
            copy.wait()

    @pl.when(even)
    def _():
        finish(0, behind_bond)

    @pl.when(jnp.logical_not(even))
    def _():
        finish(1, ahead_bond)


ENTRY_ROW, TRUCK_ROW = 48, 56
GROUP = 8


def pack_kernel(
    record, loads_in, entries_in, cells_in, piers_in, own, loads, steps_table, piers, entries, cells, sems
):
    panel = record.shape[1]
    slots, lanes = loads.shape
    steps = entries.shape[0]
    pairs = [(record, own.at[:, pl.ds(0, panel)]), (loads_in, loads), (entries_in, entries), (cells_in, cells)]
    pairs.append((piers_in, piers))
    copies = [pltpu.make_async_copy(*pair, sems.at[i]) for i, pair in enumerate(pairs)]
    for copy in copies:
        copy.start()
    own[:, panel:] = jnp.zeros((own.shape[0], own.shape[1] - panel), jnp.float32)
    steps_table[...] = jnp.zeros(steps_table.shape, jnp.float32)
    for copy in copies:
        copy.wait()
    steps_table[0:steps, 0:slots] = entries[...].astype(jnp.float32)
    steps_table[8 : 8 + steps, 0:slots] = cells[...].astype(jnp.float32)
    blocks = [loads[8 * i : 8 * i + 8, :] for i in range(slots // 8)] + [steps_table[0:8, :]]
    for i, block in enumerate(blocks):
        own[0:8, panel + i * lanes : panel + (i + 1) * lanes] = block


def lane_blocks(table, width):
    return sum(lane_roll(table[s : s + 1, :], s * width) for s in range(STEPS))


def split_kernel(panel, slots, own, behind, cells, after_this, out):
    del after_this
    tiles, _, lanes = out.shape
    pieces = panel // lanes
    third = pieces // 3
    cell_of = cells[...]
    me = lax.axis_index("line")
    group, mine = lax.div(me, tiles), lax.rem(me, tiles)
    row = lax.broadcasted_iota(jnp.int32, (4 * tiles, cell_of.shape[1]), 0)
    tile, j = lax.div(row, 4), lax.rem(row, 4)
    odd = lax.rem(tile, 2)
    first = (tile + group * tiles) * 2
    cell_x = first + jnp.where(j == 2, -1, jnp.where(j == 3, 4 * odd - 2, j))
    cell_yz = first + jnp.where(j == 3, 4 * odd - 1, j)
    record = jnp.where(group == 0, own[:, :panel], behind[:, :panel])

    def share(cell, columns):
        hit = jnp.where(cell == cell_of, 1.0, 0.0).astype(jnp.float32)
        return jnp.dot(
            hit, record[:, columns], precision=lax.Precision.HIGHEST, preferred_element_type=jnp.float32
        )

    part_x = share(cell_x, slice(0, third * lanes))
    part_yz = share(cell_yz, slice(third * lanes, panel))

    def trucks(source):
        blocks = [source[0:8, panel + i * lanes : panel + (i + 1) * lanes] for i in range(slots // 8 + 1)]
        return blocks[:-1], lane_blocks(blocks[-1], slots)

    own_rows, own_entry = trucks(own)
    far_rows, far_entry = trucks(behind)
    for tile in range(tiles):
        these = slice(4 * tile, 4 * tile + 4)
        for m in range(pieces):
            part, at = (part_x, m) if m < third else (part_yz, m - third)
            out[tile, 4 * m : 4 * m + 4, :] = part[these, at * lanes : (at + 1) * lanes]
        passed = mine < tile
        out[tile, ENTRY_ROW : ENTRY_ROW + 1, :] = jnp.where(passed, own_entry, far_entry)
        for i in range(slots // 8):
            at = TRUCK_ROW + 8 * i
            out[tile, at : at + 8, :] = jnp.where(passed, own_rows[i], far_rows[i])


def prepare_kernel(parts, loads, steps_table, force, surface, table, rows_out):
    steps, comps, width = force.shape[:3]
    lanes = parts.shape[2]
    force[...] = jnp.zeros(force.shape, jnp.float32)
    per = ENTRY_ROW // (comps * width)
    lane = lax.broadcasted_iota(jnp.int32, (per, lanes), 1)
    scale = jnp.where(lane < FZ, DT, 0.0).astype(jnp.float32)
    for s in range(steps):
        for comp in range(comps):
            for cell in range(width):
                panel = parts[s, pl.ds(comp * per * width + cell, per, stride=width), :]
                force[s, comp, cell, pl.ds(4, per, stride=2), :] = scale * panel
                force[s, comp, cell, pl.ds(5, per, stride=2), :] = scale * lane_roll(panel, FZ)

    slots = loads.shape[0]
    tiles = parts.shape[0]
    mine = lax.rem(lax.axis_index("line"), tiles)
    table[...] = jnp.zeros(table.shape, jnp.float32)
    table[0:1, :] = lane_blocks(steps_table[0:8, :], slots)
    table[STEPS + 1 : STEPS + 2, :] = lane_blocks(steps_table[8:16, :], slots)
    rows = [loads[...]]
    for k in range(1, STEPS + 1):
        source = lax.rem(mine + (tiles - k), tiles)
        rows.append(parts[source, TRUCK_ROW : TRUCK_ROW + slots, :])
        table[k : k + 1, :] = parts[source, ENTRY_ROW : ENTRY_ROW + 1, :]
    columns = table[...].T
    rows_out[...] = jnp.zeros(rows_out.shape, jnp.float32)
    for s in range(STEPS):
        block = slice(s * slots, (s + 1) * slots)
        moved = []
        for k in range(STEPS - s):
            entry = jnp.broadcast_to(columns[block, k : k + 1], rows[k].shape)
            new = rows[k]
            for slot in range(slots):
                new = jnp.where(entry == float(slot), rows[k + 1][slot : slot + 1, :], new)
            moved.append(new)
        rows = moved
        cell = jnp.broadcast_to(columns[block, STEPS + 1 : STEPS + 2], rows[0].shape)
        for c in range(2):
            load = jnp.sum(jnp.where(cell == float(c), rows[0], 0.0), axis=0, keepdims=True)
            rows_out[2 * s + c : 2 * s + c + 1, :] = load
    surface[...] = rows_out[...].T


def in_vmem(x):
    return pltpu.with_memory_space_constraint(x, pltpu.VMEM)


WHOLE = pl.BlockSpec(memory_space=pltpu.VMEM)
SCALARS = pl.BlockSpec(memory_space=pltpu.SMEM)
ANYWHERE = pl.BlockSpec(memory_space=pl.ANY)


def call(kernel, ins, specs, outs, out_specs, scratch=(), aliases=None, name=None, cost=1):
    return pl.pallas_call(
        kernel,
        out_shape=outs,
        in_specs=specs,
        out_specs=out_specs,
        scratch_shapes=list(scratch),
        input_output_aliases=aliases or {},
        compiler_params=pltpu.CompilerParams(vmem_limit_bytes=VMEM_LIMIT),
        cost_estimate=pl.CostEstimate(flops=cost, bytes_accessed=cost, transcendentals=0),
        name=name,
    )(*ins)


def body(
    velocity, stress, memory, truck_loads, pier_panels,
    lame_lambda, lame_mu, buoyancy, relax_rate, defect_mu, layer,
    truck_entry, truck_cell, pier_cell,
):
    tiles = lax.axis_size("line")
    width_x, across, depth = velocity.shape[1:]
    slots = truck_loads.shape[0]
    window = (across - FY) // 2 - 4
    f32 = jnp.float32

    near = [(i, i ^ 1) for i in range(tiles) if (i ^ 1) < tiles]
    far = [(i, i + 1) for i in range(1, tiles - 1, 2)] + [(i + 1, i) for i in range(1, tiles - 1, 2)]

    padded = across + 2 * PAD
    v_type = pltpu.VMEM((3, width_x, padded, depth), f32)
    s_type = pltpu.VMEM((6, width_x, padded, depth), f32)
    r_type = pltpu.VMEM((6, width_x, across, depth), f32)
    c_type = pltpu.VMEM((N_COEF, depth), f32)
    m_type = pltpu.VMEM((3, across, depth), f32)
    ghost = pltpu.VMEM((2, across, depth), f32)
    work = pltpu.VMEM((2, padded, depth), f32)
    square = pltpu.VMEM((across, depth), f32)

    def ahead_by(x, distance):
        return lax.ppermute(x, "line", [(i, i + distance) for i in range(tiles - distance)])

    def in_hbm(*arrays):
        return tuple(pltpu.with_memory_space_constraint(x, pltpu.HBM) for x in arrays)

    dma = pltpu.SemaphoreType.DMA
    piers, panel = pier_panels.shape[1:]
    own, loads, steps_table, pier_row = call(
        pack_kernel,
        in_hbm(pier_panels[0], truck_loads, truck_entry, truck_cell, pier_cell[None, :]),
        (ANYWHERE,) * 5,
        (
            pltpu.VMEM((piers, panel + (slots // 8 + 1) * depth), f32),
            pltpu.VMEM((slots, depth), f32),
            pltpu.VMEM((16, depth), f32),
            pltpu.VMEM((1, piers), jnp.int32),
        ),
        (WHOLE,) * 4,
        scratch=(pltpu.VMEM(truck_entry.shape, jnp.int32), pltpu.VMEM(truck_cell.shape, jnp.int32), dma((5,))),
        name="pack",
    )
    behind = ahead_by(own, GROUP)
    reach = 2 * GROUP
    index = lax.axis_index("line")
    while reach < tiles:
        record = jnp.where(index < GROUP, own, behind)[:, :panel]
        record = jnp.where(index < reach, record, ahead_by(record, reach))
        behind = jnp.concatenate([record, behind[:, panel:]], axis=1)
        reach *= 2
    tables = (lame_lambda, lame_mu, buoyancy, relax_rate, defect_mu)
    V, S, R, coef, msg_near, msg_far = call(
        start_kernel,
        in_hbm(velocity, stress, memory, layer[None, :], *tables) + (in_vmem(loads), in_vmem(steps_table)),
        (ANYWHERE,) * 9 + (WHOLE,) * 2,
        (v_type, s_type, r_type, c_type, m_type, pltpu.VMEM((6 * across + 3 * slots, depth), f32)),
        (WHOLE,) * 6,
        scratch=(
            work, pltpu.VMEM((depth, depth), f32), pltpu.VMEM((1, depth), jnp.int32),
            *(pltpu.SMEM(table.shape, f32) for table in tables), dma((21,)),
        ),
        name="start",
        cost=8 * 1024 * 1024,
    )
    msg_far = lax.ppermute(msg_far, "line", far)
    msg_near = lax.ppermute(msg_near, "line", near)
    parts = call(
        functools.partial(split_kernel, panel, slots),
        (own, behind, in_vmem(pier_row), coef),
        (WHOLE,) * 3 + (ANYWHERE,),
        jax.ShapeDtypeStruct((GROUP, TRUCK_ROW + slots, depth), f32),
        WHOLE,
        name="split",
    )
    groups = [list(range(at, at + GROUP)) for at in range(0, tiles, GROUP)]
    parts = lax.all_to_all(parts, "line", 0, 0, axis_index_groups=groups, tiled=True)
    force, surface = call(
        prepare_kernel,
        (parts, in_vmem(loads), in_vmem(steps_table)),
        (WHOLE,) * 3,
        (pltpu.VMEM((STEPS, 3, 4, 16, depth), f32), pltpu.VMEM((across, depth), f32)),
        (WHOLE,) * 2,
        scratch=(pltpu.VMEM((depth, depth), f32), pltpu.VMEM((depth, across), f32)),
        name="prepare",
    )
    state = (v_type, s_type, r_type)
    same = {0: 0, 1: 1, 2: 2}
    missing = None
    for step in range(STEPS):
        more = step < STEPS - 1
        ins = tuple(in_vmem(x) for x in (V, S, R, coef, force, surface, msg_near))
        outs = state + ((m_type,) if more else ())
        V, S, R, *msg = call(
            functools.partial(near_kernel, step, window),
            ins,
            (WHOLE,) * len(ins),
            outs,
            (WHOLE,) * len(outs),
            scratch=(ghost,),
            aliases=same,
            name="near" + str(step),
        )
        if more:
            msg_near = lax.ppermute(msg[0], "line", near)
        ins = (V, S, R, coef, force, surface, msg_far, missing if step else loads)
        ins = tuple(in_vmem(x) for x in ins)
        if more:
            outs = state + (m_type,) + ((m_type,) if step < STEPS - 2 else ())
            V, S, R, missing, *msg = call(
                functools.partial(far_kernel, step, window),
                ins,
                (WHOLE,) * len(ins),
                outs,
                (WHOLE,) * len(outs),
                scratch=(ghost, work) + (() if step else (pltpu.VMEM((5, padded, depth), f32),) + (square,) * 2),
                aliases=same,
                name="far" + str(step),
            )
            if step > 0:
                msg_far = early
            if msg:
                early = lax.ppermute(msg[0], "line", far)
    results = call(
        functools.partial(last_kernel, STEPS - 1, window),
        ins,
        (WHOLE,) * len(ins),
        state + tuple(jax.ShapeDtypeStruct(x.shape, f32) for x in (velocity, stress, memory)),
        (WHOLE,) * 3 + (ANYWHERE,) * 3,
        scratch=(ghost, pltpu.SemaphoreType.DMA((2, 3))),
        aliases=same,
        name="last",
    )
    return results[3:]


def solution(mesh):
    placed = (
        P(None, ("runs", "line"), None, None),
        P(None, ("runs", "line"), None, None),
        P(None, ("runs", "line"), None, None),
        P(("runs", "line"), None),
        P("line", "runs", None),
        P(),
        P(),
        P(),
        P(),
        P(),
        P(),
        P(None, ("runs", "line")),
        P(None, ("runs", "line")),
        P(),
    )
    return jax.shard_map(
        body,
        mesh=mesh,
        in_specs=placed,
        out_specs=(
            P(None, ("runs", "line"), None, None),
            P(None, ("runs", "line"), None, None),
            P(None, ("runs", "line"), None, None),
        ),
        check_vma=False,
    )
```

```python
import functools

import jax
import jax.numpy as jnp
import numpy as np
from jax import lax
from jax.experimental import pallas as pl
from jax.experimental.pallas import tpu as pltpu
from jax.sharding import PartitionSpec as P

STEPS = 6
FY = 8
FZ = 64
DT = 0.25
PAD = 8
ROWS = 16
UNROLL = 8
VMEM_LIMIT = 32 * 1024 * 1024

C_B, C_B0, C_B1, C_M0, C_M1, C_LAM, C_MU2, C_MU, C_K1, C_K2, C_K2H, C_L0 = range(12)
N_COEF = 16

VX, VY, VZ = range(3)
XX, YY, ZZ, XY, XZ, YZ = range(6)


def lane_roll(x, shift):
    return pltpu.roll(x, shift % x.shape[-1], x.ndim - 1)


def before(x):
    return lane_roll(x, 1)


def after(x):
    return lane_roll(x, -1)


def over_rows(count, work):
    def step(i, carry):
        work(pl.multiple_of(i * ROWS, ROWS))
        return carry

    lax.fori_loop(0, count // ROWS, step, 0, unroll=UNROLL)


class Planes:
    def __init__(self, ref, first, across):
        self.ref, self.first, self.shape = ref, first, (3, across, ref.shape[1])

    def rows(self, at):
        plane, out = at
        return pl.ds((self.first + plane) * self.shape[1] + out.start, out.size)

    def __getitem__(self, at):
        return self.ref[self.rows(at)]

    def __setitem__(self, at, value):
        self.ref[self.rows(at)] = value


def coefs(coef_ref, ids):
    return [coef_ref[i : i + 1, :] for i in ids]


def place():
    index = lax.axis_index("line")
    return lax.rem(index, 2) == 0, index > 0, index < lax.axis_size("line") - 1


def spans(r):
    return pl.ds(PAD + r, ROWS), pl.ds(PAD + r - 1, ROWS), pl.ds(PAD + r + 1, ROWS), pl.ds(r, ROWS)


def zero_edges(ref):
    across = ref.shape[-2] - 2 * PAD
    edge = jnp.zeros((PAD, ref.shape[-1]), jnp.float32)
    for where in np.ndindex(*ref.shape[:-2]):
        ref[(*where, pl.ds(0, PAD))] = edge
        ref[(*where, pl.ds(PAD + across, PAD))] = edge


def add_force(ref, index, force, which, first_row):
    rows = pl.ds(first_row, 16)
    ref[(*index, rows)] = ref[(*index, rows)] + force[which]


def pre_ahead(V, S, coef_ref, msg, force, window):
    b, b0 = coefs(coef_ref, (C_B, C_B0))

    def work(r):
        here, up, _, out = spans(r)
        sxy, sxz = S[XY, 1, here], S[XZ, 1, here]
        px = V[VX, 1, here] + b * (sxy - S[XY, 1, up] + sxz - S[XX, 1, here]) - b0 * before(sxz)
        V[VX, 1, here] = px
        if msg is not None:
            msg[0, out] = sxy
            msg[1, out] = sxz
            msg[2, out] = px

    over_rows(V.shape[2] - 2 * PAD, work)
    if force is not None:
        add_force(V, (VX, 1), force, (VX, 1), PAD + window)
        if msg is not None:
            add_force(msg, (2,), force, (VX, 1), window)


def pre_behind(V, S, coef_ref, msg, force, window):
    b, b0, b1 = coefs(coef_ref, (C_B, C_B0, C_B1))

    def work(r):
        here, up, down, out = spans(r)
        syz, szz = S[YZ, 0, here], S[ZZ, 0, here]
        qy = V[VY, 0, here] + b * (S[XY, 0, here] + S[YY, 0, down] - S[YY, 0, here] + syz) - b0 * before(syz)
        qz = V[VZ, 0, here] + b * (S[XZ, 0, here] + syz - S[YZ, 0, up] - szz) + b1 * after(szz)
        V[VY, 0, here] = qy
        V[VZ, 0, here] = qz
        if msg is not None:
            msg[0, out] = S[XX, 0, here]
            msg[1, out] = qy
            msg[2, out] = qz

    over_rows(V.shape[2] - 2 * PAD, work)
    if force is not None:
        add_force(V, (VY, 0), force, (VY, 0), PAD + window)
        add_force(V, (VZ, 0), force, (VZ, 0), PAD + window)
        if msg is not None:
            add_force(msg, (1,), force, (VY, 0), window)
            add_force(msg, (2,), force, (VZ, 0), window)


def inner(V, S, coef_ref, force, window):
    b, b0, b1 = coefs(coef_ref, (C_B, C_B0, C_B1))

    def work(r):
        here, up, down, _ = spans(r)
        sxy, sxz = S[XY, 0, here], S[XZ, 0, here]
        V[VX, 0, here] = (
            V[VX, 0, here]
            + b * (S[XX, 1, here] - S[XX, 0, here] + sxy - S[XY, 0, up] + sxz)
            - b0 * before(sxz)
        )
        syz, szz = S[YZ, 1, here], S[ZZ, 1, here]
        V[VY, 1, here] = (
            V[VY, 1, here]
            + b * (S[XY, 1, here] - sxy + S[YY, 1, down] - S[YY, 1, here] + syz)
            - b0 * before(syz)
        )
        V[VZ, 1, here] = (
            V[VZ, 1, here]
            + b * (S[XZ, 1, here] - sxz + syz - S[YZ, 1, up] - szz)
            + b1 * after(szz)
        )

    over_rows(V.shape[2] - 2 * PAD, work)
    if force is not None:
        add_force(V, (VX, 0), force, (VX, 0), PAD + window)
        add_force(V, (VY, 1), force, (VY, 1), PAD + window)
        add_force(V, (VZ, 1), force, (VZ, 1), PAD + window)


def post(V, S, R, coef_ref, surface, cell, column, behind_x, ahead_y, ahead_z):
    m0, m1, lam, mu2, mu, k1, k2, k2h, l0 = coefs(
        coef_ref, (C_M0, C_M1, C_LAM, C_MU2, C_MU, C_K1, C_K2, C_K2H, C_L0)
    )

    def work(r):
        here, up, down, out = spans(r)
        vx, vy, vz = V[VX, cell, here], V[VY, cell, here], V[VZ, cell, here]
        exx = vx - behind_x(r)
        eyy = vy - V[VY, cell, up]
        ezz = vz - m0 * before(vz)
        exy = V[VX, cell, down] - vx + (ahead_y(r) - vy)
        exz = m1 * after(vx) - vx + (ahead_z(r) - vz)
        eyz = m1 * after(vy) - vy + (V[VZ, cell, down] - vz)
        volume = lam * (exx + eyy + ezz)
        for comp, e in ((XX, exx), (YY, eyy), (ZZ, ezz)):
            old = R[comp, cell, out]
            new = S[comp, cell, here] + (volume + mu2 * e) + DT * old
            if comp == ZZ:
                new = new + l0 * lane_roll(surface[out, :], -column)
            S[comp, cell, here] = new
            R[comp, cell, out] = k1 * old - k2 * e
        for comp, e in ((XY, exy), (XZ, exz), (YZ, eyz)):
            old = R[comp, cell, out]
            S[comp, cell, here] = S[comp, cell, here] + mu * e + DT * old
            R[comp, cell, out] = k1 * old - k2h * e

    over_rows(R.shape[2], work)


def response_behind(V, S, coef_ref, D, W):
    b, b0, b1, m0, m1, lam, mu2, mu = coefs(coef_ref, (C_B, C_B0, C_B1, C_M0, C_M1, C_LAM, C_MU2, C_MU))

    def work(r):
        here, up, down, out = spans(r)
        sxy = S[XY, 1, here]
        vy, vz = -b * sxy, -b * S[XZ, 1, here]
        exx = -V[VX, 1, here]
        eyy = b * (S[XY, 1, up] - sxy)
        ezz = vz - m0 * before(vz)
        volume = lam * (exx + eyy + ezz)
        dyy, dzz = volume + mu2 * eyy, volume + mu2 * ezz
        dyz = mu * (m1 * after(vy) - vy - b * S[XZ, 1, down] - vz)
        W[0, here] = dyy
        W[1, here] = dyz
        D[0, out] = volume + mu2 * exx
        D[1, out] = vy + b * (dyz - mu * vy - dyy) - b0 * before(dyz)
        D[2, out] = vz + b * (dyz - mu * vz - dzz) + b1 * after(dzz)

    over_rows(D.shape[1], work)

    def rest(r):
        _, up, down, out = spans(r)
        D[1, out] = D[1, out] + b * W[0, down]
        D[2, out] = D[2, out] - b * W[1, up]

    over_rows(D.shape[1], rest)


def response_ahead(V, S, coef_ref, D, W):
    b, b0, m1, lam, mu2, mu = coefs(coef_ref, (C_B, C_B0, C_M1, C_LAM, C_MU2, C_MU))

    def work(r):
        here, _, down, out = spans(r)
        vx = b * S[XX, 0, here]
        dxy = mu * (b * S[XX, 0, down] - vx + V[VY, 0, here])
        dxz = mu * (m1 * after(vx) - vx + V[VZ, 0, here])
        W[0, here] = dxy
        D[0, out] = dxy
        D[1, out] = dxz
        D[2, out] = vx + b * (dxy + dxz - (lam + mu2) * vx) - b0 * before(dxz)

    over_rows(D.shape[1], work)

    def rest(r):
        _, up, _, out = spans(r)
        D[2, out] = D[2, out] - b * W[0, up]

    over_rows(D.shape[1], rest)


def first_response_behind(V, S, coef_ref, force, load, D, W, A, window):
    b, b0, b1, m0, m1, lam, mu2, mu, l0 = coefs(
        coef_ref, (C_B, C_B0, C_B1, C_M0, C_M1, C_LAM, C_MU2, C_MU, C_L0)
    )
    A[...] = jnp.zeros(A.shape, jnp.float32)

    def given(r):
        here, _, _, _ = spans(r)
        A[1, here] = -b * S[XY, 1, here]
        A[2, here] = -b * S[XZ, 1, here]

    over_rows(D.shape[1], given)
    for i, which in enumerate(((VX, 3), (VY, 2), (VZ, 2), (VY, 3), (VZ, 3))):
        add_force(A, (i,), force, which, PAD + window)

    def work(r):
        here, up, down, out = spans(r)
        vx, vy, vz = A[0, here], A[1, here], A[2, here]
        exx = vx - V[VX, 1, here]
        eyy = vy - A[1, up]
        ezz = vz - m0 * before(vz)
        volume = lam * (exx + eyy + ezz)
        dyy = volume + mu2 * eyy
        dzz = volume + mu2 * ezz + l0 * load[out, :]
        dxy = mu * (A[0, down] - vx + (A[3, here] - vy))
        dxz = mu * (m1 * after(vx) - vx + (A[4, here] - vz))
        dyz = mu * (m1 * after(vy) - vy + (A[2, down] - vz))
        W[0, here] = dyy
        W[1, here] = dyz
        D[0, out] = volume + mu2 * exx
        D[1, out] = vy + b * (dxy - dyy + dyz) - b0 * before(dyz)
        D[2, out] = vz + b * (dxz + dyz - dzz) + b1 * after(dzz)

    over_rows(D.shape[1], work)

    def rest(r):
        _, up, down, out = spans(r)
        D[1, out] = D[1, out] + b * W[0, down]
        D[2, out] = D[2, out] - b * W[1, up]

    over_rows(D.shape[1], rest)


def first_response_ahead(V, S, coef_ref, force, D, W, A, window):
    b, b0, m0, m1, lam, mu2, mu = coefs(coef_ref, (C_B, C_B0, C_M0, C_M1, C_LAM, C_MU2, C_MU))
    A[...] = jnp.zeros(A.shape, jnp.float32)

    def given(r):
        here, _, _, _ = spans(r)
        A[0, here] = b * S[XX, 0, here]

    over_rows(D.shape[1], given)
    for i, which in enumerate(((VX, 2), (VY, 3), (VZ, 3), (VX, 3))):
        add_force(A, (i,), force, which, PAD + window)

    def work(r):
        here, up, down, out = spans(r)
        vx, vy, vz = A[0, here], A[1, here], A[2, here]
        exx = vx - A[3, here]
        dxx = lam * (exx + (vy - A[1, up]) + (vz - m0 * before(vz))) + mu2 * exx
        dxy = mu * (A[0, down] - vx + (V[VY, 0, here] - vy))
        dxz = mu * (m1 * after(vx) - vx + (V[VZ, 0, here] - vz))
        W[0, here] = dxy
        D[0, out] = dxy
        D[1, out] = dxz
        D[2, out] = vx + b * (dxy + dxz - dxx) - b0 * before(dxz)

    over_rows(D.shape[1], work)

    def rest(r):
        _, up, _, out = spans(r)
        D[2, out] = D[2, out] - b * W[0, up]

    over_rows(D.shape[1], rest)


def early_ahead(V, S, R, coef_ref, msg, W, force, window):
    b, b0, m0, m1, lam, mu2, mu = coefs(coef_ref, (C_B, C_B0, C_M0, C_M1, C_LAM, C_MU2, C_MU))

    def work(r):
        here, up, down, out = spans(r)
        vx, vy, vz = V[VX, 1, here], V[VY, 1, here], V[VZ, 1, here]
        exx = vx - V[VX, 0, here]
        volume = lam * (exx + (vy - V[VY, 1, up]) + (vz - m0 * before(vz)))
        sxx = S[XX, 1, here] + (volume + mu2 * exx) + DT * R[XX, 1, out]
        sxy = S[XY, 1, here] + mu * (V[VX, 1, down] - vx - vy) + DT * R[XY, 1, out]
        sxz = S[XZ, 1, here] + mu * (m1 * after(vx) - vx - vz) + DT * R[XZ, 1, out]
        W[0, here] = sxy
        msg[0, out] = sxy
        msg[1, out] = sxz
        msg[2, out] = vx + b * (sxy + sxz - sxx) - b0 * before(sxz)

    over_rows(msg.shape[1], work)

    def rest(r):
        _, up, _, out = spans(r)
        msg[2, out] = msg[2, out] - b * W[0, up]

    over_rows(msg.shape[1], rest)
    if force is not None:
        add_force(msg, (2,), force, (VX, 1), window)


def early_behind(V, S, R, coef_ref, surface, column, msg, W, force, window):
    b, b0, b1, m0, m1, lam, mu2, mu, l0 = coefs(
        coef_ref, (C_B, C_B0, C_B1, C_M0, C_M1, C_LAM, C_MU2, C_MU, C_L0)
    )

    def work(r):
        here, up, down, out = spans(r)
        vx, vy, vz = V[VX, 0, here], V[VY, 0, here], V[VZ, 0, here]
        eyy = vy - V[VY, 0, up]
        ezz = vz - m0 * before(vz)
        volume = lam * (vx + eyy + ezz)
        sxx = S[XX, 0, here] + (volume + mu2 * vx) + DT * R[XX, 0, out]
        syy = S[YY, 0, here] + (volume + mu2 * eyy) + DT * R[YY, 0, out]
        szz = S[ZZ, 0, here] + (volume + mu2 * ezz) + DT * R[ZZ, 0, out]
        if surface is not None:
            szz = szz + l0 * lane_roll(surface[out, :], -column)
        sxy = S[XY, 0, here] + mu * (V[VX, 0, down] - vx + (V[VY, 1, here] - vy)) + DT * R[XY, 0, out]
        sxz = S[XZ, 0, here] + mu * (m1 * after(vx) - vx + (V[VZ, 1, here] - vz)) + DT * R[XZ, 0, out]
        syz = S[YZ, 0, here] + mu * (m1 * after(vy) - vy + (V[VZ, 0, down] - vz)) + DT * R[YZ, 0, out]
        W[0, here] = syy
        W[1, here] = syz
        msg[0, out] = sxx
        msg[1, out] = vy + b * (sxy - syy + syz) - b0 * before(syz)
        msg[2, out] = vz + b * (sxz + syz - szz) + b1 * after(szz)

    over_rows(msg.shape[1], work)

    def rest(r):
        _, up, down, out = spans(r)
        msg[1, out] = msg[1, out] + b * W[0, down]
        msg[2, out] = msg[2, out] - b * W[1, up]

    over_rows(msg.shape[1], rest)
    if force is not None:
        add_force(msg, (1,), force, (VY, 0), window)
        add_force(msg, (2,), force, (VZ, 0), window)


def ahead_bond(V, S, R, coef_ref, force, surface, msg, missing, G, step, window, unforced=0, respond=None):
    (b,) = coefs(coef_ref, (C_B,))
    _, _, has_ahead = place()
    keep = jnp.where(has_ahead, 1.0, 0.0).astype(jnp.float32)

    def got(i, out):
        return msg[i, out] if missing is None else msg[i, out] + missing[i, out]

    def work(r):
        here, _, _, out = spans(r)
        V[VX, 1, here] = V[VX, 1, here] + (keep * b) * got(0, out)
        G[0, out] = keep * (got(1, out) - b * S[XY, 1, here])
        G[1, out] = keep * (got(2, out) - b * S[XZ, 1, here])

    over_rows(R.shape[2], work)
    if step < unforced:
        add_force(G, (0,), force, (VY, 2), window)
        add_force(G, (1,), force, (VZ, 2), window)
    if respond is not None:
        respond()
    post(
        V, S, R, coef_ref, surface, 1, 2 * step + 1,
        lambda r: V[VX, 0, pl.ds(PAD + r, ROWS)],
        lambda r: G[0, pl.ds(r, ROWS)],
        lambda r: G[1, pl.ds(r, ROWS)],
    )


def behind_bond(V, S, R, coef_ref, force, surface, msg, missing, G, step, window, unforced=0, respond=None):
    (b,) = coefs(coef_ref, (C_B,))
    _, has_behind, _ = place()
    keep = jnp.where(has_behind, 1.0, 0.0).astype(jnp.float32)

    def got(i, out):
        return msg[i, out] if missing is None else msg[i, out] + missing[i, out]

    def work(r):
        here, _, _, out = spans(r)
        V[VY, 0, here] = V[VY, 0, here] - (keep * b) * got(0, out)
        V[VZ, 0, here] = V[VZ, 0, here] - (keep * b) * got(1, out)
        G[0, out] = keep * (got(2, out) + b * S[XX, 0, here])

    over_rows(R.shape[2], work)
    if step < unforced:
        add_force(G, (0,), force, (VX, 2), window)
    if respond is not None:
        respond()
    post(
        V, S, R, coef_ref, surface, 0, 2 * step,
        lambda r: G[0, pl.ds(r, ROWS)],
        lambda r: V[VY, 1, pl.ds(PAD + r, ROWS)],
        lambda r: V[VZ, 1, pl.ds(PAD + r, ROWS)],
    )


def start_kernel(
    velocity, stress, memory, layer_in, lam_in, mu_in, buoy_in, rate_in, defect_in, loads, steps_table,
    V, S, R, coef_ref, msg_near, msg_far, W, table, layer_ref, lam, mu, buoy, rate, defect, sems,
):
    across = velocity.shape[2]
    inside = pl.ds(PAD, across)
    pairs = [
        (layer_in, layer_ref), (lam_in, lam), (mu_in, mu), (buoy_in, buoy), (rate_in, rate), (defect_in, defect),
    ]
    pairs += [(stress.at[i], S.at[i, :, inside]) for i in range(6)]
    pairs += [(velocity.at[i], V.at[i, :, inside]) for i in range(3)]
    pairs += [(memory.at[i], R.at[i]) for i in range(6)]
    copies = [pltpu.make_async_copy(*pair, sems.at[i]) for i, pair in enumerate(pairs)]
    for copy in copies:
        copy.start()
    slots = loads.shape[0]
    zero_edges(V)
    zero_edges(S)
    zero_edges(W)
    table[...] = jnp.zeros(table.shape, jnp.float32)
    table[0:16, :] = steps_table[...]
    columns = table[...].T
    trucks = 6 * across
    msg_far[trucks : trucks + slots, :] = loads[...]
    for i, at in enumerate((0, 8)):
        first_row = trucks + (1 + i) * slots
        column = columns[0:slots, at : at + 1]
        msg_far[first_row : first_row + slots, :] = jnp.broadcast_to(column, loads.shape)
    for copy in copies[:6]:
        copy.wait()
    layer = layer_ref[...]

    def per_depth(table):
        row = jnp.zeros(layer.shape, jnp.float32)
        for level in range(table.shape[0]):
            row = jnp.where(layer == level, table[level], row)
        return row

    lane = lax.broadcasted_iota(jnp.int32, layer.shape, 1)
    not_first = jnp.where(lane > 0, 1.0, 0.0).astype(jnp.float32)
    not_last = jnp.where(lane < layer.shape[1] - 1, 1.0, 0.0).astype(jnp.float32)
    b = DT * per_depth(buoy)
    two_mu = (2.0 * DT) * per_depth(mu)
    decay = DT * per_depth(rate)
    drop = 2.0 * decay * per_depth(defect)
    for row, value in (
        (C_B, b),
        (C_B0, b * not_first),
        (C_B1, b * not_last),
        (C_M0, not_first),
        (C_M1, not_last),
        (C_LAM, DT * per_depth(lam)),
        (C_MU2, two_mu),
        (C_MU, 0.5 * two_mu),
        (C_K1, 1.0 - decay),
        (C_K2, drop),
        (C_K2H, 0.5 * drop),
        (C_L0, DT * (1.0 - not_first)),
    ):
        coef_ref[row : row + 1, :] = value
    coef_ref[12:16, :] = jnp.zeros((4, layer.shape[1]), jnp.float32)
    for copy in copies[6:15]:
        copy.wait()
    even, _, _ = place()
    now, then = Planes(msg_far, 0, across), Planes(msg_far, 3, across)

    @pl.when(even)
    def _():
        pre_ahead(V, S, coef_ref, msg_near, None, 0)
        pre_behind(V, S, coef_ref, now, None, 0)

    @pl.when(jnp.logical_not(even))
    def _():
        pre_behind(V, S, coef_ref, msg_near, None, 0)
        pre_ahead(V, S, coef_ref, now, None, 0)

    inner(V, S, coef_ref, None, 0)
    for copy in copies[15:]:
        copy.wait()

    @pl.when(even)
    def _():
        early_behind(V, S, R, coef_ref, None, 0, then, W, None, 0)

    @pl.when(jnp.logical_not(even))
    def _():
        early_ahead(V, S, R, coef_ref, then, W, None, 0)


def near_kernel(step, window, V0, S0, R0, coef_ref, force, surface, msg, V, S, R, *rest):
    G = rest[-1]
    if step == 0:
        for comp in range(3):
            for cell in range(2):
                add_force(V, (comp, cell), force, (0, comp, cell), PAD + window)
    even, _, _ = place()
    more = step < STEPS - 1

    @pl.when(even)
    def _():
        ahead_bond(V, S, R, coef_ref, force.at[step], surface, msg, None, G, step, window, 1)
        if more:
            pre_ahead(V, S, coef_ref, rest[0], force.at[step + 1], window)

    @pl.when(jnp.logical_not(even))
    def _():
        behind_bond(V, S, R, coef_ref, force.at[step], surface, msg, None, G, step, window, 1)
        if more:
            pre_behind(V, S, coef_ref, rest[0], force.at[step + 1], window)


def meet_kernel(across, msg, loads, load, rows_out):
    slots = loads.shape[0]
    rows, entry, cell = (msg[6 * across + i * slots : 6 * across + (i + 1) * slots, :] for i in range(3))
    for slot in range(slots):
        rows = jnp.where(entry == float(slot), loads[slot : slot + 1, :], rows)
    rows_out[...] = jnp.zeros(rows_out.shape, jnp.float32)
    rows_out[0:1, :] = jnp.sum(jnp.where(cell == 0.0, rows, 0.0), axis=0, keepdims=True)
    load[...] = rows_out[...].T


def far_kernel(step, window, V0, S0, R0, coef_ref, force, surface, msg, *rest):
    rest = list(rest)
    other = rest.pop(0)
    V, S, R, D = rest[:4]
    early = rest[4] if step < STEPS - 2 else None
    across = R.shape[2]
    even, _, _ = place()
    here, then = force.at[step], force.at[step + 1]
    got = Planes(msg, 3 * step, across) if step < 2 else msg
    if step == 0:
        missing, load = None, other
        G, W, A = rest[-3:]
    else:
        missing = other
        G, W = rest[-2:]
    zero_edges(W)

    @pl.when(even)
    def _():
        if step == 0:
            respond = lambda: first_response_ahead(V, S, coef_ref, here, D, W, A, window)
        else:
            respond = lambda: response_ahead(V, S, coef_ref, D, W)
        behind_bond(
            V, S, R, coef_ref, here, surface, got, missing, G, step, window, 2, respond
        )
        pre_behind(V, S, coef_ref, None, then, window)

    @pl.when(jnp.logical_not(even))
    def _():
        if step == 0:
            respond = lambda: first_response_behind(V, S, coef_ref, here, load, D, W, A, window)
        else:
            respond = lambda: response_behind(V, S, coef_ref, D, W)
        ahead_bond(
            V, S, R, coef_ref, here, surface, got, missing, G, step, window, 2, respond
        )
        pre_ahead(V, S, coef_ref, None, then, window)

    inner(V, S, coef_ref, then, window)
    if early is not None:
        later = force.at[step + 2]

        @pl.when(even)
        def _():
            early_behind(V, S, R, coef_ref, surface, 2 * (step + 1), early, W, later, window)

        @pl.when(jnp.logical_not(even))
        def _():
            early_ahead(V, S, R, coef_ref, early, W, later, window)


def last_kernel(
    step, window, V0, S0, R0, coef_ref, force, surface, msg, missing, V, S, R, v_out, s_out, r_out, G, sems
):
    even, _, _ = place()
    here = force.at[step]
    inside = pl.ds(PAD, R.shape[2])

    def copies(cell):
        return [
            pltpu.make_async_copy(V.at[:, cell, inside], v_out.at[:, cell], sems.at[cell, 0]),
            pltpu.make_async_copy(S.at[:, cell, inside], s_out.at[:, cell], sems.at[cell, 1]),
            pltpu.make_async_copy(R.at[:, cell], r_out.at[:, cell], sems.at[cell, 2]),
        ]

    def finish(cell, bond):
        done, other = copies(1 - cell), copies(cell)
        for copy in done:
            copy.start()
        bond(V, S, R, coef_ref, here, surface, msg, missing, G, step, window)
        for copy in other:
            copy.start()
        for copy in done + other:
            copy.wait()

    @pl.when(even)
    def _():
        finish(0, behind_bond)

    @pl.when(jnp.logical_not(even))
    def _():
        finish(1, ahead_bond)


ENTRY_ROW, TRUCK_ROW = 48, 56
GROUP = 8


def pack_kernel(
    record, loads_in, entries_in, cells_in, piers_in, own, loads, steps_table, piers, entries, cells, sems
):
    panel = record.shape[1]
    slots, lanes = loads.shape
    steps = entries.shape[0]
    pairs = [(record, own.at[:, pl.ds(0, panel)]), (loads_in, loads), (entries_in, entries), (cells_in, cells)]
    pairs.append((piers_in, piers))
    copies = [pltpu.make_async_copy(*pair, sems.at[i]) for i, pair in enumerate(pairs)]
    for copy in copies:
        copy.start()
    own[:, panel:] = jnp.zeros((own.shape[0], own.shape[1] - panel), jnp.float32)
    steps_table[...] = jnp.zeros(steps_table.shape, jnp.float32)
    for copy in copies:
        copy.wait()
    steps_table[0:steps, 0:slots] = entries[...].astype(jnp.float32)
    steps_table[8 : 8 + steps, 0:slots] = cells[...].astype(jnp.float32)
    blocks = [loads[8 * i : 8 * i + 8, :] for i in range(slots // 8)] + [steps_table[0:8, :]]
    for i, block in enumerate(blocks):
        own[0:8, panel + i * lanes : panel + (i + 1) * lanes] = block


def lane_blocks(table, width):
    return sum(lane_roll(table[s : s + 1, :], s * width) for s in range(STEPS))


def split_kernel(panel, slots, own, behind, cells, after_this, out):
    del after_this
    tiles, _, lanes = out.shape
    pieces = panel // lanes
    third = pieces // 3
    cell_of = cells[...]
    me = lax.axis_index("line")
    group, mine = lax.div(me, tiles), lax.rem(me, tiles)
    piers = cell_of.shape[1]
    row = lax.broadcasted_iota(jnp.int32, (4 * tiles, lanes), 0)
    tile, j = lax.div(row, 4), lax.rem(row, 4)
    odd = lax.rem(tile, 2)
    first = (tile + group * tiles) * 2
    cell_x = first + jnp.where(j == 2, -1, jnp.where(j == 3, 4 * odd - 2, j))
    cell_yz = first + jnp.where(j == 3, 4 * odd - 1, j)
    record = jnp.where(group == 0, own[:, :panel], behind[:, :panel])

    def hits(cell):
        return [jnp.where(cell == cell_of[0:1, p : p + 1], 1.0, 0.0).astype(jnp.float32) for p in range(piers)]

    hit_x, hit_yz = hits(cell_x), hits(cell_yz)

    def share(m):
        hit = hit_x if m < third else hit_yz
        return sum(hit[p] * record[p : p + 1, m * lanes : (m + 1) * lanes] for p in range(piers))

    parts = [share(m) for m in range(pieces)]

    def trucks(source):
        blocks = [source[0:8, panel + i * lanes : panel + (i + 1) * lanes] for i in range(slots // 8 + 1)]
        return blocks[:-1], lane_blocks(blocks[-1], slots)

    own_rows, own_entry = trucks(own)
    far_rows, far_entry = trucks(behind)
    for tile in range(tiles):
        these = slice(4 * tile, 4 * tile + 4)
        for m in range(pieces):
            out[tile, 4 * m : 4 * m + 4, :] = parts[m][these, :]
        passed = mine < tile
        out[tile, ENTRY_ROW : ENTRY_ROW + 1, :] = jnp.where(passed, own_entry, far_entry)
        for i in range(slots // 8):
            at = TRUCK_ROW + 8 * i
            out[tile, at : at + 8, :] = jnp.where(passed, own_rows[i], far_rows[i])


def prepare_kernel(parts, loads, steps_table, after_this, force, surface, table, rows_out):
    del after_this
    steps, comps, width = force.shape[:3]
    lanes = parts.shape[2]
    force[...] = jnp.zeros(force.shape, jnp.float32)
    per = ENTRY_ROW // (comps * width)
    lane = lax.broadcasted_iota(jnp.int32, (per, lanes), 1)
    scale = jnp.where(lane < FZ, DT, 0.0).astype(jnp.float32)
    for s in range(steps):
        for comp in range(comps):
            for cell in range(width):
                panel = parts[s, pl.ds(comp * per * width + cell, per, stride=width), :]
                force[s, comp, cell, pl.ds(4, per, stride=2), :] = scale * panel
                force[s, comp, cell, pl.ds(5, per, stride=2), :] = scale * lane_roll(panel, FZ)

    slots = loads.shape[0]
    tiles = parts.shape[0]
    mine = lax.rem(lax.axis_index("line"), tiles)
    table[...] = jnp.zeros(table.shape, jnp.float32)
    table[0:1, :] = lane_blocks(steps_table[0:8, :], slots)
    table[STEPS + 1 : STEPS + 2, :] = lane_blocks(steps_table[8:16, :], slots)
    rows = [loads[...]]
    for k in range(1, STEPS + 1):
        source = lax.rem(mine + (tiles - k), tiles)
        rows.append(parts[source, TRUCK_ROW : TRUCK_ROW + slots, :])
        table[k : k + 1, :] = parts[source, ENTRY_ROW : ENTRY_ROW + 1, :]
    columns = table[...].T
    rows_out[...] = jnp.zeros(rows_out.shape, jnp.float32)
    for s in range(STEPS):
        block = slice(s * slots, (s + 1) * slots)
        moved = []
        for k in range(STEPS - s):
            entry = jnp.broadcast_to(columns[block, k : k + 1], rows[k].shape)
            new = rows[k]
            for slot in range(slots):
                new = jnp.where(entry == float(slot), rows[k + 1][slot : slot + 1, :], new)
            moved.append(new)
        rows = moved
        cell = jnp.broadcast_to(columns[block, STEPS + 1 : STEPS + 2], rows[0].shape)
        for c in range(2):
            load = jnp.sum(jnp.where(cell == float(c), rows[0], 0.0), axis=0, keepdims=True)
            rows_out[2 * s + c : 2 * s + c + 1, :] = load
    surface[...] = rows_out[...].T


def in_vmem(x):
    return pltpu.with_memory_space_constraint(x, pltpu.VMEM)


WHOLE = pl.BlockSpec(memory_space=pltpu.VMEM)
SCALARS = pl.BlockSpec(memory_space=pltpu.SMEM)
ANYWHERE = pl.BlockSpec(memory_space=pl.ANY)


def call(kernel, ins, specs, outs, out_specs, scratch=(), aliases=None, name=None, cost=1):
    return pl.pallas_call(
        kernel,
        out_shape=outs,
        in_specs=specs,
        out_specs=out_specs,
        scratch_shapes=list(scratch),
        input_output_aliases=aliases or {},
        compiler_params=pltpu.CompilerParams(vmem_limit_bytes=VMEM_LIMIT),
        cost_estimate=pl.CostEstimate(flops=cost, bytes_accessed=cost, transcendentals=0),
        name=name,
    )(*ins)


def body(
    velocity, stress, memory, truck_loads, pier_panels,
    lame_lambda, lame_mu, buoyancy, relax_rate, defect_mu, layer,
    truck_entry, truck_cell, pier_cell,
):
    tiles = lax.axis_size("line")
    width_x, across, depth = velocity.shape[1:]
    slots = truck_loads.shape[0]
    window = (across - FY) // 2 - 4
    f32 = jnp.float32

    near = [(i, i ^ 1) for i in range(tiles) if (i ^ 1) < tiles]
    far = [(i, i + 1) for i in range(1, tiles - 1, 2)] + [(i + 1, i) for i in range(1, tiles - 1, 2)]

    padded = across + 2 * PAD
    v_type = pltpu.VMEM((3, width_x, padded, depth), f32)
    s_type = pltpu.VMEM((6, width_x, padded, depth), f32)
    r_type = pltpu.VMEM((6, width_x, across, depth), f32)
    c_type = pltpu.VMEM((N_COEF, depth), f32)
    m_type = pltpu.VMEM((3, across, depth), f32)
    ghost = pltpu.VMEM((2, across, depth), f32)
    work = pltpu.VMEM((2, padded, depth), f32)
    square = pltpu.VMEM((across, depth), f32)

    def ahead_by(x, distance):
        return lax.ppermute(x, "line", [(i, i + distance) for i in range(tiles - distance)])

    def in_hbm(*arrays):
        return tuple(pltpu.with_memory_space_constraint(x, pltpu.HBM) for x in arrays)

    dma = pltpu.SemaphoreType.DMA
    piers, panel = pier_panels.shape[1:]
    own, loads, steps_table, pier_row = call(
        pack_kernel,
        in_hbm(pier_panels[0], truck_loads, truck_entry, truck_cell, pier_cell[None, :]),
        (ANYWHERE,) * 5,
        (
            pltpu.VMEM((piers, panel + (slots // 8 + 1) * depth), f32),
            pltpu.VMEM((slots, depth), f32),
            pltpu.VMEM((16, depth), f32),
            pltpu.VMEM((1, piers), jnp.int32),
        ),
        (WHOLE,) * 4,
        scratch=(pltpu.VMEM(truck_entry.shape, jnp.int32), pltpu.VMEM(truck_cell.shape, jnp.int32), dma((5,))),
        name="pack",
    )
    behind = ahead_by(own, GROUP)
    reach = 2 * GROUP
    index = lax.axis_index("line")
    while reach < tiles:
        record = jnp.where(index < GROUP, own, behind)[:, :panel]
        record = jnp.where(index < reach, record, ahead_by(record, reach))
        behind = jnp.concatenate([record, behind[:, panel:]], axis=1)
        reach *= 2
    tables = (lame_lambda, lame_mu, buoyancy, relax_rate, defect_mu)
    V, S, R, coef, msg_near, msg_far = call(
        start_kernel,
        in_hbm(velocity, stress, memory, layer[None, :], *tables) + (in_vmem(loads), in_vmem(steps_table)),
        (ANYWHERE,) * 9 + (WHOLE,) * 2,
        (v_type, s_type, r_type, c_type, m_type, pltpu.VMEM((6 * across + 3 * slots, depth), f32)),
        (WHOLE,) * 6,
        scratch=(
            work, pltpu.VMEM((depth, depth), f32), pltpu.VMEM((1, depth), jnp.int32),
            *(pltpu.SMEM(table.shape, f32) for table in tables), dma((21,)),
        ),
        name="start",
        cost=8 * 1024 * 1024,
    )
    msg_far = lax.ppermute(msg_far, "line", far)
    msg_near = lax.ppermute(msg_near, "line", near)
    parts = call(
        functools.partial(split_kernel, panel, slots),
        (own, behind, in_vmem(pier_row), coef),
        (WHOLE,) * 3 + (ANYWHERE,),
        jax.ShapeDtypeStruct((GROUP, TRUCK_ROW + slots, depth), f32),
        WHOLE,
        name="split",
    )
    groups = [list(range(at, at + GROUP)) for at in range(0, tiles, GROUP)]
    parts = lax.all_to_all(parts, "line", 0, 0, axis_index_groups=groups, tiled=True)
    load = call(
        functools.partial(meet_kernel, across),
        (in_vmem(msg_far), in_vmem(loads)),
        (WHOLE,) * 2,
        square,
        WHOLE,
        scratch=(pltpu.VMEM((depth, across), f32),),
        name="meet",
        cost=64 * 1024 * 1024,
    )
    force, surface = call(
        prepare_kernel,
        (parts, in_vmem(loads), in_vmem(steps_table), load),
        (WHOLE,) * 3 + (ANYWHERE,),
        (pltpu.VMEM((STEPS, 3, 4, 16, depth), f32), pltpu.VMEM((across, depth), f32)),
        (WHOLE,) * 2,
        scratch=(pltpu.VMEM((depth, depth), f32), pltpu.VMEM((depth, across), f32)),
        name="prepare",
    )
    state = (v_type, s_type, r_type)
    same = {0: 0, 1: 1, 2: 2}
    missing = None
    for step in range(STEPS):
        more = step < STEPS - 1
        ins = tuple(in_vmem(x) for x in (V, S, R, coef, force, surface, msg_near))
        outs = state + ((m_type,) if more else ())
        V, S, R, *msg = call(
            functools.partial(near_kernel, step, window),
            ins,
            (WHOLE,) * len(ins),
            outs,
            (WHOLE,) * len(outs),
            scratch=(ghost,),
            aliases=same,
            name="near" + str(step),
        )
        if more:
            msg_near = lax.ppermute(msg[0], "line", near)
        ins = (V, S, R, coef, force, surface, msg_far, missing if step else load)
        ins = tuple(in_vmem(x) for x in ins)
        if more:
            outs = state + (m_type,) + ((m_type,) if step < STEPS - 2 else ())
            V, S, R, missing, *msg = call(
                functools.partial(far_kernel, step, window),
                ins,
                (WHOLE,) * len(ins),
                outs,
                (WHOLE,) * len(outs),
                scratch=(ghost, work) + (() if step else (pltpu.VMEM((5, padded, depth), f32),)),
                aliases=same,
                name="far" + str(step),
            )
            if step > 0:
                msg_far = early
            if msg:
                early = lax.ppermute(msg[0], "line", far)
    results = call(
        functools.partial(last_kernel, STEPS - 1, window),
        ins,
        (WHOLE,) * len(ins),
        state + tuple(jax.ShapeDtypeStruct(x.shape, f32) for x in (velocity, stress, memory)),
        (WHOLE,) * 3 + (ANYWHERE,) * 3,
        scratch=(ghost, pltpu.SemaphoreType.DMA((2, 3))),
        aliases=same,
        name="last",
    )
    return results[3:]


def solution(mesh):
    placed = (
        P(None, ("runs", "line"), None, None),
        P(None, ("runs", "line"), None, None),
        P(None, ("runs", "line"), None, None),
        P(("runs", "line"), None),
        P("line", "runs", None),
        P(),
        P(),
        P(),
        P(),
        P(),
        P(),
        P(None, ("runs", "line")),
        P(None, ("runs", "line")),
        P(),
    )
    return jax.shard_map(
        body,
        mesh=mesh,
        in_specs=placed,
        out_specs=(
            P(None, ("runs", "line"), None, None),
            P(None, ("runs", "line"), None, None),
            P(None, ("runs", "line"), None, None),
        ),
        check_vma=False,
    )
```

```python
import functools

import jax
import jax.numpy as jnp
import numpy as np
from jax import lax
from jax.experimental import pallas as pl
from jax.experimental.pallas import tpu as pltpu
from jax.sharding import PartitionSpec as P

STEPS = 6
FY = 8
FZ = 64
DT = 0.25
PAD = 8
ROWS = 16
UNROLL = 8
VMEM_LIMIT = 32 * 1024 * 1024

C_B, C_B0, C_B1, C_M0, C_M1, C_LAM, C_MU2, C_MU, C_K1, C_K2, C_K2H, C_L0 = range(12)
N_COEF = 16

VX, VY, VZ = range(3)
XX, YY, ZZ, XY, XZ, YZ = range(6)


def lane_roll(x, shift):
    return pltpu.roll(x, shift % x.shape[-1], x.ndim - 1)


def before(x):
    return lane_roll(x, 1)


def after(x):
    return lane_roll(x, -1)


def over_rows(count, work):
    def step(i, carry):
        work(pl.multiple_of(i * ROWS, ROWS))
        return carry

    lax.fori_loop(0, count // ROWS, step, 0, unroll=UNROLL)


class Planes:
    def __init__(self, ref, first, across):
        self.ref, self.first, self.shape = ref, first, (3, across, ref.shape[1])

    def rows(self, at):
        plane, out = at
        return pl.ds(self.first * self.shape[1] + plane * self.shape[1] + out.start, out.size)

    def __getitem__(self, at):
        return self.ref[self.rows(at)]

    def __setitem__(self, at, value):
        self.ref[self.rows(at)] = value


def coefs(coef_ref, ids):
    return [coef_ref[i : i + 1, :] for i in ids]


def place():
    index = lax.axis_index("line")
    return lax.rem(index, 2) == 0, index > 0, index < lax.axis_size("line") - 1


def spans(r):
    return pl.ds(PAD + r, ROWS), pl.ds(PAD + r - 1, ROWS), pl.ds(PAD + r + 1, ROWS), pl.ds(r, ROWS)


def zero_edges(ref):
    across = ref.shape[-2] - 2 * PAD
    edge = jnp.zeros((PAD, ref.shape[-1]), jnp.float32)
    for where in np.ndindex(*ref.shape[:-2]):
        ref[(*where, pl.ds(0, PAD))] = edge
        ref[(*where, pl.ds(PAD + across, PAD))] = edge


def add_force(ref, index, force, which, first_row):
    rows = pl.ds(first_row, 16)
    ref[(*index, rows)] = ref[(*index, rows)] + force[which]


def pre_ahead(V, S, coef_ref, msg, force, window):
    b, b0 = coefs(coef_ref, (C_B, C_B0))

    def work(r):
        here, up, _, out = spans(r)
        sxy, sxz = S[XY, 1, here], S[XZ, 1, here]
        px = V[VX, 1, here] + b * (sxy - S[XY, 1, up] + sxz - S[XX, 1, here]) - b0 * before(sxz)
        V[VX, 1, here] = px
        if msg is not None:
            msg[0, out] = sxy
            msg[1, out] = sxz
            msg[2, out] = px

    over_rows(V.shape[2] - 2 * PAD, work)
    if force is not None:
        add_force(V, (VX, 1), force, (VX, 1), PAD + window)
        if msg is not None:
            add_force(msg, (2,), force, (VX, 1), window)


def pre_behind(V, S, coef_ref, msg, force, window):
    b, b0, b1 = coefs(coef_ref, (C_B, C_B0, C_B1))

    def work(r):
        here, up, down, out = spans(r)
        syz, szz = S[YZ, 0, here], S[ZZ, 0, here]
        qy = V[VY, 0, here] + b * (S[XY, 0, here] + S[YY, 0, down] - S[YY, 0, here] + syz) - b0 * before(syz)
        qz = V[VZ, 0, here] + b * (S[XZ, 0, here] + syz - S[YZ, 0, up] - szz) + b1 * after(szz)
        V[VY, 0, here] = qy
        V[VZ, 0, here] = qz
        if msg is not None:
            msg[0, out] = S[XX, 0, here]
            msg[1, out] = qy
            msg[2, out] = qz

    over_rows(V.shape[2] - 2 * PAD, work)
    if force is not None:
        add_force(V, (VY, 0), force, (VY, 0), PAD + window)
        add_force(V, (VZ, 0), force, (VZ, 0), PAD + window)
        if msg is not None:
            add_force(msg, (1,), force, (VY, 0), window)
            add_force(msg, (2,), force, (VZ, 0), window)


def inner(V, S, coef_ref, force, window):
    b, b0, b1 = coefs(coef_ref, (C_B, C_B0, C_B1))

    def work(r):
        here, up, down, _ = spans(r)
        sxy, sxz = S[XY, 0, here], S[XZ, 0, here]
        V[VX, 0, here] = (
            V[VX, 0, here]
            + b * (S[XX, 1, here] - S[XX, 0, here] + sxy - S[XY, 0, up] + sxz)
            - b0 * before(sxz)
        )
        syz, szz = S[YZ, 1, here], S[ZZ, 1, here]
        V[VY, 1, here] = (
            V[VY, 1, here]
            + b * (S[XY, 1, here] - sxy + S[YY, 1, down] - S[YY, 1, here] + syz)
            - b0 * before(syz)
        )
        V[VZ, 1, here] = (
            V[VZ, 1, here]
            + b * (S[XZ, 1, here] - sxz + syz - S[YZ, 1, up] - szz)
            + b1 * after(szz)
        )

    over_rows(V.shape[2] - 2 * PAD, work)
    if force is not None:
        add_force(V, (VX, 0), force, (VX, 0), PAD + window)
        add_force(V, (VY, 1), force, (VY, 1), PAD + window)
        add_force(V, (VZ, 1), force, (VZ, 1), PAD + window)


def post(V, S, R, coef_ref, surface, cell, column, behind_x, ahead_y, ahead_z):
    m0, m1, lam, mu2, mu, k1, k2, k2h, l0 = coefs(
        coef_ref, (C_M0, C_M1, C_LAM, C_MU2, C_MU, C_K1, C_K2, C_K2H, C_L0)
    )

    def work(r):
        here, up, down, out = spans(r)
        vx, vy, vz = V[VX, cell, here], V[VY, cell, here], V[VZ, cell, here]
        exx = vx - behind_x(r)
        eyy = vy - V[VY, cell, up]
        ezz = vz - m0 * before(vz)
        exy = V[VX, cell, down] - vx + (ahead_y(r) - vy)
        exz = m1 * after(vx) - vx + (ahead_z(r) - vz)
        eyz = m1 * after(vy) - vy + (V[VZ, cell, down] - vz)
        volume = lam * (exx + eyy + ezz)
        for comp, e in ((XX, exx), (YY, eyy), (ZZ, ezz)):
            old = R[comp, cell, out]
            new = S[comp, cell, here] + (volume + mu2 * e) + DT * old
            if comp == ZZ:
                new = new + l0 * lane_roll(surface[out, :], -column)
            S[comp, cell, here] = new
            R[comp, cell, out] = k1 * old - k2 * e
        for comp, e in ((XY, exy), (XZ, exz), (YZ, eyz)):
            old = R[comp, cell, out]
            S[comp, cell, here] = S[comp, cell, here] + mu * e + DT * old
            R[comp, cell, out] = k1 * old - k2h * e

    over_rows(R.shape[2], work)


def response_behind(V, S, coef_ref, D, W):
    b, b0, b1, m0, m1, lam, mu2, mu = coefs(coef_ref, (C_B, C_B0, C_B1, C_M0, C_M1, C_LAM, C_MU2, C_MU))

    def work(r):
        here, up, down, out = spans(r)
        sxy = S[XY, 1, here]
        vy, vz = -b * sxy, -b * S[XZ, 1, here]
        exx = -V[VX, 1, here]
        eyy = b * (S[XY, 1, up] - sxy)
        ezz = vz - m0 * before(vz)
        volume = lam * (exx + eyy + ezz)
        dyy, dzz = volume + mu2 * eyy, volume + mu2 * ezz
        dyz = mu * (m1 * after(vy) - vy - b * S[XZ, 1, down] - vz)
        W[0, here] = dyy
        W[1, here] = dyz
        D[0, out] = volume + mu2 * exx
        D[1, out] = vy + b * (dyz - mu * vy - dyy) - b0 * before(dyz)
        D[2, out] = vz + b * (dyz - mu * vz - dzz) + b1 * after(dzz)

    over_rows(D.shape[1], work)

    def rest(r):
        _, up, down, out = spans(r)
        D[1, out] = D[1, out] + b * W[0, down]
        D[2, out] = D[2, out] - b * W[1, up]

    over_rows(D.shape[1], rest)


def response_ahead(V, S, coef_ref, D, W):
    b, b0, m1, lam, mu2, mu = coefs(coef_ref, (C_B, C_B0, C_M1, C_LAM, C_MU2, C_MU))

    def work(r):
        here, _, down, out = spans(r)
        vx = b * S[XX, 0, here]
        dxy = mu * (b * S[XX, 0, down] - vx + V[VY, 0, here])
        dxz = mu * (m1 * after(vx) - vx + V[VZ, 0, here])
        W[0, here] = dxy
        D[0, out] = dxy
        D[1, out] = dxz
        D[2, out] = vx + b * (dxy + dxz - (lam + mu2) * vx) - b0 * before(dxz)

    over_rows(D.shape[1], work)

    def rest(r):
        _, up, _, out = spans(r)
        D[2, out] = D[2, out] - b * W[0, up]

    over_rows(D.shape[1], rest)


def first_response_behind(V, S, coef_ref, force, load, D, W, A, window):
    b, b0, b1, m0, m1, lam, mu2, mu, l0 = coefs(
        coef_ref, (C_B, C_B0, C_B1, C_M0, C_M1, C_LAM, C_MU2, C_MU, C_L0)
    )
    A[...] = jnp.zeros(A.shape, jnp.float32)

    def given(r):
        here, _, _, _ = spans(r)
        A[1, here] = -b * S[XY, 1, here]
        A[2, here] = -b * S[XZ, 1, here]

    over_rows(D.shape[1], given)
    for i, which in enumerate(((VX, 3), (VY, 2), (VZ, 2), (VY, 3), (VZ, 3))):
        add_force(A, (i,), force, which, PAD + window)

    def work(r):
        here, up, down, out = spans(r)
        vx, vy, vz = A[0, here], A[1, here], A[2, here]
        exx = vx - V[VX, 1, here]
        eyy = vy - A[1, up]
        ezz = vz - m0 * before(vz)
        volume = lam * (exx + eyy + ezz)
        dyy = volume + mu2 * eyy
        dzz = volume + mu2 * ezz + l0 * load[out, :]
        dxy = mu * (A[0, down] - vx + (A[3, here] - vy))
        dxz = mu * (m1 * after(vx) - vx + (A[4, here] - vz))
        dyz = mu * (m1 * after(vy) - vy + (A[2, down] - vz))
        W[0, here] = dyy
        W[1, here] = dyz
        D[0, out] = volume + mu2 * exx
        D[1, out] = vy + b * (dxy - dyy + dyz) - b0 * before(dyz)
        D[2, out] = vz + b * (dxz + dyz - dzz) + b1 * after(dzz)

    over_rows(D.shape[1], work)

    def rest(r):
        _, up, down, out = spans(r)
        D[1, out] = D[1, out] + b * W[0, down]
        D[2, out] = D[2, out] - b * W[1, up]

    over_rows(D.shape[1], rest)


def first_response_ahead(V, S, coef_ref, force, D, W, A, window):
    b, b0, m0, m1, lam, mu2, mu = coefs(coef_ref, (C_B, C_B0, C_M0, C_M1, C_LAM, C_MU2, C_MU))
    A[...] = jnp.zeros(A.shape, jnp.float32)

    def given(r):
        here, _, _, _ = spans(r)
        A[0, here] = b * S[XX, 0, here]

    over_rows(D.shape[1], given)
    for i, which in enumerate(((VX, 2), (VY, 3), (VZ, 3), (VX, 3))):
        add_force(A, (i,), force, which, PAD + window)

    def work(r):
        here, up, down, out = spans(r)
        vx, vy, vz = A[0, here], A[1, here], A[2, here]
        exx = vx - A[3, here]
        dxx = lam * (exx + (vy - A[1, up]) + (vz - m0 * before(vz))) + mu2 * exx
        dxy = mu * (A[0, down] - vx + (V[VY, 0, here] - vy))
        dxz = mu * (m1 * after(vx) - vx + (V[VZ, 0, here] - vz))
        W[0, here] = dxy
        D[0, out] = dxy
        D[1, out] = dxz
        D[2, out] = vx + b * (dxy + dxz - dxx) - b0 * before(dxz)

    over_rows(D.shape[1], work)

    def rest(r):
        _, up, _, out = spans(r)
        D[2, out] = D[2, out] - b * W[0, up]

    over_rows(D.shape[1], rest)


def early_ahead(V, S, R, coef_ref, msg, W, force, window):
    b, b0, m0, m1, lam, mu2, mu = coefs(coef_ref, (C_B, C_B0, C_M0, C_M1, C_LAM, C_MU2, C_MU))

    def work(r):
        here, up, down, out = spans(r)
        vx, vy, vz = V[VX, 1, here], V[VY, 1, here], V[VZ, 1, here]
        exx = vx - V[VX, 0, here]
        volume = lam * (exx + (vy - V[VY, 1, up]) + (vz - m0 * before(vz)))
        sxx = S[XX, 1, here] + (volume + mu2 * exx) + DT * R[XX, 1, out]
        sxy = S[XY, 1, here] + mu * (V[VX, 1, down] - vx - vy) + DT * R[XY, 1, out]
        sxz = S[XZ, 1, here] + mu * (m1 * after(vx) - vx - vz) + DT * R[XZ, 1, out]
        W[0, here] = sxy
        msg[0, out] = sxy
        msg[1, out] = sxz
        msg[2, out] = vx + b * (sxy + sxz - sxx) - b0 * before(sxz)

    over_rows(msg.shape[1], work)

    def rest(r):
        _, up, _, out = spans(r)
        msg[2, out] = msg[2, out] - b * W[0, up]

    over_rows(msg.shape[1], rest)
    if force is not None:
        add_force(msg, (2,), force, (VX, 1), window)


def early_behind(V, S, R, coef_ref, surface, column, msg, W, force, window):
    b, b0, b1, m0, m1, lam, mu2, mu, l0 = coefs(
        coef_ref, (C_B, C_B0, C_B1, C_M0, C_M1, C_LAM, C_MU2, C_MU, C_L0)
    )

    def work(r):
        here, up, down, out = spans(r)
        vx, vy, vz = V[VX, 0, here], V[VY, 0, here], V[VZ, 0, here]
        eyy = vy - V[VY, 0, up]
        ezz = vz - m0 * before(vz)
        volume = lam * (vx + eyy + ezz)
        sxx = S[XX, 0, here] + (volume + mu2 * vx) + DT * R[XX, 0, out]
        syy = S[YY, 0, here] + (volume + mu2 * eyy) + DT * R[YY, 0, out]
        szz = S[ZZ, 0, here] + (volume + mu2 * ezz) + DT * R[ZZ, 0, out]
        if surface is not None:
            szz = szz + l0 * lane_roll(surface[out, :], -column)
        sxy = S[XY, 0, here] + mu * (V[VX, 0, down] - vx + (V[VY, 1, here] - vy)) + DT * R[XY, 0, out]
        sxz = S[XZ, 0, here] + mu * (m1 * after(vx) - vx + (V[VZ, 1, here] - vz)) + DT * R[XZ, 0, out]
        syz = S[YZ, 0, here] + mu * (m1 * after(vy) - vy + (V[VZ, 0, down] - vz)) + DT * R[YZ, 0, out]
        W[0, here] = syy
        W[1, here] = syz
        msg[0, out] = sxx
        msg[1, out] = vy + b * (sxy - syy + syz) - b0 * before(syz)
        msg[2, out] = vz + b * (sxz + syz - szz) + b1 * after(szz)

    over_rows(msg.shape[1], work)

    def rest(r):
        _, up, down, out = spans(r)
        msg[1, out] = msg[1, out] + b * W[0, down]
        msg[2, out] = msg[2, out] - b * W[1, up]

    over_rows(msg.shape[1], rest)
    if force is not None:
        add_force(msg, (1,), force, (VY, 0), window)
        add_force(msg, (2,), force, (VZ, 0), window)


def ahead_bond(V, S, R, coef_ref, force, surface, msg, missing, G, step, window, unforced=0, respond=None):
    (b,) = coefs(coef_ref, (C_B,))
    _, _, has_ahead = place()
    keep = jnp.where(has_ahead, 1.0, 0.0).astype(jnp.float32)

    def got(i, out):
        return msg[i, out] if missing is None else msg[i, out] + missing[i, out]

    def work(r):
        here, _, _, out = spans(r)
        V[VX, 1, here] = V[VX, 1, here] + (keep * b) * got(0, out)
        G[0, out] = keep * (got(1, out) - b * S[XY, 1, here])
        G[1, out] = keep * (got(2, out) - b * S[XZ, 1, here])

    over_rows(R.shape[2], work)
    if step < unforced:
        add_force(G, (0,), force, (VY, 2), window)
        add_force(G, (1,), force, (VZ, 2), window)
    if respond is not None:
        respond()
    post(
        V, S, R, coef_ref, surface, 1, 2 * step + 1,
        lambda r: V[VX, 0, pl.ds(PAD + r, ROWS)],
        lambda r: G[0, pl.ds(r, ROWS)],
        lambda r: G[1, pl.ds(r, ROWS)],
    )


def behind_bond(V, S, R, coef_ref, force, surface, msg, missing, G, step, window, unforced=0, respond=None):
    (b,) = coefs(coef_ref, (C_B,))
    _, has_behind, _ = place()
    keep = jnp.where(has_behind, 1.0, 0.0).astype(jnp.float32)

    def got(i, out):
        return msg[i, out] if missing is None else msg[i, out] + missing[i, out]

    def work(r):
        here, _, _, out = spans(r)
        V[VY, 0, here] = V[VY, 0, here] - (keep * b) * got(0, out)
        V[VZ, 0, here] = V[VZ, 0, here] - (keep * b) * got(1, out)
        G[0, out] = keep * (got(2, out) + b * S[XX, 0, here])

    over_rows(R.shape[2], work)
    if step < unforced:
        add_force(G, (0,), force, (VX, 2), window)
    if respond is not None:
        respond()
    post(
        V, S, R, coef_ref, surface, 0, 2 * step,
        lambda r: G[0, pl.ds(r, ROWS)],
        lambda r: V[VY, 1, pl.ds(PAD + r, ROWS)],
        lambda r: V[VZ, 1, pl.ds(PAD + r, ROWS)],
    )


def start_kernel(
    velocity, stress, memory, layer_in, lam_in, mu_in, buoy_in, rate_in, defect_in, loads, steps_table,
    V, S, R, coef_ref, msg_near, msg_far, W, table, layer_ref, lam, mu, buoy, rate, defect, sems,
):
    across = velocity.shape[2]
    inside = pl.ds(PAD, across)
    pairs = [
        (layer_in, layer_ref), (lam_in, lam), (mu_in, mu), (buoy_in, buoy), (rate_in, rate), (defect_in, defect),
    ]
    pairs += [(stress.at[i], S.at[i, :, inside]) for i in range(6)]
    pairs += [(velocity.at[i], V.at[i, :, inside]) for i in range(3)]
    pairs += [(memory.at[i], R.at[i]) for i in range(6)]
    copies = [pltpu.make_async_copy(*pair, sems.at[i]) for i, pair in enumerate(pairs)]
    for copy in copies:
        copy.start()
    slots = loads.shape[0]
    zero_edges(V)
    zero_edges(S)
    zero_edges(W)
    table[...] = jnp.zeros(table.shape, jnp.float32)
    table[0:16, :] = steps_table[...]
    columns = table[...].T
    entry, cell = (jnp.broadcast_to(columns[0:slots, at : at + 1], loads.shape) for at in (0, 8))
    for copy in copies[:6]:
        copy.wait()
    layer = layer_ref[...]

    def per_depth(table):
        row = jnp.zeros(layer.shape, jnp.float32)
        for level in range(table.shape[0]):
            row = jnp.where(layer == level, table[level], row)
        return row

    lane = lax.broadcasted_iota(jnp.int32, layer.shape, 1)
    not_first = jnp.where(lane > 0, 1.0, 0.0).astype(jnp.float32)
    not_last = jnp.where(lane < layer.shape[1] - 1, 1.0, 0.0).astype(jnp.float32)
    b = DT * per_depth(buoy)
    two_mu = (2.0 * DT) * per_depth(mu)
    decay = DT * per_depth(rate)
    drop = 2.0 * decay * per_depth(defect)
    for row, value in (
        (C_B, b),
        (C_B0, b * not_first),
        (C_B1, b * not_last),
        (C_M0, not_first),
        (C_M1, not_last),
        (C_LAM, DT * per_depth(lam)),
        (C_MU2, two_mu),
        (C_MU, 0.5 * two_mu),
        (C_K1, 1.0 - decay),
        (C_K2, drop),
        (C_K2H, 0.5 * drop),
        (C_L0, DT * (1.0 - not_first)),
    ):
        coef_ref[row : row + 1, :] = value
    coef_ref[12:16, :] = jnp.zeros((4, layer.shape[1]), jnp.float32)
    for copy in copies[6:15]:
        copy.wait()
    even, _, _ = place()

    def send(side, near, far, early):
        to = msg_far.at[side]
        near(V, S, coef_ref, msg_near, None, 0)
        far(V, S, coef_ref, Planes(to, 0, across), None, 0)
        inner(V, S, coef_ref, None, 0)
        for i, block in enumerate((loads[...], entry, cell)):
            first_row = 6 * across + i * slots
            to[first_row : first_row + slots, :] = block
        for copy in copies[15:]:
            copy.wait()
        early(Planes(to, 3, across))

    @pl.when(even)
    def _():
        send(
            0, pre_ahead, pre_behind,
            lambda out: early_behind(V, S, R, coef_ref, None, 0, out, W, None, 0),
        )

    @pl.when(jnp.logical_not(even))
    def _():
        send(
            1, pre_behind, pre_ahead,
            lambda out: early_ahead(V, S, R, coef_ref, out, W, None, 0),
        )


def near_kernel(step, window, V0, S0, R0, coef_ref, force, surface, msg, V, S, R, *rest):
    G = rest[-1]
    if step == 0:
        for comp in range(3):
            for cell in range(2):
                add_force(V, (comp, cell), force, (0, comp, cell), PAD + window)
    even, _, _ = place()
    more = step < STEPS - 1

    @pl.when(even)
    def _():
        ahead_bond(V, S, R, coef_ref, force.at[step], surface, msg, None, G, step, window, 1)
        if more:
            pre_ahead(V, S, coef_ref, rest[0], force.at[step + 1], window)

    @pl.when(jnp.logical_not(even))
    def _():
        behind_bond(V, S, R, coef_ref, force.at[step], surface, msg, None, G, step, window, 1)
        if more:
            pre_behind(V, S, coef_ref, rest[0], force.at[step + 1], window)


def meet_kernel(across, msg, loads, load, rows_out):
    slots = loads.shape[0]
    rows, entry, cell = (msg[1, 6 * across + i * slots : 6 * across + (i + 1) * slots, :] for i in range(3))
    for slot in range(slots):
        rows = jnp.where(entry == float(slot), loads[slot : slot + 1, :], rows)
    rows_out[...] = jnp.zeros(rows_out.shape, jnp.float32)
    rows_out[0:1, :] = jnp.sum(jnp.where(cell == 0.0, rows, 0.0), axis=0, keepdims=True)
    load[...] = rows_out[...].T


def far_kernel(step, window, V0, S0, R0, coef_ref, force, surface, msg, *rest):
    rest = list(rest)
    other = rest.pop(0)
    V, S, R, D = rest[:4]
    early = rest[4] if step < STEPS - 2 else None
    across = R.shape[2]
    even, _, _ = place()
    here, then = force.at[step], force.at[step + 1]

    def got(side):
        return Planes(msg.at[side], 3 * step, across) if step < 2 else msg

    if step == 0:
        missing, load = None, other
        G, W, A = rest[-3:]
    else:
        missing = other
        G, W = rest[-2:]
    zero_edges(W)

    @pl.when(even)
    def _():
        if step == 0:
            respond = lambda: first_response_ahead(V, S, coef_ref, here, D, W, A, window)
        else:
            respond = lambda: response_ahead(V, S, coef_ref, D, W)
        behind_bond(
            V, S, R, coef_ref, here, surface, got(0), missing, G, step, window, 2, respond
        )
        pre_behind(V, S, coef_ref, None, then, window)

    @pl.when(jnp.logical_not(even))
    def _():
        if step == 0:
            respond = lambda: first_response_behind(V, S, coef_ref, here, load, D, W, A, window)
        else:
            respond = lambda: response_behind(V, S, coef_ref, D, W)
        ahead_bond(
            V, S, R, coef_ref, here, surface, got(1), missing, G, step, window, 2, respond
        )
        pre_ahead(V, S, coef_ref, None, then, window)

    inner(V, S, coef_ref, then, window)
    if early is not None:
        later = force.at[step + 2]

        @pl.when(even)
        def _():
            early_behind(V, S, R, coef_ref, surface, 2 * (step + 1), early, W, later, window)

        @pl.when(jnp.logical_not(even))
        def _():
            early_ahead(V, S, R, coef_ref, early, W, later, window)


def last_kernel(
    step, window, V0, S0, R0, coef_ref, force, surface, msg, missing, V, S, R, v_out, s_out, r_out, G, sems
):
    even, _, _ = place()
    here = force.at[step]
    inside = pl.ds(PAD, R.shape[2])

    def copies(cell):
        return [
            pltpu.make_async_copy(V.at[:, cell, inside], v_out.at[:, cell], sems.at[cell, 0]),
            pltpu.make_async_copy(S.at[:, cell, inside], s_out.at[:, cell], sems.at[cell, 1]),
            pltpu.make_async_copy(R.at[:, cell], r_out.at[:, cell], sems.at[cell, 2]),
        ]

    def finish(cell, bond):
        done, other = copies(1 - cell), copies(cell)
        for copy in done:
            copy.start()
        bond(V, S, R, coef_ref, here, surface, msg, missing, G, step, window)
        for copy in other:
            copy.start()
        for copy in done + other:
            copy.wait()

    @pl.when(even)
    def _():
        finish(0, behind_bond)

    @pl.when(jnp.logical_not(even))
    def _():
        finish(1, ahead_bond)


ENTRY_ROW, TRUCK_ROW = 48, 56
GROUP = 8


def pack_kernel(
    record, loads_in, entries_in, cells_in, piers_in, own, loads, steps_table, piers, entries, cells, sems
):
    panel = record.shape[1]
    slots, lanes = loads.shape
    steps = entries.shape[0]
    pairs = [(record, own.at[:, pl.ds(0, panel)]), (loads_in, loads), (entries_in, entries), (cells_in, cells)]
    pairs.append((piers_in, piers))
    copies = [pltpu.make_async_copy(*pair, sems.at[i]) for i, pair in enumerate(pairs)]
    for copy in copies:
        copy.start()
    own[:, panel:] = jnp.zeros((own.shape[0], own.shape[1] - panel), jnp.float32)
    steps_table[...] = jnp.zeros(steps_table.shape, jnp.float32)
    for copy in copies:
        copy.wait()
    steps_table[0:steps, 0:slots] = entries[...].astype(jnp.float32)
    steps_table[8 : 8 + steps, 0:slots] = cells[...].astype(jnp.float32)
    blocks = [loads[8 * i : 8 * i + 8, :] for i in range(slots // 8)] + [steps_table[0:8, :]]
    for i, block in enumerate(blocks):
        own[0:8, panel + i * lanes : panel + (i + 1) * lanes] = block


def lane_blocks(table, width):
    return sum(lane_roll(table[s : s + 1, :], s * width) for s in range(STEPS))


def split_kernel(panel, slots, own, behind, cells, after_this, out):
    del after_this
    tiles, _, lanes = out.shape
    pieces = panel // lanes
    third = pieces // 3
    cell_of = cells[...]
    me = lax.axis_index("line")
    group, mine = lax.div(me, tiles), lax.rem(me, tiles)
    piers = cell_of.shape[1]
    row = lax.broadcasted_iota(jnp.int32, (4 * tiles, lanes), 0)
    tile, j = lax.div(row, 4), lax.rem(row, 4)
    odd = lax.rem(tile, 2)
    first = (tile + group * tiles) * 2
    cell_x = first + jnp.where(j == 2, -1, jnp.where(j == 3, 4 * odd - 2, j))
    cell_yz = first + jnp.where(j == 3, 4 * odd - 1, j)
    record = jnp.where(group == 0, own[:, :panel], behind[:, :panel])

    def hits(cell):
        return [jnp.where(cell == cell_of[0:1, p : p + 1], 1.0, 0.0).astype(jnp.float32) for p in range(piers)]

    hit_x, hit_yz = hits(cell_x), hits(cell_yz)

    def share(m):
        hit = hit_x if m < third else hit_yz
        return sum(hit[p] * record[p : p + 1, m * lanes : (m + 1) * lanes] for p in range(piers))

    parts = [share(m) for m in range(pieces)]

    def trucks(source):
        blocks = [source[0:8, panel + i * lanes : panel + (i + 1) * lanes] for i in range(slots // 8 + 1)]
        return blocks[:-1], lane_blocks(blocks[-1], slots)

    own_rows, own_entry = trucks(own)
    far_rows, far_entry = trucks(behind)
    for tile in range(tiles):
        these = slice(4 * tile, 4 * tile + 4)
        for m in range(pieces):
            out[tile, 4 * m : 4 * m + 4, :] = parts[m][these, :]
        passed = mine < tile
        out[tile, ENTRY_ROW : ENTRY_ROW + 1, :] = jnp.where(passed, own_entry, far_entry)
        for i in range(slots // 8):
            at = TRUCK_ROW + 8 * i
            out[tile, at : at + 8, :] = jnp.where(passed, own_rows[i], far_rows[i])


def prepare_kernel(parts, loads, steps_table, after_this, force, surface, table, rows_out):
    del after_this
    steps, comps, width = force.shape[:3]
    lanes = parts.shape[2]
    force[...] = jnp.zeros(force.shape, jnp.float32)
    per = ENTRY_ROW // (comps * width)
    lane = lax.broadcasted_iota(jnp.int32, (per, lanes), 1)
    scale = jnp.where(lane < FZ, DT, 0.0).astype(jnp.float32)
    for s in range(steps):
        for comp in range(comps):
            for cell in range(width):
                panel = parts[s, pl.ds(comp * per * width + cell, per, stride=width), :]
                force[s, comp, cell, pl.ds(4, per, stride=2), :] = scale * panel
                force[s, comp, cell, pl.ds(5, per, stride=2), :] = scale * lane_roll(panel, FZ)

    slots = loads.shape[0]
    tiles = parts.shape[0]
    mine = lax.rem(lax.axis_index("line"), tiles)
    table[...] = jnp.zeros(table.shape, jnp.float32)
    table[0:1, :] = lane_blocks(steps_table[0:8, :], slots)
    table[STEPS + 1 : STEPS + 2, :] = lane_blocks(steps_table[8:16, :], slots)
    rows = [loads[...]]
    for k in range(1, STEPS + 1):
        source = lax.rem(mine + (tiles - k), tiles)
        rows.append(parts[source, TRUCK_ROW : TRUCK_ROW + slots, :])
        table[k : k + 1, :] = parts[source, ENTRY_ROW : ENTRY_ROW + 1, :]
    columns = table[...].T
    rows_out[...] = jnp.zeros(rows_out.shape, jnp.float32)
    for s in range(STEPS):
        block = slice(s * slots, (s + 1) * slots)
        moved = []
        for k in range(STEPS - s):
            entry = jnp.broadcast_to(columns[block, k : k + 1], rows[k].shape)
            new = rows[k]
            for slot in range(slots):
                new = jnp.where(entry == float(slot), rows[k + 1][slot : slot + 1, :], new)
            moved.append(new)
        rows = moved
        cell = jnp.broadcast_to(columns[block, STEPS + 1 : STEPS + 2], rows[0].shape)
        for c in range(2):
            load = jnp.sum(jnp.where(cell == float(c), rows[0], 0.0), axis=0, keepdims=True)
            rows_out[2 * s + c : 2 * s + c + 1, :] = load
    surface[...] = rows_out[...].T


def in_vmem(x):
    return pltpu.with_memory_space_constraint(x, pltpu.VMEM)


WHOLE = pl.BlockSpec(memory_space=pltpu.VMEM)
SCALARS = pl.BlockSpec(memory_space=pltpu.SMEM)
ANYWHERE = pl.BlockSpec(memory_space=pl.ANY)


def call(kernel, ins, specs, outs, out_specs, scratch=(), aliases=None, name=None, cost=1):
    return pl.pallas_call(
        kernel,
        out_shape=outs,
        in_specs=specs,
        out_specs=out_specs,
        scratch_shapes=list(scratch),
        input_output_aliases=aliases or {},
        compiler_params=pltpu.CompilerParams(vmem_limit_bytes=VMEM_LIMIT),
        cost_estimate=pl.CostEstimate(flops=cost, bytes_accessed=cost, transcendentals=0),
        name=name,
    )(*ins)


def body(
    velocity, stress, memory, truck_loads, pier_panels,
    lame_lambda, lame_mu, buoyancy, relax_rate, defect_mu, layer,
    truck_entry, truck_cell, pier_cell,
):
    tiles = lax.axis_size("line")
    width_x, across, depth = velocity.shape[1:]
    slots = truck_loads.shape[0]
    window = (across - FY) // 2 - 4
    f32 = jnp.float32

    near = [(i, i ^ 1) for i in range(tiles) if (i ^ 1) < tiles]
    far = [(i, i + 1) for i in range(1, tiles - 1, 2)] + [(i + 1, i) for i in range(1, tiles - 1, 2)]

    padded = across + 2 * PAD
    v_type = pltpu.VMEM((3, width_x, padded, depth), f32)
    s_type = pltpu.VMEM((6, width_x, padded, depth), f32)
    r_type = pltpu.VMEM((6, width_x, across, depth), f32)
    c_type = pltpu.VMEM((N_COEF, depth), f32)
    m_type = pltpu.VMEM((3, across, depth), f32)
    ghost = pltpu.VMEM((2, across, depth), f32)
    work = pltpu.VMEM((2, padded, depth), f32)
    square = pltpu.VMEM((across, depth), f32)

    def ahead_by(x, distance):
        return lax.ppermute(x, "line", [(i, i + distance) for i in range(tiles - distance)])

    def in_hbm(*arrays):
        return tuple(pltpu.with_memory_space_constraint(x, pltpu.HBM) for x in arrays)

    dma = pltpu.SemaphoreType.DMA
    piers, panel = pier_panels.shape[1:]
    own, loads, steps_table, pier_row = call(
        pack_kernel,
        in_hbm(pier_panels[0], truck_loads, truck_entry, truck_cell, pier_cell[None, :]),
        (ANYWHERE,) * 5,
        (
            pltpu.VMEM((piers, panel + (slots // 8 + 1) * depth), f32),
            pltpu.VMEM((slots, depth), f32),
            pltpu.VMEM((16, depth), f32),
            pltpu.VMEM((1, piers), jnp.int32),
        ),
        (WHOLE,) * 4,
        scratch=(pltpu.VMEM(truck_entry.shape, jnp.int32), pltpu.VMEM(truck_cell.shape, jnp.int32), dma((5,))),
        name="pack",
    )
    behind = ahead_by(own, GROUP)
    reach = 2 * GROUP
    index = lax.axis_index("line")
    while reach < tiles:
        record = jnp.where(index < GROUP, own, behind)[:, :panel]
        record = jnp.where(index < reach, record, ahead_by(record, reach))
        behind = jnp.concatenate([record, behind[:, panel:]], axis=1)
        reach *= 2
    tables = (lame_lambda, lame_mu, buoyancy, relax_rate, defect_mu)
    V, S, R, coef, msg_near, msg_far = call(
        start_kernel,
        in_hbm(velocity, stress, memory, layer[None, :], *tables) + (in_vmem(loads), in_vmem(steps_table)),
        (ANYWHERE,) * 9 + (WHOLE,) * 2,
        (v_type, s_type, r_type, c_type, m_type, pltpu.VMEM((2, 6 * across + 3 * slots, depth), f32)),
        (WHOLE,) * 6,
        scratch=(
            work, pltpu.VMEM((depth, depth), f32), pltpu.VMEM((1, depth), jnp.int32),
            *(pltpu.SMEM(table.shape, f32) for table in tables), dma((21,)),
        ),
        name="start",
        cost=8 * 1024 * 1024,
    )
    pairs = [[i, (i + 1) % tiles] for i in range(1, tiles, 2)]
    msg_far = lax.all_to_all(msg_far, "line", 0, 0, axis_index_groups=pairs, tiled=True)
    msg_near = lax.ppermute(msg_near, "line", near)
    parts = call(
        functools.partial(split_kernel, panel, slots),
        (own, behind, in_vmem(pier_row), coef),
        (WHOLE,) * 3 + (ANYWHERE,),
        jax.ShapeDtypeStruct((GROUP, TRUCK_ROW + slots, depth), f32),
        WHOLE,
        name="split",
    )
    groups = [list(range(at, at + GROUP)) for at in range(0, tiles, GROUP)]
    parts = lax.all_to_all(parts, "line", 0, 0, axis_index_groups=groups, tiled=True)
    load = call(
        functools.partial(meet_kernel, across),
        (in_vmem(msg_far), in_vmem(loads)),
        (WHOLE,) * 2,
        square,
        WHOLE,
        scratch=(pltpu.VMEM((depth, across), f32),),
        name="meet",
        cost=64 * 1024 * 1024,
    )
    force, surface = call(
        prepare_kernel,
        (parts, in_vmem(loads), in_vmem(steps_table), load),
        (WHOLE,) * 3 + (ANYWHERE,),
        (pltpu.VMEM((STEPS, 3, 4, 16, depth), f32), pltpu.VMEM((across, depth), f32)),
        (WHOLE,) * 2,
        scratch=(pltpu.VMEM((depth, depth), f32), pltpu.VMEM((depth, across), f32)),
        name="prepare",
    )
    state = (v_type, s_type, r_type)
    same = {0: 0, 1: 1, 2: 2}
    missing = None
    for step in range(STEPS):
        more = step < STEPS - 1
        ins = tuple(in_vmem(x) for x in (V, S, R, coef, force, surface, msg_near))
        outs = state + ((m_type,) if more else ())
        V, S, R, *msg = call(
            functools.partial(near_kernel, step, window),
            ins,
            (WHOLE,) * len(ins),
            outs,
            (WHOLE,) * len(outs),
            scratch=(ghost,),
            aliases=same,
            name="near" + str(step),
        )
        if more:
            msg_near = lax.ppermute(msg[0], "line", near)
        ins = (V, S, R, coef, force, surface, msg_far, missing if step else load)
        ins = tuple(in_vmem(x) for x in ins)
        if more:
            outs = state + (m_type,) + ((m_type,) if step < STEPS - 2 else ())
            V, S, R, missing, *msg = call(
                functools.partial(far_kernel, step, window),
                ins,
                (WHOLE,) * len(ins),
                outs,
                (WHOLE,) * len(outs),
                scratch=(ghost, work) + (() if step else (pltpu.VMEM((5, padded, depth), f32),)),
                aliases=same,
                name="far" + str(step),
            )
            if step > 0:
                msg_far = early
            if msg:
                early = lax.ppermute(msg[0], "line", far)
    results = call(
        functools.partial(last_kernel, STEPS - 1, window),
        ins,
        (WHOLE,) * len(ins),
        state + tuple(jax.ShapeDtypeStruct(x.shape, f32) for x in (velocity, stress, memory)),
        (WHOLE,) * 3 + (ANYWHERE,) * 3,
        scratch=(ghost, pltpu.SemaphoreType.DMA((2, 3))),
        aliases=same,
        name="last",
    )
    return results[3:]


def solution(mesh):
    placed = (
        P(None, ("runs", "line"), None, None),
        P(None, ("runs", "line"), None, None),
        P(None, ("runs", "line"), None, None),
        P(("runs", "line"), None),
        P("line", "runs", None),
        P(),
        P(),
        P(),
        P(),
        P(),
        P(),
        P(None, ("runs", "line")),
        P(None, ("runs", "line")),
        P(),
    )
    return jax.shard_map(
        body,
        mesh=mesh,
        in_specs=placed,
        out_specs=(
            P(None, ("runs", "line"), None, None),
            P(None, ("runs", "line"), None, None),
            P(None, ("runs", "line"), None, None),
        ),
        check_vma=False,
    )
```

```python
import functools

import jax
import jax.numpy as jnp
import numpy as np
from jax import lax
from jax.experimental import pallas as pl
from jax.experimental.pallas import tpu as pltpu
from jax.sharding import PartitionSpec as P

STEPS = 6
FY = 8
FZ = 64
DT = 0.25
PAD = 8
ROWS = 16
UNROLL = 8
VMEM_LIMIT = 32 * 1024 * 1024

C_B, C_B0, C_B1, C_M0, C_M1, C_LAM, C_MU2, C_MU, C_K1, C_K2, C_K2H, C_L0 = range(12)
N_COEF = 16

VX, VY, VZ = range(3)
XX, YY, ZZ, XY, XZ, YZ = range(6)


def lane_roll(x, shift):
    return pltpu.roll(x, shift % x.shape[-1], x.ndim - 1)


def before(x):
    return lane_roll(x, 1)


def after(x):
    return lane_roll(x, -1)


def over_rows(count, work):
    def step(i, carry):
        work(pl.multiple_of(i * ROWS, ROWS))
        return carry

    lax.fori_loop(0, count // ROWS, step, 0, unroll=UNROLL)


class Planes:
    def __init__(self, ref, first, across):
        self.ref, self.first, self.shape = ref, first, (3, across, ref.shape[1])

    def rows(self, at):
        plane, out = at
        return pl.ds((self.first + plane) * self.shape[1] + out.start, out.size)

    def __getitem__(self, at):
        return self.ref[self.rows(at)]

    def __setitem__(self, at, value):
        self.ref[self.rows(at)] = value


def coefs(coef_ref, ids):
    return [coef_ref[i : i + 1, :] for i in ids]


def place():
    index = lax.axis_index("line")
    return lax.rem(index, 2) == 0, index > 0, index < lax.axis_size("line") - 1


def spans(r):
    return pl.ds(PAD + r, ROWS), pl.ds(PAD + r - 1, ROWS), pl.ds(PAD + r + 1, ROWS), pl.ds(r, ROWS)


def zero_edges(ref):
    across = ref.shape[-2] - 2 * PAD
    edge = jnp.zeros((PAD, ref.shape[-1]), jnp.float32)
    for where in np.ndindex(*ref.shape[:-2]):
        ref[(*where, pl.ds(0, PAD))] = edge
        ref[(*where, pl.ds(PAD + across, PAD))] = edge


def add_force(ref, index, force, which, first_row):
    rows = pl.ds(first_row, 16)
    ref[(*index, rows)] = ref[(*index, rows)] + force[which]


def pre_ahead(V, S, coef_ref, msg, force, window):
    b, b0 = coefs(coef_ref, (C_B, C_B0))

    def work(r):
        here, up, _, out = spans(r)
        sxy, sxz = S[XY, 1, here], S[XZ, 1, here]
        px = V[VX, 1, here] + b * (sxy - S[XY, 1, up] + sxz - S[XX, 1, here]) - b0 * before(sxz)
        V[VX, 1, here] = px
        if msg is not None:
            msg[0, out] = sxy
            msg[1, out] = sxz
            msg[2, out] = px

    over_rows(V.shape[2] - 2 * PAD, work)
    if force is not None:
        add_force(V, (VX, 1), force, (VX, 1), PAD + window)
        if msg is not None:
            add_force(msg, (2,), force, (VX, 1), window)


def pre_behind(V, S, coef_ref, msg, force, window):
    b, b0, b1 = coefs(coef_ref, (C_B, C_B0, C_B1))

    def work(r):
        here, up, down, out = spans(r)
        syz, szz = S[YZ, 0, here], S[ZZ, 0, here]
        qy = V[VY, 0, here] + b * (S[XY, 0, here] + S[YY, 0, down] - S[YY, 0, here] + syz) - b0 * before(syz)
        qz = V[VZ, 0, here] + b * (S[XZ, 0, here] + syz - S[YZ, 0, up] - szz) + b1 * after(szz)
        V[VY, 0, here] = qy
        V[VZ, 0, here] = qz
        if msg is not None:
            msg[0, out] = S[XX, 0, here]
            msg[1, out] = qy
            msg[2, out] = qz

    over_rows(V.shape[2] - 2 * PAD, work)
    if force is not None:
        add_force(V, (VY, 0), force, (VY, 0), PAD + window)
        add_force(V, (VZ, 0), force, (VZ, 0), PAD + window)
        if msg is not None:
            add_force(msg, (1,), force, (VY, 0), window)
            add_force(msg, (2,), force, (VZ, 0), window)


def inner(V, S, coef_ref, force, window):
    b, b0, b1 = coefs(coef_ref, (C_B, C_B0, C_B1))

    def work(r):
        here, up, down, _ = spans(r)
        sxy, sxz = S[XY, 0, here], S[XZ, 0, here]
        V[VX, 0, here] = (
            V[VX, 0, here]
            + b * (S[XX, 1, here] - S[XX, 0, here] + sxy - S[XY, 0, up] + sxz)
            - b0 * before(sxz)
        )
        syz, szz = S[YZ, 1, here], S[ZZ, 1, here]
        V[VY, 1, here] = (
            V[VY, 1, here]
            + b * (S[XY, 1, here] - sxy + S[YY, 1, down] - S[YY, 1, here] + syz)
            - b0 * before(syz)
        )
        V[VZ, 1, here] = (
            V[VZ, 1, here]
            + b * (S[XZ, 1, here] - sxz + syz - S[YZ, 1, up] - szz)
            + b1 * after(szz)
        )

    over_rows(V.shape[2] - 2 * PAD, work)
    if force is not None:
        add_force(V, (VX, 0), force, (VX, 0), PAD + window)
        add_force(V, (VY, 1), force, (VY, 1), PAD + window)
        add_force(V, (VZ, 1), force, (VZ, 1), PAD + window)


def post(V, S, R, coef_ref, surface, cell, column, behind_x, ahead_y, ahead_z):
    m0, m1, lam, mu2, mu, k1, k2, k2h, l0 = coefs(
        coef_ref, (C_M0, C_M1, C_LAM, C_MU2, C_MU, C_K1, C_K2, C_K2H, C_L0)
    )

    def work(r):
        here, up, down, out = spans(r)
        vx, vy, vz = V[VX, cell, here], V[VY, cell, here], V[VZ, cell, here]
        exx = vx - behind_x(r)
        eyy = vy - V[VY, cell, up]
        ezz = vz - m0 * before(vz)
        exy = V[VX, cell, down] - vx + (ahead_y(r) - vy)
        exz = m1 * after(vx) - vx + (ahead_z(r) - vz)
        eyz = m1 * after(vy) - vy + (V[VZ, cell, down] - vz)
        volume = lam * (exx + eyy + ezz)
        for comp, e in ((XX, exx), (YY, eyy), (ZZ, ezz)):
            old = R[comp, cell, out]
            new = S[comp, cell, here] + (volume + mu2 * e) + DT * old
            if comp == ZZ:
                new = new + l0 * lane_roll(surface[out, :], -column)
            S[comp, cell, here] = new
            R[comp, cell, out] = k1 * old - k2 * e
        for comp, e in ((XY, exy), (XZ, exz), (YZ, eyz)):
            old = R[comp, cell, out]
            S[comp, cell, here] = S[comp, cell, here] + mu * e + DT * old
            R[comp, cell, out] = k1 * old - k2h * e

    over_rows(R.shape[2], work)


def response_behind(V, S, coef_ref, D, W):
    b, b0, b1, m0, m1, lam, mu2, mu = coefs(coef_ref, (C_B, C_B0, C_B1, C_M0, C_M1, C_LAM, C_MU2, C_MU))

    def work(r):
        here, up, down, out = spans(r)
        sxy = S[XY, 1, here]
        vy, vz = -b * sxy, -b * S[XZ, 1, here]
        exx = -V[VX, 1, here]
        eyy = b * (S[XY, 1, up] - sxy)
        ezz = vz - m0 * before(vz)
        volume = lam * (exx + eyy + ezz)
        dyy, dzz = volume + mu2 * eyy, volume + mu2 * ezz
        dyz = mu * (m1 * after(vy) - vy - b * S[XZ, 1, down] - vz)
        W[0, here] = dyy
        W[1, here] = dyz
        D[0, out] = volume + mu2 * exx
        D[1, out] = vy + b * (dyz - mu * vy - dyy) - b0 * before(dyz)
        D[2, out] = vz + b * (dyz - mu * vz - dzz) + b1 * after(dzz)

    over_rows(D.shape[1], work)

    def rest(r):
        _, up, down, out = spans(r)
        D[1, out] = D[1, out] + b * W[0, down]
        D[2, out] = D[2, out] - b * W[1, up]

    over_rows(D.shape[1], rest)


def response_ahead(V, S, coef_ref, D, W):
    b, b0, m1, lam, mu2, mu = coefs(coef_ref, (C_B, C_B0, C_M1, C_LAM, C_MU2, C_MU))

    def work(r):
        here, _, down, out = spans(r)
        vx = b * S[XX, 0, here]
        dxy = mu * (b * S[XX, 0, down] - vx + V[VY, 0, here])
        dxz = mu * (m1 * after(vx) - vx + V[VZ, 0, here])
        W[0, here] = dxy
        D[0, out] = dxy
        D[1, out] = dxz
        D[2, out] = vx + b * (dxy + dxz - (lam + mu2) * vx) - b0 * before(dxz)

    over_rows(D.shape[1], work)

    def rest(r):
        _, up, _, out = spans(r)
        D[2, out] = D[2, out] - b * W[0, up]

    over_rows(D.shape[1], rest)


def first_response_behind(V, S, coef_ref, force, load, D, W, A, window):
    b, b0, b1, m0, m1, lam, mu2, mu, l0 = coefs(
        coef_ref, (C_B, C_B0, C_B1, C_M0, C_M1, C_LAM, C_MU2, C_MU, C_L0)
    )
    A[...] = jnp.zeros(A.shape, jnp.float32)

    def given(r):
        here, _, _, _ = spans(r)
        A[1, here] = -b * S[XY, 1, here]
        A[2, here] = -b * S[XZ, 1, here]

    over_rows(D.shape[1], given)
    for i, which in enumerate(((VX, 3), (VY, 2), (VZ, 2), (VY, 3), (VZ, 3))):
        add_force(A, (i,), force, which, PAD + window)

    def work(r):
        here, up, down, out = spans(r)
        vx, vy, vz = A[0, here], A[1, here], A[2, here]
        exx = vx - V[VX, 1, here]
        eyy = vy - A[1, up]
        ezz = vz - m0 * before(vz)
        volume = lam * (exx + eyy + ezz)
        dyy = volume + mu2 * eyy
        dzz = volume + mu2 * ezz + l0 * load[out, :]
        dxy = mu * (A[0, down] - vx + (A[3, here] - vy))
        dxz = mu * (m1 * after(vx) - vx + (A[4, here] - vz))
        dyz = mu * (m1 * after(vy) - vy + (A[2, down] - vz))
        W[0, here] = dyy
        W[1, here] = dyz
        D[0, out] = volume + mu2 * exx
        D[1, out] = vy + b * (dxy - dyy + dyz) - b0 * before(dyz)
        D[2, out] = vz + b * (dxz + dyz - dzz) + b1 * after(dzz)

    over_rows(D.shape[1], work)

    def rest(r):
        _, up, down, out = spans(r)
        D[1, out] = D[1, out] + b * W[0, down]
        D[2, out] = D[2, out] - b * W[1, up]

    over_rows(D.shape[1], rest)


def first_response_ahead(V, S, coef_ref, force, D, W, A, window):
    b, b0, m0, m1, lam, mu2, mu = coefs(coef_ref, (C_B, C_B0, C_M0, C_M1, C_LAM, C_MU2, C_MU))
    A[...] = jnp.zeros(A.shape, jnp.float32)

    def given(r):
        here, _, _, _ = spans(r)
        A[0, here] = b * S[XX, 0, here]

    over_rows(D.shape[1], given)
    for i, which in enumerate(((VX, 2), (VY, 3), (VZ, 3), (VX, 3))):
        add_force(A, (i,), force, which, PAD + window)

    def work(r):
        here, up, down, out = spans(r)
        vx, vy, vz = A[0, here], A[1, here], A[2, here]
        exx = vx - A[3, here]
        dxx = lam * (exx + (vy - A[1, up]) + (vz - m0 * before(vz))) + mu2 * exx
        dxy = mu * (A[0, down] - vx + (V[VY, 0, here] - vy))
        dxz = mu * (m1 * after(vx) - vx + (V[VZ, 0, here] - vz))
        W[0, here] = dxy
        D[0, out] = dxy
        D[1, out] = dxz
        D[2, out] = vx + b * (dxy + dxz - dxx) - b0 * before(dxz)

    over_rows(D.shape[1], work)

    def rest(r):
        _, up, _, out = spans(r)
        D[2, out] = D[2, out] - b * W[0, up]

    over_rows(D.shape[1], rest)


def early_ahead(V, S, R, coef_ref, msg, W, force, window):
    b, b0, m0, m1, lam, mu2, mu = coefs(coef_ref, (C_B, C_B0, C_M0, C_M1, C_LAM, C_MU2, C_MU))

    def work(r):
        here, up, down, out = spans(r)
        vx, vy, vz = V[VX, 1, here], V[VY, 1, here], V[VZ, 1, here]
        exx = vx - V[VX, 0, here]
        volume = lam * (exx + (vy - V[VY, 1, up]) + (vz - m0 * before(vz)))
        sxx = S[XX, 1, here] + (volume + mu2 * exx) + DT * R[XX, 1, out]
        sxy = S[XY, 1, here] + mu * (V[VX, 1, down] - vx - vy) + DT * R[XY, 1, out]
        sxz = S[XZ, 1, here] + mu * (m1 * after(vx) - vx - vz) + DT * R[XZ, 1, out]
        W[0, here] = sxy
        msg[0, out] = sxy
        msg[1, out] = sxz
        msg[2, out] = vx + b * (sxy + sxz - sxx) - b0 * before(sxz)

    over_rows(msg.shape[1], work)

    def rest(r):
        _, up, _, out = spans(r)
        msg[2, out] = msg[2, out] - b * W[0, up]

    over_rows(msg.shape[1], rest)
    if force is not None:
        add_force(msg, (2,), force, (VX, 1), window)


def early_behind(V, S, R, coef_ref, surface, column, msg, W, force, window):
    b, b0, b1, m0, m1, lam, mu2, mu, l0 = coefs(
        coef_ref, (C_B, C_B0, C_B1, C_M0, C_M1, C_LAM, C_MU2, C_MU, C_L0)
    )

    def work(r):
        here, up, down, out = spans(r)
        vx, vy, vz = V[VX, 0, here], V[VY, 0, here], V[VZ, 0, here]
        eyy = vy - V[VY, 0, up]
        ezz = vz - m0 * before(vz)
        volume = lam * (vx + eyy + ezz)
        sxx = S[XX, 0, here] + (volume + mu2 * vx) + DT * R[XX, 0, out]
        syy = S[YY, 0, here] + (volume + mu2 * eyy) + DT * R[YY, 0, out]
        szz = S[ZZ, 0, here] + (volume + mu2 * ezz) + DT * R[ZZ, 0, out]
        if surface is not None:
            szz = szz + l0 * lane_roll(surface[out, :], -column)
        sxy = S[XY, 0, here] + mu * (V[VX, 0, down] - vx + (V[VY, 1, here] - vy)) + DT * R[XY, 0, out]
        sxz = S[XZ, 0, here] + mu * (m1 * after(vx) - vx + (V[VZ, 1, here] - vz)) + DT * R[XZ, 0, out]
        syz = S[YZ, 0, here] + mu * (m1 * after(vy) - vy + (V[VZ, 0, down] - vz)) + DT * R[YZ, 0, out]
        W[0, here] = syy
        W[1, here] = syz
        msg[0, out] = sxx
        msg[1, out] = vy + b * (sxy - syy + syz) - b0 * before(syz)
        msg[2, out] = vz + b * (sxz + syz - szz) + b1 * after(szz)

    over_rows(msg.shape[1], work)

    def rest(r):
        _, up, down, out = spans(r)
        msg[1, out] = msg[1, out] + b * W[0, down]
        msg[2, out] = msg[2, out] - b * W[1, up]

    over_rows(msg.shape[1], rest)
    if force is not None:
        add_force(msg, (1,), force, (VY, 0), window)
        add_force(msg, (2,), force, (VZ, 0), window)


def ahead_bond(V, S, R, coef_ref, force, surface, msg, missing, G, step, window, unforced=0, respond=None):
    (b,) = coefs(coef_ref, (C_B,))
    _, _, has_ahead = place()
    keep = jnp.where(has_ahead, 1.0, 0.0).astype(jnp.float32)

    def got(i, out):
        return msg[i, out] if missing is None else msg[i, out] + missing[i, out]

    def work(r):
        here, _, _, out = spans(r)
        V[VX, 1, here] = V[VX, 1, here] + (keep * b) * got(0, out)
        G[0, out] = keep * (got(1, out) - b * S[XY, 1, here])
        G[1, out] = keep * (got(2, out) - b * S[XZ, 1, here])

    over_rows(R.shape[2], work)
    if step < unforced:
        add_force(G, (0,), force, (VY, 2), window)
        add_force(G, (1,), force, (VZ, 2), window)
    if respond is not None:
        respond()
    post(
        V, S, R, coef_ref, surface, 1, 2 * step + 1,
        lambda r: V[VX, 0, pl.ds(PAD + r, ROWS)],
        lambda r: G[0, pl.ds(r, ROWS)],
        lambda r: G[1, pl.ds(r, ROWS)],
    )


def behind_bond(V, S, R, coef_ref, force, surface, msg, missing, G, step, window, unforced=0, respond=None):
    (b,) = coefs(coef_ref, (C_B,))
    _, has_behind, _ = place()
    keep = jnp.where(has_behind, 1.0, 0.0).astype(jnp.float32)

    def got(i, out):
        return msg[i, out] if missing is None else msg[i, out] + missing[i, out]

    def work(r):
        here, _, _, out = spans(r)
        V[VY, 0, here] = V[VY, 0, here] - (keep * b) * got(0, out)
        V[VZ, 0, here] = V[VZ, 0, here] - (keep * b) * got(1, out)
        G[0, out] = keep * (got(2, out) + b * S[XX, 0, here])

    over_rows(R.shape[2], work)
    if step < unforced:
        add_force(G, (0,), force, (VX, 2), window)
    if respond is not None:
        respond()
    post(
        V, S, R, coef_ref, surface, 0, 2 * step,
        lambda r: G[0, pl.ds(r, ROWS)],
        lambda r: V[VY, 1, pl.ds(PAD + r, ROWS)],
        lambda r: V[VZ, 1, pl.ds(PAD + r, ROWS)],
    )


def start_kernel(
    velocity, stress, memory, layer_in, lam_in, mu_in, buoy_in, rate_in, defect_in, loads, steps_table,
    V, S, R, coef_ref, msg_near, msg_far, msg_early, W, table, layer_ref, lam, mu, buoy, rate, defect, sems,
):
    across = velocity.shape[2]
    inside = pl.ds(PAD, across)
    pairs = [
        (layer_in, layer_ref), (lam_in, lam), (mu_in, mu), (buoy_in, buoy), (rate_in, rate), (defect_in, defect),
    ]
    pairs += [(stress.at[i], S.at[i, :, inside]) for i in range(6)]
    pairs += [(velocity.at[i], V.at[i, :, inside]) for i in range(3)]
    pairs += [(memory.at[i], R.at[i]) for i in range(6)]
    copies = [pltpu.make_async_copy(*pair, sems.at[i]) for i, pair in enumerate(pairs)]
    for copy in copies:
        copy.start()
    slots = loads.shape[0]
    zero_edges(V)
    zero_edges(S)
    zero_edges(W)
    table[...] = jnp.zeros(table.shape, jnp.float32)
    table[0:16, :] = steps_table[...]
    columns = table[...].T
    trucks = 3 * across
    msg_far[trucks : trucks + slots, :] = loads[...]
    for i, at in enumerate((0, 8)):
        first_row = trucks + (1 + i) * slots
        column = columns[0:slots, at : at + 1]
        msg_far[first_row : first_row + slots, :] = jnp.broadcast_to(column, loads.shape)
    for copy in copies[:6]:
        copy.wait()
    layer = layer_ref[...]

    def per_depth(table):
        row = jnp.zeros(layer.shape, jnp.float32)
        for level in range(table.shape[0]):
            row = jnp.where(layer == level, table[level], row)
        return row

    lane = lax.broadcasted_iota(jnp.int32, layer.shape, 1)
    not_first = jnp.where(lane > 0, 1.0, 0.0).astype(jnp.float32)
    not_last = jnp.where(lane < layer.shape[1] - 1, 1.0, 0.0).astype(jnp.float32)
    b = DT * per_depth(buoy)
    two_mu = (2.0 * DT) * per_depth(mu)
    decay = DT * per_depth(rate)
    drop = 2.0 * decay * per_depth(defect)
    for row, value in (
        (C_B, b),
        (C_B0, b * not_first),
        (C_B1, b * not_last),
        (C_M0, not_first),
        (C_M1, not_last),
        (C_LAM, DT * per_depth(lam)),
        (C_MU2, two_mu),
        (C_MU, 0.5 * two_mu),
        (C_K1, 1.0 - decay),
        (C_K2, drop),
        (C_K2H, 0.5 * drop),
        (C_L0, DT * (1.0 - not_first)),
    ):
        coef_ref[row : row + 1, :] = value
    coef_ref[12:16, :] = jnp.zeros((4, layer.shape[1]), jnp.float32)
    for copy in copies[6:15]:
        copy.wait()
    even, _, _ = place()
    now = Planes(msg_far, 0, across)

    @pl.when(even)
    def _():
        pre_ahead(V, S, coef_ref, msg_near, None, 0)
        pre_behind(V, S, coef_ref, now, None, 0)

    @pl.when(jnp.logical_not(even))
    def _():
        pre_behind(V, S, coef_ref, msg_near, None, 0)
        pre_ahead(V, S, coef_ref, now, None, 0)

    inner(V, S, coef_ref, None, 0)
    for copy in copies[15:]:
        copy.wait()

    @pl.when(even)
    def _():
        early_behind(V, S, R, coef_ref, None, 0, msg_early, W, None, 0)

    @pl.when(jnp.logical_not(even))
    def _():
        early_ahead(V, S, R, coef_ref, msg_early, W, None, 0)


def near_kernel(step, window, V0, S0, R0, coef_ref, force, surface, msg, V, S, R, *rest):
    G = rest[-1]
    if step == 0:
        for comp in range(3):
            for cell in range(2):
                add_force(V, (comp, cell), force, (0, comp, cell), PAD + window)
    even, _, _ = place()
    more = step < STEPS - 1

    @pl.when(even)
    def _():
        ahead_bond(V, S, R, coef_ref, force.at[step], surface, msg, None, G, step, window, 1)
        if more:
            pre_ahead(V, S, coef_ref, rest[0], force.at[step + 1], window)

    @pl.when(jnp.logical_not(even))
    def _():
        behind_bond(V, S, R, coef_ref, force.at[step], surface, msg, None, G, step, window, 1)
        if more:
            pre_behind(V, S, coef_ref, rest[0], force.at[step + 1], window)


def meet_kernel(across, msg, loads, load, rows_out):
    slots = loads.shape[0]
    rows, entry, cell = (msg[3 * across + i * slots : 3 * across + (i + 1) * slots, :] for i in range(3))
    for slot in range(slots):
        rows = jnp.where(entry == float(slot), loads[slot : slot + 1, :], rows)
    rows_out[...] = jnp.zeros(rows_out.shape, jnp.float32)
    rows_out[0:1, :] = jnp.sum(jnp.where(cell == 0.0, rows, 0.0), axis=0, keepdims=True)
    load[...] = rows_out[...].T


def far_kernel(step, window, V0, S0, R0, coef_ref, force, surface, msg, *rest):
    rest = list(rest)
    other = rest.pop(0)
    V, S, R, D = rest[:4]
    early = rest[4] if step < STEPS - 2 else None
    across = R.shape[2]
    even, _, _ = place()
    here, then = force.at[step], force.at[step + 1]
    got = Planes(msg, 0, across) if step == 0 else msg
    if step == 0:
        missing, load = None, other
        G, W, A = rest[-3:]
    else:
        missing = other
        G, W = rest[-2:]
    zero_edges(W)

    @pl.when(even)
    def _():
        if step == 0:
            respond = lambda: first_response_ahead(V, S, coef_ref, here, D, W, A, window)
        else:
            respond = lambda: response_ahead(V, S, coef_ref, D, W)
        behind_bond(
            V, S, R, coef_ref, here, surface, got, missing, G, step, window, 2, respond
        )
        pre_behind(V, S, coef_ref, None, then, window)

    @pl.when(jnp.logical_not(even))
    def _():
        if step == 0:
            respond = lambda: first_response_behind(V, S, coef_ref, here, load, D, W, A, window)
        else:
            respond = lambda: response_behind(V, S, coef_ref, D, W)
        ahead_bond(
            V, S, R, coef_ref, here, surface, got, missing, G, step, window, 2, respond
        )
        pre_ahead(V, S, coef_ref, None, then, window)

    inner(V, S, coef_ref, then, window)
    if early is not None:
        later = force.at[step + 2]

        @pl.when(even)
        def _():
            early_behind(V, S, R, coef_ref, surface, 2 * (step + 1), early, W, later, window)

        @pl.when(jnp.logical_not(even))
        def _():
            early_ahead(V, S, R, coef_ref, early, W, later, window)


def last_kernel(
    step, window, V0, S0, R0, coef_ref, force, surface, msg, missing, V, S, R, v_out, s_out, r_out, G, sems
):
    even, _, _ = place()
    here = force.at[step]
    inside = pl.ds(PAD, R.shape[2])

    def copies(cell):
        return [
            pltpu.make_async_copy(V.at[:, cell, inside], v_out.at[:, cell], sems.at[cell, 0]),
            pltpu.make_async_copy(S.at[:, cell, inside], s_out.at[:, cell], sems.at[cell, 1]),
            pltpu.make_async_copy(R.at[:, cell], r_out.at[:, cell], sems.at[cell, 2]),
        ]

    def finish(cell, bond):
        done, other = copies(1 - cell), copies(cell)
        for copy in done:
            copy.start()
        bond(V, S, R, coef_ref, here, surface, msg, missing, G, step, window)
        for copy in other:
            copy.start()
        for copy in done + other:
            copy.wait()

    @pl.when(even)
    def _():
        finish(0, behind_bond)

    @pl.when(jnp.logical_not(even))
    def _():
        finish(1, ahead_bond)


ENTRY_ROW, TRUCK_ROW = 48, 56
GROUP = 8


def pack_kernel(
    record, loads_in, entries_in, cells_in, piers_in, own, loads, steps_table, piers, entries, cells, sems
):
    panel = record.shape[1]
    slots, lanes = loads.shape
    steps = entries.shape[0]
    pairs = [(record, own.at[:, pl.ds(0, panel)]), (loads_in, loads), (entries_in, entries), (cells_in, cells)]
    pairs.append((piers_in, piers))
    copies = [pltpu.make_async_copy(*pair, sems.at[i]) for i, pair in enumerate(pairs)]
    for copy in copies:
        copy.start()
    own[:, panel:] = jnp.zeros((own.shape[0], own.shape[1] - panel), jnp.float32)
    steps_table[...] = jnp.zeros(steps_table.shape, jnp.float32)
    for copy in copies:
        copy.wait()
    steps_table[0:steps, 0:slots] = entries[...].astype(jnp.float32)
    steps_table[8 : 8 + steps, 0:slots] = cells[...].astype(jnp.float32)
    blocks = [loads[8 * i : 8 * i + 8, :] for i in range(slots // 8)] + [steps_table[0:8, :]]
    for i, block in enumerate(blocks):
        own[0:8, panel + i * lanes : panel + (i + 1) * lanes] = block


def lane_blocks(table, width):
    return sum(lane_roll(table[s : s + 1, :], s * width) for s in range(STEPS))


def split_kernel(panel, slots, own, behind, cells, after_this, out):
    del after_this
    tiles, _, lanes = out.shape
    pieces = panel // lanes
    third = pieces // 3
    cell_of = cells[...]
    me = lax.axis_index("line")
    group, mine = lax.div(me, tiles), lax.rem(me, tiles)
    piers = cell_of.shape[1]
    row = lax.broadcasted_iota(jnp.int32, (4 * tiles, lanes), 0)
    tile, j = lax.div(row, 4), lax.rem(row, 4)
    odd = lax.rem(tile, 2)
    first = (tile + group * tiles) * 2
    cell_x = first + jnp.where(j == 2, -1, jnp.where(j == 3, 4 * odd - 2, j))
    cell_yz = first + jnp.where(j == 3, 4 * odd - 1, j)
    record = jnp.where(group == 0, own[:, :panel], behind[:, :panel])

    def hits(cell):
        return [jnp.where(cell == cell_of[0:1, p : p + 1], 1.0, 0.0).astype(jnp.float32) for p in range(piers)]

    hit_x, hit_yz = hits(cell_x), hits(cell_yz)

    def share(m):
        hit = hit_x if m < third else hit_yz
        return sum(hit[p] * record[p : p + 1, m * lanes : (m + 1) * lanes] for p in range(piers))

    parts = [share(m) for m in range(pieces)]

    def trucks(source):
        blocks = [source[0:8, panel + i * lanes : panel + (i + 1) * lanes] for i in range(slots // 8 + 1)]
        return blocks[:-1], lane_blocks(blocks[-1], slots)

    own_rows, own_entry = trucks(own)
    far_rows, far_entry = trucks(behind)
    for tile in range(tiles):
        these = slice(4 * tile, 4 * tile + 4)
        for m in range(pieces):
            out[tile, 4 * m : 4 * m + 4, :] = parts[m][these, :]
        passed = mine < tile
        out[tile, ENTRY_ROW : ENTRY_ROW + 1, :] = jnp.where(passed, own_entry, far_entry)
        for i in range(slots // 8):
            at = TRUCK_ROW + 8 * i
            out[tile, at : at + 8, :] = jnp.where(passed, own_rows[i], far_rows[i])


def prepare_kernel(parts, loads, steps_table, force, surface, table, rows_out):
    steps, comps, width = force.shape[:3]
    lanes = parts.shape[2]
    force[...] = jnp.zeros(force.shape, jnp.float32)
    per = ENTRY_ROW // (comps * width)
    lane = lax.broadcasted_iota(jnp.int32, (per, lanes), 1)
    scale = jnp.where(lane < FZ, DT, 0.0).astype(jnp.float32)
    for s in range(steps):
        for comp in range(comps):
            for cell in range(width):
                panel = parts[s, pl.ds(comp * per * width + cell, per, stride=width), :]
                force[s, comp, cell, pl.ds(4, per, stride=2), :] = scale * panel
                force[s, comp, cell, pl.ds(5, per, stride=2), :] = scale * lane_roll(panel, FZ)

    slots = loads.shape[0]
    tiles = parts.shape[0]
    mine = lax.rem(lax.axis_index("line"), tiles)
    table[...] = jnp.zeros(table.shape, jnp.float32)
    table[0:1, :] = lane_blocks(steps_table[0:8, :], slots)
    table[STEPS + 1 : STEPS + 2, :] = lane_blocks(steps_table[8:16, :], slots)
    rows = [loads[...]]
    for k in range(1, STEPS + 1):
        source = lax.rem(mine + (tiles - k), tiles)
        rows.append(parts[source, TRUCK_ROW : TRUCK_ROW + slots, :])
        table[k : k + 1, :] = parts[source, ENTRY_ROW : ENTRY_ROW + 1, :]
    columns = table[...].T
    rows_out[...] = jnp.zeros(rows_out.shape, jnp.float32)
    for s in range(STEPS):
        block = slice(s * slots, (s + 1) * slots)
        moved = []
        for k in range(STEPS - s):
            entry = jnp.broadcast_to(columns[block, k : k + 1], rows[k].shape)
            new = rows[k]
            for slot in range(slots):
                new = jnp.where(entry == float(slot), rows[k + 1][slot : slot + 1, :], new)
            moved.append(new)
        rows = moved
        cell = jnp.broadcast_to(columns[block, STEPS + 1 : STEPS + 2], rows[0].shape)
        for c in range(2):
            load = jnp.sum(jnp.where(cell == float(c), rows[0], 0.0), axis=0, keepdims=True)
            rows_out[2 * s + c : 2 * s + c + 1, :] = load
    surface[...] = rows_out[...].T


def in_vmem(x):
    return pltpu.with_memory_space_constraint(x, pltpu.VMEM)


WHOLE = pl.BlockSpec(memory_space=pltpu.VMEM)
SCALARS = pl.BlockSpec(memory_space=pltpu.SMEM)
ANYWHERE = pl.BlockSpec(memory_space=pl.ANY)


def call(kernel, ins, specs, outs, out_specs, scratch=(), aliases=None, name=None, cost=1):
    return pl.pallas_call(
        kernel,
        out_shape=outs,
        in_specs=specs,
        out_specs=out_specs,
        scratch_shapes=list(scratch),
        input_output_aliases=aliases or {},
        compiler_params=pltpu.CompilerParams(vmem_limit_bytes=VMEM_LIMIT),
        cost_estimate=pl.CostEstimate(flops=cost, bytes_accessed=cost, transcendentals=0),
        name=name,
    )(*ins)


def body(
    velocity, stress, memory, truck_loads, pier_panels,
    lame_lambda, lame_mu, buoyancy, relax_rate, defect_mu, layer,
    truck_entry, truck_cell, pier_cell,
):
    tiles = lax.axis_size("line")
    width_x, across, depth = velocity.shape[1:]
    slots = truck_loads.shape[0]
    window = (across - FY) // 2 - 4
    f32 = jnp.float32

    near = [(i, i ^ 1) for i in range(tiles) if (i ^ 1) < tiles]
    far = [(i, i + 1) for i in range(1, tiles - 1, 2)] + [(i + 1, i) for i in range(1, tiles - 1, 2)]

    padded = across + 2 * PAD
    v_type = pltpu.VMEM((3, width_x, padded, depth), f32)
    s_type = pltpu.VMEM((6, width_x, padded, depth), f32)
    r_type = pltpu.VMEM((6, width_x, across, depth), f32)
    c_type = pltpu.VMEM((N_COEF, depth), f32)
    m_type = pltpu.VMEM((3, across, depth), f32)
    ghost = pltpu.VMEM((2, across, depth), f32)
    work = pltpu.VMEM((2, padded, depth), f32)
    square = pltpu.VMEM((across, depth), f32)

    def ahead_by(x, distance):
        return lax.ppermute(x, "line", [(i, i + distance) for i in range(tiles - distance)])

    def in_hbm(*arrays):
        return tuple(pltpu.with_memory_space_constraint(x, pltpu.HBM) for x in arrays)

    dma = pltpu.SemaphoreType.DMA
    piers, panel = pier_panels.shape[1:]
    own, loads, steps_table, pier_row = call(
        pack_kernel,
        in_hbm(pier_panels[0], truck_loads, truck_entry, truck_cell, pier_cell[None, :]),
        (ANYWHERE,) * 5,
        (
            pltpu.VMEM((piers, panel + (slots // 8 + 1) * depth), f32),
            pltpu.VMEM((slots, depth), f32),
            pltpu.VMEM((16, depth), f32),
            pltpu.VMEM((1, piers), jnp.int32),
        ),
        (WHOLE,) * 4,
        scratch=(pltpu.VMEM(truck_entry.shape, jnp.int32), pltpu.VMEM(truck_cell.shape, jnp.int32), dma((5,))),
        name="pack",
    )
    behind = ahead_by(own, GROUP)
    reach = 2 * GROUP
    index = lax.axis_index("line")
    while reach < tiles:
        record = jnp.where(index < GROUP, own, behind)[:, :panel]
        record = jnp.where(index < reach, record, ahead_by(record, reach))
        behind = jnp.concatenate([record, behind[:, panel:]], axis=1)
        reach *= 2
    tables = (lame_lambda, lame_mu, buoyancy, relax_rate, defect_mu)
    V, S, R, coef, msg_near, msg_far, early = call(
        start_kernel,
        in_hbm(velocity, stress, memory, layer[None, :], *tables) + (in_vmem(loads), in_vmem(steps_table)),
        (ANYWHERE,) * 9 + (WHOLE,) * 2,
        (v_type, s_type, r_type, c_type, m_type, pltpu.VMEM((3 * across + 3 * slots, depth), f32), m_type),
        (WHOLE,) * 7,
        scratch=(
            work, pltpu.VMEM((depth, depth), f32), pltpu.VMEM((1, depth), jnp.int32),
            *(pltpu.SMEM(table.shape, f32) for table in tables), dma((21,)),
        ),
        name="start",
        cost=8 * 1024 * 1024,
    )
    msg_far = lax.ppermute(msg_far, "line", far)
    early = lax.ppermute(early, "line", far)
    msg_near = lax.ppermute(msg_near, "line", near)
    parts = call(
        functools.partial(split_kernel, panel, slots),
        (own, behind, in_vmem(pier_row), coef),
        (WHOLE,) * 3 + (ANYWHERE,),
        jax.ShapeDtypeStruct((GROUP, TRUCK_ROW + slots, depth), f32),
        WHOLE,
        name="split",
    )
    groups = [list(range(at, at + GROUP)) for at in range(0, tiles, GROUP)]
    parts = lax.all_to_all(parts, "line", 0, 0, axis_index_groups=groups, tiled=True)
    load = call(
        functools.partial(meet_kernel, across),
        (in_vmem(msg_far), in_vmem(loads)),
        (WHOLE,) * 2,
        square,
        WHOLE,
        scratch=(pltpu.VMEM((depth, across), f32),),
        name="meet",
    )
    force, surface = call(
        prepare_kernel,
        (parts, in_vmem(loads), in_vmem(steps_table)),
        (WHOLE,) * 3,
        (pltpu.VMEM((STEPS, 3, 4, 16, depth), f32), pltpu.VMEM((across, depth), f32)),
        (WHOLE,) * 2,
        scratch=(pltpu.VMEM((depth, depth), f32), pltpu.VMEM((depth, across), f32)),
        name="prepare",
    )
    state = (v_type, s_type, r_type)
    same = {0: 0, 1: 1, 2: 2}
    missing = None
    for step in range(STEPS):
        more = step < STEPS - 1
        ins = tuple(in_vmem(x) for x in (V, S, R, coef, force, surface, msg_near))
        outs = state + ((m_type,) if more else ())
        V, S, R, *msg = call(
            functools.partial(near_kernel, step, window),
            ins,
            (WHOLE,) * len(ins),
            outs,
            (WHOLE,) * len(outs),
            scratch=(ghost,),
            aliases=same,
            name="near" + str(step),
        )
        if more:
            msg_near = lax.ppermute(msg[0], "line", near)
        ins = (V, S, R, coef, force, surface, msg_far, missing if step else load)
        ins = tuple(in_vmem(x) for x in ins)
        if more:
            outs = state + (m_type,) + ((m_type,) if step < STEPS - 2 else ())
            V, S, R, missing, *msg = call(
                functools.partial(far_kernel, step, window),
                ins,
                (WHOLE,) * len(ins),
                outs,
                (WHOLE,) * len(outs),
                scratch=(ghost, work) + (() if step else (pltpu.VMEM((5, padded, depth), f32),)),
                aliases=same,
                name="far" + str(step),
            )
            msg_far = early
            if msg:
                early = lax.ppermute(msg[0], "line", far)
    results = call(
        functools.partial(last_kernel, STEPS - 1, window),
        ins,
        (WHOLE,) * len(ins),
        state + tuple(jax.ShapeDtypeStruct(x.shape, f32) for x in (velocity, stress, memory)),
        (WHOLE,) * 3 + (ANYWHERE,) * 3,
        scratch=(ghost, pltpu.SemaphoreType.DMA((2, 3))),
        aliases=same,
        name="last",
    )
    return results[3:]


def solution(mesh):
    placed = (
        P(None, ("runs", "line"), None, None),
        P(None, ("runs", "line"), None, None),
        P(None, ("runs", "line"), None, None),
        P(("runs", "line"), None),
        P("line", "runs", None),
        P(),
        P(),
        P(),
        P(),
        P(),
        P(),
        P(None, ("runs", "line")),
        P(None, ("runs", "line")),
        P(),
    )
    return jax.shard_map(
        body,
        mesh=mesh,
        in_specs=placed,
        out_specs=(
            P(None, ("runs", "line"), None, None),
            P(None, ("runs", "line"), None, None),
            P(None, ("runs", "line"), None, None),
        ),
        check_vma=False,
    )
```

```python
import functools

import jax
import jax.numpy as jnp
import numpy as np
from jax import lax
from jax.experimental import pallas as pl
from jax.experimental.pallas import tpu as pltpu
from jax.sharding import PartitionSpec as P

STEPS = 6
FY = 8
FZ = 64
DT = 0.25
PAD = 8
ROWS = 16
UNROLL = 8
VMEM_LIMIT = 32 * 1024 * 1024

C_B, C_B0, C_B1, C_M0, C_M1, C_LAM, C_MU2, C_MU, C_K1, C_K2, C_K2H, C_L0 = range(12)
N_COEF = 16

VX, VY, VZ = range(3)
XX, YY, ZZ, XY, XZ, YZ = range(6)


def lane_roll(x, shift):
    return pltpu.roll(x, shift % x.shape[-1], x.ndim - 1)


def before(x):
    return lane_roll(x, 1)


def after(x):
    return lane_roll(x, -1)


def over_rows(count, work):
    def step(i, carry):
        work(pl.multiple_of(i * ROWS, ROWS))
        return carry

    lax.fori_loop(0, count // ROWS, step, 0, unroll=UNROLL)


def coefs(coef_ref, ids):
    return [coef_ref[i : i + 1, :] for i in ids]


def place():
    index = lax.axis_index("line")
    return lax.rem(index, 2) == 0, index > 0, index < lax.axis_size("line") - 1


def spans(r):
    return pl.ds(PAD + r, ROWS), pl.ds(PAD + r - 1, ROWS), pl.ds(PAD + r + 1, ROWS), pl.ds(r, ROWS)


def zero_edges(ref):
    across = ref.shape[-2] - 2 * PAD
    edge = jnp.zeros((PAD, ref.shape[-1]), jnp.float32)
    for where in np.ndindex(*ref.shape[:-2]):
        ref[(*where, pl.ds(0, PAD))] = edge
        ref[(*where, pl.ds(PAD + across, PAD))] = edge


def add_force(ref, index, force, which, first_row):
    rows = pl.ds(first_row, 16)
    ref[(*index, rows)] = ref[(*index, rows)] + force[which]


def pre_ahead(V, S, coef_ref, msg, force, window):
    b, b0 = coefs(coef_ref, (C_B, C_B0))

    def work(r):
        here, up, _, out = spans(r)
        sxy, sxz = S[XY, 1, here], S[XZ, 1, here]
        px = V[VX, 1, here] + b * (sxy - S[XY, 1, up] + sxz - S[XX, 1, here]) - b0 * before(sxz)
        V[VX, 1, here] = px
        if msg is not None:
            msg[0, out] = sxy
            msg[1, out] = sxz
            msg[2, out] = px

    over_rows(V.shape[2] - 2 * PAD, work)
    if force is not None:
        add_force(V, (VX, 1), force, (VX, 1), PAD + window)
        if msg is not None:
            add_force(msg, (2,), force, (VX, 1), window)


def pre_behind(V, S, coef_ref, msg, force, window):
    b, b0, b1 = coefs(coef_ref, (C_B, C_B0, C_B1))

    def work(r):
        here, up, down, out = spans(r)
        syz, szz = S[YZ, 0, here], S[ZZ, 0, here]
        qy = V[VY, 0, here] + b * (S[XY, 0, here] + S[YY, 0, down] - S[YY, 0, here] + syz) - b0 * before(syz)
        qz = V[VZ, 0, here] + b * (S[XZ, 0, here] + syz - S[YZ, 0, up] - szz) + b1 * after(szz)
        V[VY, 0, here] = qy
        V[VZ, 0, here] = qz
        if msg is not None:
            msg[0, out] = S[XX, 0, here]
            msg[1, out] = qy
            msg[2, out] = qz

    over_rows(V.shape[2] - 2 * PAD, work)
    if force is not None:
        add_force(V, (VY, 0), force, (VY, 0), PAD + window)
        add_force(V, (VZ, 0), force, (VZ, 0), PAD + window)
        if msg is not None:
            add_force(msg, (1,), force, (VY, 0), window)
            add_force(msg, (2,), force, (VZ, 0), window)


def inner(V, S, coef_ref, force, window):
    b, b0, b1 = coefs(coef_ref, (C_B, C_B0, C_B1))

    def work(r):
        here, up, down, _ = spans(r)
        sxy, sxz = S[XY, 0, here], S[XZ, 0, here]
        V[VX, 0, here] = (
            V[VX, 0, here]
            + b * (S[XX, 1, here] - S[XX, 0, here] + sxy - S[XY, 0, up] + sxz)
            - b0 * before(sxz)
        )
        syz, szz = S[YZ, 1, here], S[ZZ, 1, here]
        V[VY, 1, here] = (
            V[VY, 1, here]
            + b * (S[XY, 1, here] - sxy + S[YY, 1, down] - S[YY, 1, here] + syz)
            - b0 * before(syz)
        )
        V[VZ, 1, here] = (
            V[VZ, 1, here]
            + b * (S[XZ, 1, here] - sxz + syz - S[YZ, 1, up] - szz)
            + b1 * after(szz)
        )

    over_rows(V.shape[2] - 2 * PAD, work)
    if force is not None:
        add_force(V, (VX, 0), force, (VX, 0), PAD + window)
        add_force(V, (VY, 1), force, (VY, 1), PAD + window)
        add_force(V, (VZ, 1), force, (VZ, 1), PAD + window)


def post(V, S, R, coef_ref, surface, cell, column, behind_x, ahead_y, ahead_z):
    m0, m1, lam, mu2, mu, k1, k2, k2h, l0 = coefs(
        coef_ref, (C_M0, C_M1, C_LAM, C_MU2, C_MU, C_K1, C_K2, C_K2H, C_L0)
    )

    def work(r):
        here, up, down, out = spans(r)
        vx, vy, vz = V[VX, cell, here], V[VY, cell, here], V[VZ, cell, here]
        exx = vx - behind_x(r)
        eyy = vy - V[VY, cell, up]
        ezz = vz - m0 * before(vz)
        exy = V[VX, cell, down] - vx + (ahead_y(r) - vy)
        exz = m1 * after(vx) - vx + (ahead_z(r) - vz)
        eyz = m1 * after(vy) - vy + (V[VZ, cell, down] - vz)
        volume = lam * (exx + eyy + ezz)
        for comp, e in ((XX, exx), (YY, eyy), (ZZ, ezz)):
            old = R[comp, cell, out]
            new = S[comp, cell, here] + (volume + mu2 * e) + DT * old
            if comp == ZZ:
                new = new + l0 * lane_roll(surface[out, :], -column)
            S[comp, cell, here] = new
            R[comp, cell, out] = k1 * old - k2 * e
        for comp, e in ((XY, exy), (XZ, exz), (YZ, eyz)):
            old = R[comp, cell, out]
            S[comp, cell, here] = S[comp, cell, here] + mu * e + DT * old
            R[comp, cell, out] = k1 * old - k2h * e

    over_rows(R.shape[2], work)


def response_behind(V, S, coef_ref, D, W):
    b, b0, b1, m0, m1, lam, mu2, mu = coefs(coef_ref, (C_B, C_B0, C_B1, C_M0, C_M1, C_LAM, C_MU2, C_MU))

    def work(r):
        here, up, down, out = spans(r)
        sxy = S[XY, 1, here]
        vy, vz = -b * sxy, -b * S[XZ, 1, here]
        exx = -V[VX, 1, here]
        eyy = b * (S[XY, 1, up] - sxy)
        ezz = vz - m0 * before(vz)
        volume = lam * (exx + eyy + ezz)
        dyy, dzz = volume + mu2 * eyy, volume + mu2 * ezz
        dyz = mu * (m1 * after(vy) - vy - b * S[XZ, 1, down] - vz)
        W[0, here] = dyy
        W[1, here] = dyz
        D[0, out] = volume + mu2 * exx
        D[1, out] = vy + b * (dyz - mu * vy - dyy) - b0 * before(dyz)
        D[2, out] = vz + b * (dyz - mu * vz - dzz) + b1 * after(dzz)

    over_rows(D.shape[1], work)

    def rest(r):
        _, up, down, out = spans(r)
        D[1, out] = D[1, out] + b * W[0, down]
        D[2, out] = D[2, out] - b * W[1, up]

    over_rows(D.shape[1], rest)


def response_ahead(V, S, coef_ref, D, W):
    b, b0, m1, lam, mu2, mu = coefs(coef_ref, (C_B, C_B0, C_M1, C_LAM, C_MU2, C_MU))

    def work(r):
        here, _, down, out = spans(r)
        vx = b * S[XX, 0, here]
        dxy = mu * (b * S[XX, 0, down] - vx + V[VY, 0, here])
        dxz = mu * (m1 * after(vx) - vx + V[VZ, 0, here])
        W[0, here] = dxy
        D[0, out] = dxy
        D[1, out] = dxz
        D[2, out] = vx + b * (dxy + dxz - (lam + mu2) * vx) - b0 * before(dxz)

    over_rows(D.shape[1], work)

    def rest(r):
        _, up, _, out = spans(r)
        D[2, out] = D[2, out] - b * W[0, up]

    over_rows(D.shape[1], rest)


def early_ahead(V, S, R, coef_ref, msg, W, force, window):
    b, b0, m0, m1, lam, mu2, mu = coefs(coef_ref, (C_B, C_B0, C_M0, C_M1, C_LAM, C_MU2, C_MU))

    def work(r):
        here, up, down, out = spans(r)
        vx, vy, vz = V[VX, 1, here], V[VY, 1, here], V[VZ, 1, here]
        exx = vx - V[VX, 0, here]
        volume = lam * (exx + (vy - V[VY, 1, up]) + (vz - m0 * before(vz)))
        sxx = S[XX, 1, here] + (volume + mu2 * exx) + DT * R[XX, 1, out]
        sxy = S[XY, 1, here] + mu * (V[VX, 1, down] - vx - vy) + DT * R[XY, 1, out]
        sxz = S[XZ, 1, here] + mu * (m1 * after(vx) - vx - vz) + DT * R[XZ, 1, out]
        W[0, here] = sxy
        msg[0, out] = sxy
        msg[1, out] = sxz
        msg[2, out] = vx + b * (sxy + sxz - sxx) - b0 * before(sxz)

    over_rows(msg.shape[1], work)

    def rest(r):
        _, up, _, out = spans(r)
        msg[2, out] = msg[2, out] - b * W[0, up]

    over_rows(msg.shape[1], rest)
    if force is not None:
        add_force(msg, (2,), force, (VX, 1), window)


def early_behind(V, S, R, coef_ref, surface, column, msg, W, force, window):
    b, b0, b1, m0, m1, lam, mu2, mu, l0 = coefs(
        coef_ref, (C_B, C_B0, C_B1, C_M0, C_M1, C_LAM, C_MU2, C_MU, C_L0)
    )

    def work(r):
        here, up, down, out = spans(r)
        vx, vy, vz = V[VX, 0, here], V[VY, 0, here], V[VZ, 0, here]
        eyy = vy - V[VY, 0, up]
        ezz = vz - m0 * before(vz)
        volume = lam * (vx + eyy + ezz)
        sxx = S[XX, 0, here] + (volume + mu2 * vx) + DT * R[XX, 0, out]
        syy = S[YY, 0, here] + (volume + mu2 * eyy) + DT * R[YY, 0, out]
        szz = S[ZZ, 0, here] + (volume + mu2 * ezz) + DT * R[ZZ, 0, out]
        if surface is not None:
            szz = szz + l0 * lane_roll(surface[out, :], -column)
        sxy = S[XY, 0, here] + mu * (V[VX, 0, down] - vx + (V[VY, 1, here] - vy)) + DT * R[XY, 0, out]
        sxz = S[XZ, 0, here] + mu * (m1 * after(vx) - vx + (V[VZ, 1, here] - vz)) + DT * R[XZ, 0, out]
        syz = S[YZ, 0, here] + mu * (m1 * after(vy) - vy + (V[VZ, 0, down] - vz)) + DT * R[YZ, 0, out]
        W[0, here] = syy
        W[1, here] = syz
        msg[0, out] = sxx
        msg[1, out] = vy + b * (sxy - syy + syz) - b0 * before(syz)
        msg[2, out] = vz + b * (sxz + syz - szz) + b1 * after(szz)

    over_rows(msg.shape[1], work)

    def rest(r):
        _, up, down, out = spans(r)
        msg[1, out] = msg[1, out] + b * W[0, down]
        msg[2, out] = msg[2, out] - b * W[1, up]

    over_rows(msg.shape[1], rest)
    if force is not None:
        add_force(msg, (1,), force, (VY, 0), window)
        add_force(msg, (2,), force, (VZ, 0), window)


def ahead_bond(V, S, R, coef_ref, force, surface, msg, missing, G, step, window, unforced=0, respond=None):
    (b,) = coefs(coef_ref, (C_B,))
    _, _, has_ahead = place()
    keep = jnp.where(has_ahead, 1.0, 0.0).astype(jnp.float32)

    def got(i, out):
        return msg[i, out] if missing is None else msg[i, out] + missing[i, out]

    def work(r):
        here, _, _, out = spans(r)
        V[VX, 1, here] = V[VX, 1, here] + (keep * b) * got(0, out)
        G[0, out] = keep * (got(1, out) - b * S[XY, 1, here])
        G[1, out] = keep * (got(2, out) - b * S[XZ, 1, here])

    over_rows(R.shape[2], work)
    if step < unforced:
        add_force(G, (0,), force, (VY, 2), window)
        add_force(G, (1,), force, (VZ, 2), window)
    if respond is not None:
        respond()
    post(
        V, S, R, coef_ref, surface, 1, 2 * step + 1,
        lambda r: V[VX, 0, pl.ds(PAD + r, ROWS)],
        lambda r: G[0, pl.ds(r, ROWS)],
        lambda r: G[1, pl.ds(r, ROWS)],
    )


def behind_bond(V, S, R, coef_ref, force, surface, msg, missing, G, step, window, unforced=0, respond=None):
    (b,) = coefs(coef_ref, (C_B,))
    _, has_behind, _ = place()
    keep = jnp.where(has_behind, 1.0, 0.0).astype(jnp.float32)

    def got(i, out):
        return msg[i, out] if missing is None else msg[i, out] + missing[i, out]

    def work(r):
        here, _, _, out = spans(r)
        V[VY, 0, here] = V[VY, 0, here] - (keep * b) * got(0, out)
        V[VZ, 0, here] = V[VZ, 0, here] - (keep * b) * got(1, out)
        G[0, out] = keep * (got(2, out) + b * S[XX, 0, here])

    over_rows(R.shape[2], work)
    if step < unforced:
        add_force(G, (0,), force, (VX, 2), window)
    if respond is not None:
        respond()
    post(
        V, S, R, coef_ref, surface, 0, 2 * step,
        lambda r: G[0, pl.ds(r, ROWS)],
        lambda r: V[VY, 1, pl.ds(PAD + r, ROWS)],
        lambda r: V[VZ, 1, pl.ds(PAD + r, ROWS)],
    )


def start_kernel(
    velocity, stress, memory, layer_in, lam_in, mu_in, buoy_in, rate_in, defect_in, after_this,
    V, S, R, coef_ref, msg_near, msg_far, layer_ref, lam, mu, buoy, rate, defect, sems,
):
    del after_this
    across = velocity.shape[2]
    inside = pl.ds(PAD, across)
    pairs = [
        (layer_in, layer_ref), (lam_in, lam), (mu_in, mu), (buoy_in, buoy), (rate_in, rate), (defect_in, defect),
    ]
    pairs += [(stress.at[i], S.at[i, :, inside]) for i in range(6)]
    pairs += [(velocity.at[i], V.at[i, :, inside]) for i in range(3)]
    pairs += [(memory.at[i], R.at[i]) for i in range(6)]
    copies = [pltpu.make_async_copy(*pair, sems.at[i]) for i, pair in enumerate(pairs)]
    for copy in copies:
        copy.start()
    zero_edges(V)
    zero_edges(S)
    for copy in copies[:6]:
        copy.wait()
    layer = layer_ref[...]

    def per_depth(table):
        row = jnp.zeros(layer.shape, jnp.float32)
        for level in range(table.shape[0]):
            row = jnp.where(layer == level, table[level], row)
        return row

    lane = lax.broadcasted_iota(jnp.int32, layer.shape, 1)
    not_first = jnp.where(lane > 0, 1.0, 0.0).astype(jnp.float32)
    not_last = jnp.where(lane < layer.shape[1] - 1, 1.0, 0.0).astype(jnp.float32)
    b = DT * per_depth(buoy)
    two_mu = (2.0 * DT) * per_depth(mu)
    decay = DT * per_depth(rate)
    drop = 2.0 * decay * per_depth(defect)
    for row, value in (
        (C_B, b),
        (C_B0, b * not_first),
        (C_B1, b * not_last),
        (C_M0, not_first),
        (C_M1, not_last),
        (C_LAM, DT * per_depth(lam)),
        (C_MU2, two_mu),
        (C_MU, 0.5 * two_mu),
        (C_K1, 1.0 - decay),
        (C_K2, drop),
        (C_K2H, 0.5 * drop),
        (C_L0, DT * (1.0 - not_first)),
    ):
        coef_ref[row : row + 1, :] = value
    coef_ref[12:16, :] = jnp.zeros((4, layer.shape[1]), jnp.float32)
    for copy in copies[6:15]:
        copy.wait()
    even, _, _ = place()

    @pl.when(even)
    def _():
        pre_ahead(V, S, coef_ref, msg_near, None, 0)
        pre_behind(V, S, coef_ref, msg_far, None, 0)

    @pl.when(jnp.logical_not(even))
    def _():
        pre_behind(V, S, coef_ref, msg_near, None, 0)
        pre_ahead(V, S, coef_ref, msg_far, None, 0)

    for copy in copies[15:]:
        copy.wait()


def first_kernel(window, V0, S, R, coef_ref, force, surface, V, msg, W):
    even, _, _ = place()
    zero_edges(W)
    now, then = force.at[0], force.at[1]
    add_force(V, (VX, 1), now, (VX, 1), PAD + window)
    add_force(V, (VY, 0), now, (VY, 0), PAD + window)
    add_force(V, (VZ, 0), now, (VZ, 0), PAD + window)
    inner(V, S, coef_ref, now, window)

    @pl.when(even)
    def _():
        early_behind(V, S, R, coef_ref, surface, 0, msg, W, then, window)

    @pl.when(jnp.logical_not(even))
    def _():
        early_ahead(V, S, R, coef_ref, msg, W, then, window)


def write_out(V, S, R, results, sems, cell):
    inside = pl.ds(PAD, R.shape[2])
    pairs = [(V.at[:, cell, inside], results[0]), (S.at[:, cell, inside], results[1]), (R.at[:, cell], results[2])]
    copies = [
        pltpu.make_async_copy(source, result.at[:, cell], sems.at[i]) for i, (source, result) in enumerate(pairs)
    ]
    for copy in copies:
        copy.start()
    for copy in copies:
        copy.wait()


def near_kernel(step, window, V0, S0, R0, coef_ref, force, surface, msg, V, S, R, *rest):
    G = rest[-1]
    even, _, _ = place()
    more = step < STEPS - 1

    @pl.when(even)
    def _():
        ahead_bond(V, S, R, coef_ref, force.at[step], surface, msg, None, G, step, window, 1)
        if more:
            pre_ahead(V, S, coef_ref, rest[0], force.at[step + 1], window)
        else:
            write_out(V, S, R, rest[:3], rest[-2], 1)

    @pl.when(jnp.logical_not(even))
    def _():
        behind_bond(V, S, R, coef_ref, force.at[step], surface, msg, None, G, step, window, 1)
        if more:
            pre_behind(V, S, coef_ref, rest[0], force.at[step + 1], window)
        else:
            write_out(V, S, R, rest[:3], rest[-2], 0)


def far_kernel(step, window, V0, S0, R0, coef_ref, force, surface, msg, *rest):
    rest = list(rest)
    missing = rest.pop(0) if step > 0 else None
    V, S, R, D = rest[:4]
    G, W = rest[-2:]
    early = rest[4] if step < STEPS - 2 else None
    even, _, _ = place()
    zero_edges(W)
    here, then = force.at[step], force.at[step + 1]

    @pl.when(even)
    def _():
        behind_bond(
            V, S, R, coef_ref, here, surface, msg, missing, G, step, window, 1,
            lambda: response_ahead(V, S, coef_ref, D, W),
        )
        pre_behind(V, S, coef_ref, None, then, window)

    @pl.when(jnp.logical_not(even))
    def _():
        ahead_bond(
            V, S, R, coef_ref, here, surface, msg, missing, G, step, window, 1,
            lambda: response_behind(V, S, coef_ref, D, W),
        )
        pre_ahead(V, S, coef_ref, None, then, window)

    inner(V, S, coef_ref, then, window)
    if early is not None:
        later = force.at[step + 2]

        @pl.when(even)
        def _():
            early_behind(V, S, R, coef_ref, surface, 2 * (step + 1), early, W, later, window)

        @pl.when(jnp.logical_not(even))
        def _():
            early_ahead(V, S, R, coef_ref, early, W, later, window)


def last_kernel(step, window, V0, S0, R0, coef_ref, force, surface, msg, missing, v0, s0, r0, V, S, R, *rest):
    *results, G, sems = rest
    even, _, _ = place()
    here = force.at[step]

    @pl.when(even)
    def _():
        behind_bond(V, S, R, coef_ref, here, surface, msg, missing, G, step, window)
        write_out(V, S, R, results, sems, 0)

    @pl.when(jnp.logical_not(even))
    def _():
        ahead_bond(V, S, R, coef_ref, here, surface, msg, missing, G, step, window)
        write_out(V, S, R, results, sems, 1)


ENTRY_ROW, TRUCK_ROW = 36, 40
GROUP = 8


def pack_kernel(
    record, loads_in, entries_in, cells_in, piers_in, own, loads, steps_table, piers, entries, cells, sems
):
    panel = record.shape[1]
    slots, lanes = loads.shape
    steps = entries.shape[0]
    pairs = [(record, own.at[:, pl.ds(0, panel)]), (loads_in, loads), (entries_in, entries), (cells_in, cells)]
    pairs.append((piers_in, piers))
    copies = [pltpu.make_async_copy(*pair, sems.at[i]) for i, pair in enumerate(pairs)]
    for copy in copies:
        copy.start()
    own[:, panel:] = jnp.zeros((own.shape[0], own.shape[1] - panel), jnp.float32)
    steps_table[...] = jnp.zeros(steps_table.shape, jnp.float32)
    for copy in copies:
        copy.wait()
    steps_table[0:steps, 0:slots] = entries[...].astype(jnp.float32)
    steps_table[8 : 8 + steps, 0:slots] = cells[...].astype(jnp.float32)
    blocks = [loads[8 * i : 8 * i + 8, :] for i in range(slots // 8)] + [steps_table[0:8, :]]
    for i, block in enumerate(blocks):
        own[0:8, panel + i * lanes : panel + (i + 1) * lanes] = block


def lane_blocks(table, width):
    return sum(lane_roll(table[s : s + 1, :], s * width) for s in range(STEPS))


def split_kernel(panel, slots, own, behind, cells, after_this, out):
    del after_this
    tiles, _, lanes = out.shape
    pieces = panel // lanes
    third = pieces // 3
    cell_of = cells[...]
    me = lax.axis_index("line")
    group, mine = lax.div(me, tiles), lax.rem(me, tiles)
    piers = cell_of.shape[1]
    row = lax.broadcasted_iota(jnp.int32, (3 * tiles, lanes), 0)
    j = lax.rem(row, 3)
    first = (lax.div(row, 3) + group * tiles) * 2
    cell_x, cell_yz = first + jnp.where(j == 2, -1, j), first + j
    record = jnp.where(group == 0, own[:, :panel], behind[:, :panel])

    def hits(cell):
        return [jnp.where(cell == cell_of[0:1, p : p + 1], 1.0, 0.0).astype(jnp.float32) for p in range(piers)]

    hit_x, hit_yz = hits(cell_x), hits(cell_yz)

    def share(m):
        hit = hit_x if m < third else hit_yz
        return sum(hit[p] * record[p : p + 1, m * lanes : (m + 1) * lanes] for p in range(piers))

    parts = [share(m) for m in range(pieces)]

    def trucks(source):
        blocks = [source[0:8, panel + i * lanes : panel + (i + 1) * lanes] for i in range(slots // 8 + 1)]
        return blocks[:-1], lane_blocks(blocks[-1], slots)

    own_rows, own_entry = trucks(own)
    far_rows, far_entry = trucks(behind)
    for tile in range(tiles):
        these = slice(3 * tile, 3 * tile + 3)
        for m in range(pieces):
            out[tile, 3 * m : 3 * m + 3, :] = parts[m][these, :]
        passed = mine < tile
        out[tile, ENTRY_ROW : ENTRY_ROW + 1, :] = jnp.where(passed, own_entry, far_entry)
        for i in range(slots // 8):
            at = TRUCK_ROW + 8 * i
            out[tile, at : at + 8, :] = jnp.where(passed, own_rows[i], far_rows[i])


def prepare_kernel(parts, loads, steps_table, force, surface, table, rows_out):
    steps, comps, width = force.shape[:3]
    lanes = parts.shape[2]
    force[...] = jnp.zeros(force.shape, jnp.float32)
    per = ENTRY_ROW // (comps * width)
    lane = lax.broadcasted_iota(jnp.int32, (per, lanes), 1)
    scale = jnp.where(lane < FZ, DT, 0.0).astype(jnp.float32)
    for s in range(steps):
        for comp in range(comps):
            for cell in range(width):
                panel = parts[s, pl.ds(comp * per * width + cell, per, stride=width), :]
                force[s, comp, cell, pl.ds(4, per, stride=2), :] = scale * panel
                force[s, comp, cell, pl.ds(5, per, stride=2), :] = scale * lane_roll(panel, FZ)

    slots = loads.shape[0]
    tiles = parts.shape[0]
    mine = lax.rem(lax.axis_index("line"), tiles)
    table[...] = jnp.zeros(table.shape, jnp.float32)
    table[0:1, :] = lane_blocks(steps_table[0:8, :], slots)
    table[STEPS + 1 : STEPS + 2, :] = lane_blocks(steps_table[8:16, :], slots)
    rows = [loads[...]]
    for k in range(1, STEPS + 1):
        source = lax.rem(mine + (tiles - k), tiles)
        rows.append(parts[source, TRUCK_ROW : TRUCK_ROW + slots, :])
        table[k : k + 1, :] = parts[source, ENTRY_ROW : ENTRY_ROW + 1, :]
    columns = table[...].T
    rows_out[...] = jnp.zeros(rows_out.shape, jnp.float32)
    for s in range(STEPS):
        block = slice(s * slots, (s + 1) * slots)
        moved = []
        for k in range(STEPS - s):
            entry = jnp.broadcast_to(columns[block, k : k + 1], rows[k].shape)
            new = rows[k]
            for slot in range(slots):
                new = jnp.where(entry == float(slot), rows[k + 1][slot : slot + 1, :], new)
            moved.append(new)
        rows = moved
        cell = jnp.broadcast_to(columns[block, STEPS + 1 : STEPS + 2], rows[0].shape)
        for c in range(2):
            load = jnp.sum(jnp.where(cell == float(c), rows[0], 0.0), axis=0, keepdims=True)
            rows_out[2 * s + c : 2 * s + c + 1, :] = load
    surface[...] = rows_out[...].T


def in_vmem(x):
    return pltpu.with_memory_space_constraint(x, pltpu.VMEM)


WHOLE = pl.BlockSpec(memory_space=pltpu.VMEM)
SCALARS = pl.BlockSpec(memory_space=pltpu.SMEM)
ANYWHERE = pl.BlockSpec(memory_space=pl.ANY)


def call(kernel, ins, specs, outs, out_specs, scratch=(), aliases=None, name=None, cost=1):
    return pl.pallas_call(
        kernel,
        out_shape=outs,
        in_specs=specs,
        out_specs=out_specs,
        scratch_shapes=list(scratch),
        input_output_aliases=aliases or {},
        compiler_params=pltpu.CompilerParams(vmem_limit_bytes=VMEM_LIMIT),
        cost_estimate=pl.CostEstimate(flops=cost, bytes_accessed=cost, transcendentals=0),
        name=name,
    )(*ins)


def body(
    velocity, stress, memory, truck_loads, pier_panels,
    lame_lambda, lame_mu, buoyancy, relax_rate, defect_mu, layer,
    truck_entry, truck_cell, pier_cell,
):
    tiles = lax.axis_size("line")
    width_x, across, depth = velocity.shape[1:]
    slots = truck_loads.shape[0]
    window = (across - FY) // 2 - 4
    f32 = jnp.float32

    near = [(i, i ^ 1) for i in range(tiles) if (i ^ 1) < tiles]
    far = [(i, i + 1) for i in range(1, tiles - 1, 2)] + [(i + 1, i) for i in range(1, tiles - 1, 2)]

    padded = across + 2 * PAD
    v_type = pltpu.VMEM((3, width_x, padded, depth), f32)
    s_type = pltpu.VMEM((6, width_x, padded, depth), f32)
    r_type = pltpu.VMEM((6, width_x, across, depth), f32)
    c_type = pltpu.VMEM((N_COEF, depth), f32)
    m_type = pltpu.VMEM((3, across, depth), f32)
    ghost = pltpu.VMEM((2, across, depth), f32)
    work = pltpu.VMEM((2, padded, depth), f32)

    def ahead_by(x, distance):
        return lax.ppermute(x, "line", [(i, i + distance) for i in range(tiles - distance)])

    def in_hbm(*arrays):
        return tuple(pltpu.with_memory_space_constraint(x, pltpu.HBM) for x in arrays)

    dma = pltpu.SemaphoreType.DMA
    piers, panel = pier_panels.shape[1:]
    own, loads, steps_table, pier_row = call(
        pack_kernel,
        in_hbm(pier_panels[0], truck_loads, truck_entry, truck_cell, pier_cell[None, :]),
        (ANYWHERE,) * 5,
        (
            pltpu.VMEM((piers, panel + (slots // 8 + 1) * depth), f32),
            pltpu.VMEM((slots, depth), f32),
            pltpu.VMEM((16, depth), f32),
            pltpu.VMEM((1, piers), jnp.int32),
        ),
        (WHOLE,) * 4,
        scratch=(pltpu.VMEM(truck_entry.shape, jnp.int32), pltpu.VMEM(truck_cell.shape, jnp.int32), dma((5,))),
        name="pack",
    )
    behind = ahead_by(own, GROUP)
    reach = 2 * GROUP
    index = lax.axis_index("line")
    while reach < tiles:
        record = jnp.where(index < GROUP, own, behind)[:, :panel]
        record = jnp.where(index < reach, record, ahead_by(record, reach))
        behind = jnp.concatenate([record, behind[:, panel:]], axis=1)
        reach *= 2
    tables = (lame_lambda, lame_mu, buoyancy, relax_rate, defect_mu)
    V, S, R, coef, msg_near, msg_far = call(
        start_kernel,
        in_hbm(velocity, stress, memory, layer[None, :], *tables) + (steps_table,),
        (ANYWHERE,) * 10,
        (v_type, s_type, r_type, c_type, m_type, m_type),
        (WHOLE,) * 6,
        scratch=(
            pltpu.VMEM((1, depth), jnp.int32), *(pltpu.SMEM(table.shape, f32) for table in tables), dma((21,)),
        ),
        name="start",
        cost=8 * 1024 * 1024,
    )
    msg_far = lax.ppermute(msg_far, "line", far)
    msg_near = lax.ppermute(msg_near, "line", near)
    parts = call(
        functools.partial(split_kernel, panel, slots),
        (own, behind, in_vmem(pier_row), coef),
        (WHOLE,) * 3 + (ANYWHERE,),
        jax.ShapeDtypeStruct((GROUP, TRUCK_ROW + slots, depth), f32),
        WHOLE,
        name="split",
    )
    groups = [list(range(at, at + GROUP)) for at in range(0, tiles, GROUP)]
    parts = lax.all_to_all(parts, "line", 0, 0, axis_index_groups=groups, tiled=True)
    force, surface = call(
        prepare_kernel,
        (parts, in_vmem(loads), in_vmem(steps_table)),
        (WHOLE,) * 3,
        (pltpu.VMEM((STEPS, 3, 3, 16, depth), f32), pltpu.VMEM((across, depth), f32)),
        (WHOLE,) * 2,
        scratch=(pltpu.VMEM((depth, depth), f32), pltpu.VMEM((depth, across), f32)),
        name="prepare",
    )
    V, early = call(
        functools.partial(first_kernel, window),
        tuple(in_vmem(x) for x in (V, S, R, coef, force, surface)),
        (WHOLE,) * 6,
        (v_type, m_type),
        (WHOLE,) * 2,
        scratch=(work,),
        aliases={0: 0},
        name="first",
    )
    early = lax.ppermute(early, "line", far)
    state = (v_type, s_type, r_type)
    results = tuple(jax.ShapeDtypeStruct(x.shape, f32) for x in (velocity, stress, memory))
    same = {0: 0, 1: 1, 2: 2}
    missing = None
    for step in range(STEPS):
        more = step < STEPS - 1
        ins = tuple(in_vmem(x) for x in (V, S, R, coef, force, surface, msg_near))
        outs = state + ((m_type,) if more else results)
        V, S, R, *msg = call(
            functools.partial(near_kernel, step, window),
            ins,
            (WHOLE,) * len(ins),
            outs,
            (WHOLE,) * 4 if more else (WHOLE,) * 3 + (ANYWHERE,) * 3,
            scratch=(ghost,) if more else (dma((3,)), ghost),
            aliases=same,
            name="near" + str(step),
        )
        if more:
            msg_near = lax.ppermute(msg[0], "line", near)
        ins = (V, S, R, coef, force, surface, msg_far) + ((missing,) if step else ())
        ins = tuple(in_vmem(x) for x in ins)
        if more:
            outs = state + (m_type,) + ((m_type,) if step < STEPS - 2 else ())
            V, S, R, missing, *msg = call(
                functools.partial(far_kernel, step, window),
                ins,
                (WHOLE,) * len(ins),
                outs,
                (WHOLE,) * len(outs),
                scratch=(ghost, work),
                aliases=same,
                name="far" + str(step),
            )
            msg_far = early
            if msg:
                early = lax.ppermute(msg[0], "line", far)
    ends = call(
        functools.partial(last_kernel, STEPS - 1, window),
        ins + tuple(msg),
        (WHOLE,) * 8 + (ANYWHERE,) * 3,
        state + results,
        (WHOLE,) * 3 + (ANYWHERE,) * 3,
        scratch=(ghost, dma((3,))),
        aliases={**same, 8: 3, 9: 4, 10: 5},
        name="last",
    )
    return ends[3:]


def solution(mesh):
    placed = (
        P(None, ("runs", "line"), None, None),
        P(None, ("runs", "line"), None, None),
        P(None, ("runs", "line"), None, None),
        P(("runs", "line"), None),
        P("line", "runs", None),
        P(),
        P(),
        P(),
        P(),
        P(),
        P(),
        P(None, ("runs", "line")),
        P(None, ("runs", "line")),
        P(),
    )
    return jax.shard_map(
        body,
        mesh=mesh,
        in_specs=placed,
        out_specs=(
            P(None, ("runs", "line"), None, None),
            P(None, ("runs", "line"), None, None),
            P(None, ("runs", "line"), None, None),
        ),
        check_vma=False,
    )
```

```python
import functools

import jax
import jax.numpy as jnp
import numpy as np
from jax import lax
from jax.experimental import pallas as pl
from jax.experimental.pallas import tpu as pltpu
from jax.sharding import PartitionSpec as P

STEPS = 6
FY = 8
FZ = 64
DT = 0.25
PAD = 8
ROWS = 16
UNROLL = 8
VMEM_LIMIT = 32 * 1024 * 1024

C_B, C_B0, C_B1, C_M0, C_M1, C_LAM, C_MU2, C_MU, C_K1, C_K2, C_K2H, C_L0 = range(12)
N_COEF = 16

VX, VY, VZ = range(3)
XX, YY, ZZ, XY, XZ, YZ = range(6)


def lane_roll(x, shift):
    return pltpu.roll(x, shift % x.shape[-1], x.ndim - 1)


def before(x):
    return lane_roll(x, 1)


def after(x):
    return lane_roll(x, -1)


def over_rows(count, work):
    def step(i, carry):
        work(pl.multiple_of(i * ROWS, ROWS))
        return carry

    lax.fori_loop(0, count // ROWS, step, 0, unroll=UNROLL)


def coefs(coef_ref, ids):
    return [coef_ref[i : i + 1, :] for i in ids]


def place():
    index = lax.axis_index("line")
    return lax.rem(index, 2) == 0, index > 0, index < lax.axis_size("line") - 1


def spans(r):
    return pl.ds(PAD + r, ROWS), pl.ds(PAD + r - 1, ROWS), pl.ds(PAD + r + 1, ROWS), pl.ds(r, ROWS)


def zero_edges(ref):
    across = ref.shape[-2] - 2 * PAD
    edge = jnp.zeros((PAD, ref.shape[-1]), jnp.float32)
    for where in np.ndindex(*ref.shape[:-2]):
        ref[(*where, pl.ds(0, PAD))] = edge
        ref[(*where, pl.ds(PAD + across, PAD))] = edge


def add_force(ref, index, force, which, first_row):
    rows = pl.ds(first_row, 16)
    ref[(*index, rows)] = ref[(*index, rows)] + force[which]


def pre_ahead(V, S, coef_ref, msg, force, window):
    b, b0 = coefs(coef_ref, (C_B, C_B0))

    def work(r):
        here, up, _, out = spans(r)
        sxy, sxz = S[XY, 1, here], S[XZ, 1, here]
        px = V[VX, 1, here] + b * (sxy - S[XY, 1, up] + sxz - S[XX, 1, here]) - b0 * before(sxz)
        V[VX, 1, here] = px
        if msg is not None:
            msg[0, out] = sxy
            msg[1, out] = sxz
            msg[2, out] = px

    over_rows(V.shape[2] - 2 * PAD, work)
    if force is not None:
        add_force(V, (VX, 1), force, (VX, 1), PAD + window)
        if msg is not None:
            add_force(msg, (2,), force, (VX, 1), window)


def pre_behind(V, S, coef_ref, msg, force, window):
    b, b0, b1 = coefs(coef_ref, (C_B, C_B0, C_B1))

    def work(r):
        here, up, down, out = spans(r)
        syz, szz = S[YZ, 0, here], S[ZZ, 0, here]
        qy = V[VY, 0, here] + b * (S[XY, 0, here] + S[YY, 0, down] - S[YY, 0, here] + syz) - b0 * before(syz)
        qz = V[VZ, 0, here] + b * (S[XZ, 0, here] + syz - S[YZ, 0, up] - szz) + b1 * after(szz)
        V[VY, 0, here] = qy
        V[VZ, 0, here] = qz
        if msg is not None:
            msg[0, out] = S[XX, 0, here]
            msg[1, out] = qy
            msg[2, out] = qz

    over_rows(V.shape[2] - 2 * PAD, work)
    if force is not None:
        add_force(V, (VY, 0), force, (VY, 0), PAD + window)
        add_force(V, (VZ, 0), force, (VZ, 0), PAD + window)
        if msg is not None:
            add_force(msg, (1,), force, (VY, 0), window)
            add_force(msg, (2,), force, (VZ, 0), window)


def inner(V, S, coef_ref, force, window):
    b, b0, b1 = coefs(coef_ref, (C_B, C_B0, C_B1))

    def work(r):
        here, up, down, _ = spans(r)
        sxy, sxz = S[XY, 0, here], S[XZ, 0, here]
        V[VX, 0, here] = (
            V[VX, 0, here]
            + b * (S[XX, 1, here] - S[XX, 0, here] + sxy - S[XY, 0, up] + sxz)
            - b0 * before(sxz)
        )
        syz, szz = S[YZ, 1, here], S[ZZ, 1, here]
        V[VY, 1, here] = (
            V[VY, 1, here]
            + b * (S[XY, 1, here] - sxy + S[YY, 1, down] - S[YY, 1, here] + syz)
            - b0 * before(syz)
        )
        V[VZ, 1, here] = (
            V[VZ, 1, here]
            + b * (S[XZ, 1, here] - sxz + syz - S[YZ, 1, up] - szz)
            + b1 * after(szz)
        )

    over_rows(V.shape[2] - 2 * PAD, work)
    if force is not None:
        add_force(V, (VX, 0), force, (VX, 0), PAD + window)
        add_force(V, (VY, 1), force, (VY, 1), PAD + window)
        add_force(V, (VZ, 1), force, (VZ, 1), PAD + window)


def post(V, S, R, coef_ref, surface, cell, column, behind_x, ahead_y, ahead_z):
    m0, m1, lam, mu2, mu, k1, k2, k2h, l0 = coefs(
        coef_ref, (C_M0, C_M1, C_LAM, C_MU2, C_MU, C_K1, C_K2, C_K2H, C_L0)
    )

    def work(r):
        here, up, down, out = spans(r)
        vx, vy, vz = V[VX, cell, here], V[VY, cell, here], V[VZ, cell, here]
        exx = vx - behind_x(r)
        eyy = vy - V[VY, cell, up]
        ezz = vz - m0 * before(vz)
        exy = V[VX, cell, down] - vx + (ahead_y(r) - vy)
        exz = m1 * after(vx) - vx + (ahead_z(r) - vz)
        eyz = m1 * after(vy) - vy + (V[VZ, cell, down] - vz)
        volume = lam * (exx + eyy + ezz)
        for comp, e in ((XX, exx), (YY, eyy), (ZZ, ezz)):
            old = R[comp, cell, out]
            new = S[comp, cell, here] + (volume + mu2 * e) + DT * old
            if comp == ZZ:
                new = new + l0 * lane_roll(surface[out, :], -column)
            S[comp, cell, here] = new
            R[comp, cell, out] = k1 * old - k2 * e
        for comp, e in ((XY, exy), (XZ, exz), (YZ, eyz)):
            old = R[comp, cell, out]
            S[comp, cell, here] = S[comp, cell, here] + mu * e + DT * old
            R[comp, cell, out] = k1 * old - k2h * e

    over_rows(R.shape[2], work)


def response_behind(V, S, coef_ref, D, W):
    b, b0, b1, m0, m1, lam, mu2, mu = coefs(coef_ref, (C_B, C_B0, C_B1, C_M0, C_M1, C_LAM, C_MU2, C_MU))

    def work(r):
        here, up, down, out = spans(r)
        sxy = S[XY, 1, here]
        vy, vz = -b * sxy, -b * S[XZ, 1, here]
        exx = -V[VX, 1, here]
        eyy = b * (S[XY, 1, up] - sxy)
        ezz = vz - m0 * before(vz)
        volume = lam * (exx + eyy + ezz)
        dyy, dzz = volume + mu2 * eyy, volume + mu2 * ezz
        dyz = mu * (m1 * after(vy) - vy - b * S[XZ, 1, down] - vz)
        W[0, here] = dyy
        W[1, here] = dyz
        D[0, out] = volume + mu2 * exx
        D[1, out] = vy + b * (dyz - mu * vy - dyy) - b0 * before(dyz)
        D[2, out] = vz + b * (dyz - mu * vz - dzz) + b1 * after(dzz)

    over_rows(D.shape[1], work)

    def rest(r):
        _, up, down, out = spans(r)
        D[1, out] = D[1, out] + b * W[0, down]
        D[2, out] = D[2, out] - b * W[1, up]

    over_rows(D.shape[1], rest)


def response_ahead(V, S, coef_ref, D, W):
    b, b0, m1, lam, mu2, mu = coefs(coef_ref, (C_B, C_B0, C_M1, C_LAM, C_MU2, C_MU))

    def work(r):
        here, _, down, out = spans(r)
        vx = b * S[XX, 0, here]
        dxy = mu * (b * S[XX, 0, down] - vx + V[VY, 0, here])
        dxz = mu * (m1 * after(vx) - vx + V[VZ, 0, here])
        W[0, here] = dxy
        D[0, out] = dxy
        D[1, out] = dxz
        D[2, out] = vx + b * (dxy + dxz - (lam + mu2) * vx) - b0 * before(dxz)

    over_rows(D.shape[1], work)

    def rest(r):
        _, up, _, out = spans(r)
        D[2, out] = D[2, out] - b * W[0, up]

    over_rows(D.shape[1], rest)


def early_ahead(V, S, R, coef_ref, msg, W, force, window, ready):
    b, b0, m0, m1, lam, mu2, mu = coefs(coef_ref, (C_B, C_B0, C_M0, C_M1, C_LAM, C_MU2, C_MU))

    def work(r):
        here, up, down, out = spans(r)
        vx, vy, vz = V[VX, 1, here], V[VY, 1, here], V[VZ, 1, here]
        exx = vx - V[VX, 0, here]
        volume = lam * (exx + (vy - V[VY, 1, up]) + (vz - m0 * before(vz)))
        sxx = S[XX, 1, here] + (volume + mu2 * exx) + DT * R[XX, 1, out]
        sxy = S[XY, 1, here] + mu * (V[VX, 1, down] - vx - vy) + DT * R[XY, 1, out]
        sxz = S[XZ, 1, here] + mu * (m1 * after(vx) - vx - vz) + DT * R[XZ, 1, out]
        W[0, here] = sxy
        msg[0, out] = sxy
        msg[1, out] = sxz
        msg[2, out] = vx + b * (sxy + sxz - sxx) - b0 * before(sxz)

    over_rows(msg.shape[1], work)
    ready(0)
    ready(1)

    def rest(r):
        _, up, _, out = spans(r)
        msg[2, out] = msg[2, out] - b * W[0, up]

    over_rows(msg.shape[1], rest)
    add_force(msg, (2,), force, (VX, 1), window)
    ready(2)


def early_behind(V, S, R, coef_ref, surface, column, msg, W, force, window, ready):
    b, b0, b1, m0, m1, lam, mu2, mu, l0 = coefs(
        coef_ref, (C_B, C_B0, C_B1, C_M0, C_M1, C_LAM, C_MU2, C_MU, C_L0)
    )

    def work(r):
        here, up, down, out = spans(r)
        vx, vy, vz = V[VX, 0, here], V[VY, 0, here], V[VZ, 0, here]
        eyy = vy - V[VY, 0, up]
        ezz = vz - m0 * before(vz)
        volume = lam * (vx + eyy + ezz)
        sxx = S[XX, 0, here] + (volume + mu2 * vx) + DT * R[XX, 0, out]
        syy = S[YY, 0, here] + (volume + mu2 * eyy) + DT * R[YY, 0, out]
        szz = S[ZZ, 0, here] + (volume + mu2 * ezz) + DT * R[ZZ, 0, out]
        szz = szz + l0 * lane_roll(surface[out, :], -column)
        sxy = S[XY, 0, here] + mu * (V[VX, 0, down] - vx + (V[VY, 1, here] - vy)) + DT * R[XY, 0, out]
        sxz = S[XZ, 0, here] + mu * (m1 * after(vx) - vx + (V[VZ, 1, here] - vz)) + DT * R[XZ, 0, out]
        syz = S[YZ, 0, here] + mu * (m1 * after(vy) - vy + (V[VZ, 0, down] - vz)) + DT * R[YZ, 0, out]
        W[0, here] = syy
        W[1, here] = syz
        msg[0, out] = sxx
        msg[1, out] = vy + b * (sxy - syy + syz) - b0 * before(syz)
        msg[2, out] = vz + b * (sxz + syz - szz) + b1 * after(szz)

    over_rows(msg.shape[1], work)
    ready(0)

    def rest(r):
        _, up, down, out = spans(r)
        msg[1, out] = msg[1, out] + b * W[0, down]
        msg[2, out] = msg[2, out] - b * W[1, up]

    over_rows(msg.shape[1], rest)
    add_force(msg, (1,), force, (VY, 0), window)
    add_force(msg, (2,), force, (VZ, 0), window)
    ready(1)
    ready(2)


class Outgoing:
    def __init__(self, msg, out, sems, chunk):
        self.copies = [pltpu.make_async_copy(msg.at[i], out.at[chunk, i], sems.at[i]) for i in range(3)]

    def ready(self, i):
        self.copies[i].start()

    def finish(self):
        for copy in self.copies:
            copy.wait()


def ahead_bond(V, S, R, coef_ref, force, surface, msg, missing, G, step, window, unforced=0, respond=None):
    (b,) = coefs(coef_ref, (C_B,))
    _, _, has_ahead = place()

    def got(i, out):
        plane = msg[i, out] if missing is None else msg[i, out] + missing[i, out]
        return jnp.where(has_ahead, plane, 0.0)

    def work(r):
        here, _, _, out = spans(r)
        V[VX, 1, here] = V[VX, 1, here] + b * got(0, out)
        G[0, out] = jnp.where(has_ahead, got(1, out) - b * S[XY, 1, here], 0.0)
        G[1, out] = jnp.where(has_ahead, got(2, out) - b * S[XZ, 1, here], 0.0)

    over_rows(R.shape[2], work)
    if step < unforced:
        add_force(G, (0,), force, (VY, 2), window)
        add_force(G, (1,), force, (VZ, 2), window)
    if respond is not None:
        respond()
    post(
        V, S, R, coef_ref, surface, 1, 2 * step + 1,
        lambda r: V[VX, 0, pl.ds(PAD + r, ROWS)],
        lambda r: G[0, pl.ds(r, ROWS)],
        lambda r: G[1, pl.ds(r, ROWS)],
    )


def behind_bond(V, S, R, coef_ref, force, surface, msg, missing, G, step, window, unforced=0, respond=None):
    (b,) = coefs(coef_ref, (C_B,))
    _, has_behind, _ = place()

    def got(i, out):
        plane = msg[i, out] if missing is None else msg[i, out] + missing[i, out]
        return jnp.where(has_behind, plane, 0.0)

    def work(r):
        here, _, _, out = spans(r)
        V[VY, 0, here] = V[VY, 0, here] - b * got(0, out)
        V[VZ, 0, here] = V[VZ, 0, here] - b * got(1, out)
        G[0, out] = jnp.where(has_behind, got(2, out) + b * S[XX, 0, here], 0.0)

    over_rows(R.shape[2], work)
    if step < unforced:
        add_force(G, (0,), force, (VX, 2), window)
    if respond is not None:
        respond()
    post(
        V, S, R, coef_ref, surface, 0, 2 * step,
        lambda r: G[0, pl.ds(r, ROWS)],
        lambda r: V[VY, 1, pl.ds(PAD + r, ROWS)],
        lambda r: V[VZ, 1, pl.ds(PAD + r, ROWS)],
    )


def start_kernel(
    velocity, stress, memory, layer_in, lam_in, mu_in, buoy_in, rate_in, defect_in, after_this,
    V, S, R, coef_ref, msg_near, msg_far, layer_ref, lam, mu, buoy, rate, defect, sems,
):
    del after_this
    across = velocity.shape[2]
    inside = pl.ds(PAD, across)
    pairs = [
        (layer_in, layer_ref), (lam_in, lam), (mu_in, mu), (buoy_in, buoy), (rate_in, rate), (defect_in, defect),
    ]
    pairs += [(stress.at[i], S.at[i, :, inside]) for i in range(6)]
    pairs += [(velocity.at[i], V.at[i, :, inside]) for i in range(3)]
    pairs += [(memory.at[i], R.at[i]) for i in range(6)]
    copies = [pltpu.make_async_copy(*pair, sems.at[i]) for i, pair in enumerate(pairs)]
    for copy in copies:
        copy.start()
    zero_edges(V)
    zero_edges(S)
    for copy in copies[:6]:
        copy.wait()
    layer = layer_ref[...]

    def per_depth(table):
        row = jnp.zeros(layer.shape, jnp.float32)
        for level in range(table.shape[0]):
            row = jnp.where(layer == level, table[level], row)
        return row

    lane = lax.broadcasted_iota(jnp.int32, layer.shape, 1)
    not_first = jnp.where(lane > 0, 1.0, 0.0).astype(jnp.float32)
    not_last = jnp.where(lane < layer.shape[1] - 1, 1.0, 0.0).astype(jnp.float32)
    b = DT * per_depth(buoy)
    two_mu = (2.0 * DT) * per_depth(mu)
    decay = DT * per_depth(rate)
    drop = 2.0 * decay * per_depth(defect)
    for row, value in (
        (C_B, b),
        (C_B0, b * not_first),
        (C_B1, b * not_last),
        (C_M0, not_first),
        (C_M1, not_last),
        (C_LAM, DT * per_depth(lam)),
        (C_MU2, two_mu),
        (C_MU, 0.5 * two_mu),
        (C_K1, 1.0 - decay),
        (C_K2, drop),
        (C_K2H, 0.5 * drop),
        (C_L0, DT * (1.0 - not_first)),
    ):
        coef_ref[row : row + 1, :] = value
    coef_ref[12:16, :] = jnp.zeros((4, layer.shape[1]), jnp.float32)
    for copy in copies[6:15]:
        copy.wait()
    even, _, _ = place()

    @pl.when(even)
    def _():
        pre_ahead(V, S, coef_ref, msg_near, None, 0)
        pre_behind(V, S, coef_ref, msg_far, None, 0)

    @pl.when(jnp.logical_not(even))
    def _():
        pre_behind(V, S, coef_ref, msg_near, None, 0)
        pre_ahead(V, S, coef_ref, msg_far, None, 0)

    for copy in copies[15:]:
        copy.wait()


def first_kernel(window, V0, S, R, coef_ref, force, surface, V, out, msg, W, sems):
    even, _, _ = place()
    zero_edges(W)
    now, then = force.at[0], force.at[1]
    add_force(V, (VX, 1), now, (VX, 1), PAD + window)
    add_force(V, (VY, 0), now, (VY, 0), PAD + window)
    add_force(V, (VZ, 0), now, (VZ, 0), PAD + window)
    inner(V, S, coef_ref, now, window)

    @pl.when(even)
    def _():
        outgoing = Outgoing(msg, out, sems, 0)
        early_behind(V, S, R, coef_ref, surface, 0, msg, W, then, window, outgoing.ready)
        outgoing.finish()

    @pl.when(jnp.logical_not(even))
    def _():
        outgoing = Outgoing(msg, out, sems, 1)
        early_ahead(V, S, R, coef_ref, msg, W, then, window, outgoing.ready)
        outgoing.finish()


def write_out(V, S, R, results, sems, cell):
    inside = pl.ds(PAD, R.shape[2])
    pairs = [(V.at[:, cell, inside], results[0]), (S.at[:, cell, inside], results[1]), (R.at[:, cell], results[2])]
    copies = [
        pltpu.make_async_copy(source, result.at[:, cell], sems.at[i]) for i, (source, result) in enumerate(pairs)
    ]
    for copy in copies:
        copy.start()
    for copy in copies:
        copy.wait()


def near_kernel(step, window, V0, S0, R0, coef_ref, force, surface, msg, V, S, R, *rest):
    G = rest[-1]
    even, _, _ = place()
    more = step < STEPS - 1

    @pl.when(even)
    def _():
        ahead_bond(V, S, R, coef_ref, force.at[step], surface, msg, None, G, step, window, 1)
        if more:
            pre_ahead(V, S, coef_ref, rest[0], force.at[step + 1], window)
        else:
            write_out(V, S, R, rest[:3], rest[-2], 1)

    @pl.when(jnp.logical_not(even))
    def _():
        behind_bond(V, S, R, coef_ref, force.at[step], surface, msg, None, G, step, window, 1)
        if more:
            pre_behind(V, S, coef_ref, rest[0], force.at[step + 1], window)
        else:
            write_out(V, S, R, rest[:3], rest[-2], 0)


def far_kernel(step, window, V0, S0, R0, coef_ref, force, surface, msg, *rest):
    rest = list(rest)
    missing = rest.pop(0) if step > 0 else None
    V, S, R, D = rest[:4]
    more = step < STEPS - 2
    if more:
        out, G, W, early, sems = rest[4:]
    else:
        G, W = rest[4:]
    even, _, _ = place()
    zero_edges(W)
    here, then = force.at[step], force.at[step + 1]

    @pl.when(even)
    def _():
        behind_bond(
            V, S, R, coef_ref, here, surface, msg if step == 0 else msg.at[0], missing, G, step, window, 1,
            lambda: response_ahead(V, S, coef_ref, D, W),
        )
        pre_behind(V, S, coef_ref, None, then, window)

    @pl.when(jnp.logical_not(even))
    def _():
        ahead_bond(
            V, S, R, coef_ref, here, surface, msg if step == 0 else msg.at[1], missing, G, step, window, 1,
            lambda: response_behind(V, S, coef_ref, D, W),
        )
        pre_ahead(V, S, coef_ref, None, then, window)

    inner(V, S, coef_ref, then, window)
    if more:
        later = force.at[step + 2]

        @pl.when(even)
        def _():
            outgoing = Outgoing(early, out, sems, 0)
            early_behind(
                V, S, R, coef_ref, surface, 2 * (step + 1), early, W, later, window, outgoing.ready
            )
            outgoing.finish()

        @pl.when(jnp.logical_not(even))
        def _():
            outgoing = Outgoing(early, out, sems, 1)
            early_ahead(V, S, R, coef_ref, early, W, later, window, outgoing.ready)
            outgoing.finish()


def last_kernel(step, window, V0, S0, R0, coef_ref, force, surface, msg, missing, v0, s0, r0, V, S, R, *rest):
    *results, G, sems = rest
    even, _, _ = place()
    here = force.at[step]

    @pl.when(even)
    def _():
        behind_bond(V, S, R, coef_ref, here, surface, msg.at[0], missing, G, step, window)
        write_out(V, S, R, results, sems, 0)

    @pl.when(jnp.logical_not(even))
    def _():
        ahead_bond(V, S, R, coef_ref, here, surface, msg.at[1], missing, G, step, window)
        write_out(V, S, R, results, sems, 1)


ENTRY_ROW, TRUCK_ROW = 36, 40
GROUP = 8


def pack_kernel(
    record, loads_in, entries_in, cells_in, piers_in, own, loads, steps_table, piers, entries, cells, sems
):
    panel = record.shape[1]
    slots, lanes = loads.shape
    steps = entries.shape[0]
    pairs = [(record, own.at[:, pl.ds(0, panel)]), (loads_in, loads), (entries_in, entries), (cells_in, cells)]
    pairs.append((piers_in, piers))
    copies = [pltpu.make_async_copy(*pair, sems.at[i]) for i, pair in enumerate(pairs)]
    for copy in copies:
        copy.start()
    own[:, panel:] = jnp.zeros((own.shape[0], own.shape[1] - panel), jnp.float32)
    steps_table[...] = jnp.zeros(steps_table.shape, jnp.float32)
    for copy in copies:
        copy.wait()
    steps_table[0:steps, 0:slots] = entries[...].astype(jnp.float32)
    steps_table[8 : 8 + steps, 0:slots] = cells[...].astype(jnp.float32)
    blocks = [loads[8 * i : 8 * i + 8, :] for i in range(slots // 8)] + [steps_table[0:8, :]]
    for i, block in enumerate(blocks):
        own[0:8, panel + i * lanes : panel + (i + 1) * lanes] = block


def lane_blocks(table, width):
    return sum(lane_roll(table[s : s + 1, :], s * width) for s in range(STEPS))


def split_kernel(panel, slots, own, behind, cells, after_this, out):
    del after_this
    tiles, _, lanes = out.shape
    pieces = panel // lanes
    third = pieces // 3
    cell_of = cells[...]
    me = lax.axis_index("line")
    group, mine = lax.div(me, tiles), lax.rem(me, tiles)
    piers = cell_of.shape[1]
    row = lax.broadcasted_iota(jnp.int32, (3 * tiles, lanes), 0)
    j = lax.rem(row, 3)
    first = (lax.div(row, 3) + group * tiles) * 2
    cell_x, cell_yz = first + jnp.where(j == 2, -1, j), first + j
    record = jnp.where(group == 0, own[:, :panel], behind[:, :panel])

    def hits(cell):
        return [jnp.where(cell == cell_of[0:1, p : p + 1], 1.0, 0.0).astype(jnp.float32) for p in range(piers)]

    hit_x, hit_yz = hits(cell_x), hits(cell_yz)

    def share(m):
        hit = hit_x if m < third else hit_yz
        return sum(hit[p] * record[p : p + 1, m * lanes : (m + 1) * lanes] for p in range(piers))

    parts = [share(m) for m in range(pieces)]

    def trucks(source):
        blocks = [source[0:8, panel + i * lanes : panel + (i + 1) * lanes] for i in range(slots // 8 + 1)]
        return blocks[:-1], lane_blocks(blocks[-1], slots)

    own_rows, own_entry = trucks(own)
    far_rows, far_entry = trucks(behind)
    for tile in range(tiles):
        these = slice(3 * tile, 3 * tile + 3)
        for m in range(pieces):
            out[tile, 3 * m : 3 * m + 3, :] = parts[m][these, :]
        passed = mine < tile
        out[tile, ENTRY_ROW : ENTRY_ROW + 1, :] = jnp.where(passed, own_entry, far_entry)
        for i in range(slots // 8):
            at = TRUCK_ROW + 8 * i
            out[tile, at : at + 8, :] = jnp.where(passed, own_rows[i], far_rows[i])


def prepare_kernel(parts, loads, steps_table, force, surface, table, rows_out):
    steps, comps, width = force.shape[:3]
    lanes = parts.shape[2]
    force[...] = jnp.zeros(force.shape, jnp.float32)
    per = ENTRY_ROW // (comps * width)
    lane = lax.broadcasted_iota(jnp.int32, (per, lanes), 1)
    scale = jnp.where(lane < FZ, DT, 0.0).astype(jnp.float32)
    for s in range(steps):
        for comp in range(comps):
            for cell in range(width):
                panel = parts[s, pl.ds(comp * per * width + cell, per, stride=width), :]
                force[s, comp, cell, pl.ds(4, per, stride=2), :] = scale * panel
                force[s, comp, cell, pl.ds(5, per, stride=2), :] = scale * lane_roll(panel, FZ)

    slots = loads.shape[0]
    tiles = parts.shape[0]
    mine = lax.rem(lax.axis_index("line"), tiles)
    table[...] = jnp.zeros(table.shape, jnp.float32)
    table[0:1, :] = lane_blocks(steps_table[0:8, :], slots)
    table[STEPS + 1 : STEPS + 2, :] = lane_blocks(steps_table[8:16, :], slots)
    rows = [loads[...]]
    for k in range(1, STEPS + 1):
        source = lax.rem(mine + (tiles - k), tiles)
        rows.append(parts[source, TRUCK_ROW : TRUCK_ROW + slots, :])
        table[k : k + 1, :] = parts[source, ENTRY_ROW : ENTRY_ROW + 1, :]
    columns = table[...].T
    rows_out[...] = jnp.zeros(rows_out.shape, jnp.float32)
    for s in range(STEPS):
        block = slice(s * slots, (s + 1) * slots)
        moved = []
        for k in range(STEPS - s):
            entry = jnp.broadcast_to(columns[block, k : k + 1], rows[k].shape)
            new = rows[k]
            for slot in range(slots):
                new = jnp.where(entry == float(slot), rows[k + 1][slot : slot + 1, :], new)
            moved.append(new)
        rows = moved
        cell = jnp.broadcast_to(columns[block, STEPS + 1 : STEPS + 2], rows[0].shape)
        for c in range(2):
            load = jnp.sum(jnp.where(cell == float(c), rows[0], 0.0), axis=0, keepdims=True)
            rows_out[2 * s + c : 2 * s + c + 1, :] = load
    surface[...] = rows_out[...].T


def in_vmem(x):
    return pltpu.with_memory_space_constraint(x, pltpu.VMEM)


WHOLE = pl.BlockSpec(memory_space=pltpu.VMEM)
SCALARS = pl.BlockSpec(memory_space=pltpu.SMEM)
ANYWHERE = pl.BlockSpec(memory_space=pl.ANY)


def call(kernel, ins, specs, outs, out_specs, scratch=(), aliases=None, name=None, cost=1):
    return pl.pallas_call(
        kernel,
        out_shape=outs,
        in_specs=specs,
        out_specs=out_specs,
        scratch_shapes=list(scratch),
        input_output_aliases=aliases or {},
        compiler_params=pltpu.CompilerParams(vmem_limit_bytes=VMEM_LIMIT),
        cost_estimate=pl.CostEstimate(flops=cost, bytes_accessed=cost, transcendentals=0),
        name=name,
    )(*ins)


def body(
    velocity, stress, memory, truck_loads, pier_panels,
    lame_lambda, lame_mu, buoyancy, relax_rate, defect_mu, layer,
    truck_entry, truck_cell, pier_cell,
):
    tiles = lax.axis_size("line")
    width_x, across, depth = velocity.shape[1:]
    slots = truck_loads.shape[0]
    window = (across - FY) // 2 - 4
    f32 = jnp.float32

    near = [(i, i ^ 1) for i in range(tiles) if (i ^ 1) < tiles]
    far = [(i, i + 1) for i in range(1, tiles - 1, 2)] + [(i + 1, i) for i in range(1, tiles - 1, 2)]

    padded = across + 2 * PAD
    v_type = pltpu.VMEM((3, width_x, padded, depth), f32)
    s_type = pltpu.VMEM((6, width_x, padded, depth), f32)
    r_type = pltpu.VMEM((6, width_x, across, depth), f32)
    c_type = pltpu.VMEM((N_COEF, depth), f32)
    m_type = pltpu.VMEM((3, across, depth), f32)
    ghost = pltpu.VMEM((2, across, depth), f32)
    work = pltpu.VMEM((2, padded, depth), f32)

    def ahead_by(x, distance):
        return lax.ppermute(x, "line", [(i, i + distance) for i in range(tiles - distance)])

    runs = lax.axis_size("runs")
    couples = [[run * tiles + i, run * tiles + i + 1] for run in range(runs) for i in range(1, tiles - 1, 2)]
    couples += [
        [run * tiles + end, (run + 1) * tiles + end] for run in range(0, runs, 2) for end in (0, tiles - 1)
    ]

    def swapped(x):
        return lax.all_to_all(x, ("runs", "line"), 0, 0, axis_index_groups=couples, tiled=True)

    def in_hbm(*arrays):
        return tuple(pltpu.with_memory_space_constraint(x, pltpu.HBM) for x in arrays)

    dma = pltpu.SemaphoreType.DMA
    piers, panel = pier_panels.shape[1:]
    own, loads, steps_table, pier_row = call(
        pack_kernel,
        in_hbm(pier_panels[0], truck_loads, truck_entry, truck_cell, pier_cell[None, :]),
        (ANYWHERE,) * 5,
        (
            pltpu.VMEM((piers, panel + (slots // 8 + 1) * depth), f32),
            pltpu.VMEM((slots, depth), f32),
            pltpu.VMEM((16, depth), f32),
            pltpu.VMEM((1, piers), jnp.int32),
        ),
        (WHOLE,) * 4,
        scratch=(pltpu.VMEM(truck_entry.shape, jnp.int32), pltpu.VMEM(truck_cell.shape, jnp.int32), dma((5,))),
        name="pack",
    )
    behind = ahead_by(own, GROUP)
    reach = 2 * GROUP
    index = lax.axis_index("line")
    while reach < tiles:
        record = jnp.where(index < GROUP, own, behind)[:, :panel]
        record = jnp.where(index < reach, record, ahead_by(record, reach))
        behind = jnp.concatenate([record, behind[:, panel:]], axis=1)
        reach *= 2
    tables = (lame_lambda, lame_mu, buoyancy, relax_rate, defect_mu)
    V, S, R, coef, msg_near, msg_far = call(
        start_kernel,
        in_hbm(velocity, stress, memory, layer[None, :], *tables) + (steps_table,),
        (ANYWHERE,) * 10,
        (v_type, s_type, r_type, c_type, m_type, m_type),
        (WHOLE,) * 6,
        scratch=(
            pltpu.VMEM((1, depth), jnp.int32), *(pltpu.SMEM(table.shape, f32) for table in tables), dma((21,)),
        ),
        name="start",
        cost=8 * 1024 * 1024,
    )
    msg_far = lax.ppermute(msg_far, "line", far)
    msg_near = lax.ppermute(msg_near, "line", near)
    parts = call(
        functools.partial(split_kernel, panel, slots),
        (own, behind, in_vmem(pier_row), coef),
        (WHOLE,) * 3 + (ANYWHERE,),
        jax.ShapeDtypeStruct((GROUP, TRUCK_ROW + slots, depth), f32),
        WHOLE,
        name="split",
    )
    groups = [list(range(at, at + GROUP)) for at in range(0, tiles, GROUP)]
    parts = lax.all_to_all(parts, "line", 0, 0, axis_index_groups=groups, tiled=True)
    force, surface = call(
        prepare_kernel,
        (parts, in_vmem(loads), in_vmem(steps_table)),
        (WHOLE,) * 3,
        (pltpu.VMEM((STEPS, 3, 3, 16, depth), f32), pltpu.VMEM((across, depth), f32)),
        (WHOLE,) * 2,
        scratch=(pltpu.VMEM((depth, depth), f32), pltpu.VMEM((depth, across), f32)),
        name="prepare",
    )
    chunks = jax.ShapeDtypeStruct((2, 3, across, depth), f32)
    V, early = call(
        functools.partial(first_kernel, window),
        tuple(in_vmem(x) for x in (V, S, R, coef, force, surface)),
        (WHOLE,) * 6,
        (v_type, chunks),
        (WHOLE, ANYWHERE),
        scratch=(m_type, work, dma((3,))),
        aliases={0: 0},
        name="first",
    )
    early = swapped(early)
    state = (v_type, s_type, r_type)
    results = tuple(jax.ShapeDtypeStruct(x.shape, f32) for x in (velocity, stress, memory))
    same = {0: 0, 1: 1, 2: 2}
    missing = None
    for step in range(STEPS):
        more = step < STEPS - 1
        ins = tuple(in_vmem(x) for x in (V, S, R, coef, force, surface, msg_near))
        outs = state + ((m_type,) if more else results)
        V, S, R, *msg = call(
            functools.partial(near_kernel, step, window),
            ins,
            (WHOLE,) * len(ins),
            outs,
            (WHOLE,) * 4 if more else (WHOLE,) * 3 + (ANYWHERE,) * 3,
            scratch=(ghost,) if more else (dma((3,)), ghost),
            aliases=same,
            name="near" + str(step),
        )
        if more:
            msg_near = lax.ppermute(msg[0], "line", near)
        ins = (V, S, R, coef, force, surface, msg_far) + ((missing,) if step else ())
        ins = tuple(in_vmem(x) for x in ins)
        if more:
            sends = step < STEPS - 2
            outs = state + (m_type,) + ((chunks,) if sends else ())
            V, S, R, missing, *msg = call(
                functools.partial(far_kernel, step, window),
                ins,
                (WHOLE,) * len(ins),
                outs,
                (WHOLE,) * 4 + ((ANYWHERE,) if sends else ()),
                scratch=(ghost, work) + ((m_type, dma((3,))) if sends else ()),
                aliases=same,
                name="far" + str(step),
            )
            msg_far = early
            if sends:
                early = swapped(msg[0])
    ends = call(
        functools.partial(last_kernel, STEPS - 1, window),
        ins + tuple(msg),
        (WHOLE,) * 8 + (ANYWHERE,) * 3,
        state + results,
        (WHOLE,) * 3 + (ANYWHERE,) * 3,
        scratch=(ghost, dma((3,))),
        aliases={**same, 8: 3, 9: 4, 10: 5},
        name="last",
    )
    return ends[3:]


def solution(mesh):
    placed = (
        P(None, ("runs", "line"), None, None),
        P(None, ("runs", "line"), None, None),
        P(None, ("runs", "line"), None, None),
        P(("runs", "line"), None),
        P("line", "runs", None),
        P(),
        P(),
        P(),
        P(),
        P(),
        P(),
        P(None, ("runs", "line")),
        P(None, ("runs", "line")),
        P(),
    )
    return jax.shard_map(
        body,
        mesh=mesh,
        in_specs=placed,
        out_specs=(
            P(None, ("runs", "line"), None, None),
            P(None, ("runs", "line"), None, None),
            P(None, ("runs", "line"), None, None),
        ),
        check_vma=False,
    )
```

```python
import functools

import jax
import jax.numpy as jnp
import numpy as np
from jax import lax
from jax.experimental import pallas as pl
from jax.experimental.pallas import tpu as pltpu
from jax.sharding import PartitionSpec as P

STEPS = 6
FY = 8
FZ = 64
DT = 0.25
PAD = 8
ROWS = 16
UNROLL = 8
VMEM_LIMIT = 32 * 1024 * 1024

C_B, C_B0, C_B1, C_M0, C_M1, C_LAM, C_MU2, C_MU, C_K1, C_K2, C_K2H, C_L0 = range(12)
N_COEF = 16

VX, VY, VZ = range(3)
XX, YY, ZZ, XY, XZ, YZ = range(6)


def lane_roll(x, shift):
    return pltpu.roll(x, shift % x.shape[-1], x.ndim - 1)


def before(x):
    return lane_roll(x, 1)


def after(x):
    return lane_roll(x, -1)


def over_rows(count, work):
    def step(i, carry):
        work(pl.multiple_of(i * ROWS, ROWS))
        return carry

    lax.fori_loop(0, count // ROWS, step, 0, unroll=UNROLL)


def coefs(coef_ref, ids):
    return [coef_ref[i : i + 1, :] for i in ids]


def place():
    index = lax.axis_index("line")
    return lax.rem(index, 2) == 0, index > 0, index < lax.axis_size("line") - 1


def spans(r):
    return pl.ds(PAD + r, ROWS), pl.ds(PAD + r - 1, ROWS), pl.ds(PAD + r + 1, ROWS), pl.ds(r, ROWS)


def zero_edges(ref):
    across = ref.shape[-2] - 2 * PAD
    edge = jnp.zeros((PAD, ref.shape[-1]), jnp.float32)
    for where in np.ndindex(*ref.shape[:-2]):
        ref[(*where, pl.ds(0, PAD))] = edge
        ref[(*where, pl.ds(PAD + across, PAD))] = edge


class Parts:
    def __init__(self, refs):
        self.refs = refs

    def __getitem__(self, at):
        return self.refs[at[0]][at[1]]

    def __setitem__(self, at, value):
        self.refs[at[0]][at[1]] = value


def add_force(ref, index, force, which, first_row):
    rows = pl.ds(first_row, 16)
    ref[(*index, rows)] = ref[(*index, rows)] + force[which]


def pre_ahead(V, S, coef_ref, msg, force, window):
    b, b0 = coefs(coef_ref, (C_B, C_B0))

    def work(r):
        here, up, _, out = spans(r)
        sxy, sxz = S[XY, 1, here], S[XZ, 1, here]
        px = V[VX, 1, here] + b * (sxy - S[XY, 1, up] + sxz - S[XX, 1, here]) - b0 * before(sxz)
        V[VX, 1, here] = px
        if msg is not None:
            msg[0, out] = sxy
            msg[1, out] = sxz
            msg[2, out] = px

    over_rows(V.shape[2] - 2 * PAD, work)
    if force is not None:
        add_force(V, (VX, 1), force, (VX, 1), PAD + window)
        if msg is not None:
            add_force(msg, (2,), force, (VX, 1), window)


def pre_behind(V, S, coef_ref, msg, force, window):
    b, b0, b1 = coefs(coef_ref, (C_B, C_B0, C_B1))

    def work(r):
        here, up, down, out = spans(r)
        syz, szz = S[YZ, 0, here], S[ZZ, 0, here]
        qy = V[VY, 0, here] + b * (S[XY, 0, here] + S[YY, 0, down] - S[YY, 0, here] + syz) - b0 * before(syz)
        qz = V[VZ, 0, here] + b * (S[XZ, 0, here] + syz - S[YZ, 0, up] - szz) + b1 * after(szz)
        V[VY, 0, here] = qy
        V[VZ, 0, here] = qz
        if msg is not None:
            msg[0, out] = S[XX, 0, here]
            msg[1, out] = qy
            msg[2, out] = qz

    over_rows(V.shape[2] - 2 * PAD, work)
    if force is not None:
        add_force(V, (VY, 0), force, (VY, 0), PAD + window)
        add_force(V, (VZ, 0), force, (VZ, 0), PAD + window)
        if msg is not None:
            add_force(msg, (1,), force, (VY, 0), window)
            add_force(msg, (2,), force, (VZ, 0), window)


def inner(V, S, coef_ref, force, window):
    b, b0, b1 = coefs(coef_ref, (C_B, C_B0, C_B1))

    def work(r):
        here, up, down, _ = spans(r)
        sxy, sxz = S[XY, 0, here], S[XZ, 0, here]
        V[VX, 0, here] = (
            V[VX, 0, here]
            + b * (S[XX, 1, here] - S[XX, 0, here] + sxy - S[XY, 0, up] + sxz)
            - b0 * before(sxz)
        )
        syz, szz = S[YZ, 1, here], S[ZZ, 1, here]
        V[VY, 1, here] = (
            V[VY, 1, here]
            + b * (S[XY, 1, here] - sxy + S[YY, 1, down] - S[YY, 1, here] + syz)
            - b0 * before(syz)
        )
        V[VZ, 1, here] = (
            V[VZ, 1, here]
            + b * (S[XZ, 1, here] - sxz + syz - S[YZ, 1, up] - szz)
            + b1 * after(szz)
        )

    over_rows(V.shape[2] - 2 * PAD, work)
    if force is not None:
        add_force(V, (VX, 0), force, (VX, 0), PAD + window)
        add_force(V, (VY, 1), force, (VY, 1), PAD + window)
        add_force(V, (VZ, 1), force, (VZ, 1), PAD + window)


def post(V, S, R, coef_ref, surface, cell, column, behind_x, ahead_y, ahead_z):
    m0, m1, lam, mu2, mu, k1, k2, k2h, l0 = coefs(
        coef_ref, (C_M0, C_M1, C_LAM, C_MU2, C_MU, C_K1, C_K2, C_K2H, C_L0)
    )

    def work(r):
        here, up, down, out = spans(r)
        vx, vy, vz = V[VX, cell, here], V[VY, cell, here], V[VZ, cell, here]
        exx = vx - behind_x(r)
        eyy = vy - V[VY, cell, up]
        ezz = vz - m0 * before(vz)
        exy = V[VX, cell, down] - vx + (ahead_y(r) - vy)
        exz = m1 * after(vx) - vx + (ahead_z(r) - vz)
        eyz = m1 * after(vy) - vy + (V[VZ, cell, down] - vz)
        volume = lam * (exx + eyy + ezz)
        for comp, e in ((XX, exx), (YY, eyy), (ZZ, ezz)):
            old = R[comp, cell, out]
            new = S[comp, cell, here] + (volume + mu2 * e) + DT * old
            if comp == ZZ:
                new = new + l0 * lane_roll(surface[out, :], -column)
            S[comp, cell, here] = new
            R[comp, cell, out] = k1 * old - k2 * e
        for comp, e in ((XY, exy), (XZ, exz), (YZ, eyz)):
            old = R[comp, cell, out]
            S[comp, cell, here] = S[comp, cell, here] + mu * e + DT * old
            R[comp, cell, out] = k1 * old - k2h * e

    over_rows(R.shape[2], work)


def response_behind(V, S, coef_ref, D, W):
    b, b0, b1, m0, m1, lam, mu2, mu = coefs(coef_ref, (C_B, C_B0, C_B1, C_M0, C_M1, C_LAM, C_MU2, C_MU))

    def work(r):
        here, up, down, out = spans(r)
        sxy = S[XY, 1, here]
        vy, vz = -b * sxy, -b * S[XZ, 1, here]
        exx = -V[VX, 1, here]
        eyy = b * (S[XY, 1, up] - sxy)
        ezz = vz - m0 * before(vz)
        volume = lam * (exx + eyy + ezz)
        dyy, dzz = volume + mu2 * eyy, volume + mu2 * ezz
        dyz = mu * (m1 * after(vy) - vy - b * S[XZ, 1, down] - vz)
        W[0, here] = dyy
        W[1, here] = dyz
        D[0, out] = volume + mu2 * exx
        D[1, out] = vy + b * (dyz - mu * vy - dyy) - b0 * before(dyz)
        D[2, out] = vz + b * (dyz - mu * vz - dzz) + b1 * after(dzz)

    over_rows(D.shape[1], work)

    def rest(r):
        _, up, down, out = spans(r)
        D[1, out] = D[1, out] + b * W[0, down]
        D[2, out] = D[2, out] - b * W[1, up]

    over_rows(D.shape[1], rest)


def response_ahead(V, S, coef_ref, D, W):
    b, b0, m1, lam, mu2, mu = coefs(coef_ref, (C_B, C_B0, C_M1, C_LAM, C_MU2, C_MU))

    def work(r):
        here, _, down, out = spans(r)
        vx = b * S[XX, 0, here]
        dxy = mu * (b * S[XX, 0, down] - vx + V[VY, 0, here])
        dxz = mu * (m1 * after(vx) - vx + V[VZ, 0, here])
        W[0, here] = dxy
        D[0, out] = dxy
        D[1, out] = dxz
        D[2, out] = vx + b * (dxy + dxz - (lam + mu2) * vx) - b0 * before(dxz)

    over_rows(D.shape[1], work)

    def rest(r):
        _, up, _, out = spans(r)
        D[2, out] = D[2, out] - b * W[0, up]

    over_rows(D.shape[1], rest)


def early_ahead(V, S, R, coef_ref, msg, W, force, window):
    b, b0, m0, m1, lam, mu2, mu = coefs(coef_ref, (C_B, C_B0, C_M0, C_M1, C_LAM, C_MU2, C_MU))

    def work(r):
        here, up, down, out = spans(r)
        vx, vy, vz = V[VX, 1, here], V[VY, 1, here], V[VZ, 1, here]
        exx = vx - V[VX, 0, here]
        volume = lam * (exx + (vy - V[VY, 1, up]) + (vz - m0 * before(vz)))
        sxx = S[XX, 1, here] + (volume + mu2 * exx) + DT * R[XX, 1, out]
        sxy = S[XY, 1, here] + mu * (V[VX, 1, down] - vx - vy) + DT * R[XY, 1, out]
        sxz = S[XZ, 1, here] + mu * (m1 * after(vx) - vx - vz) + DT * R[XZ, 1, out]
        W[0, here] = sxy
        msg[0, out] = sxy
        msg[1, out] = sxz
        msg[2, out] = vx + b * (sxy + sxz - sxx) - b0 * before(sxz)

    over_rows(msg.shape[1], work)

    def rest(r):
        _, up, _, out = spans(r)
        msg[2, out] = msg[2, out] - b * W[0, up]

    over_rows(msg.shape[1], rest)
    if force is not None:
        add_force(msg, (2,), force, (VX, 1), window)


def early_behind(V, S, R, coef_ref, surface, column, msg, W, force, window):
    b, b0, b1, m0, m1, lam, mu2, mu, l0 = coefs(
        coef_ref, (C_B, C_B0, C_B1, C_M0, C_M1, C_LAM, C_MU2, C_MU, C_L0)
    )

    def work(r):
        here, up, down, out = spans(r)
        vx, vy, vz = V[VX, 0, here], V[VY, 0, here], V[VZ, 0, here]
        eyy = vy - V[VY, 0, up]
        ezz = vz - m0 * before(vz)
        volume = lam * (vx + eyy + ezz)
        sxx = S[XX, 0, here] + (volume + mu2 * vx) + DT * R[XX, 0, out]
        syy = S[YY, 0, here] + (volume + mu2 * eyy) + DT * R[YY, 0, out]
        szz = S[ZZ, 0, here] + (volume + mu2 * ezz) + DT * R[ZZ, 0, out]
        if surface is not None:
            szz = szz + l0 * lane_roll(surface[out, :], -column)
        sxy = S[XY, 0, here] + mu * (V[VX, 0, down] - vx + (V[VY, 1, here] - vy)) + DT * R[XY, 0, out]
        sxz = S[XZ, 0, here] + mu * (m1 * after(vx) - vx + (V[VZ, 1, here] - vz)) + DT * R[XZ, 0, out]
        syz = S[YZ, 0, here] + mu * (m1 * after(vy) - vy + (V[VZ, 0, down] - vz)) + DT * R[YZ, 0, out]
        W[0, here] = syy
        W[1, here] = syz
        msg[0, out] = sxx
        msg[1, out] = vy + b * (sxy - syy + syz) - b0 * before(syz)
        msg[2, out] = vz + b * (sxz + syz - szz) + b1 * after(szz)

    over_rows(msg.shape[1], work)

    def rest(r):
        _, up, down, out = spans(r)
        msg[1, out] = msg[1, out] + b * W[0, down]
        msg[2, out] = msg[2, out] - b * W[1, up]

    over_rows(msg.shape[1], rest)
    if force is not None:
        add_force(msg, (1,), force, (VY, 0), window)
        add_force(msg, (2,), force, (VZ, 0), window)


def ahead_bond(V, S, R, coef_ref, force, surface, msg, missing, G, step, window, unforced=0, respond=None):
    (b,) = coefs(coef_ref, (C_B,))
    _, _, has_ahead = place()
    keep = jnp.where(has_ahead, 1.0, 0.0).astype(jnp.float32)

    def got(i, out):
        return msg[i, out] if missing is None else msg[i, out] + missing[i, out]

    def work(r):
        here, _, _, out = spans(r)
        V[VX, 1, here] = V[VX, 1, here] + (keep * b) * got(0, out)
        G[0, out] = keep * (got(1, out) - b * S[XY, 1, here])
        G[1, out] = keep * (got(2, out) - b * S[XZ, 1, here])

    over_rows(R.shape[2], work)
    if step < unforced:
        add_force(G, (0,), force, (VY, 2), window)
        add_force(G, (1,), force, (VZ, 2), window)
    if respond is not None:
        respond()
    post(
        V, S, R, coef_ref, surface, 1, 2 * step + 1,
        lambda r: V[VX, 0, pl.ds(PAD + r, ROWS)],
        lambda r: G[0, pl.ds(r, ROWS)],
        lambda r: G[1, pl.ds(r, ROWS)],
    )


def behind_bond(V, S, R, coef_ref, force, surface, msg, missing, G, step, window, unforced=0, respond=None):
    (b,) = coefs(coef_ref, (C_B,))
    _, has_behind, _ = place()
    keep = jnp.where(has_behind, 1.0, 0.0).astype(jnp.float32)

    def got(i, out):
        return msg[i, out] if missing is None else msg[i, out] + missing[i, out]

    def work(r):
        here, _, _, out = spans(r)
        V[VY, 0, here] = V[VY, 0, here] - (keep * b) * got(0, out)
        V[VZ, 0, here] = V[VZ, 0, here] - (keep * b) * got(1, out)
        G[0, out] = keep * (got(2, out) + b * S[XX, 0, here])

    over_rows(R.shape[2], work)
    if step < unforced:
        add_force(G, (0,), force, (VX, 2), window)
    if respond is not None:
        respond()
    post(
        V, S, R, coef_ref, surface, 0, 2 * step,
        lambda r: G[0, pl.ds(r, ROWS)],
        lambda r: V[VY, 1, pl.ds(PAD + r, ROWS)],
        lambda r: V[VZ, 1, pl.ds(PAD + r, ROWS)],
    )


def start_kernel(
    velocity, stress, memory, layer_in, lam_in, mu_in, buoy_in, rate_in, defect_in, after_this,
    V, S, R, coef_ref, near_x, near_y, near_z, msg_far, layer_ref, lam, mu, buoy, rate, defect, sems,
):
    del after_this
    msg_near = Parts((near_x, near_y, near_z))
    across = velocity.shape[2]
    inside = pl.ds(PAD, across)
    pairs = [
        (layer_in, layer_ref), (lam_in, lam), (mu_in, mu), (buoy_in, buoy), (rate_in, rate), (defect_in, defect),
    ]
    pairs += [(stress.at[i], S.at[i, :, inside]) for i in range(6)]
    pairs += [(velocity.at[i], V.at[i, :, inside]) for i in range(3)]
    pairs += [(memory.at[i], R.at[i]) for i in range(6)]
    copies = [pltpu.make_async_copy(*pair, sems.at[i]) for i, pair in enumerate(pairs)]
    for copy in copies:
        copy.start()
    zero_edges(V)
    zero_edges(S)
    for copy in copies[:6]:
        copy.wait()
    layer = layer_ref[...]

    def per_depth(table):
        row = jnp.zeros(layer.shape, jnp.float32)
        for level in range(table.shape[0]):
            row = jnp.where(layer == level, table[level], row)
        return row

    lane = lax.broadcasted_iota(jnp.int32, layer.shape, 1)
    not_first = jnp.where(lane > 0, 1.0, 0.0).astype(jnp.float32)
    not_last = jnp.where(lane < layer.shape[1] - 1, 1.0, 0.0).astype(jnp.float32)
    b = DT * per_depth(buoy)
    two_mu = (2.0 * DT) * per_depth(mu)
    decay = DT * per_depth(rate)
    drop = 2.0 * decay * per_depth(defect)
    for row, value in (
        (C_B, b),
        (C_B0, b * not_first),
        (C_B1, b * not_last),
        (C_M0, not_first),
        (C_M1, not_last),
        (C_LAM, DT * per_depth(lam)),
        (C_MU2, two_mu),
        (C_MU, 0.5 * two_mu),
        (C_K1, 1.0 - decay),
        (C_K2, drop),
        (C_K2H, 0.5 * drop),
        (C_L0, DT * (1.0 - not_first)),
    ):
        coef_ref[row : row + 1, :] = value
    coef_ref[12:16, :] = jnp.zeros((4, layer.shape[1]), jnp.float32)
    for copy in copies[6:15]:
        copy.wait()
    even, _, _ = place()

    @pl.when(even)
    def _():
        pre_ahead(V, S, coef_ref, msg_near, None, 0)
        pre_behind(V, S, coef_ref, msg_far, None, 0)

    @pl.when(jnp.logical_not(even))
    def _():
        pre_behind(V, S, coef_ref, msg_near, None, 0)
        pre_ahead(V, S, coef_ref, msg_far, None, 0)

    for copy in copies[15:]:
        copy.wait()


def first_kernel(window, V0, S, R, coef_ref, force, surface, V, msg, W):
    even, _, _ = place()
    zero_edges(W)
    now, then = force.at[0], force.at[1]
    add_force(V, (VX, 1), now, (VX, 1), PAD + window)
    add_force(V, (VY, 0), now, (VY, 0), PAD + window)
    add_force(V, (VZ, 0), now, (VZ, 0), PAD + window)
    inner(V, S, coef_ref, now, window)

    @pl.when(even)
    def _():
        early_behind(V, S, R, coef_ref, surface, 0, msg, W, then, window)

    @pl.when(jnp.logical_not(even))
    def _():
        early_ahead(V, S, R, coef_ref, msg, W, then, window)


def results_out(V, S, R, results, sems, cell):
    inside = pl.ds(PAD, R.shape[2])
    pairs = [(V.at[i, cell, inside], results[0].at[i, cell]) for i in range(3)]
    pairs += [(S.at[i, cell, inside], results[1].at[i, cell]) for i in range(6)]
    pairs += [(R.at[i, cell], results[2].at[i, cell]) for i in range(6)]
    return [pltpu.make_async_copy(*pair, sems.at[i]) for i, pair in enumerate(pairs)]


def start_all(copies):
    for copy in copies:
        copy.start()


def wait_all(copies):
    for copy in copies:
        copy.wait()


def near_kernel(step, window, V0, S0, R0, coef_ref, force, surface, msg_x, msg_y, msg_z, V, S, R, *rest):
    G = rest[-1]
    msg = Parts((msg_x, msg_y, msg_z))
    send = Parts(rest[:3])
    even, _, _ = place()
    more = step < STEPS - 1

    @pl.when(even)
    def _():
        ahead_bond(V, S, R, coef_ref, force.at[step], surface, msg, None, G, step, window, 1)
        if more:
            pre_ahead(V, S, coef_ref, send, force.at[step + 1], window)
        else:
            copies = results_out(V, S, R, rest[:3], rest[-2], 1)
            start_all(copies)
            wait_all(copies)

    @pl.when(jnp.logical_not(even))
    def _():
        behind_bond(V, S, R, coef_ref, force.at[step], surface, msg, None, G, step, window, 1)
        if more:
            pre_behind(V, S, coef_ref, send, force.at[step + 1], window)
        else:
            copies = results_out(V, S, R, rest[:3], rest[-2], 0)
            start_all(copies)
            wait_all(copies)


def far_kernel(step, window, V0, S0, R0, coef_ref, force, surface, msg, *rest):
    rest = list(rest)
    missing = rest.pop(0) if step > 0 else None
    V, S, R, D = rest[:4]
    G, W = rest[-2:]
    early = rest[4] if step < STEPS - 2 else None
    even, _, _ = place()
    zero_edges(W)
    here, then = force.at[step], force.at[step + 1]

    @pl.when(even)
    def _():
        behind_bond(
            V, S, R, coef_ref, here, surface, msg, missing, G, step, window, 1,
            lambda: response_ahead(V, S, coef_ref, D, W),
        )
        pre_behind(V, S, coef_ref, None, then, window)

    @pl.when(jnp.logical_not(even))
    def _():
        ahead_bond(
            V, S, R, coef_ref, here, surface, msg, missing, G, step, window, 1,
            lambda: response_behind(V, S, coef_ref, D, W),
        )
        pre_ahead(V, S, coef_ref, None, then, window)

    inner(V, S, coef_ref, then, window)
    if early is not None:
        later = force.at[step + 2]

        @pl.when(even)
        def _():
            early_behind(V, S, R, coef_ref, surface, 2 * (step + 1), early, W, later, window)

        @pl.when(jnp.logical_not(even))
        def _():
            early_ahead(V, S, R, coef_ref, early, W, later, window)


def last_kernel(step, window, V0, S0, R0, coef_ref, force, surface, msg, missing, v0, s0, r0, V, S, R, *rest):
    *results, G, sems = rest
    even, _, _ = place()
    here = force.at[step]

    @pl.when(even)
    def _():
        copies = results_out(V, S, R, results, sems, 0)
        behind_bond(
            V, S, R, coef_ref, here, surface, msg, missing, G, step, window, 0, lambda: start_all(copies[:3])
        )
        start_all(copies[3:])
        wait_all(copies)

    @pl.when(jnp.logical_not(even))
    def _():
        copies = results_out(V, S, R, results, sems, 1)
        ahead_bond(
            V, S, R, coef_ref, here, surface, msg, missing, G, step, window, 0, lambda: start_all(copies[:3])
        )
        start_all(copies[3:])
        wait_all(copies)


ENTRY_ROW, TRUCK_ROW = 36, 40
GROUP = 8


def pack_kernel(
    record, loads_in, entries_in, cells_in, piers_in, own, loads, steps_table, piers, entries, cells, sems
):
    panel = record.shape[1]
    slots, lanes = loads.shape
    steps = entries.shape[0]
    pairs = [(record, own.at[:, pl.ds(0, panel)]), (loads_in, loads), (entries_in, entries), (cells_in, cells)]
    pairs.append((piers_in, piers))
    copies = [pltpu.make_async_copy(*pair, sems.at[i]) for i, pair in enumerate(pairs)]
    for copy in copies:
        copy.start()
    own[:, panel:] = jnp.zeros((own.shape[0], own.shape[1] - panel), jnp.float32)
    steps_table[...] = jnp.zeros(steps_table.shape, jnp.float32)
    for copy in copies:
        copy.wait()
    steps_table[0:steps, 0:slots] = entries[...].astype(jnp.float32)
    steps_table[8 : 8 + steps, 0:slots] = cells[...].astype(jnp.float32)
    blocks = [loads[8 * i : 8 * i + 8, :] for i in range(slots // 8)] + [steps_table[0:8, :]]
    for i, block in enumerate(blocks):
        own[0:8, panel + i * lanes : panel + (i + 1) * lanes] = block


def lane_blocks(table, width):
    return sum(lane_roll(table[s : s + 1, :], s * width) for s in range(STEPS))


def split_kernel(panel, slots, own, behind, cells, after_this, out):
    del after_this
    tiles, _, lanes = out.shape
    pieces = panel // lanes
    third = pieces // 3
    cell_of = cells[...]
    me = lax.axis_index("line")
    group, mine = lax.div(me, tiles), lax.rem(me, tiles)
    piers = cell_of.shape[1]
    row = lax.broadcasted_iota(jnp.int32, (3 * tiles, lanes), 0)
    j = lax.rem(row, 3)
    first = (lax.div(row, 3) + group * tiles) * 2
    cell_x, cell_yz = first + jnp.where(j == 2, -1, j), first + j
    record = jnp.where(group == 0, own[:, :panel], behind[:, :panel])

    def hits(cell):
        return [jnp.where(cell == cell_of[0:1, p : p + 1], 1.0, 0.0).astype(jnp.float32) for p in range(piers)]

    hit_x, hit_yz = hits(cell_x), hits(cell_yz)

    def share(m):
        hit = hit_x if m < third else hit_yz
        return sum(hit[p] * record[p : p + 1, m * lanes : (m + 1) * lanes] for p in range(piers))

    parts = [share(m) for m in range(pieces)]

    def trucks(source):
        blocks = [source[0:8, panel + i * lanes : panel + (i + 1) * lanes] for i in range(slots // 8 + 1)]
        return blocks[:-1], lane_blocks(blocks[-1], slots)

    own_rows, own_entry = trucks(own)
    far_rows, far_entry = trucks(behind)
    for tile in range(tiles):
        these = slice(3 * tile, 3 * tile + 3)
        for m in range(pieces):
            out[tile, 3 * m : 3 * m + 3, :] = parts[m][these, :]
        passed = mine < tile
        out[tile, ENTRY_ROW : ENTRY_ROW + 1, :] = jnp.where(passed, own_entry, far_entry)
        for i in range(slots // 8):
            at = TRUCK_ROW + 8 * i
            out[tile, at : at + 8, :] = jnp.where(passed, own_rows[i], far_rows[i])


def prepare_kernel(parts, loads, steps_table, force, surface, table, rows_out):
    steps, comps, width = force.shape[:3]
    lanes = parts.shape[2]
    force[...] = jnp.zeros(force.shape, jnp.float32)
    per = ENTRY_ROW // (comps * width)
    lane = lax.broadcasted_iota(jnp.int32, (per, lanes), 1)
    scale = jnp.where(lane < FZ, DT, 0.0).astype(jnp.float32)
    for s in range(steps):
        for comp in range(comps):
            for cell in range(width):
                panel = parts[s, pl.ds(comp * per * width + cell, per, stride=width), :]
                force[s, comp, cell, pl.ds(4, per, stride=2), :] = scale * panel
                force[s, comp, cell, pl.ds(5, per, stride=2), :] = scale * lane_roll(panel, FZ)

    slots = loads.shape[0]
    tiles = parts.shape[0]
    mine = lax.rem(lax.axis_index("line"), tiles)
    table[...] = jnp.zeros(table.shape, jnp.float32)
    table[0:1, :] = lane_blocks(steps_table[0:8, :], slots)
    table[STEPS + 1 : STEPS + 2, :] = lane_blocks(steps_table[8:16, :], slots)
    rows = [loads[...]]
    for k in range(1, STEPS + 1):
        source = lax.rem(mine + (tiles - k), tiles)
        rows.append(parts[source, TRUCK_ROW : TRUCK_ROW + slots, :])
        table[k : k + 1, :] = parts[source, ENTRY_ROW : ENTRY_ROW + 1, :]
    columns = table[...].T
    rows_out[...] = jnp.zeros(rows_out.shape, jnp.float32)
    for s in range(STEPS):
        block = slice(s * slots, (s + 1) * slots)
        moved = []
        for k in range(STEPS - s):
            entry = jnp.broadcast_to(columns[block, k : k + 1], rows[k].shape)
            new = rows[k]
            for slot in range(slots):
                new = jnp.where(entry == float(slot), rows[k + 1][slot : slot + 1, :], new)
            moved.append(new)
        rows = moved
        cell = jnp.broadcast_to(columns[block, STEPS + 1 : STEPS + 2], rows[0].shape)
        for c in range(2):
            load = jnp.sum(jnp.where(cell == float(c), rows[0], 0.0), axis=0, keepdims=True)
            rows_out[2 * s + c : 2 * s + c + 1, :] = load
    surface[...] = rows_out[...].T


def in_vmem(x):
    return pltpu.with_memory_space_constraint(x, pltpu.VMEM)


WHOLE = pl.BlockSpec(memory_space=pltpu.VMEM)
SCALARS = pl.BlockSpec(memory_space=pltpu.SMEM)
ANYWHERE = pl.BlockSpec(memory_space=pl.ANY)


def call(kernel, ins, specs, outs, out_specs, scratch=(), aliases=None, name=None, cost=1):
    return pl.pallas_call(
        kernel,
        out_shape=outs,
        in_specs=specs,
        out_specs=out_specs,
        scratch_shapes=list(scratch),
        input_output_aliases=aliases or {},
        compiler_params=pltpu.CompilerParams(vmem_limit_bytes=VMEM_LIMIT),
        cost_estimate=pl.CostEstimate(flops=cost, bytes_accessed=cost, transcendentals=0),
        name=name,
    )(*ins)


def body(
    velocity, stress, memory, truck_loads, pier_panels,
    lame_lambda, lame_mu, buoyancy, relax_rate, defect_mu, layer,
    truck_entry, truck_cell, pier_cell,
):
    tiles = lax.axis_size("line")
    width_x, across, depth = velocity.shape[1:]
    slots = truck_loads.shape[0]
    window = (across - FY) // 2 - 4
    f32 = jnp.float32

    near = [(i, i ^ 1) for i in range(tiles) if (i ^ 1) < tiles]
    far = [(i, i + 1) for i in range(1, tiles - 1, 2)] + [(i + 1, i) for i in range(1, tiles - 1, 2)]

    padded = across + 2 * PAD
    v_type = pltpu.VMEM((3, width_x, padded, depth), f32)
    s_type = pltpu.VMEM((6, width_x, padded, depth), f32)
    r_type = pltpu.VMEM((6, width_x, across, depth), f32)
    c_type = pltpu.VMEM((N_COEF, depth), f32)
    m_type = pltpu.VMEM((3, across, depth), f32)
    planes = (pltpu.VMEM((across, depth), f32),) * 3
    ghost = pltpu.VMEM((2, across, depth), f32)
    work = pltpu.VMEM((2, padded, depth), f32)

    def ahead_by(x, distance):
        return lax.ppermute(x, "line", [(i, i + distance) for i in range(tiles - distance)])

    def in_hbm(*arrays):
        return tuple(pltpu.with_memory_space_constraint(x, pltpu.HBM) for x in arrays)

    dma = pltpu.SemaphoreType.DMA
    piers, panel = pier_panels.shape[1:]
    own, loads, steps_table, pier_row = call(
        pack_kernel,
        in_hbm(pier_panels[0], truck_loads, truck_entry, truck_cell, pier_cell[None, :]),
        (ANYWHERE,) * 5,
        (
            pltpu.VMEM((piers, panel + (slots // 8 + 1) * depth), f32),
            pltpu.VMEM((slots, depth), f32),
            pltpu.VMEM((16, depth), f32),
            pltpu.VMEM((1, piers), jnp.int32),
        ),
        (WHOLE,) * 4,
        scratch=(pltpu.VMEM(truck_entry.shape, jnp.int32), pltpu.VMEM(truck_cell.shape, jnp.int32), dma((5,))),
        name="pack",
    )
    behind = ahead_by(own, GROUP)
    reach = 2 * GROUP
    index = lax.axis_index("line")
    while reach < tiles:
        record = jnp.where(index < GROUP, own, behind)[:, :panel]
        record = jnp.where(index < reach, record, ahead_by(record, reach))
        behind = jnp.concatenate([record, behind[:, panel:]], axis=1)
        reach *= 2
    tables = (lame_lambda, lame_mu, buoyancy, relax_rate, defect_mu)
    V, S, R, coef, *msg_near, msg_far = call(
        start_kernel,
        in_hbm(velocity, stress, memory, layer[None, :], *tables) + (steps_table,),
        (ANYWHERE,) * 10,
        (v_type, s_type, r_type, c_type, *planes, m_type),
        (WHOLE,) * 8,
        scratch=(
            pltpu.VMEM((1, depth), jnp.int32), *(pltpu.SMEM(table.shape, f32) for table in tables), dma((21,)),
        ),
        name="start",
        cost=8 * 1024 * 1024,
    )
    msg_far = lax.ppermute(msg_far, "line", far)
    msg_near = [lax.ppermute(plane, "line", near) for plane in msg_near]
    parts = call(
        functools.partial(split_kernel, panel, slots),
        (own, behind, in_vmem(pier_row), coef),
        (WHOLE,) * 3 + (ANYWHERE,),
        pltpu.VMEM((GROUP, TRUCK_ROW + slots, depth), f32),
        WHOLE,
        name="split",
    )
    groups = [list(range(at, at + GROUP)) for at in range(0, tiles, GROUP)]
    parts = lax.all_to_all(parts, "line", 0, 0, axis_index_groups=groups, tiled=True)
    force, surface = call(
        prepare_kernel,
        (parts, in_vmem(loads), in_vmem(steps_table)),
        (WHOLE,) * 3,
        (pltpu.VMEM((STEPS, 3, 3, 16, depth), f32), pltpu.VMEM((across, depth), f32)),
        (WHOLE,) * 2,
        scratch=(pltpu.VMEM((depth, depth), f32), pltpu.VMEM((depth, across), f32)),
        name="prepare",
    )
    V, early = call(
        functools.partial(first_kernel, window),
        tuple(in_vmem(x) for x in (V, S, R, coef, force, surface)),
        (WHOLE,) * 6,
        (v_type, m_type),
        (WHOLE,) * 2,
        scratch=(work,),
        aliases={0: 0},
        name="first",
    )
    early = lax.ppermute(early, "line", far)
    state = (v_type, s_type, r_type)
    results = tuple(jax.ShapeDtypeStruct(x.shape, f32) for x in (velocity, stress, memory))
    same = {0: 0, 1: 1, 2: 2}
    missing = None
    for step in range(STEPS):
        more = step < STEPS - 1
        ins = tuple(in_vmem(x) for x in (V, S, R, coef, force, surface, *msg_near))
        outs = state + (planes if more else results)
        V, S, R, *msg = call(
            functools.partial(near_kernel, step, window),
            ins,
            (WHOLE,) * len(ins),
            outs,
            (WHOLE,) * 6 if more else (WHOLE,) * 3 + (ANYWHERE,) * 3,
            scratch=(ghost,) if more else (dma((15,)), ghost),
            aliases=same,
            name="near" + str(step),
        )
        if more:
            msg_near = [lax.ppermute(plane, "line", near) for plane in msg]
        ins = (V, S, R, coef, force, surface, msg_far) + ((missing,) if step else ())
        ins = tuple(in_vmem(x) for x in ins)
        if more:
            outs = state + (m_type,) + ((m_type,) if step < STEPS - 2 else ())
            V, S, R, missing, *msg = call(
                functools.partial(far_kernel, step, window),
                ins,
                (WHOLE,) * len(ins),
                outs,
                (WHOLE,) * len(outs),
                scratch=(ghost, work),
                aliases=same,
                name="far" + str(step),
            )
            msg_far = early
            if msg:
                early = lax.ppermute(msg[0], "line", far)
    ends = call(
        functools.partial(last_kernel, STEPS - 1, window),
        ins + tuple(msg),
        (WHOLE,) * 8 + (ANYWHERE,) * 3,
        state + results,
        (WHOLE,) * 3 + (ANYWHERE,) * 3,
        scratch=(ghost, dma((15,))),
        aliases={**same, 8: 3, 9: 4, 10: 5},
        name="last",
    )
    return ends[3:]


def solution(mesh):
    placed = (
        P(None, ("runs", "line"), None, None),
        P(None, ("runs", "line"), None, None),
        P(None, ("runs", "line"), None, None),
        P(("runs", "line"), None),
        P("line", "runs", None),
        P(),
        P(),
        P(),
        P(),
        P(),
        P(),
        P(None, ("runs", "line")),
        P(None, ("runs", "line")),
        P(),
    )
    return jax.shard_map(
        body,
        mesh=mesh,
        in_specs=placed,
        out_specs=(
            P(None, ("runs", "line"), None, None),
            P(None, ("runs", "line"), None, None),
            P(None, ("runs", "line"), None, None),
        ),
        check_vma=False,
    )
```

```python
import functools

import jax
import jax.numpy as jnp
import numpy as np
from jax import lax
from jax.experimental import pallas as pl
from jax.experimental.pallas import tpu as pltpu
from jax.sharding import PartitionSpec as P

STEPS = 6
FY = 8
FZ = 64
DT = 0.25
PAD = 8
ROWS = 16
UNROLL = 8
VMEM_LIMIT = 32 * 1024 * 1024

C_B, C_B0, C_B1, C_M0, C_M1, C_LAM, C_MU2, C_MU, C_K1, C_K2, C_K2H, C_L0 = range(12)
N_COEF = 16

VX, VY, VZ = range(3)
XX, YY, ZZ, XY, XZ, YZ = range(6)


def lane_roll(x, shift):
    return pltpu.roll(x, shift % x.shape[-1], x.ndim - 1)


def before(x):
    return lane_roll(x, 1)


def after(x):
    return lane_roll(x, -1)


def over_rows(count, work, first=0):
    def step(i, carry):
        work(pl.multiple_of(first + i * ROWS, ROWS))
        return carry

    lax.fori_loop(0, count // ROWS, step, 0, unroll=UNROLL)


def coefs(coef_ref, ids):
    return [coef_ref[i : i + 1, :] for i in ids]


def place():
    index = lax.axis_index("line")
    return lax.rem(index, 2) == 0, index > 0, index < lax.axis_size("line") - 1


def spans(r):
    return pl.ds(PAD + r, ROWS), pl.ds(PAD + r - 1, ROWS), pl.ds(PAD + r + 1, ROWS), pl.ds(r, ROWS)


def zero_edges(ref):
    across = ref.shape[-2] - 2 * PAD
    edge = jnp.zeros((PAD, ref.shape[-1]), jnp.float32)
    for where in np.ndindex(*ref.shape[:-2]):
        ref[(*where, pl.ds(0, PAD))] = edge
        ref[(*where, pl.ds(PAD + across, PAD))] = edge


class Halves:
    def __init__(self, *refs):
        self.refs, self.half, self.rows = refs, 0, refs[0].shape[1]

    def at(self, out):
        return pl.ds(out.start - self.half * self.rows, out.size)

    def __getitem__(self, at):
        return self.refs[self.half][at[0], self.at(at[1])]

    def __setitem__(self, at, value):
        self.refs[self.half][at[0], self.at(at[1])] = value

    def add_force(self, plane, force, which, first_row):
        upper, lower = self.refs
        above = self.rows - first_row
        upper[plane, pl.ds(first_row, above)] = upper[plane, pl.ds(first_row, above)] + force[which][:above]
        lower[plane, pl.ds(0, 16 - above)] = lower[plane, pl.ds(0, 16 - above)] + force[which][above:]


def over_message(count, work, msg):
    if not isinstance(msg, Halves):
        over_rows(count, work)
        return
    for half in range(2):
        msg.half = half
        over_rows(msg.rows, work, half * msg.rows)


def add_force(ref, index, force, which, first_row):
    if isinstance(ref, Halves):
        ref.add_force(*index, force, which, first_row)
        return
    rows = pl.ds(first_row, 16)
    ref[(*index, rows)] = ref[(*index, rows)] + force[which]


def pre_ahead(V, S, coef_ref, msg, force, window):
    b, b0 = coefs(coef_ref, (C_B, C_B0))

    def work(r):
        here, up, _, out = spans(r)
        sxy, sxz = S[XY, 1, here], S[XZ, 1, here]
        px = V[VX, 1, here] + b * (sxy - S[XY, 1, up] + sxz - S[XX, 1, here]) - b0 * before(sxz)
        V[VX, 1, here] = px
        if msg is not None:
            msg[0, out] = sxy
            msg[1, out] = sxz
            msg[2, out] = px

    over_message(V.shape[2] - 2 * PAD, work, msg)
    if force is not None:
        add_force(V, (VX, 1), force, (VX, 1), PAD + window)
        if msg is not None:
            add_force(msg, (2,), force, (VX, 1), window)


def pre_behind(V, S, coef_ref, msg, force, window):
    b, b0, b1 = coefs(coef_ref, (C_B, C_B0, C_B1))

    def work(r):
        here, up, down, out = spans(r)
        syz, szz = S[YZ, 0, here], S[ZZ, 0, here]
        qy = V[VY, 0, here] + b * (S[XY, 0, here] + S[YY, 0, down] - S[YY, 0, here] + syz) - b0 * before(syz)
        qz = V[VZ, 0, here] + b * (S[XZ, 0, here] + syz - S[YZ, 0, up] - szz) + b1 * after(szz)
        V[VY, 0, here] = qy
        V[VZ, 0, here] = qz
        if msg is not None:
            msg[0, out] = S[XX, 0, here]
            msg[1, out] = qy
            msg[2, out] = qz

    over_message(V.shape[2] - 2 * PAD, work, msg)
    if force is not None:
        add_force(V, (VY, 0), force, (VY, 0), PAD + window)
        add_force(V, (VZ, 0), force, (VZ, 0), PAD + window)
        if msg is not None:
            add_force(msg, (1,), force, (VY, 0), window)
            add_force(msg, (2,), force, (VZ, 0), window)


def inner(V, S, coef_ref, force, window):
    b, b0, b1 = coefs(coef_ref, (C_B, C_B0, C_B1))

    def work(r):
        here, up, down, _ = spans(r)
        sxy, sxz = S[XY, 0, here], S[XZ, 0, here]
        V[VX, 0, here] = (
            V[VX, 0, here]
            + b * (S[XX, 1, here] - S[XX, 0, here] + sxy - S[XY, 0, up] + sxz)
            - b0 * before(sxz)
        )
        syz, szz = S[YZ, 1, here], S[ZZ, 1, here]
        V[VY, 1, here] = (
            V[VY, 1, here]
            + b * (S[XY, 1, here] - sxy + S[YY, 1, down] - S[YY, 1, here] + syz)
            - b0 * before(syz)
        )
        V[VZ, 1, here] = (
            V[VZ, 1, here]
            + b * (S[XZ, 1, here] - sxz + syz - S[YZ, 1, up] - szz)
            + b1 * after(szz)
        )

    over_rows(V.shape[2] - 2 * PAD, work)
    if force is not None:
        add_force(V, (VX, 0), force, (VX, 0), PAD + window)
        add_force(V, (VY, 1), force, (VY, 1), PAD + window)
        add_force(V, (VZ, 1), force, (VZ, 1), PAD + window)


def post(V, S, R, coef_ref, surface, cell, column, behind_x, ahead_y, ahead_z):
    m0, m1, lam, mu2, mu, k1, k2, k2h, l0 = coefs(
        coef_ref, (C_M0, C_M1, C_LAM, C_MU2, C_MU, C_K1, C_K2, C_K2H, C_L0)
    )

    def work(r):
        here, up, down, out = spans(r)
        vx, vy, vz = V[VX, cell, here], V[VY, cell, here], V[VZ, cell, here]
        exx = vx - behind_x(r)
        eyy = vy - V[VY, cell, up]
        ezz = vz - m0 * before(vz)
        exy = V[VX, cell, down] - vx + (ahead_y(r) - vy)
        exz = m1 * after(vx) - vx + (ahead_z(r) - vz)
        eyz = m1 * after(vy) - vy + (V[VZ, cell, down] - vz)
        volume = lam * (exx + eyy + ezz)
        for comp, e in ((XX, exx), (YY, eyy), (ZZ, ezz)):
            old = R[comp, cell, out]
            new = S[comp, cell, here] + (volume + mu2 * e) + DT * old
            if comp == ZZ:
                new = new + l0 * lane_roll(surface[out, :], -column)
            S[comp, cell, here] = new
            R[comp, cell, out] = k1 * old - k2 * e
        for comp, e in ((XY, exy), (XZ, exz), (YZ, eyz)):
            old = R[comp, cell, out]
            S[comp, cell, here] = S[comp, cell, here] + mu * e + DT * old
            R[comp, cell, out] = k1 * old - k2h * e

    over_rows(R.shape[2], work)


def response_behind(V, S, coef_ref, D, W):
    b, b0, b1, m0, m1, lam, mu2, mu = coefs(coef_ref, (C_B, C_B0, C_B1, C_M0, C_M1, C_LAM, C_MU2, C_MU))

    def work(r):
        here, up, down, out = spans(r)
        sxy = S[XY, 1, here]
        vy, vz = -b * sxy, -b * S[XZ, 1, here]
        exx = -V[VX, 1, here]
        eyy = b * (S[XY, 1, up] - sxy)
        ezz = vz - m0 * before(vz)
        volume = lam * (exx + eyy + ezz)
        dyy, dzz = volume + mu2 * eyy, volume + mu2 * ezz
        dyz = mu * (m1 * after(vy) - vy - b * S[XZ, 1, down] - vz)
        W[0, here] = dyy
        W[1, here] = dyz
        D[0, out] = volume + mu2 * exx
        D[1, out] = vy + b * (dyz - mu * vy - dyy) - b0 * before(dyz)
        D[2, out] = vz + b * (dyz - mu * vz - dzz) + b1 * after(dzz)

    over_rows(D.shape[1], work)

    def rest(r):
        _, up, down, out = spans(r)
        D[1, out] = D[1, out] + b * W[0, down]
        D[2, out] = D[2, out] - b * W[1, up]

    over_rows(D.shape[1], rest)


def response_ahead(V, S, coef_ref, D, W):
    b, b0, m1, lam, mu2, mu = coefs(coef_ref, (C_B, C_B0, C_M1, C_LAM, C_MU2, C_MU))

    def work(r):
        here, _, down, out = spans(r)
        vx = b * S[XX, 0, here]
        dxy = mu * (b * S[XX, 0, down] - vx + V[VY, 0, here])
        dxz = mu * (m1 * after(vx) - vx + V[VZ, 0, here])
        W[0, here] = dxy
        D[0, out] = dxy
        D[1, out] = dxz
        D[2, out] = vx + b * (dxy + dxz - (lam + mu2) * vx) - b0 * before(dxz)

    over_rows(D.shape[1], work)

    def rest(r):
        _, up, _, out = spans(r)
        D[2, out] = D[2, out] - b * W[0, up]

    over_rows(D.shape[1], rest)


def early_ahead(V, S, R, coef_ref, msg, W, force, window):
    b, b0, m0, m1, lam, mu2, mu = coefs(coef_ref, (C_B, C_B0, C_M0, C_M1, C_LAM, C_MU2, C_MU))

    def work(r):
        here, up, down, out = spans(r)
        vx, vy, vz = V[VX, 1, here], V[VY, 1, here], V[VZ, 1, here]
        exx = vx - V[VX, 0, here]
        volume = lam * (exx + (vy - V[VY, 1, up]) + (vz - m0 * before(vz)))
        sxx = S[XX, 1, here] + (volume + mu2 * exx) + DT * R[XX, 1, out]
        sxy = S[XY, 1, here] + mu * (V[VX, 1, down] - vx - vy) + DT * R[XY, 1, out]
        sxz = S[XZ, 1, here] + mu * (m1 * after(vx) - vx - vz) + DT * R[XZ, 1, out]
        W[0, here] = sxy
        msg[0, out] = sxy
        msg[1, out] = sxz
        msg[2, out] = vx + b * (sxy + sxz - sxx) - b0 * before(sxz)

    over_rows(msg.shape[1], work)

    def rest(r):
        _, up, _, out = spans(r)
        msg[2, out] = msg[2, out] - b * W[0, up]

    over_rows(msg.shape[1], rest)
    if force is not None:
        add_force(msg, (2,), force, (VX, 1), window)


def early_behind(V, S, R, coef_ref, surface, column, msg, W, force, window):
    b, b0, b1, m0, m1, lam, mu2, mu, l0 = coefs(
        coef_ref, (C_B, C_B0, C_B1, C_M0, C_M1, C_LAM, C_MU2, C_MU, C_L0)
    )

    def work(r):
        here, up, down, out = spans(r)
        vx, vy, vz = V[VX, 0, here], V[VY, 0, here], V[VZ, 0, here]
        eyy = vy - V[VY, 0, up]
        ezz = vz - m0 * before(vz)
        volume = lam * (vx + eyy + ezz)
        sxx = S[XX, 0, here] + (volume + mu2 * vx) + DT * R[XX, 0, out]
        syy = S[YY, 0, here] + (volume + mu2 * eyy) + DT * R[YY, 0, out]
        szz = S[ZZ, 0, here] + (volume + mu2 * ezz) + DT * R[ZZ, 0, out]
        if surface is not None:
            szz = szz + l0 * lane_roll(surface[out, :], -column)
        sxy = S[XY, 0, here] + mu * (V[VX, 0, down] - vx + (V[VY, 1, here] - vy)) + DT * R[XY, 0, out]
        sxz = S[XZ, 0, here] + mu * (m1 * after(vx) - vx + (V[VZ, 1, here] - vz)) + DT * R[XZ, 0, out]
        syz = S[YZ, 0, here] + mu * (m1 * after(vy) - vy + (V[VZ, 0, down] - vz)) + DT * R[YZ, 0, out]
        W[0, here] = syy
        W[1, here] = syz
        msg[0, out] = sxx
        msg[1, out] = vy + b * (sxy - syy + syz) - b0 * before(syz)
        msg[2, out] = vz + b * (sxz + syz - szz) + b1 * after(szz)

    over_rows(msg.shape[1], work)

    def rest(r):
        _, up, down, out = spans(r)
        msg[1, out] = msg[1, out] + b * W[0, down]
        msg[2, out] = msg[2, out] - b * W[1, up]

    over_rows(msg.shape[1], rest)
    if force is not None:
        add_force(msg, (1,), force, (VY, 0), window)
        add_force(msg, (2,), force, (VZ, 0), window)


def ahead_bond(V, S, R, coef_ref, force, surface, msg, missing, G, step, window, unforced=0, respond=None):
    (b,) = coefs(coef_ref, (C_B,))
    _, _, has_ahead = place()
    keep = jnp.where(has_ahead, 1.0, 0.0).astype(jnp.float32)

    def got(i, out):
        return msg[i, out] if missing is None else msg[i, out] + missing[i, out]

    def work(r):
        here, _, _, out = spans(r)
        V[VX, 1, here] = V[VX, 1, here] + (keep * b) * got(0, out)
        G[0, out] = keep * (got(1, out) - b * S[XY, 1, here])
        G[1, out] = keep * (got(2, out) - b * S[XZ, 1, here])

    over_message(R.shape[2], work, msg)
    if step < unforced:
        add_force(G, (0,), force, (VY, 2), window)
        add_force(G, (1,), force, (VZ, 2), window)
    if respond is not None:
        respond()
    post(
        V, S, R, coef_ref, surface, 1, 2 * step + 1,
        lambda r: V[VX, 0, pl.ds(PAD + r, ROWS)],
        lambda r: G[0, pl.ds(r, ROWS)],
        lambda r: G[1, pl.ds(r, ROWS)],
    )


def behind_bond(V, S, R, coef_ref, force, surface, msg, missing, G, step, window, unforced=0, respond=None):
    (b,) = coefs(coef_ref, (C_B,))
    _, has_behind, _ = place()
    keep = jnp.where(has_behind, 1.0, 0.0).astype(jnp.float32)

    def got(i, out):
        return msg[i, out] if missing is None else msg[i, out] + missing[i, out]

    def work(r):
        here, _, _, out = spans(r)
        V[VY, 0, here] = V[VY, 0, here] - (keep * b) * got(0, out)
        V[VZ, 0, here] = V[VZ, 0, here] - (keep * b) * got(1, out)
        G[0, out] = keep * (got(2, out) + b * S[XX, 0, here])

    over_message(R.shape[2], work, msg)
    if step < unforced:
        add_force(G, (0,), force, (VX, 2), window)
    if respond is not None:
        respond()
    post(
        V, S, R, coef_ref, surface, 0, 2 * step,
        lambda r: G[0, pl.ds(r, ROWS)],
        lambda r: V[VY, 1, pl.ds(PAD + r, ROWS)],
        lambda r: V[VZ, 1, pl.ds(PAD + r, ROWS)],
    )


def start_kernel(
    velocity, stress, memory, layer_in, lam_in, mu_in, buoy_in, rate_in, defect_in, after_this,
    V, S, R, coef_ref, near_upper, near_lower, msg_far, layer_ref, lam, mu, buoy, rate, defect, sems,
):
    del after_this
    msg_near = Halves(near_upper, near_lower)
    across = velocity.shape[2]
    inside = pl.ds(PAD, across)
    pairs = [
        (layer_in, layer_ref), (lam_in, lam), (mu_in, mu), (buoy_in, buoy), (rate_in, rate), (defect_in, defect),
    ]
    pairs += [(stress.at[i], S.at[i, :, inside]) for i in range(6)]
    pairs += [(velocity.at[i], V.at[i, :, inside]) for i in range(3)]
    pairs += [(memory.at[i], R.at[i]) for i in range(6)]
    copies = [pltpu.make_async_copy(*pair, sems.at[i]) for i, pair in enumerate(pairs)]
    for copy in copies:
        copy.start()
    zero_edges(V)
    zero_edges(S)
    for copy in copies[:6]:
        copy.wait()
    layer = layer_ref[...]

    def per_depth(table):
        row = jnp.zeros(layer.shape, jnp.float32)
        for level in range(table.shape[0]):
            row = jnp.where(layer == level, table[level], row)
        return row

    lane = lax.broadcasted_iota(jnp.int32, layer.shape, 1)
    not_first = jnp.where(lane > 0, 1.0, 0.0).astype(jnp.float32)
    not_last = jnp.where(lane < layer.shape[1] - 1, 1.0, 0.0).astype(jnp.float32)
    b = DT * per_depth(buoy)
    two_mu = (2.0 * DT) * per_depth(mu)
    decay = DT * per_depth(rate)
    drop = 2.0 * decay * per_depth(defect)
    for row, value in (
        (C_B, b),
        (C_B0, b * not_first),
        (C_B1, b * not_last),
        (C_M0, not_first),
        (C_M1, not_last),
        (C_LAM, DT * per_depth(lam)),
        (C_MU2, two_mu),
        (C_MU, 0.5 * two_mu),
        (C_K1, 1.0 - decay),
        (C_K2, drop),
        (C_K2H, 0.5 * drop),
        (C_L0, DT * (1.0 - not_first)),
    ):
        coef_ref[row : row + 1, :] = value
    coef_ref[12:16, :] = jnp.zeros((4, layer.shape[1]), jnp.float32)
    for copy in copies[6:15]:
        copy.wait()
    even, _, _ = place()

    @pl.when(even)
    def _():
        pre_ahead(V, S, coef_ref, msg_near, None, 0)
        pre_behind(V, S, coef_ref, msg_far, None, 0)

    @pl.when(jnp.logical_not(even))
    def _():
        pre_behind(V, S, coef_ref, msg_near, None, 0)
        pre_ahead(V, S, coef_ref, msg_far, None, 0)

    for copy in copies[15:]:
        copy.wait()


def first_kernel(window, V0, S, R, coef_ref, force, surface, V, msg, W):
    even, _, _ = place()
    zero_edges(W)
    now, then = force.at[0], force.at[1]
    add_force(V, (VX, 1), now, (VX, 1), PAD + window)
    add_force(V, (VY, 0), now, (VY, 0), PAD + window)
    add_force(V, (VZ, 0), now, (VZ, 0), PAD + window)
    inner(V, S, coef_ref, now, window)

    @pl.when(even)
    def _():
        early_behind(V, S, R, coef_ref, surface, 0, msg, W, then, window)

    @pl.when(jnp.logical_not(even))
    def _():
        early_ahead(V, S, R, coef_ref, msg, W, then, window)


def results_out(V, S, R, results, sems, cell):
    inside = pl.ds(PAD, R.shape[2])
    pairs = [(V.at[i, cell, inside], results[0].at[i, cell]) for i in range(3)]
    pairs += [(S.at[i, cell, inside], results[1].at[i, cell]) for i in range(6)]
    pairs += [(R.at[i, cell], results[2].at[i, cell]) for i in range(6)]
    return [pltpu.make_async_copy(*pair, sems.at[i]) for i, pair in enumerate(pairs)]


def start_all(copies):
    for copy in copies:
        copy.start()


def wait_all(copies):
    for copy in copies:
        copy.wait()


def near_kernel(step, window, V0, S0, R0, coef_ref, force, surface, upper, lower, V, S, R, *rest):
    G = rest[-1]
    msg = Halves(upper, lower)
    even, _, _ = place()
    more = step < STEPS - 1
    send = Halves(*rest[:2]) if more else None

    @pl.when(even)
    def _():
        ahead_bond(V, S, R, coef_ref, force.at[step], surface, msg, None, G, step, window, 1)
        if more:
            pre_ahead(V, S, coef_ref, send, force.at[step + 1], window)
        else:
            copies = results_out(V, S, R, rest[:3], rest[-2], 1)
            start_all(copies)
            wait_all(copies)

    @pl.when(jnp.logical_not(even))
    def _():
        behind_bond(V, S, R, coef_ref, force.at[step], surface, msg, None, G, step, window, 1)
        if more:
            pre_behind(V, S, coef_ref, send, force.at[step + 1], window)
        else:
            copies = results_out(V, S, R, rest[:3], rest[-2], 0)
            start_all(copies)
            wait_all(copies)


def far_kernel(step, window, V0, S0, R0, coef_ref, force, surface, msg, *rest):
    rest = list(rest)
    missing = rest.pop(0) if step > 0 else None
    V, S, R, D = rest[:4]
    G, W = rest[-2:]
    early = rest[4] if step < STEPS - 2 else None
    even, _, _ = place()
    zero_edges(W)
    here, then = force.at[step], force.at[step + 1]

    @pl.when(even)
    def _():
        behind_bond(
            V, S, R, coef_ref, here, surface, msg, missing, G, step, window, 1,
            lambda: response_ahead(V, S, coef_ref, D, W),
        )
        pre_behind(V, S, coef_ref, None, then, window)

    @pl.when(jnp.logical_not(even))
    def _():
        ahead_bond(
            V, S, R, coef_ref, here, surface, msg, missing, G, step, window, 1,
            lambda: response_behind(V, S, coef_ref, D, W),
        )
        pre_ahead(V, S, coef_ref, None, then, window)

    inner(V, S, coef_ref, then, window)
    if early is not None:
        later = force.at[step + 2]

        @pl.when(even)
        def _():
            early_behind(V, S, R, coef_ref, surface, 2 * (step + 1), early, W, later, window)

        @pl.when(jnp.logical_not(even))
        def _():
            early_ahead(V, S, R, coef_ref, early, W, later, window)


def last_kernel(step, window, V0, S0, R0, coef_ref, force, surface, msg, missing, v0, s0, r0, V, S, R, *rest):
    *results, G, sems = rest
    even, _, _ = place()
    here = force.at[step]

    @pl.when(even)
    def _():
        copies = results_out(V, S, R, results, sems, 0)
        behind_bond(
            V, S, R, coef_ref, here, surface, msg, missing, G, step, window, 0, lambda: start_all(copies[:3])
        )
        start_all(copies[3:])
        wait_all(copies)

    @pl.when(jnp.logical_not(even))
    def _():
        copies = results_out(V, S, R, results, sems, 1)
        ahead_bond(
            V, S, R, coef_ref, here, surface, msg, missing, G, step, window, 0, lambda: start_all(copies[:3])
        )
        start_all(copies[3:])
        wait_all(copies)


ENTRY_ROW, TRUCK_ROW = 36, 40
GROUP = 8


def pack_kernel(
    record, loads_in, entries_in, cells_in, piers_in, own, loads, steps_table, piers, entries, cells, sems
):
    panel = record.shape[1]
    slots, lanes = loads.shape
    steps = entries.shape[0]
    pairs = [(record, own.at[:, pl.ds(0, panel)]), (loads_in, loads), (entries_in, entries), (cells_in, cells)]
    pairs.append((piers_in, piers))
    copies = [pltpu.make_async_copy(*pair, sems.at[i]) for i, pair in enumerate(pairs)]
    for copy in copies:
        copy.start()
    own[:, panel:] = jnp.zeros((own.shape[0], own.shape[1] - panel), jnp.float32)
    steps_table[...] = jnp.zeros(steps_table.shape, jnp.float32)
    for copy in copies:
        copy.wait()
    steps_table[0:steps, 0:slots] = entries[...].astype(jnp.float32)
    steps_table[8 : 8 + steps, 0:slots] = cells[...].astype(jnp.float32)
    blocks = [loads[8 * i : 8 * i + 8, :] for i in range(slots // 8)] + [steps_table[0:8, :]]
    for i, block in enumerate(blocks):
        own[0:8, panel + i * lanes : panel + (i + 1) * lanes] = block


def lane_blocks(table, width):
    return sum(lane_roll(table[s : s + 1, :], s * width) for s in range(STEPS))


def split_kernel(panel, slots, own, behind, cells, after_this, out):
    del after_this
    tiles, _, lanes = out.shape
    pieces = panel // lanes
    third = pieces // 3
    cell_of = cells[...]
    me = lax.axis_index("line")
    group, mine = lax.div(me, tiles), lax.rem(me, tiles)
    piers = cell_of.shape[1]
    row = lax.broadcasted_iota(jnp.int32, (3 * tiles, lanes), 0)
    j = lax.rem(row, 3)
    first = (lax.div(row, 3) + group * tiles) * 2
    cell_x, cell_yz = first + jnp.where(j == 2, -1, j), first + j
    record = jnp.where(group == 0, own[:, :panel], behind[:, :panel])

    def hits(cell):
        return [jnp.where(cell == cell_of[0:1, p : p + 1], 1.0, 0.0).astype(jnp.float32) for p in range(piers)]

    hit_x, hit_yz = hits(cell_x), hits(cell_yz)

    def share(m):
        hit = hit_x if m < third else hit_yz
        return sum(hit[p] * record[p : p + 1, m * lanes : (m + 1) * lanes] for p in range(piers))

    parts = [share(m) for m in range(pieces)]

    def trucks(source):
        blocks = [source[0:8, panel + i * lanes : panel + (i + 1) * lanes] for i in range(slots // 8 + 1)]
        return blocks[:-1], lane_blocks(blocks[-1], slots)

    own_rows, own_entry = trucks(own)
    far_rows, far_entry = trucks(behind)
    for tile in range(tiles):
        these = slice(3 * tile, 3 * tile + 3)
        for m in range(pieces):
            out[tile, 3 * m : 3 * m + 3, :] = parts[m][these, :]
        passed = mine < tile
        out[tile, ENTRY_ROW : ENTRY_ROW + 1, :] = jnp.where(passed, own_entry, far_entry)
        for i in range(slots // 8):
            at = TRUCK_ROW + 8 * i
            out[tile, at : at + 8, :] = jnp.where(passed, own_rows[i], far_rows[i])


def prepare_kernel(parts, loads, steps_table, force, surface, table, rows_out):
    steps, comps, width = force.shape[:3]
    lanes = parts.shape[2]
    force[...] = jnp.zeros(force.shape, jnp.float32)
    per = ENTRY_ROW // (comps * width)
    lane = lax.broadcasted_iota(jnp.int32, (per, lanes), 1)
    scale = jnp.where(lane < FZ, DT, 0.0).astype(jnp.float32)
    for s in range(steps):
        for comp in range(comps):
            for cell in range(width):
                panel = parts[s, pl.ds(comp * per * width + cell, per, stride=width), :]
                force[s, comp, cell, pl.ds(4, per, stride=2), :] = scale * panel
                force[s, comp, cell, pl.ds(5, per, stride=2), :] = scale * lane_roll(panel, FZ)

    slots = loads.shape[0]
    tiles = parts.shape[0]
    mine = lax.rem(lax.axis_index("line"), tiles)
    table[...] = jnp.zeros(table.shape, jnp.float32)
    table[0:1, :] = lane_blocks(steps_table[0:8, :], slots)
    table[STEPS + 1 : STEPS + 2, :] = lane_blocks(steps_table[8:16, :], slots)
    rows = [loads[...]]
    for k in range(1, STEPS + 1):
        source = lax.rem(mine + (tiles - k), tiles)
        rows.append(parts[source, TRUCK_ROW : TRUCK_ROW + slots, :])
        table[k : k + 1, :] = parts[source, ENTRY_ROW : ENTRY_ROW + 1, :]
    columns = table[...].T
    rows_out[...] = jnp.zeros(rows_out.shape, jnp.float32)
    for s in range(STEPS):
        block = slice(s * slots, (s + 1) * slots)
        moved = []
        for k in range(STEPS - s):
            entry = jnp.broadcast_to(columns[block, k : k + 1], rows[k].shape)
            new = rows[k]
            for slot in range(slots):
                new = jnp.where(entry == float(slot), rows[k + 1][slot : slot + 1, :], new)
            moved.append(new)
        rows = moved
        cell = jnp.broadcast_to(columns[block, STEPS + 1 : STEPS + 2], rows[0].shape)
        for c in range(2):
            load = jnp.sum(jnp.where(cell == float(c), rows[0], 0.0), axis=0, keepdims=True)
            rows_out[2 * s + c : 2 * s + c + 1, :] = load
    surface[...] = rows_out[...].T


def in_vmem(x):
    return pltpu.with_memory_space_constraint(x, pltpu.VMEM)


WHOLE = pl.BlockSpec(memory_space=pltpu.VMEM)
SCALARS = pl.BlockSpec(memory_space=pltpu.SMEM)
ANYWHERE = pl.BlockSpec(memory_space=pl.ANY)


def call(kernel, ins, specs, outs, out_specs, scratch=(), aliases=None, name=None, cost=1):
    return pl.pallas_call(
        kernel,
        out_shape=outs,
        in_specs=specs,
        out_specs=out_specs,
        scratch_shapes=list(scratch),
        input_output_aliases=aliases or {},
        compiler_params=pltpu.CompilerParams(vmem_limit_bytes=VMEM_LIMIT),
        cost_estimate=pl.CostEstimate(flops=cost, bytes_accessed=cost, transcendentals=0),
        name=name,
    )(*ins)


def body(
    velocity, stress, memory, truck_loads, pier_panels,
    lame_lambda, lame_mu, buoyancy, relax_rate, defect_mu, layer,
    truck_entry, truck_cell, pier_cell,
):
    tiles = lax.axis_size("line")
    width_x, across, depth = velocity.shape[1:]
    slots = truck_loads.shape[0]
    window = (across - FY) // 2 - 4
    f32 = jnp.float32

    near = [(i, i ^ 1) for i in range(tiles) if (i ^ 1) < tiles]
    far = [(i, i + 1) for i in range(1, tiles - 1, 2)] + [(i + 1, i) for i in range(1, tiles - 1, 2)]

    padded = across + 2 * PAD
    v_type = pltpu.VMEM((3, width_x, padded, depth), f32)
    s_type = pltpu.VMEM((6, width_x, padded, depth), f32)
    r_type = pltpu.VMEM((6, width_x, across, depth), f32)
    c_type = pltpu.VMEM((N_COEF, depth), f32)
    m_type = pltpu.VMEM((3, across, depth), f32)
    planes = (pltpu.VMEM((3, across // 2, depth), f32),) * 2
    ghost = pltpu.VMEM((2, across, depth), f32)
    work = pltpu.VMEM((2, padded, depth), f32)

    def ahead_by(x, distance):
        return lax.ppermute(x, "line", [(i, i + distance) for i in range(tiles - distance)])

    def in_hbm(*arrays):
        return tuple(pltpu.with_memory_space_constraint(x, pltpu.HBM) for x in arrays)

    dma = pltpu.SemaphoreType.DMA
    piers, panel = pier_panels.shape[1:]
    own, loads, steps_table, pier_row = call(
        pack_kernel,
        in_hbm(pier_panels[0], truck_loads, truck_entry, truck_cell, pier_cell[None, :]),
        (ANYWHERE,) * 5,
        (
            pltpu.VMEM((piers, panel + (slots // 8 + 1) * depth), f32),
            pltpu.VMEM((slots, depth), f32),
            pltpu.VMEM((16, depth), f32),
            pltpu.VMEM((1, piers), jnp.int32),
        ),
        (WHOLE,) * 4,
        scratch=(pltpu.VMEM(truck_entry.shape, jnp.int32), pltpu.VMEM(truck_cell.shape, jnp.int32), dma((5,))),
        name="pack",
    )
    behind = ahead_by(own, GROUP)
    reach = 2 * GROUP
    index = lax.axis_index("line")
    while reach < tiles:
        record = jnp.where(index < GROUP, own, behind)[:, :panel]
        record = jnp.where(index < reach, record, ahead_by(record, reach))
        behind = jnp.concatenate([record, behind[:, panel:]], axis=1)
        reach *= 2
    tables = (lame_lambda, lame_mu, buoyancy, relax_rate, defect_mu)
    V, S, R, coef, *msg_near, msg_far = call(
        start_kernel,
        in_hbm(velocity, stress, memory, layer[None, :], *tables) + (steps_table,),
        (ANYWHERE,) * 10,
        (v_type, s_type, r_type, c_type, *planes, m_type),
        (WHOLE,) * 7,
        scratch=(
            pltpu.VMEM((1, depth), jnp.int32), *(pltpu.SMEM(table.shape, f32) for table in tables), dma((21,)),
        ),
        name="start",
        cost=8 * 1024 * 1024,
    )
    msg_far = lax.ppermute(msg_far, "line", far)
    msg_near = [lax.ppermute(plane, "line", near) for plane in msg_near]
    parts = call(
        functools.partial(split_kernel, panel, slots),
        (own, behind, in_vmem(pier_row), coef),
        (WHOLE,) * 3 + (ANYWHERE,),
        pltpu.VMEM((GROUP, TRUCK_ROW + slots, depth), f32),
        WHOLE,
        name="split",
    )
    groups = [list(range(at, at + GROUP)) for at in range(0, tiles, GROUP)]
    parts = lax.all_to_all(parts, "line", 0, 0, axis_index_groups=groups, tiled=True)
    force, surface = call(
        prepare_kernel,
        (parts, in_vmem(loads), in_vmem(steps_table)),
        (WHOLE,) * 3,
        (pltpu.VMEM((STEPS, 3, 3, 16, depth), f32), pltpu.VMEM((across, depth), f32)),
        (WHOLE,) * 2,
        scratch=(pltpu.VMEM((depth, depth), f32), pltpu.VMEM((depth, across), f32)),
        name="prepare",
    )
    V, early = call(
        functools.partial(first_kernel, window),
        tuple(in_vmem(x) for x in (V, S, R, coef, force, surface)),
        (WHOLE,) * 6,
        (v_type, m_type),
        (WHOLE,) * 2,
        scratch=(work,),
        aliases={0: 0},
        name="first",
    )
    early = lax.ppermute(early, "line", far)
    state = (v_type, s_type, r_type)
    results = tuple(jax.ShapeDtypeStruct(x.shape, f32) for x in (velocity, stress, memory))
    same = {0: 0, 1: 1, 2: 2}
    missing = None
    for step in range(STEPS):
        more = step < STEPS - 1
        ins = tuple(in_vmem(x) for x in (V, S, R, coef, force, surface, *msg_near))
        outs = state + (planes if more else results)
        V, S, R, *msg = call(
            functools.partial(near_kernel, step, window),
            ins,
            (WHOLE,) * len(ins),
            outs,
            (WHOLE,) * 5 if more else (WHOLE,) * 3 + (ANYWHERE,) * 3,
            scratch=(ghost,) if more else (dma((15,)), ghost),
            aliases=same,
            name="near" + str(step),
        )
        if more:
            msg_near = [lax.ppermute(plane, "line", near) for plane in msg]
        ins = (V, S, R, coef, force, surface, msg_far) + ((missing,) if step else ())
        ins = tuple(in_vmem(x) for x in ins)
        if more:
            outs = state + (m_type,) + ((m_type,) if step < STEPS - 2 else ())
            V, S, R, missing, *msg = call(
                functools.partial(far_kernel, step, window),
                ins,
                (WHOLE,) * len(ins),
                outs,
                (WHOLE,) * len(outs),
                scratch=(ghost, work),
                aliases=same,
                name="far" + str(step),
            )
            msg_far = early
            if msg:
                early = lax.ppermute(msg[0], "line", far)
    ends = call(
        functools.partial(last_kernel, STEPS - 1, window),
        ins + tuple(msg),
        (WHOLE,) * 8 + (ANYWHERE,) * 3,
        state + results,
        (WHOLE,) * 3 + (ANYWHERE,) * 3,
        scratch=(ghost, dma((15,))),
        aliases={**same, 8: 3, 9: 4, 10: 5},
        name="last",
    )
    return ends[3:]


def solution(mesh):
    placed = (
        P(None, ("runs", "line"), None, None),
        P(None, ("runs", "line"), None, None),
        P(None, ("runs", "line"), None, None),
        P(("runs", "line"), None),
        P("line", "runs", None),
        P(),
        P(),
        P(),
        P(),
        P(),
        P(),
        P(None, ("runs", "line")),
        P(None, ("runs", "line")),
        P(),
    )
    return jax.shard_map(
        body,
        mesh=mesh,
        in_specs=placed,
        out_specs=(
            P(None, ("runs", "line"), None, None),
            P(None, ("runs", "line"), None, None),
            P(None, ("runs", "line"), None, None),
        ),
        check_vma=False,
    )
```

```python
import functools

import jax
import jax.numpy as jnp
import numpy as np
from jax import lax
from jax.experimental import pallas as pl
from jax.experimental.pallas import tpu as pltpu
from jax.sharding import PartitionSpec as P

STEPS = 6
FY = 8
FZ = 64
DT = 0.25
PAD = 8
ROWS = 16
VMEM_LIMIT = 32 * 1024 * 1024

C_B, C_B0, C_B1, C_M0, C_M1, C_LAM, C_MU2, C_MU, C_K1, C_K2, C_K2H, C_L0 = range(12)
N_COEF = 16

VX, VY, VZ = range(3)
XX, YY, ZZ, XY, XZ, YZ = range(6)


def lane_roll(x, shift):
    return pltpu.roll(x, shift % x.shape[-1], x.ndim - 1)


def before(x):
    return lane_roll(x, 1)


def after(x):
    return lane_roll(x, -1)


def over_rows(count, work, first=0):
    def step(i, carry):
        work(pl.multiple_of(first + i * ROWS, ROWS))
        return carry

    lax.fori_loop(0, count // ROWS, step, 0, unroll=count // ROWS)


def coefs(coef_ref, ids):
    return [coef_ref[i : i + 1, :] for i in ids]


def place():
    index = lax.axis_index("line")
    return lax.rem(index, 2) == 0, index > 0, index < lax.axis_size("line") - 1


def spans(r):
    return pl.ds(PAD + r, ROWS), pl.ds(PAD + r - 1, ROWS), pl.ds(PAD + r + 1, ROWS), pl.ds(r, ROWS)


def zero_edges(ref):
    across = ref.shape[-2] - 2 * PAD
    edge = jnp.zeros((PAD, ref.shape[-1]), jnp.float32)
    for where in np.ndindex(*ref.shape[:-2]):
        ref[(*where, pl.ds(0, PAD))] = edge
        ref[(*where, pl.ds(PAD + across, PAD))] = edge


class Halves:
    def __init__(self, *refs):
        self.refs, self.half, self.rows = refs, 0, refs[0].shape[1]

    def at(self, out):
        return pl.ds(out.start - self.half * self.rows, out.size)

    def __getitem__(self, at):
        return self.refs[self.half][at[0], self.at(at[1])]

    def __setitem__(self, at, value):
        self.refs[self.half][at[0], self.at(at[1])] = value

    def add_force(self, plane, force, which, first_row):
        upper, lower = self.refs
        above = self.rows - first_row
        upper[plane, pl.ds(first_row, above)] = upper[plane, pl.ds(first_row, above)] + force[which][:above]
        lower[plane, pl.ds(0, 16 - above)] = lower[plane, pl.ds(0, 16 - above)] + force[which][above:]


def over_message(count, work, msg):
    if not isinstance(msg, Halves):
        over_rows(count, work)
        return
    for half in range(2):
        msg.half = half
        over_rows(msg.rows, work, half * msg.rows)


def add_force(ref, index, force, which, first_row):
    if isinstance(ref, Halves):
        ref.add_force(*index, force, which, first_row)
        return
    rows = pl.ds(first_row, 16)
    ref[(*index, rows)] = ref[(*index, rows)] + force[which]


def pre_ahead(V, S, coef_ref, msg, force, window):
    b, b0 = coefs(coef_ref, (C_B, C_B0))

    def work(r):
        here, up, _, out = spans(r)
        sxy, sxz = S[XY, 1, here], S[XZ, 1, here]
        px = V[VX, 1, here] + b * (sxy - S[XY, 1, up] + sxz - S[XX, 1, here]) - b0 * before(sxz)
        V[VX, 1, here] = px
        if msg is not None:
            msg[0, out] = sxy
            msg[1, out] = sxz
            msg[2, out] = px

    over_message(V.shape[2] - 2 * PAD, work, msg)
    if force is not None:
        add_force(V, (VX, 1), force, (VX, 1), PAD + window)
        if msg is not None:
            add_force(msg, (2,), force, (VX, 1), window)


def pre_behind(V, S, coef_ref, msg, force, window):
    b, b0, b1 = coefs(coef_ref, (C_B, C_B0, C_B1))

    def work(r):
        here, up, down, out = spans(r)
        syz, szz = S[YZ, 0, here], S[ZZ, 0, here]
        qy = V[VY, 0, here] + b * (S[XY, 0, here] + S[YY, 0, down] - S[YY, 0, here] + syz) - b0 * before(syz)
        qz = V[VZ, 0, here] + b * (S[XZ, 0, here] + syz - S[YZ, 0, up] - szz) + b1 * after(szz)
        V[VY, 0, here] = qy
        V[VZ, 0, here] = qz
        if msg is not None:
            msg[0, out] = S[XX, 0, here]
            msg[1, out] = qy
            msg[2, out] = qz

    over_message(V.shape[2] - 2 * PAD, work, msg)
    if force is not None:
        add_force(V, (VY, 0), force, (VY, 0), PAD + window)
        add_force(V, (VZ, 0), force, (VZ, 0), PAD + window)
        if msg is not None:
            add_force(msg, (1,), force, (VY, 0), window)
            add_force(msg, (2,), force, (VZ, 0), window)


def inner(V, S, coef_ref, force, window):
    b, b0, b1 = coefs(coef_ref, (C_B, C_B0, C_B1))

    def work(r):
        here, up, down, _ = spans(r)
        sxy, sxz = S[XY, 0, here], S[XZ, 0, here]
        V[VX, 0, here] = (
            V[VX, 0, here]
            + b * (S[XX, 1, here] - S[XX, 0, here] + sxy - S[XY, 0, up] + sxz)
            - b0 * before(sxz)
        )
        syz, szz = S[YZ, 1, here], S[ZZ, 1, here]
        V[VY, 1, here] = (
            V[VY, 1, here]
            + b * (S[XY, 1, here] - sxy + S[YY, 1, down] - S[YY, 1, here] + syz)
            - b0 * before(syz)
        )
        V[VZ, 1, here] = (
            V[VZ, 1, here]
            + b * (S[XZ, 1, here] - sxz + syz - S[YZ, 1, up] - szz)
            + b1 * after(szz)
        )

    over_rows(V.shape[2] - 2 * PAD, work)
    if force is not None:
        add_force(V, (VX, 0), force, (VX, 0), PAD + window)
        add_force(V, (VY, 1), force, (VY, 1), PAD + window)
        add_force(V, (VZ, 1), force, (VZ, 1), PAD + window)


def post(V, S, R, coef_ref, surface, cell, column, behind_x, ahead_y, ahead_z):
    m0, m1, lam, mu2, mu, k1, k2, k2h, l0 = coefs(
        coef_ref, (C_M0, C_M1, C_LAM, C_MU2, C_MU, C_K1, C_K2, C_K2H, C_L0)
    )

    def work(r):
        here, up, down, out = spans(r)
        vx, vy, vz = V[VX, cell, here], V[VY, cell, here], V[VZ, cell, here]
        exx = vx - behind_x(r)
        eyy = vy - V[VY, cell, up]
        ezz = vz - m0 * before(vz)
        exy = V[VX, cell, down] - vx + (ahead_y(r) - vy)
        exz = m1 * after(vx) - vx + (ahead_z(r) - vz)
        eyz = m1 * after(vy) - vy + (V[VZ, cell, down] - vz)
        volume = lam * (exx + eyy + ezz)
        for comp, e in ((XX, exx), (YY, eyy), (ZZ, ezz)):
            old = R[comp, cell, out]
            new = S[comp, cell, here] + (volume + mu2 * e) + DT * old
            if comp == ZZ:
                new = new + l0 * lane_roll(surface[out, :], -column)
            S[comp, cell, here] = new
            R[comp, cell, out] = k1 * old - k2 * e
        for comp, e in ((XY, exy), (XZ, exz), (YZ, eyz)):
            old = R[comp, cell, out]
            S[comp, cell, here] = S[comp, cell, here] + mu * e + DT * old
            R[comp, cell, out] = k1 * old - k2h * e

    over_rows(R.shape[2], work)


def response_behind(V, S, coef_ref, D, W):
    b, b0, b1, m0, m1, lam, mu2, mu = coefs(coef_ref, (C_B, C_B0, C_B1, C_M0, C_M1, C_LAM, C_MU2, C_MU))

    def work(r):
        here, up, down, out = spans(r)
        sxy = S[XY, 1, here]
        vy, vz = -b * sxy, -b * S[XZ, 1, here]
        exx = -V[VX, 1, here]
        eyy = b * (S[XY, 1, up] - sxy)
        ezz = vz - m0 * before(vz)
        volume = lam * (exx + eyy + ezz)
        dyy, dzz = volume + mu2 * eyy, volume + mu2 * ezz
        dyz = mu * (m1 * after(vy) - vy - b * S[XZ, 1, down] - vz)
        W[0, here] = dyy
        W[1, here] = dyz
        D[0, out] = volume + mu2 * exx
        D[1, out] = vy + b * (dyz - mu * vy - dyy) - b0 * before(dyz)
        D[2, out] = vz + b * (dyz - mu * vz - dzz) + b1 * after(dzz)

    over_rows(D.shape[1], work)

    def rest(r):
        _, up, down, out = spans(r)
        D[1, out] = D[1, out] + b * W[0, down]
        D[2, out] = D[2, out] - b * W[1, up]

    over_rows(D.shape[1], rest)


def response_ahead(V, S, coef_ref, D, W):
    b, b0, m1, lam, mu2, mu = coefs(coef_ref, (C_B, C_B0, C_M1, C_LAM, C_MU2, C_MU))

    def work(r):
        here, _, down, out = spans(r)
        vx = b * S[XX, 0, here]
        dxy = mu * (b * S[XX, 0, down] - vx + V[VY, 0, here])
        dxz = mu * (m1 * after(vx) - vx + V[VZ, 0, here])
        W[0, here] = dxy
        D[0, out] = dxy
        D[1, out] = dxz
        D[2, out] = vx + b * (dxy + dxz - (lam + mu2) * vx) - b0 * before(dxz)

    over_rows(D.shape[1], work)

    def rest(r):
        _, up, _, out = spans(r)
        D[2, out] = D[2, out] - b * W[0, up]

    over_rows(D.shape[1], rest)


def early_ahead(V, S, R, coef_ref, msg, W, force, window):
    b, b0, m0, m1, lam, mu2, mu = coefs(coef_ref, (C_B, C_B0, C_M0, C_M1, C_LAM, C_MU2, C_MU))

    def work(r):
        here, up, down, out = spans(r)
        vx, vy, vz = V[VX, 1, here], V[VY, 1, here], V[VZ, 1, here]
        exx = vx - V[VX, 0, here]
        volume = lam * (exx + (vy - V[VY, 1, up]) + (vz - m0 * before(vz)))
        sxx = S[XX, 1, here] + (volume + mu2 * exx) + DT * R[XX, 1, out]
        sxy = S[XY, 1, here] + mu * (V[VX, 1, down] - vx - vy) + DT * R[XY, 1, out]
        sxz = S[XZ, 1, here] + mu * (m1 * after(vx) - vx - vz) + DT * R[XZ, 1, out]
        W[0, here] = sxy
        msg[0, out] = sxy
        msg[1, out] = sxz
        msg[2, out] = vx + b * (sxy + sxz - sxx) - b0 * before(sxz)

    over_rows(msg.shape[1], work)

    def rest(r):
        _, up, _, out = spans(r)
        msg[2, out] = msg[2, out] - b * W[0, up]

    over_rows(msg.shape[1], rest)
    if force is not None:
        add_force(msg, (2,), force, (VX, 1), window)


def early_behind(V, S, R, coef_ref, surface, column, msg, W, force, window):
    b, b0, b1, m0, m1, lam, mu2, mu, l0 = coefs(
        coef_ref, (C_B, C_B0, C_B1, C_M0, C_M1, C_LAM, C_MU2, C_MU, C_L0)
    )

    def work(r):
        here, up, down, out = spans(r)
        vx, vy, vz = V[VX, 0, here], V[VY, 0, here], V[VZ, 0, here]
        eyy = vy - V[VY, 0, up]
        ezz = vz - m0 * before(vz)
        volume = lam * (vx + eyy + ezz)
        sxx = S[XX, 0, here] + (volume + mu2 * vx) + DT * R[XX, 0, out]
        syy = S[YY, 0, here] + (volume + mu2 * eyy) + DT * R[YY, 0, out]
        szz = S[ZZ, 0, here] + (volume + mu2 * ezz) + DT * R[ZZ, 0, out]
        if surface is not None:
            szz = szz + l0 * lane_roll(surface[out, :], -column)
        sxy = S[XY, 0, here] + mu * (V[VX, 0, down] - vx + (V[VY, 1, here] - vy)) + DT * R[XY, 0, out]
        sxz = S[XZ, 0, here] + mu * (m1 * after(vx) - vx + (V[VZ, 1, here] - vz)) + DT * R[XZ, 0, out]
        syz = S[YZ, 0, here] + mu * (m1 * after(vy) - vy + (V[VZ, 0, down] - vz)) + DT * R[YZ, 0, out]
        W[0, here] = syy
        W[1, here] = syz
        msg[0, out] = sxx
        msg[1, out] = vy + b * (sxy - syy + syz) - b0 * before(syz)
        msg[2, out] = vz + b * (sxz + syz - szz) + b1 * after(szz)

    over_rows(msg.shape[1], work)

    def rest(r):
        _, up, down, out = spans(r)
        msg[1, out] = msg[1, out] + b * W[0, down]
        msg[2, out] = msg[2, out] - b * W[1, up]

    over_rows(msg.shape[1], rest)
    if force is not None:
        add_force(msg, (1,), force, (VY, 0), window)
        add_force(msg, (2,), force, (VZ, 0), window)


def ahead_bond(V, S, R, coef_ref, force, surface, msg, missing, G, step, window, unforced=0, respond=None):
    (b,) = coefs(coef_ref, (C_B,))
    _, _, has_ahead = place()
    keep = jnp.where(has_ahead, 1.0, 0.0).astype(jnp.float32)

    def got(i, out):
        return msg[i, out] if missing is None else msg[i, out] + missing[i, out]

    def work(r):
        here, _, _, out = spans(r)
        V[VX, 1, here] = V[VX, 1, here] + (keep * b) * got(0, out)
        G[0, out] = keep * (got(1, out) - b * S[XY, 1, here])
        G[1, out] = keep * (got(2, out) - b * S[XZ, 1, here])

    over_message(R.shape[2], work, msg)
    if step < unforced:
        add_force(G, (0,), force, (VY, 2), window)
        add_force(G, (1,), force, (VZ, 2), window)
    if respond is not None:
        respond()
    post(
        V, S, R, coef_ref, surface, 1, 2 * step + 1,
        lambda r: V[VX, 0, pl.ds(PAD + r, ROWS)],
        lambda r: G[0, pl.ds(r, ROWS)],
        lambda r: G[1, pl.ds(r, ROWS)],
    )


def behind_bond(V, S, R, coef_ref, force, surface, msg, missing, G, step, window, unforced=0, respond=None):
    (b,) = coefs(coef_ref, (C_B,))
    _, has_behind, _ = place()
    keep = jnp.where(has_behind, 1.0, 0.0).astype(jnp.float32)

    def got(i, out):
        return msg[i, out] if missing is None else msg[i, out] + missing[i, out]

    def work(r):
        here, _, _, out = spans(r)
        V[VY, 0, here] = V[VY, 0, here] - (keep * b) * got(0, out)
        V[VZ, 0, here] = V[VZ, 0, here] - (keep * b) * got(1, out)
        G[0, out] = keep * (got(2, out) + b * S[XX, 0, here])

    over_message(R.shape[2], work, msg)
    if step < unforced:
        add_force(G, (0,), force, (VX, 2), window)
    if respond is not None:
        respond()
    post(
        V, S, R, coef_ref, surface, 0, 2 * step,
        lambda r: G[0, pl.ds(r, ROWS)],
        lambda r: V[VY, 1, pl.ds(PAD + r, ROWS)],
        lambda r: V[VZ, 1, pl.ds(PAD + r, ROWS)],
    )


def start_kernel(
    velocity, stress, memory, layer_in, lam_in, mu_in, buoy_in, rate_in, defect_in, after_this,
    V, S, R, coef_ref, near_upper, near_lower, msg_far, layer_ref, lam, mu, buoy, rate, defect, sems,
):
    del after_this
    msg_near = Halves(near_upper, near_lower)
    across = velocity.shape[2]
    inside = pl.ds(PAD, across)
    pairs = [
        (layer_in, layer_ref), (lam_in, lam), (mu_in, mu), (buoy_in, buoy), (rate_in, rate), (defect_in, defect),
    ]
    pairs += [(stress.at[i], S.at[i, :, inside]) for i in range(6)]
    pairs += [(velocity.at[i], V.at[i, :, inside]) for i in range(3)]
    pairs += [(memory.at[i], R.at[i]) for i in range(6)]
    copies = [pltpu.make_async_copy(*pair, sems.at[i]) for i, pair in enumerate(pairs)]
    for copy in copies:
        copy.start()
    zero_edges(V)
    zero_edges(S)
    for copy in copies[:6]:
        copy.wait()
    layer = layer_ref[...]

    def per_depth(table):
        row = jnp.zeros(layer.shape, jnp.float32)
        for level in range(table.shape[0]):
            row = jnp.where(layer == level, table[level], row)
        return row

    lane = lax.broadcasted_iota(jnp.int32, layer.shape, 1)
    not_first = jnp.where(lane > 0, 1.0, 0.0).astype(jnp.float32)
    not_last = jnp.where(lane < layer.shape[1] - 1, 1.0, 0.0).astype(jnp.float32)
    b = DT * per_depth(buoy)
    two_mu = (2.0 * DT) * per_depth(mu)
    decay = DT * per_depth(rate)
    drop = 2.0 * decay * per_depth(defect)
    for row, value in (
        (C_B, b),
        (C_B0, b * not_first),
        (C_B1, b * not_last),
        (C_M0, not_first),
        (C_M1, not_last),
        (C_LAM, DT * per_depth(lam)),
        (C_MU2, two_mu),
        (C_MU, 0.5 * two_mu),
        (C_K1, 1.0 - decay),
        (C_K2, drop),
        (C_K2H, 0.5 * drop),
        (C_L0, DT * (1.0 - not_first)),
    ):
        coef_ref[row : row + 1, :] = value
    coef_ref[12:16, :] = jnp.zeros((4, layer.shape[1]), jnp.float32)
    for copy in copies[6:15]:
        copy.wait()
    even, _, _ = place()

    @pl.when(even)
    def _():
        pre_ahead(V, S, coef_ref, msg_near, None, 0)
        pre_behind(V, S, coef_ref, msg_far, None, 0)

    @pl.when(jnp.logical_not(even))
    def _():
        pre_behind(V, S, coef_ref, msg_near, None, 0)
        pre_ahead(V, S, coef_ref, msg_far, None, 0)

    for copy in copies[15:]:
        copy.wait()


def first_kernel(window, V0, S, R, coef_ref, force, surface, V, msg, W):
    even, _, _ = place()
    zero_edges(W)
    now, then = force.at[0], force.at[1]
    add_force(V, (VX, 1), now, (VX, 1), PAD + window)
    add_force(V, (VY, 0), now, (VY, 0), PAD + window)
    add_force(V, (VZ, 0), now, (VZ, 0), PAD + window)
    inner(V, S, coef_ref, now, window)

    @pl.when(even)
    def _():
        early_behind(V, S, R, coef_ref, surface, 0, msg, W, then, window)

    @pl.when(jnp.logical_not(even))
    def _():
        early_ahead(V, S, R, coef_ref, msg, W, then, window)


def results_out(V, S, R, results, sems, cell):
    inside = pl.ds(PAD, R.shape[2])
    pairs = [(V.at[i, cell, inside], results[0].at[i, cell]) for i in range(3)]
    pairs += [(S.at[i, cell, inside], results[1].at[i, cell]) for i in range(6)]
    pairs += [(R.at[i, cell], results[2].at[i, cell]) for i in range(6)]
    return [pltpu.make_async_copy(*pair, sems.at[i]) for i, pair in enumerate(pairs)]


def start_all(copies):
    for copy in copies:
        copy.start()


def wait_all(copies):
    for copy in copies:
        copy.wait()


def near_kernel(step, window, V0, S0, R0, coef_ref, force, surface, upper, lower, V, S, R, *rest):
    G = rest[-1]
    msg = Halves(upper, lower)
    even, _, _ = place()
    more = step < STEPS - 1
    send = Halves(*rest[:2]) if more else None

    @pl.when(even)
    def _():
        ahead_bond(V, S, R, coef_ref, force.at[step], surface, msg, None, G, step, window, 1)
        if more:
            pre_ahead(V, S, coef_ref, send, force.at[step + 1], window)
        else:
            copies = results_out(V, S, R, rest[:3], rest[-2], 1)
            start_all(copies)
            wait_all(copies)

    @pl.when(jnp.logical_not(even))
    def _():
        behind_bond(V, S, R, coef_ref, force.at[step], surface, msg, None, G, step, window, 1)
        if more:
            pre_behind(V, S, coef_ref, send, force.at[step + 1], window)
        else:
            copies = results_out(V, S, R, rest[:3], rest[-2], 0)
            start_all(copies)
            wait_all(copies)


def far_kernel(step, window, V0, S0, R0, coef_ref, force, surface, msg, *rest):
    rest = list(rest)
    missing = rest.pop(0) if step > 0 else None
    V, S, R, D = rest[:4]
    G, W = rest[-2:]
    early = rest[4] if step < STEPS - 2 else None
    even, _, _ = place()
    zero_edges(W)
    here, then = force.at[step], force.at[step + 1]

    @pl.when(even)
    def _():
        behind_bond(
            V, S, R, coef_ref, here, surface, msg, missing, G, step, window, 1,
            lambda: response_ahead(V, S, coef_ref, D, W),
        )
        pre_behind(V, S, coef_ref, None, then, window)

    @pl.when(jnp.logical_not(even))
    def _():
        ahead_bond(
            V, S, R, coef_ref, here, surface, msg, missing, G, step, window, 1,
            lambda: response_behind(V, S, coef_ref, D, W),
        )
        pre_ahead(V, S, coef_ref, None, then, window)

    inner(V, S, coef_ref, then, window)
    if early is not None:
        later = force.at[step + 2]

        @pl.when(even)
        def _():
            early_behind(V, S, R, coef_ref, surface, 2 * (step + 1), early, W, later, window)

        @pl.when(jnp.logical_not(even))
        def _():
            early_ahead(V, S, R, coef_ref, early, W, later, window)


def last_kernel(step, window, V0, S0, R0, coef_ref, force, surface, msg, missing, v0, s0, r0, V, S, R, *rest):
    *results, G, sems = rest
    even, _, _ = place()
    here = force.at[step]

    @pl.when(even)
    def _():
        copies = results_out(V, S, R, results, sems, 0)
        behind_bond(
            V, S, R, coef_ref, here, surface, msg, missing, G, step, window, 0, lambda: start_all(copies[:3])
        )
        start_all(copies[3:])
        wait_all(copies)

    @pl.when(jnp.logical_not(even))
    def _():
        copies = results_out(V, S, R, results, sems, 1)
        ahead_bond(
            V, S, R, coef_ref, here, surface, msg, missing, G, step, window, 0, lambda: start_all(copies[:3])
        )
        start_all(copies[3:])
        wait_all(copies)


ENTRY_ROW, TRUCK_ROW = 36, 40
GROUP = 8


def pack_kernel(
    record, loads_in, entries_in, cells_in, piers_in, own, loads, steps_table, piers, entries, cells, sems
):
    panel = record.shape[1]
    slots, lanes = loads.shape
    steps = entries.shape[0]
    pairs = [(record, own.at[:, pl.ds(0, panel)]), (loads_in, loads), (entries_in, entries), (cells_in, cells)]
    pairs.append((piers_in, piers))
    copies = [pltpu.make_async_copy(*pair, sems.at[i]) for i, pair in enumerate(pairs)]
    for copy in copies:
        copy.start()
    own[:, panel:] = jnp.zeros((own.shape[0], own.shape[1] - panel), jnp.float32)
    steps_table[...] = jnp.zeros(steps_table.shape, jnp.float32)
    for copy in copies:
        copy.wait()
    steps_table[0:steps, 0:slots] = entries[...].astype(jnp.float32)
    steps_table[8 : 8 + steps, 0:slots] = cells[...].astype(jnp.float32)
    blocks = [loads[8 * i : 8 * i + 8, :] for i in range(slots // 8)] + [steps_table[0:8, :]]
    for i, block in enumerate(blocks):
        own[0:8, panel + i * lanes : panel + (i + 1) * lanes] = block


def lane_blocks(table, width):
    return sum(lane_roll(table[s : s + 1, :], s * width) for s in range(STEPS))


def split_kernel(panel, slots, own, behind, cells, after_this, out):
    del after_this
    tiles, _, lanes = out.shape
    pieces = panel // lanes
    third = pieces // 3
    cell_of = cells[...]
    me = lax.axis_index("line")
    group, mine = lax.div(me, tiles), lax.rem(me, tiles)
    piers = cell_of.shape[1]
    row = lax.broadcasted_iota(jnp.int32, (3 * tiles, lanes), 0)
    j = lax.rem(row, 3)
    first = (lax.div(row, 3) + group * tiles) * 2
    cell_x, cell_yz = first + jnp.where(j == 2, -1, j), first + j
    record = jnp.where(group == 0, own[:, :panel], behind[:, :panel])

    def hits(cell):
        return [jnp.where(cell == cell_of[0:1, p : p + 1], 1.0, 0.0).astype(jnp.float32) for p in range(piers)]

    hit_x, hit_yz = hits(cell_x), hits(cell_yz)

    def share(m):
        hit = hit_x if m < third else hit_yz
        return sum(hit[p] * record[p : p + 1, m * lanes : (m + 1) * lanes] for p in range(piers))

    parts = [share(m) for m in range(pieces)]

    def trucks(source):
        blocks = [source[0:8, panel + i * lanes : panel + (i + 1) * lanes] for i in range(slots // 8 + 1)]
        return blocks[:-1], lane_blocks(blocks[-1], slots)

    own_rows, own_entry = trucks(own)
    far_rows, far_entry = trucks(behind)
    for tile in range(tiles):
        these = slice(3 * tile, 3 * tile + 3)
        for m in range(pieces):
            out[tile, 3 * m : 3 * m + 3, :] = parts[m][these, :]
        passed = mine < tile
        out[tile, ENTRY_ROW : ENTRY_ROW + 1, :] = jnp.where(passed, own_entry, far_entry)
        for i in range(slots // 8):
            at = TRUCK_ROW + 8 * i
            out[tile, at : at + 8, :] = jnp.where(passed, own_rows[i], far_rows[i])


def prepare_kernel(parts, loads, steps_table, force, surface, table, rows_out):
    steps, comps, width = force.shape[:3]
    lanes = parts.shape[2]
    force[...] = jnp.zeros(force.shape, jnp.float32)
    per = ENTRY_ROW // (comps * width)
    lane = lax.broadcasted_iota(jnp.int32, (per, lanes), 1)
    scale = jnp.where(lane < FZ, DT, 0.0).astype(jnp.float32)
    for s in range(steps):
        for comp in range(comps):
            for cell in range(width):
                panel = parts[s, pl.ds(comp * per * width + cell, per, stride=width), :]
                force[s, comp, cell, pl.ds(4, per, stride=2), :] = scale * panel
                force[s, comp, cell, pl.ds(5, per, stride=2), :] = scale * lane_roll(panel, FZ)

    slots = loads.shape[0]
    tiles = parts.shape[0]
    mine = lax.rem(lax.axis_index("line"), tiles)
    table[...] = jnp.zeros(table.shape, jnp.float32)
    table[0:1, :] = lane_blocks(steps_table[0:8, :], slots)
    table[STEPS + 1 : STEPS + 2, :] = lane_blocks(steps_table[8:16, :], slots)
    rows = [loads[...]]
    for k in range(1, STEPS + 1):
        source = lax.rem(mine + (tiles - k), tiles)
        rows.append(parts[source, TRUCK_ROW : TRUCK_ROW + slots, :])
        table[k : k + 1, :] = parts[source, ENTRY_ROW : ENTRY_ROW + 1, :]
    columns = table[...].T
    rows_out[...] = jnp.zeros(rows_out.shape, jnp.float32)
    for s in range(STEPS):
        block = slice(s * slots, (s + 1) * slots)
        moved = []
        for k in range(STEPS - s):
            entry = jnp.broadcast_to(columns[block, k : k + 1], rows[k].shape)
            new = rows[k]
            for slot in range(slots):
                new = jnp.where(entry == float(slot), rows[k + 1][slot : slot + 1, :], new)
            moved.append(new)
        rows = moved
        cell = jnp.broadcast_to(columns[block, STEPS + 1 : STEPS + 2], rows[0].shape)
        for c in range(2):
            load = jnp.sum(jnp.where(cell == float(c), rows[0], 0.0), axis=0, keepdims=True)
            rows_out[2 * s + c : 2 * s + c + 1, :] = load
    surface[...] = rows_out[...].T


def in_vmem(x):
    return pltpu.with_memory_space_constraint(x, pltpu.VMEM)


WHOLE = pl.BlockSpec(memory_space=pltpu.VMEM)
SCALARS = pl.BlockSpec(memory_space=pltpu.SMEM)
ANYWHERE = pl.BlockSpec(memory_space=pl.ANY)


def call(kernel, ins, specs, outs, out_specs, scratch=(), aliases=None, name=None, cost=1):
    return pl.pallas_call(
        kernel,
        out_shape=outs,
        in_specs=specs,
        out_specs=out_specs,
        scratch_shapes=list(scratch),
        input_output_aliases=aliases or {},
        compiler_params=pltpu.CompilerParams(vmem_limit_bytes=VMEM_LIMIT),
        cost_estimate=pl.CostEstimate(flops=cost, bytes_accessed=cost, transcendentals=0),
        name=name,
    )(*ins)


def body(
    velocity, stress, memory, truck_loads, pier_panels,
    lame_lambda, lame_mu, buoyancy, relax_rate, defect_mu, layer,
    truck_entry, truck_cell, pier_cell,
):
    tiles = lax.axis_size("line")
    width_x, across, depth = velocity.shape[1:]
    slots = truck_loads.shape[0]
    window = (across - FY) // 2 - 4
    f32 = jnp.float32

    near = [(i, i ^ 1) for i in range(tiles) if (i ^ 1) < tiles]
    far = [(i, i + 1) for i in range(1, tiles - 1, 2)] + [(i + 1, i) for i in range(1, tiles - 1, 2)]

    padded = across + 2 * PAD
    v_type = pltpu.VMEM((3, width_x, padded, depth), f32)
    s_type = pltpu.VMEM((6, width_x, padded, depth), f32)
    r_type = pltpu.VMEM((6, width_x, across, depth), f32)
    c_type = pltpu.VMEM((N_COEF, depth), f32)
    m_type = pltpu.VMEM((3, across, depth), f32)
    planes = (pltpu.VMEM((3, across // 2, depth), f32),) * 2
    ghost = pltpu.VMEM((2, across, depth), f32)
    work = pltpu.VMEM((2, padded, depth), f32)

    def ahead_by(x, distance):
        return lax.ppermute(x, "line", [(i, i + distance) for i in range(tiles - distance)])

    def in_hbm(*arrays):
        return tuple(pltpu.with_memory_space_constraint(x, pltpu.HBM) for x in arrays)

    dma = pltpu.SemaphoreType.DMA
    piers, panel = pier_panels.shape[1:]
    own, loads, steps_table, pier_row = call(
        pack_kernel,
        in_hbm(pier_panels[0], truck_loads, truck_entry, truck_cell, pier_cell[None, :]),
        (ANYWHERE,) * 5,
        (
            pltpu.VMEM((piers, panel + (slots // 8 + 1) * depth), f32),
            pltpu.VMEM((slots, depth), f32),
            pltpu.VMEM((16, depth), f32),
            pltpu.VMEM((1, piers), jnp.int32),
        ),
        (WHOLE,) * 4,
        scratch=(pltpu.VMEM(truck_entry.shape, jnp.int32), pltpu.VMEM(truck_cell.shape, jnp.int32), dma((5,))),
        name="pack",
    )
    behind = ahead_by(own, GROUP)
    reach = 2 * GROUP
    index = lax.axis_index("line")
    while reach < tiles:
        record = jnp.where(index < GROUP, own, behind)[:, :panel]
        record = jnp.where(index < reach, record, ahead_by(record, reach))
        behind = jnp.concatenate([record, behind[:, panel:]], axis=1)
        reach *= 2
    tables = (lame_lambda, lame_mu, buoyancy, relax_rate, defect_mu)
    V, S, R, coef, *msg_near, msg_far = call(
        start_kernel,
        in_hbm(velocity, stress, memory, layer[None, :], *tables) + (steps_table,),
        (ANYWHERE,) * 10,
        (v_type, s_type, r_type, c_type, *planes, m_type),
        (WHOLE,) * 7,
        scratch=(
            pltpu.VMEM((1, depth), jnp.int32), *(pltpu.SMEM(table.shape, f32) for table in tables), dma((21,)),
        ),
        name="start",
        cost=8 * 1024 * 1024,
    )
    msg_far = lax.ppermute(msg_far, "line", far)
    msg_near = [lax.ppermute(plane, "line", near) for plane in msg_near]
    parts = call(
        functools.partial(split_kernel, panel, slots),
        (own, behind, in_vmem(pier_row), coef),
        (WHOLE,) * 3 + (ANYWHERE,),
        pltpu.VMEM((GROUP, TRUCK_ROW + slots, depth), f32),
        WHOLE,
        name="split",
    )
    groups = [list(range(at, at + GROUP)) for at in range(0, tiles, GROUP)]
    parts = lax.all_to_all(parts, "line", 0, 0, axis_index_groups=groups, tiled=True)
    force, surface = call(
        prepare_kernel,
        (parts, in_vmem(loads), in_vmem(steps_table)),
        (WHOLE,) * 3,
        (pltpu.VMEM((STEPS, 3, 3, 16, depth), f32), pltpu.VMEM((across, depth), f32)),
        (WHOLE,) * 2,
        scratch=(pltpu.VMEM((depth, depth), f32), pltpu.VMEM((depth, across), f32)),
        name="prepare",
    )
    V, early = call(
        functools.partial(first_kernel, window),
        tuple(in_vmem(x) for x in (V, S, R, coef, force, surface)),
        (WHOLE,) * 6,
        (v_type, m_type),
        (WHOLE,) * 2,
        scratch=(work,),
        aliases={0: 0},
        name="first",
    )
    early = lax.ppermute(early, "line", far)
    state = (v_type, s_type, r_type)
    results = tuple(jax.ShapeDtypeStruct(x.shape, f32) for x in (velocity, stress, memory))
    same = {0: 0, 1: 1, 2: 2}
    missing = None
    for step in range(STEPS):
        more = step < STEPS - 1
        ins = tuple(in_vmem(x) for x in (V, S, R, coef, force, surface, *msg_near))
        outs = state + (planes if more else results)
        V, S, R, *msg = call(
            functools.partial(near_kernel, step, window),
            ins,
            (WHOLE,) * len(ins),
            outs,
            (WHOLE,) * 5 if more else (WHOLE,) * 3 + (ANYWHERE,) * 3,
            scratch=(ghost,) if more else (dma((15,)), ghost),
            aliases=same,
            name="near" + str(step),
        )
        if more:
            msg_near = [lax.ppermute(plane, "line", near) for plane in msg]
        ins = (V, S, R, coef, force, surface, msg_far) + ((missing,) if step else ())
        ins = tuple(in_vmem(x) for x in ins)
        if more:
            outs = state + (m_type,) + ((m_type,) if step < STEPS - 2 else ())
            V, S, R, missing, *msg = call(
                functools.partial(far_kernel, step, window),
                ins,
                (WHOLE,) * len(ins),
                outs,
                (WHOLE,) * len(outs),
                scratch=(ghost, work),
                aliases=same,
                name="far" + str(step),
            )
            msg_far = early
            if msg:
                early = lax.ppermute(msg[0], "line", far)
    ends = call(
        functools.partial(last_kernel, STEPS - 1, window),
        ins + tuple(msg),
        (WHOLE,) * 8 + (ANYWHERE,) * 3,
        state + results,
        (WHOLE,) * 3 + (ANYWHERE,) * 3,
        scratch=(ghost, dma((15,))),
        aliases={**same, 8: 3, 9: 4, 10: 5},
        name="last",
    )
    return ends[3:]


def solution(mesh):
    placed = (
        P(None, ("runs", "line"), None, None),
        P(None, ("runs", "line"), None, None),
        P(None, ("runs", "line"), None, None),
        P(("runs", "line"), None),
        P("line", "runs", None),
        P(),
        P(),
        P(),
        P(),
        P(),
        P(),
        P(None, ("runs", "line")),
        P(None, ("runs", "line")),
        P(),
    )
    return jax.shard_map(
        body,
        mesh=mesh,
        in_specs=placed,
        out_specs=(
            P(None, ("runs", "line"), None, None),
            P(None, ("runs", "line"), None, None),
            P(None, ("runs", "line"), None, None),
        ),
        check_vma=False,
    )
```

```python
import functools

import jax
import jax.numpy as jnp
import numpy as np
from jax import lax
from jax.experimental import pallas as pl
from jax.experimental.pallas import tpu as pltpu
from jax.sharding import PartitionSpec as P

STEPS = 6
FY = 8
FZ = 64
DT = 0.25
PAD = 8
ROWS = 16
UNROLL = 8
VMEM_LIMIT = 32 * 1024 * 1024

C_B, C_B0, C_B1, C_M0, C_M1, C_LAM, C_MU2, C_MU, C_K1, C_K2, C_K2H, C_L0 = range(12)
N_COEF = 16

VX, VY, VZ = range(3)
XX, YY, ZZ, XY, XZ, YZ = range(6)


def lane_roll(x, shift):
    return pltpu.roll(x, shift % x.shape[-1], x.ndim - 1)


def before(x):
    return lane_roll(x, 1)


def after(x):
    return lane_roll(x, -1)


def over_rows(count, work):
    def step(i, carry):
        work(pl.multiple_of(i * ROWS, ROWS))
        return carry

    lax.fori_loop(0, count // ROWS, step, 0, unroll=UNROLL)


def coefs(coef_ref, ids):
    return [coef_ref[i : i + 1, :] for i in ids]


def place():
    index = lax.axis_index("line")
    return lax.rem(index, 2) == 0, index > 0, index < lax.axis_size("line") - 1


def spans(r):
    return pl.ds(PAD + r, ROWS), pl.ds(PAD + r - 1, ROWS), pl.ds(PAD + r + 1, ROWS), pl.ds(r, ROWS)


def zero_edges(ref):
    across = ref.shape[-2] - 2 * PAD
    edge = jnp.zeros((PAD, ref.shape[-1]), jnp.float32)
    for where in np.ndindex(*ref.shape[:-2]):
        ref[(*where, pl.ds(0, PAD))] = edge
        ref[(*where, pl.ds(PAD + across, PAD))] = edge


def add_force(ref, index, force, which, first_row):
    rows = pl.ds(first_row, 16)
    ref[(*index, rows)] = ref[(*index, rows)] + force[which]


def pre_ahead(V, S, coef_ref, msg, force, window):
    b, b0 = coefs(coef_ref, (C_B, C_B0))

    def work(r):
        here, up, _, out = spans(r)
        sxy, sxz = S[XY, 1, here], S[XZ, 1, here]
        px = V[VX, 1, here] + b * (sxy - S[XY, 1, up] + sxz - S[XX, 1, here]) - b0 * before(sxz)
        V[VX, 1, here] = px
        if msg is not None:
            msg[0, out] = sxy
            msg[1, out] = sxz
            msg[2, out] = px

    over_rows(V.shape[2] - 2 * PAD, work)
    if force is not None:
        add_force(V, (VX, 1), force, (VX, 1), PAD + window)
        if msg is not None:
            add_force(msg, (2,), force, (VX, 1), window)


def pre_behind(V, S, coef_ref, msg, force, window):
    b, b0, b1 = coefs(coef_ref, (C_B, C_B0, C_B1))

    def work(r):
        here, up, down, out = spans(r)
        syz, szz = S[YZ, 0, here], S[ZZ, 0, here]
        qy = V[VY, 0, here] + b * (S[XY, 0, here] + S[YY, 0, down] - S[YY, 0, here] + syz) - b0 * before(syz)
        qz = V[VZ, 0, here] + b * (S[XZ, 0, here] + syz - S[YZ, 0, up] - szz) + b1 * after(szz)
        V[VY, 0, here] = qy
        V[VZ, 0, here] = qz
        if msg is not None:
            msg[0, out] = S[XX, 0, here]
            msg[1, out] = qy
            msg[2, out] = qz

    over_rows(V.shape[2] - 2 * PAD, work)
    if force is not None:
        add_force(V, (VY, 0), force, (VY, 0), PAD + window)
        add_force(V, (VZ, 0), force, (VZ, 0), PAD + window)
        if msg is not None:
            add_force(msg, (1,), force, (VY, 0), window)
            add_force(msg, (2,), force, (VZ, 0), window)


def inner(V, S, coef_ref, force, window):
    b, b0, b1 = coefs(coef_ref, (C_B, C_B0, C_B1))

    def work(r):
        here, up, down, _ = spans(r)
        sxy, sxz = S[XY, 0, here], S[XZ, 0, here]
        V[VX, 0, here] = (
            V[VX, 0, here]
            + b * (S[XX, 1, here] - S[XX, 0, here] + sxy - S[XY, 0, up] + sxz)
            - b0 * before(sxz)
        )
        syz, szz = S[YZ, 1, here], S[ZZ, 1, here]
        V[VY, 1, here] = (
            V[VY, 1, here]
            + b * (S[XY, 1, here] - sxy + S[YY, 1, down] - S[YY, 1, here] + syz)
            - b0 * before(syz)
        )
        V[VZ, 1, here] = (
            V[VZ, 1, here]
            + b * (S[XZ, 1, here] - sxz + syz - S[YZ, 1, up] - szz)
            + b1 * after(szz)
        )

    over_rows(V.shape[2] - 2 * PAD, work)
    if force is not None:
        add_force(V, (VX, 0), force, (VX, 0), PAD + window)
        add_force(V, (VY, 1), force, (VY, 1), PAD + window)
        add_force(V, (VZ, 1), force, (VZ, 1), PAD + window)


def post(V, S, R, coef_ref, surface, cell, column, behind_x, ahead_y, ahead_z):
    m0, m1, lam, mu2, mu, k1, k2, k2h, l0 = coefs(
        coef_ref, (C_M0, C_M1, C_LAM, C_MU2, C_MU, C_K1, C_K2, C_K2H, C_L0)
    )

    def work(r):
        here, up, down, out = spans(r)
        vx, vy, vz = V[VX, cell, here], V[VY, cell, here], V[VZ, cell, here]
        exx = vx - behind_x(r)
        eyy = vy - V[VY, cell, up]
        ezz = vz - m0 * before(vz)
        exy = V[VX, cell, down] - vx + (ahead_y(r) - vy)
        exz = m1 * after(vx) - vx + (ahead_z(r) - vz)
        eyz = m1 * after(vy) - vy + (V[VZ, cell, down] - vz)
        volume = lam * (exx + eyy + ezz)
        for comp, e in ((XX, exx), (YY, eyy), (ZZ, ezz)):
            old = R[comp, cell, out]
            new = S[comp, cell, here] + (volume + mu2 * e) + DT * old
            if comp == ZZ:
                new = new + l0 * lane_roll(surface[out, :], -column)
            S[comp, cell, here] = new
            R[comp, cell, out] = k1 * old - k2 * e
        for comp, e in ((XY, exy), (XZ, exz), (YZ, eyz)):
            old = R[comp, cell, out]
            S[comp, cell, here] = S[comp, cell, here] + mu * e + DT * old
            R[comp, cell, out] = k1 * old - k2h * e

    over_rows(R.shape[2], work)


def response_behind(V, S, coef_ref, D, W):
    b, b0, b1, m0, m1, lam, mu2, mu = coefs(coef_ref, (C_B, C_B0, C_B1, C_M0, C_M1, C_LAM, C_MU2, C_MU))

    def work(r):
        here, up, down, out = spans(r)
        sxy = S[XY, 1, here]
        vy, vz = -b * sxy, -b * S[XZ, 1, here]
        exx = -V[VX, 1, here]
        eyy = b * (S[XY, 1, up] - sxy)
        ezz = vz - m0 * before(vz)
        volume = lam * (exx + eyy + ezz)
        dyy, dzz = volume + mu2 * eyy, volume + mu2 * ezz
        dyz = mu * (m1 * after(vy) - vy - b * S[XZ, 1, down] - vz)
        W[0, here] = dyy
        W[1, here] = dyz
        D[0, out] = volume + mu2 * exx
        D[1, out] = vy + b * (dyz - mu * vy - dyy) - b0 * before(dyz)
        D[2, out] = vz + b * (dyz - mu * vz - dzz) + b1 * after(dzz)

    over_rows(D.shape[1], work)

    def rest(r):
        _, up, down, out = spans(r)
        D[1, out] = D[1, out] + b * W[0, down]
        D[2, out] = D[2, out] - b * W[1, up]

    over_rows(D.shape[1], rest)


def response_ahead(V, S, coef_ref, D, W):
    b, b0, m1, lam, mu2, mu = coefs(coef_ref, (C_B, C_B0, C_M1, C_LAM, C_MU2, C_MU))

    def work(r):
        here, _, down, out = spans(r)
        vx = b * S[XX, 0, here]
        dxy = mu * (b * S[XX, 0, down] - vx + V[VY, 0, here])
        dxz = mu * (m1 * after(vx) - vx + V[VZ, 0, here])
        W[0, here] = dxy
        D[0, out] = dxy
        D[1, out] = dxz
        D[2, out] = vx + b * (dxy + dxz - (lam + mu2) * vx) - b0 * before(dxz)

    over_rows(D.shape[1], work)

    def rest(r):
        _, up, _, out = spans(r)
        D[2, out] = D[2, out] - b * W[0, up]

    over_rows(D.shape[1], rest)


def early_ahead(V, S, R, coef_ref, msg, W, force, window):
    b, b0, m0, m1, lam, mu2, mu = coefs(coef_ref, (C_B, C_B0, C_M0, C_M1, C_LAM, C_MU2, C_MU))

    def work(r):
        here, up, down, out = spans(r)
        vx, vy, vz = V[VX, 1, here], V[VY, 1, here], V[VZ, 1, here]
        exx = vx - V[VX, 0, here]
        volume = lam * (exx + (vy - V[VY, 1, up]) + (vz - m0 * before(vz)))
        sxx = S[XX, 1, here] + (volume + mu2 * exx) + DT * R[XX, 1, out]
        sxy = S[XY, 1, here] + mu * (V[VX, 1, down] - vx - vy) + DT * R[XY, 1, out]
        sxz = S[XZ, 1, here] + mu * (m1 * after(vx) - vx - vz) + DT * R[XZ, 1, out]
        W[0, here] = sxy
        msg[0, out] = sxy
        msg[1, out] = sxz
        msg[2, out] = vx + b * (sxy + sxz - sxx) - b0 * before(sxz)

    over_rows(msg.shape[1], work)

    def rest(r):
        _, up, _, out = spans(r)
        msg[2, out] = msg[2, out] - b * W[0, up]

    over_rows(msg.shape[1], rest)
    if force is not None:
        add_force(msg, (2,), force, (VX, 1), window)


def early_behind(V, S, R, coef_ref, surface, column, msg, W, force, window):
    b, b0, b1, m0, m1, lam, mu2, mu, l0 = coefs(
        coef_ref, (C_B, C_B0, C_B1, C_M0, C_M1, C_LAM, C_MU2, C_MU, C_L0)
    )

    def work(r):
        here, up, down, out = spans(r)
        vx, vy, vz = V[VX, 0, here], V[VY, 0, here], V[VZ, 0, here]
        eyy = vy - V[VY, 0, up]
        ezz = vz - m0 * before(vz)
        volume = lam * (vx + eyy + ezz)
        sxx = S[XX, 0, here] + (volume + mu2 * vx) + DT * R[XX, 0, out]
        syy = S[YY, 0, here] + (volume + mu2 * eyy) + DT * R[YY, 0, out]
        szz = S[ZZ, 0, here] + (volume + mu2 * ezz) + DT * R[ZZ, 0, out]
        if surface is not None:
            szz = szz + l0 * lane_roll(surface[out, :], -column)
        sxy = S[XY, 0, here] + mu * (V[VX, 0, down] - vx + (V[VY, 1, here] - vy)) + DT * R[XY, 0, out]
        sxz = S[XZ, 0, here] + mu * (m1 * after(vx) - vx + (V[VZ, 1, here] - vz)) + DT * R[XZ, 0, out]
        syz = S[YZ, 0, here] + mu * (m1 * after(vy) - vy + (V[VZ, 0, down] - vz)) + DT * R[YZ, 0, out]
        W[0, here] = syy
        W[1, here] = syz
        msg[0, out] = sxx
        msg[1, out] = vy + b * (sxy - syy + syz) - b0 * before(syz)
        msg[2, out] = vz + b * (sxz + syz - szz) + b1 * after(szz)

    over_rows(msg.shape[1], work)

    def rest(r):
        _, up, down, out = spans(r)
        msg[1, out] = msg[1, out] + b * W[0, down]
        msg[2, out] = msg[2, out] - b * W[1, up]

    over_rows(msg.shape[1], rest)
    if force is not None:
        add_force(msg, (1,), force, (VY, 0), window)
        add_force(msg, (2,), force, (VZ, 0), window)


def ahead_bond(V, S, R, coef_ref, force, surface, msg, missing, G, step, window, unforced=0, respond=None):
    (b,) = coefs(coef_ref, (C_B,))
    _, _, has_ahead = place()
    keep = jnp.where(has_ahead, 1.0, 0.0).astype(jnp.float32)

    def got(i, out):
        return msg[i, out] if missing is None else msg[i, out] + missing[i, out]

    def work(r):
        here, _, _, out = spans(r)
        V[VX, 1, here] = V[VX, 1, here] + (keep * b) * got(0, out)
        G[0, out] = keep * (got(1, out) - b * S[XY, 1, here])
        G[1, out] = keep * (got(2, out) - b * S[XZ, 1, here])

    over_rows(R.shape[2], work)
    if step < unforced:
        add_force(G, (0,), force, (VY, 2), window)
        add_force(G, (1,), force, (VZ, 2), window)
    if respond is not None:
        respond()
    post(
        V, S, R, coef_ref, surface, 1, 2 * step + 1,
        lambda r: V[VX, 0, pl.ds(PAD + r, ROWS)],
        lambda r: G[0, pl.ds(r, ROWS)],
        lambda r: G[1, pl.ds(r, ROWS)],
    )


def behind_bond(V, S, R, coef_ref, force, surface, msg, missing, G, step, window, unforced=0, respond=None):
    (b,) = coefs(coef_ref, (C_B,))
    _, has_behind, _ = place()
    keep = jnp.where(has_behind, 1.0, 0.0).astype(jnp.float32)

    def got(i, out):
        return msg[i, out] if missing is None else msg[i, out] + missing[i, out]

    def work(r):
        here, _, _, out = spans(r)
        V[VY, 0, here] = V[VY, 0, here] - (keep * b) * got(0, out)
        V[VZ, 0, here] = V[VZ, 0, here] - (keep * b) * got(1, out)
        G[0, out] = keep * (got(2, out) + b * S[XX, 0, here])

    over_rows(R.shape[2], work)
    if step < unforced:
        add_force(G, (0,), force, (VX, 2), window)
    if respond is not None:
        respond()
    post(
        V, S, R, coef_ref, surface, 0, 2 * step,
        lambda r: G[0, pl.ds(r, ROWS)],
        lambda r: V[VY, 1, pl.ds(PAD + r, ROWS)],
        lambda r: V[VZ, 1, pl.ds(PAD + r, ROWS)],
    )


def start_kernel(
    velocity, stress, memory, layer_in, lam_in, mu_in, buoy_in, rate_in, defect_in, after_this,
    V, S, R, coef_ref, msg_near, msg_far, layer_ref, lam, mu, buoy, rate, defect, sems,
):
    del after_this
    across = velocity.shape[2]
    inside = pl.ds(PAD, across)
    pairs = [
        (layer_in, layer_ref), (lam_in, lam), (mu_in, mu), (buoy_in, buoy), (rate_in, rate), (defect_in, defect),
    ]
    pairs += [(stress.at[i], S.at[i, :, inside]) for i in range(6)]
    pairs += [(velocity.at[i], V.at[i, :, inside]) for i in range(3)]
    pairs += [(memory.at[i], R.at[i]) for i in range(6)]
    copies = [pltpu.make_async_copy(*pair, sems.at[i]) for i, pair in enumerate(pairs)]
    for copy in copies:
        copy.start()
    zero_edges(V)
    zero_edges(S)
    for copy in copies[:6]:
        copy.wait()
    layer = layer_ref[...]

    def per_depth(table):
        row = jnp.zeros(layer.shape, jnp.float32)
        for level in range(table.shape[0]):
            row = jnp.where(layer == level, table[level], row)
        return row

    lane = lax.broadcasted_iota(jnp.int32, layer.shape, 1)
    not_first = jnp.where(lane > 0, 1.0, 0.0).astype(jnp.float32)
    not_last = jnp.where(lane < layer.shape[1] - 1, 1.0, 0.0).astype(jnp.float32)
    b = DT * per_depth(buoy)
    two_mu = (2.0 * DT) * per_depth(mu)
    decay = DT * per_depth(rate)
    drop = 2.0 * decay * per_depth(defect)
    for row, value in (
        (C_B, b),
        (C_B0, b * not_first),
        (C_B1, b * not_last),
        (C_M0, not_first),
        (C_M1, not_last),
        (C_LAM, DT * per_depth(lam)),
        (C_MU2, two_mu),
        (C_MU, 0.5 * two_mu),
        (C_K1, 1.0 - decay),
        (C_K2, drop),
        (C_K2H, 0.5 * drop),
        (C_L0, DT * (1.0 - not_first)),
    ):
        coef_ref[row : row + 1, :] = value
    coef_ref[12:16, :] = jnp.zeros((4, layer.shape[1]), jnp.float32)
    for copy in copies[6:15]:
        copy.wait()
    even, _, _ = place()

    @pl.when(even)
    def _():
        pre_ahead(V, S, coef_ref, msg_near, None, 0)
        pre_behind(V, S, coef_ref, msg_far, None, 0)

    @pl.when(jnp.logical_not(even))
    def _():
        pre_behind(V, S, coef_ref, msg_near, None, 0)
        pre_ahead(V, S, coef_ref, msg_far, None, 0)

    for copy in copies[15:]:
        copy.wait()


def first_kernel(window, V0, S, R, coef_ref, force, surface, V, msg, W):
    even, _, _ = place()
    zero_edges(W)
    now, then = force.at[0], force.at[1]
    add_force(V, (VX, 1), now, (VX, 1), PAD + window)
    add_force(V, (VY, 0), now, (VY, 0), PAD + window)
    add_force(V, (VZ, 0), now, (VZ, 0), PAD + window)
    inner(V, S, coef_ref, now, window)

    @pl.when(even)
    def _():
        early_behind(V, S, R, coef_ref, surface, 0, msg, W, then, window)

    @pl.when(jnp.logical_not(even))
    def _():
        early_ahead(V, S, R, coef_ref, msg, W, then, window)


def write_out(V, S, R, results, sems, cell):
    inside = pl.ds(PAD, R.shape[2])
    pairs = [(V.at[:, cell, inside], results[0]), (S.at[:, cell, inside], results[1]), (R.at[:, cell], results[2])]
    copies = [
        pltpu.make_async_copy(source, result.at[:, cell], sems.at[i]) for i, (source, result) in enumerate(pairs)
    ]
    for copy in copies:
        copy.start()
    for copy in copies:
        copy.wait()


def near_kernel(step, window, V0, S0, R0, coef_ref, force, surface, msg, V, S, R, *rest):
    G = rest[-1]
    even, _, _ = place()
    more = step < STEPS - 1

    @pl.when(even)
    def _():
        ahead_bond(V, S, R, coef_ref, force.at[step], surface, msg, None, G, step, window, 1)
        if more:
            pre_ahead(V, S, coef_ref, rest[0], force.at[step + 1], window)
        else:
            write_out(V, S, R, rest[:3], rest[-2], 1)

    @pl.when(jnp.logical_not(even))
    def _():
        behind_bond(V, S, R, coef_ref, force.at[step], surface, msg, None, G, step, window, 1)
        if more:
            pre_behind(V, S, coef_ref, rest[0], force.at[step + 1], window)
        else:
            write_out(V, S, R, rest[:3], rest[-2], 0)


def far_kernel(step, window, V0, S0, R0, coef_ref, force, surface, msg, *rest):
    rest = list(rest)
    missing = rest.pop(0) if step > 0 else None
    V, S, R, D = rest[:4]
    G, W = rest[-2:]
    early = rest[4] if step < STEPS - 2 else None
    even, _, _ = place()
    zero_edges(W)
    here, then = force.at[step], force.at[step + 1]

    @pl.when(even)
    def _():
        behind_bond(
            V, S, R, coef_ref, here, surface, msg, missing, G, step, window, 1,
            lambda: response_ahead(V, S, coef_ref, D, W),
        )
        pre_behind(V, S, coef_ref, None, then, window)

    @pl.when(jnp.logical_not(even))
    def _():
        ahead_bond(
            V, S, R, coef_ref, here, surface, msg, missing, G, step, window, 1,
            lambda: response_behind(V, S, coef_ref, D, W),
        )
        pre_ahead(V, S, coef_ref, None, then, window)

    inner(V, S, coef_ref, then, window)
    if early is not None:
        later = force.at[step + 2]

        @pl.when(even)
        def _():
            early_behind(V, S, R, coef_ref, surface, 2 * (step + 1), early, W, later, window)

        @pl.when(jnp.logical_not(even))
        def _():
            early_ahead(V, S, R, coef_ref, early, W, later, window)


def last_kernel(step, window, V0, S0, R0, coef_ref, force, surface, msg, missing, v0, s0, r0, V, S, R, *rest):
    *results, G, sems = rest
    even, _, _ = place()
    here = force.at[step]

    @pl.when(even)
    def _():
        behind_bond(V, S, R, coef_ref, here, surface, msg, missing, G, step, window)
        write_out(V, S, R, results, sems, 0)

    @pl.when(jnp.logical_not(even))
    def _():
        ahead_bond(V, S, R, coef_ref, here, surface, msg, missing, G, step, window)
        write_out(V, S, R, results, sems, 1)


ENTRY_ROW, TRUCK_ROW = 36, 40
GROUP = 8


def pack_kernel(
    record, loads_in, entries_in, cells_in, piers_in, own, loads, steps_table, piers, entries, cells, sems
):
    panel = record.shape[1]
    slots, lanes = loads.shape
    steps = entries.shape[0]
    pairs = [(record, own.at[:, pl.ds(0, panel)]), (loads_in, loads), (entries_in, entries), (cells_in, cells)]
    pairs.append((piers_in, piers))
    copies = [pltpu.make_async_copy(*pair, sems.at[i]) for i, pair in enumerate(pairs)]
    for copy in copies:
        copy.start()
    own[:, panel:] = jnp.zeros((own.shape[0], own.shape[1] - panel), jnp.float32)
    steps_table[...] = jnp.zeros(steps_table.shape, jnp.float32)
    for copy in copies:
        copy.wait()
    steps_table[0:steps, 0:slots] = entries[...].astype(jnp.float32)
    steps_table[8 : 8 + steps, 0:slots] = cells[...].astype(jnp.float32)
    blocks = [loads[8 * i : 8 * i + 8, :] for i in range(slots // 8)] + [steps_table[0:8, :]]
    for i, block in enumerate(blocks):
        own[0:8, panel + i * lanes : panel + (i + 1) * lanes] = block


def lane_blocks(table, width):
    return sum(lane_roll(table[s : s + 1, :], s * width) for s in range(STEPS))


def split_kernel(panel, slots, own, behind, cells, after_this, result, out, sems):
    del after_this
    tiles, _, lanes = out.shape
    pieces = panel // lanes
    third = pieces // 3
    cell_of = cells[...]
    me = lax.axis_index("line")
    group, mine = lax.div(me, tiles), lax.rem(me, tiles)
    piers = cell_of.shape[1]
    row = lax.broadcasted_iota(jnp.int32, (3 * tiles, lanes), 0)
    j = lax.rem(row, 3)
    first = (lax.div(row, 3) + group * tiles) * 2
    cell_x, cell_yz = first + jnp.where(j == 2, -1, j), first + j
    record = jnp.where(group == 0, own[:, :panel], behind[:, :panel])

    def hits(cell):
        return [jnp.where(cell == cell_of[0:1, p : p + 1], 1.0, 0.0).astype(jnp.float32) for p in range(piers)]

    hit_x, hit_yz = hits(cell_x), hits(cell_yz)

    def share(m):
        hit = hit_x if m < third else hit_yz
        return sum(hit[p] * record[p : p + 1, m * lanes : (m + 1) * lanes] for p in range(piers))

    parts = [share(m) for m in range(pieces)]

    def trucks(source):
        blocks = [source[0:8, panel + i * lanes : panel + (i + 1) * lanes] for i in range(slots // 8 + 1)]
        return blocks[:-1], lane_blocks(blocks[-1], slots)

    copies = []
    own_rows, own_entry = trucks(own)
    far_rows, far_entry = trucks(behind)
    for tile in range(tiles):
        these = slice(3 * tile, 3 * tile + 3)
        for m in range(pieces):
            out[tile, 3 * m : 3 * m + 3, :] = parts[m][these, :]
        passed = mine < tile
        out[tile, ENTRY_ROW : ENTRY_ROW + 1, :] = jnp.where(passed, own_entry, far_entry)
        for i in range(slots // 8):
            at = TRUCK_ROW + 8 * i
            out[tile, at : at + 8, :] = jnp.where(passed, own_rows[i], far_rows[i])
        copies.append(pltpu.make_async_copy(out.at[tile], result.at[tile], sems.at[tile]))
        copies[-1].start()
    for copy in copies:
        copy.wait()


def prepare_kernel(parts, loads, steps_table, force, surface, table, rows_out):
    steps, comps, width = force.shape[:3]
    lanes = parts.shape[2]
    force[...] = jnp.zeros(force.shape, jnp.float32)
    per = ENTRY_ROW // (comps * width)
    lane = lax.broadcasted_iota(jnp.int32, (per, lanes), 1)
    scale = jnp.where(lane < FZ, DT, 0.0).astype(jnp.float32)
    for s in range(steps):
        for comp in range(comps):
            for cell in range(width):
                panel = parts[s, pl.ds(comp * per * width + cell, per, stride=width), :]
                force[s, comp, cell, pl.ds(4, per, stride=2), :] = scale * panel
                force[s, comp, cell, pl.ds(5, per, stride=2), :] = scale * lane_roll(panel, FZ)
    surface_loads(1, parts, loads, steps_table, surface, table, rows_out)


def surface_kernel(parts, loads, steps_table, surface, table, rows_out):
    surface_loads(STEPS, parts, loads, steps_table, surface, table, rows_out)


def surface_loads(steps, parts, loads, steps_table, surface, table, rows_out):
    slots = loads.shape[0]
    tiles = parts.shape[0]
    mine = lax.rem(lax.axis_index("line"), tiles)
    table[...] = jnp.zeros(table.shape, jnp.float32)
    table[0:1, :] = lane_blocks(steps_table[0:8, :], slots)
    table[steps + 1 : steps + 2, :] = lane_blocks(steps_table[8:16, :], slots)
    rows = [loads[...]]
    for k in range(1, steps + 1):
        source = lax.rem(mine + (tiles - k), tiles)
        rows.append(parts[source, TRUCK_ROW : TRUCK_ROW + slots, :])
        table[k : k + 1, :] = parts[source, ENTRY_ROW : ENTRY_ROW + 1, :]
    columns = table[...].T
    rows_out[...] = jnp.zeros(rows_out.shape, jnp.float32)
    for s in range(steps):
        block = slice(s * slots, (s + 1) * slots)
        moved = []
        for k in range(steps - s):
            entry = jnp.broadcast_to(columns[block, k : k + 1], rows[k].shape)
            new = rows[k]
            for slot in range(slots):
                new = jnp.where(entry == float(slot), rows[k + 1][slot : slot + 1, :], new)
            moved.append(new)
        rows = moved
        cell = jnp.broadcast_to(columns[block, steps + 1 : steps + 2], rows[0].shape)
        for c in range(2):
            load = jnp.sum(jnp.where(cell == float(c), rows[0], 0.0), axis=0, keepdims=True)
            rows_out[2 * s + c : 2 * s + c + 1, :] = load
    surface[...] = rows_out[...].T


def in_vmem(x):
    return pltpu.with_memory_space_constraint(x, pltpu.VMEM)


WHOLE = pl.BlockSpec(memory_space=pltpu.VMEM)
SCALARS = pl.BlockSpec(memory_space=pltpu.SMEM)
ANYWHERE = pl.BlockSpec(memory_space=pl.ANY)


def call(kernel, ins, specs, outs, out_specs, scratch=(), aliases=None, name=None, cost=1):
    return pl.pallas_call(
        kernel,
        out_shape=outs,
        in_specs=specs,
        out_specs=out_specs,
        scratch_shapes=list(scratch),
        input_output_aliases=aliases or {},
        compiler_params=pltpu.CompilerParams(vmem_limit_bytes=VMEM_LIMIT),
        cost_estimate=pl.CostEstimate(flops=cost, bytes_accessed=cost, transcendentals=0),
        name=name,
    )(*ins)


def body(
    velocity, stress, memory, truck_loads, pier_panels,
    lame_lambda, lame_mu, buoyancy, relax_rate, defect_mu, layer,
    truck_entry, truck_cell, pier_cell,
):
    tiles = lax.axis_size("line")
    width_x, across, depth = velocity.shape[1:]
    slots = truck_loads.shape[0]
    window = (across - FY) // 2 - 4
    f32 = jnp.float32

    near = [(i, i ^ 1) for i in range(tiles) if (i ^ 1) < tiles]
    far = [(i, i + 1) for i in range(1, tiles - 1, 2)] + [(i + 1, i) for i in range(1, tiles - 1, 2)]

    padded = across + 2 * PAD
    v_type = pltpu.VMEM((3, width_x, padded, depth), f32)
    s_type = pltpu.VMEM((6, width_x, padded, depth), f32)
    r_type = pltpu.VMEM((6, width_x, across, depth), f32)
    c_type = pltpu.VMEM((N_COEF, depth), f32)
    m_type = pltpu.VMEM((3, across, depth), f32)
    ghost = pltpu.VMEM((2, across, depth), f32)
    work = pltpu.VMEM((2, padded, depth), f32)

    def ahead_by(x, distance):
        return lax.ppermute(x, "line", [(i, i + distance) for i in range(tiles - distance)])

    def in_hbm(*arrays):
        return tuple(pltpu.with_memory_space_constraint(x, pltpu.HBM) for x in arrays)

    dma = pltpu.SemaphoreType.DMA
    piers, panel = pier_panels.shape[1:]
    own, loads, steps_table, pier_row = call(
        pack_kernel,
        in_hbm(pier_panels[0], truck_loads, truck_entry, truck_cell, pier_cell[None, :]),
        (ANYWHERE,) * 5,
        (
            pltpu.VMEM((piers, panel + (slots // 8 + 1) * depth), f32),
            pltpu.VMEM((slots, depth), f32),
            pltpu.VMEM((16, depth), f32),
            pltpu.VMEM((1, piers), jnp.int32),
        ),
        (WHOLE,) * 4,
        scratch=(pltpu.VMEM(truck_entry.shape, jnp.int32), pltpu.VMEM(truck_cell.shape, jnp.int32), dma((5,))),
        name="pack",
    )
    behind = ahead_by(own, GROUP)
    reach = 2 * GROUP
    index = lax.axis_index("line")
    while reach < tiles:
        record = jnp.where(index < GROUP, own, behind)[:, :panel]
        record = jnp.where(index < reach, record, ahead_by(record, reach))
        behind = jnp.concatenate([record, behind[:, panel:]], axis=1)
        reach *= 2
    tables = (lame_lambda, lame_mu, buoyancy, relax_rate, defect_mu)
    V, S, R, coef, msg_near, msg_far = call(
        start_kernel,
        in_hbm(velocity, stress, memory, layer[None, :], *tables) + (steps_table,),
        (ANYWHERE,) * 10,
        (v_type, s_type, r_type, c_type, m_type, m_type),
        (WHOLE,) * 6,
        scratch=(
            pltpu.VMEM((1, depth), jnp.int32), *(pltpu.SMEM(table.shape, f32) for table in tables), dma((21,)),
        ),
        name="start",
        cost=8 * 1024 * 1024,
    )
    msg_far = lax.ppermute(msg_far, "line", far)
    msg_near = lax.ppermute(msg_near, "line", near)
    parts = call(
        functools.partial(split_kernel, panel, slots),
        (own, behind, in_vmem(pier_row), coef),
        (WHOLE,) * 3 + (ANYWHERE,),
        jax.ShapeDtypeStruct((GROUP, TRUCK_ROW + slots, depth), f32),
        ANYWHERE,
        scratch=(pltpu.VMEM((GROUP, TRUCK_ROW + slots, depth), f32), dma((GROUP,))),
        name="split",
    )
    groups = [list(range(at, at + GROUP)) for at in range(0, tiles, GROUP)]
    parts = lax.all_to_all(parts, "line", 0, 0, axis_index_groups=groups, tiled=True)
    square = pltpu.VMEM((across, depth), f32)
    turned = (pltpu.VMEM((depth, depth), f32), pltpu.VMEM((depth, across), f32))
    ins = (parts, in_vmem(loads), in_vmem(steps_table))
    force, surface = call(
        prepare_kernel,
        ins,
        (WHOLE,) * 3,
        (pltpu.VMEM((STEPS, 3, 3, 16, depth), f32), square),
        (WHOLE,) * 2,
        scratch=turned,
        name="prepare",
    )
    later = call(surface_kernel, ins, (WHOLE,) * 3, square, WHOLE, scratch=turned, name="surface")
    V, early = call(
        functools.partial(first_kernel, window),
        tuple(in_vmem(x) for x in (V, S, R, coef, force, surface)),
        (WHOLE,) * 6,
        (v_type, m_type),
        (WHOLE,) * 2,
        scratch=(work,),
        aliases={0: 0},
        name="first",
    )
    early = lax.ppermute(early, "line", far)
    state = (v_type, s_type, r_type)
    results = tuple(jax.ShapeDtypeStruct(x.shape, f32) for x in (velocity, stress, memory))
    same = {0: 0, 1: 1, 2: 2}
    missing = None
    for step in range(STEPS):
        more = step < STEPS - 1
        ins = tuple(in_vmem(x) for x in (V, S, R, coef, force, surface, msg_near))
        outs = state + ((m_type,) if more else results)
        V, S, R, *msg = call(
            functools.partial(near_kernel, step, window),
            ins,
            (WHOLE,) * len(ins),
            outs,
            (WHOLE,) * 4 if more else (WHOLE,) * 3 + (ANYWHERE,) * 3,
            scratch=(ghost,) if more else (dma((3,)), ghost),
            aliases=same,
            name="near" + str(step),
        )
        if more:
            msg_near = lax.ppermute(msg[0], "line", near)
        if step == 0:
            surface = later
        ins = (V, S, R, coef, force, surface, msg_far) + ((missing,) if step else ())
        ins = tuple(in_vmem(x) for x in ins)
        if more:
            outs = state + (m_type,) + ((m_type,) if step < STEPS - 2 else ())
            V, S, R, missing, *msg = call(
                functools.partial(far_kernel, step, window),
                ins,
                (WHOLE,) * len(ins),
                outs,
                (WHOLE,) * len(outs),
                scratch=(ghost, work),
                aliases=same,
                name="far" + str(step),
            )
            msg_far = early
            if msg:
                early = lax.ppermute(msg[0], "line", far)
    ends = call(
        functools.partial(last_kernel, STEPS - 1, window),
        ins + tuple(msg),
        (WHOLE,) * 8 + (ANYWHERE,) * 3,
        state + results,
        (WHOLE,) * 3 + (ANYWHERE,) * 3,
        scratch=(ghost, dma((3,))),
        aliases={**same, 8: 3, 9: 4, 10: 5},
        name="last",
    )
    return ends[3:]


def solution(mesh):
    placed = (
        P(None, ("runs", "line"), None, None),
        P(None, ("runs", "line"), None, None),
        P(None, ("runs", "line"), None, None),
        P(("runs", "line"), None),
        P("line", "runs", None),
        P(),
        P(),
        P(),
        P(),
        P(),
        P(),
        P(None, ("runs", "line")),
        P(None, ("runs", "line")),
        P(),
    )
    return jax.shard_map(
        body,
        mesh=mesh,
        in_specs=placed,
        out_specs=(
            P(None, ("runs", "line"), None, None),
            P(None, ("runs", "line"), None, None),
            P(None, ("runs", "line"), None, None),
        ),
        check_vma=False,
    )
```

```python
import functools

import jax
import jax.numpy as jnp
import numpy as np
from jax import lax
from jax.experimental import pallas as pl
from jax.experimental.pallas import tpu as pltpu
from jax.sharding import PartitionSpec as P

STEPS = 6
SOON = 3
FY = 8
FZ = 64
DT = 0.25
PAD = 8
ROWS = 16
UNROLL = 8
VMEM_LIMIT = 32 * 1024 * 1024

C_B, C_B0, C_B1, C_M0, C_M1, C_LAM, C_MU2, C_MU, C_K1, C_K2, C_K2H, C_L0 = range(12)
N_COEF = 16

VX, VY, VZ = range(3)
XX, YY, ZZ, XY, XZ, YZ = range(6)


def lane_roll(x, shift):
    return pltpu.roll(x, shift % x.shape[-1], x.ndim - 1)


def before(x):
    return lane_roll(x, 1)


def after(x):
    return lane_roll(x, -1)


def over_rows(count, work):
    def step(i, carry):
        work(pl.multiple_of(i * ROWS, ROWS))
        return carry

    lax.fori_loop(0, count // ROWS, step, 0, unroll=UNROLL)


def coefs(coef_ref, ids):
    return [coef_ref[i : i + 1, :] for i in ids]


def place():
    index = lax.axis_index("line")
    return lax.rem(index, 2) == 0, index > 0, index < lax.axis_size("line") - 1


def spans(r):
    return pl.ds(PAD + r, ROWS), pl.ds(PAD + r - 1, ROWS), pl.ds(PAD + r + 1, ROWS), pl.ds(r, ROWS)


def zero_edges(ref):
    across = ref.shape[-2] - 2 * PAD
    edge = jnp.zeros((PAD, ref.shape[-1]), jnp.float32)
    for where in np.ndindex(*ref.shape[:-2]):
        ref[(*where, pl.ds(0, PAD))] = edge
        ref[(*where, pl.ds(PAD + across, PAD))] = edge


def add_force(ref, index, force, which, first_row):
    rows = pl.ds(first_row, 16)
    ref[(*index, rows)] = ref[(*index, rows)] + force[which]


def pre_ahead(V, S, coef_ref, msg, force, window):
    b, b0 = coefs(coef_ref, (C_B, C_B0))

    def work(r):
        here, up, _, out = spans(r)
        sxy, sxz = S[XY, 1, here], S[XZ, 1, here]
        px = V[VX, 1, here] + b * (sxy - S[XY, 1, up] + sxz - S[XX, 1, here]) - b0 * before(sxz)
        V[VX, 1, here] = px
        if msg is not None:
            msg[0, out] = sxy
            msg[1, out] = sxz
            msg[2, out] = px

    over_rows(V.shape[2] - 2 * PAD, work)
    if force is not None:
        add_force(V, (VX, 1), force, (VX, 1), PAD + window)
        if msg is not None:
            add_force(msg, (2,), force, (VX, 1), window)


def pre_behind(V, S, coef_ref, msg, force, window):
    b, b0, b1 = coefs(coef_ref, (C_B, C_B0, C_B1))

    def work(r):
        here, up, down, out = spans(r)
        syz, szz = S[YZ, 0, here], S[ZZ, 0, here]
        qy = V[VY, 0, here] + b * (S[XY, 0, here] + S[YY, 0, down] - S[YY, 0, here] + syz) - b0 * before(syz)
        qz = V[VZ, 0, here] + b * (S[XZ, 0, here] + syz - S[YZ, 0, up] - szz) + b1 * after(szz)
        V[VY, 0, here] = qy
        V[VZ, 0, here] = qz
        if msg is not None:
            msg[0, out] = S[XX, 0, here]
            msg[1, out] = qy
            msg[2, out] = qz

    over_rows(V.shape[2] - 2 * PAD, work)
    if force is not None:
        add_force(V, (VY, 0), force, (VY, 0), PAD + window)
        add_force(V, (VZ, 0), force, (VZ, 0), PAD + window)
        if msg is not None:
            add_force(msg, (1,), force, (VY, 0), window)
            add_force(msg, (2,), force, (VZ, 0), window)


def inner(V, S, coef_ref, force, window):
    b, b0, b1 = coefs(coef_ref, (C_B, C_B0, C_B1))

    def work(r):
        here, up, down, _ = spans(r)
        sxy, sxz = S[XY, 0, here], S[XZ, 0, here]
        V[VX, 0, here] = (
            V[VX, 0, here]
            + b * (S[XX, 1, here] - S[XX, 0, here] + sxy - S[XY, 0, up] + sxz)
            - b0 * before(sxz)
        )
        syz, szz = S[YZ, 1, here], S[ZZ, 1, here]
        V[VY, 1, here] = (
            V[VY, 1, here]
            + b * (S[XY, 1, here] - sxy + S[YY, 1, down] - S[YY, 1, here] + syz)
            - b0 * before(syz)
        )
        V[VZ, 1, here] = (
            V[VZ, 1, here]
            + b * (S[XZ, 1, here] - sxz + syz - S[YZ, 1, up] - szz)
            + b1 * after(szz)
        )

    over_rows(V.shape[2] - 2 * PAD, work)
    if force is not None:
        add_force(V, (VX, 0), force, (VX, 0), PAD + window)
        add_force(V, (VY, 1), force, (VY, 1), PAD + window)
        add_force(V, (VZ, 1), force, (VZ, 1), PAD + window)


def post(V, S, R, coef_ref, surface, cell, column, behind_x, ahead_y, ahead_z):
    m0, m1, lam, mu2, mu, k1, k2, k2h, l0 = coefs(
        coef_ref, (C_M0, C_M1, C_LAM, C_MU2, C_MU, C_K1, C_K2, C_K2H, C_L0)
    )

    def work(r):
        here, up, down, out = spans(r)
        vx, vy, vz = V[VX, cell, here], V[VY, cell, here], V[VZ, cell, here]
        exx = vx - behind_x(r)
        eyy = vy - V[VY, cell, up]
        ezz = vz - m0 * before(vz)
        exy = V[VX, cell, down] - vx + (ahead_y(r) - vy)
        exz = m1 * after(vx) - vx + (ahead_z(r) - vz)
        eyz = m1 * after(vy) - vy + (V[VZ, cell, down] - vz)
        volume = lam * (exx + eyy + ezz)
        for comp, e in ((XX, exx), (YY, eyy), (ZZ, ezz)):
            old = R[comp, cell, out]
            new = S[comp, cell, here] + (volume + mu2 * e) + DT * old
            if comp == ZZ:
                new = new + l0 * lane_roll(surface[out, :], -column)
            S[comp, cell, here] = new
            R[comp, cell, out] = k1 * old - k2 * e
        for comp, e in ((XY, exy), (XZ, exz), (YZ, eyz)):
            old = R[comp, cell, out]
            S[comp, cell, here] = S[comp, cell, here] + mu * e + DT * old
            R[comp, cell, out] = k1 * old - k2h * e

    over_rows(R.shape[2], work)


def response_behind(V, S, coef_ref, D, W):
    b, b0, b1, m0, m1, lam, mu2, mu = coefs(coef_ref, (C_B, C_B0, C_B1, C_M0, C_M1, C_LAM, C_MU2, C_MU))

    def work(r):
        here, up, down, out = spans(r)
        sxy = S[XY, 1, here]
        vy, vz = -b * sxy, -b * S[XZ, 1, here]
        exx = -V[VX, 1, here]
        eyy = b * (S[XY, 1, up] - sxy)
        ezz = vz - m0 * before(vz)
        volume = lam * (exx + eyy + ezz)
        dyy, dzz = volume + mu2 * eyy, volume + mu2 * ezz
        dyz = mu * (m1 * after(vy) - vy - b * S[XZ, 1, down] - vz)
        W[0, here] = dyy
        W[1, here] = dyz
        D[0, out] = volume + mu2 * exx
        D[1, out] = vy + b * (dyz - mu * vy - dyy) - b0 * before(dyz)
        D[2, out] = vz + b * (dyz - mu * vz - dzz) + b1 * after(dzz)

    over_rows(D.shape[1], work)

    def rest(r):
        _, up, down, out = spans(r)
        D[1, out] = D[1, out] + b * W[0, down]
        D[2, out] = D[2, out] - b * W[1, up]

    over_rows(D.shape[1], rest)


def response_ahead(V, S, coef_ref, D, W):
    b, b0, m1, lam, mu2, mu = coefs(coef_ref, (C_B, C_B0, C_M1, C_LAM, C_MU2, C_MU))

    def work(r):
        here, _, down, out = spans(r)
        vx = b * S[XX, 0, here]
        dxy = mu * (b * S[XX, 0, down] - vx + V[VY, 0, here])
        dxz = mu * (m1 * after(vx) - vx + V[VZ, 0, here])
        W[0, here] = dxy
        D[0, out] = dxy
        D[1, out] = dxz
        D[2, out] = vx + b * (dxy + dxz - (lam + mu2) * vx) - b0 * before(dxz)

    over_rows(D.shape[1], work)

    def rest(r):
        _, up, _, out = spans(r)
        D[2, out] = D[2, out] - b * W[0, up]

    over_rows(D.shape[1], rest)


def early_ahead(V, S, R, coef_ref, msg, W, force, window):
    b, b0, m0, m1, lam, mu2, mu = coefs(coef_ref, (C_B, C_B0, C_M0, C_M1, C_LAM, C_MU2, C_MU))

    def work(r):
        here, up, down, out = spans(r)
        vx, vy, vz = V[VX, 1, here], V[VY, 1, here], V[VZ, 1, here]
        exx = vx - V[VX, 0, here]
        volume = lam * (exx + (vy - V[VY, 1, up]) + (vz - m0 * before(vz)))
        sxx = S[XX, 1, here] + (volume + mu2 * exx) + DT * R[XX, 1, out]
        sxy = S[XY, 1, here] + mu * (V[VX, 1, down] - vx - vy) + DT * R[XY, 1, out]
        sxz = S[XZ, 1, here] + mu * (m1 * after(vx) - vx - vz) + DT * R[XZ, 1, out]
        W[0, here] = sxy
        msg[0, out] = sxy
        msg[1, out] = sxz
        msg[2, out] = vx + b * (sxy + sxz - sxx) - b0 * before(sxz)

    over_rows(msg.shape[1], work)

    def rest(r):
        _, up, _, out = spans(r)
        msg[2, out] = msg[2, out] - b * W[0, up]

    over_rows(msg.shape[1], rest)
    if force is not None:
        add_force(msg, (2,), force, (VX, 1), window)


def early_behind(V, S, R, coef_ref, surface, column, msg, W, force, window):
    b, b0, b1, m0, m1, lam, mu2, mu, l0 = coefs(
        coef_ref, (C_B, C_B0, C_B1, C_M0, C_M1, C_LAM, C_MU2, C_MU, C_L0)
    )

    def work(r):
        here, up, down, out = spans(r)
        vx, vy, vz = V[VX, 0, here], V[VY, 0, here], V[VZ, 0, here]
        eyy = vy - V[VY, 0, up]
        ezz = vz - m0 * before(vz)
        volume = lam * (vx + eyy + ezz)
        sxx = S[XX, 0, here] + (volume + mu2 * vx) + DT * R[XX, 0, out]
        syy = S[YY, 0, here] + (volume + mu2 * eyy) + DT * R[YY, 0, out]
        szz = S[ZZ, 0, here] + (volume + mu2 * ezz) + DT * R[ZZ, 0, out]
        if surface is not None:
            szz = szz + l0 * lane_roll(surface[out, :], -column)
        sxy = S[XY, 0, here] + mu * (V[VX, 0, down] - vx + (V[VY, 1, here] - vy)) + DT * R[XY, 0, out]
        sxz = S[XZ, 0, here] + mu * (m1 * after(vx) - vx + (V[VZ, 1, here] - vz)) + DT * R[XZ, 0, out]
        syz = S[YZ, 0, here] + mu * (m1 * after(vy) - vy + (V[VZ, 0, down] - vz)) + DT * R[YZ, 0, out]
        W[0, here] = syy
        W[1, here] = syz
        msg[0, out] = sxx
        msg[1, out] = vy + b * (sxy - syy + syz) - b0 * before(syz)
        msg[2, out] = vz + b * (sxz + syz - szz) + b1 * after(szz)

    over_rows(msg.shape[1], work)

    def rest(r):
        _, up, down, out = spans(r)
        msg[1, out] = msg[1, out] + b * W[0, down]
        msg[2, out] = msg[2, out] - b * W[1, up]

    over_rows(msg.shape[1], rest)
    if force is not None:
        add_force(msg, (1,), force, (VY, 0), window)
        add_force(msg, (2,), force, (VZ, 0), window)


def ahead_bond(V, S, R, coef_ref, force, surface, msg, missing, G, step, window, unforced=0, respond=None):
    (b,) = coefs(coef_ref, (C_B,))
    _, _, has_ahead = place()
    keep = jnp.where(has_ahead, 1.0, 0.0).astype(jnp.float32)

    def got(i, out):
        return msg[i, out] if missing is None else msg[i, out] + missing[i, out]

    def work(r):
        here, _, _, out = spans(r)
        V[VX, 1, here] = V[VX, 1, here] + (keep * b) * got(0, out)
        G[0, out] = keep * (got(1, out) - b * S[XY, 1, here])
        G[1, out] = keep * (got(2, out) - b * S[XZ, 1, here])

    over_rows(R.shape[2], work)
    if step < unforced:
        add_force(G, (0,), force, (VY, 2), window)
        add_force(G, (1,), force, (VZ, 2), window)
    if respond is not None:
        respond()
    post(
        V, S, R, coef_ref, surface, 1, 2 * step + 1,
        lambda r: V[VX, 0, pl.ds(PAD + r, ROWS)],
        lambda r: G[0, pl.ds(r, ROWS)],
        lambda r: G[1, pl.ds(r, ROWS)],
    )


def behind_bond(V, S, R, coef_ref, force, surface, msg, missing, G, step, window, unforced=0, respond=None):
    (b,) = coefs(coef_ref, (C_B,))
    _, has_behind, _ = place()
    keep = jnp.where(has_behind, 1.0, 0.0).astype(jnp.float32)

    def got(i, out):
        return msg[i, out] if missing is None else msg[i, out] + missing[i, out]

    def work(r):
        here, _, _, out = spans(r)
        V[VY, 0, here] = V[VY, 0, here] - (keep * b) * got(0, out)
        V[VZ, 0, here] = V[VZ, 0, here] - (keep * b) * got(1, out)
        G[0, out] = keep * (got(2, out) + b * S[XX, 0, here])

    over_rows(R.shape[2], work)
    if step < unforced:
        add_force(G, (0,), force, (VX, 2), window)
    if respond is not None:
        respond()
    post(
        V, S, R, coef_ref, surface, 0, 2 * step,
        lambda r: G[0, pl.ds(r, ROWS)],
        lambda r: V[VY, 1, pl.ds(PAD + r, ROWS)],
        lambda r: V[VZ, 1, pl.ds(PAD + r, ROWS)],
    )


def start_kernel(
    velocity, stress, memory, layer_in, lam_in, mu_in, buoy_in, rate_in, defect_in, after_this,
    V, S, R, coef_ref, msg_near, msg_far, layer_ref, lam, mu, buoy, rate, defect, sems,
):
    del after_this
    across = velocity.shape[2]
    inside = pl.ds(PAD, across)
    pairs = [
        (layer_in, layer_ref), (lam_in, lam), (mu_in, mu), (buoy_in, buoy), (rate_in, rate), (defect_in, defect),
    ]
    pairs += [(stress.at[i], S.at[i, :, inside]) for i in range(6)]
    pairs += [(velocity.at[i], V.at[i, :, inside]) for i in range(3)]
    pairs += [(memory.at[i], R.at[i]) for i in range(6)]
    copies = [pltpu.make_async_copy(*pair, sems.at[i]) for i, pair in enumerate(pairs)]
    for copy in copies:
        copy.start()
    zero_edges(V)
    zero_edges(S)
    for copy in copies[:6]:
        copy.wait()
    layer = layer_ref[...]

    def per_depth(table):
        row = jnp.zeros(layer.shape, jnp.float32)
        for level in range(table.shape[0]):
            row = jnp.where(layer == level, table[level], row)
        return row

    lane = lax.broadcasted_iota(jnp.int32, layer.shape, 1)
    not_first = jnp.where(lane > 0, 1.0, 0.0).astype(jnp.float32)
    not_last = jnp.where(lane < layer.shape[1] - 1, 1.0, 0.0).astype(jnp.float32)
    b = DT * per_depth(buoy)
    two_mu = (2.0 * DT) * per_depth(mu)
    decay = DT * per_depth(rate)
    drop = 2.0 * decay * per_depth(defect)
    for row, value in (
        (C_B, b),
        (C_B0, b * not_first),
        (C_B1, b * not_last),
        (C_M0, not_first),
        (C_M1, not_last),
        (C_LAM, DT * per_depth(lam)),
        (C_MU2, two_mu),
        (C_MU, 0.5 * two_mu),
        (C_K1, 1.0 - decay),
        (C_K2, drop),
        (C_K2H, 0.5 * drop),
        (C_L0, DT * (1.0 - not_first)),
    ):
        coef_ref[row : row + 1, :] = value
    coef_ref[12:16, :] = jnp.zeros((4, layer.shape[1]), jnp.float32)
    for copy in copies[6:15]:
        copy.wait()
    even, _, _ = place()

    @pl.when(even)
    def _():
        pre_ahead(V, S, coef_ref, msg_near, None, 0)
        pre_behind(V, S, coef_ref, msg_far, None, 0)

    @pl.when(jnp.logical_not(even))
    def _():
        pre_behind(V, S, coef_ref, msg_near, None, 0)
        pre_ahead(V, S, coef_ref, msg_far, None, 0)

    for copy in copies[15:]:
        copy.wait()


def first_kernel(window, V0, S, R, coef_ref, force, surface, V, msg, W):
    even, _, _ = place()
    zero_edges(W)
    now, then = force.at[0], force.at[1]
    add_force(V, (VX, 1), now, (VX, 1), PAD + window)
    add_force(V, (VY, 0), now, (VY, 0), PAD + window)
    add_force(V, (VZ, 0), now, (VZ, 0), PAD + window)
    inner(V, S, coef_ref, now, window)

    @pl.when(even)
    def _():
        early_behind(V, S, R, coef_ref, surface, 0, msg, W, then, window)

    @pl.when(jnp.logical_not(even))
    def _():
        early_ahead(V, S, R, coef_ref, msg, W, then, window)


def write_out(V, S, R, results, sems, cell):
    inside = pl.ds(PAD, R.shape[2])
    pairs = [(V.at[:, cell, inside], results[0]), (S.at[:, cell, inside], results[1]), (R.at[:, cell], results[2])]
    copies = [
        pltpu.make_async_copy(source, result.at[:, cell], sems.at[i]) for i, (source, result) in enumerate(pairs)
    ]
    for copy in copies:
        copy.start()
    for copy in copies:
        copy.wait()


def near_kernel(step, window, V0, S0, R0, coef_ref, force, surface, msg, V, S, R, *rest):
    G = rest[-1]
    even, _, _ = place()
    more = step < STEPS - 1

    @pl.when(even)
    def _():
        ahead_bond(V, S, R, coef_ref, force.at[step], surface, msg, None, G, step, window, 1)
        if more:
            pre_ahead(V, S, coef_ref, rest[0], force.at[step + 1], window)
        else:
            write_out(V, S, R, rest[:3], rest[-2], 1)

    @pl.when(jnp.logical_not(even))
    def _():
        behind_bond(V, S, R, coef_ref, force.at[step], surface, msg, None, G, step, window, 1)
        if more:
            pre_behind(V, S, coef_ref, rest[0], force.at[step + 1], window)
        else:
            write_out(V, S, R, rest[:3], rest[-2], 0)


def far_kernel(step, window, V0, S0, R0, coef_ref, force, surface, msg, *rest):
    rest = list(rest)
    missing = rest.pop(0) if step > 0 else None
    V, S, R, D = rest[:4]
    G, W = rest[-2:]
    early = rest[4] if step < STEPS - 2 else None
    even, _, _ = place()
    zero_edges(W)
    here, then = force.at[step], force.at[step + 1]

    @pl.when(even)
    def _():
        behind_bond(
            V, S, R, coef_ref, here, surface, msg, missing, G, step, window, 1,
            lambda: response_ahead(V, S, coef_ref, D, W),
        )
        pre_behind(V, S, coef_ref, None, then, window)

    @pl.when(jnp.logical_not(even))
    def _():
        ahead_bond(
            V, S, R, coef_ref, here, surface, msg, missing, G, step, window, 1,
            lambda: response_behind(V, S, coef_ref, D, W),
        )
        pre_ahead(V, S, coef_ref, None, then, window)

    inner(V, S, coef_ref, then, window)
    if early is not None:
        later = force.at[step + 2]

        @pl.when(even)
        def _():
            early_behind(V, S, R, coef_ref, surface, 2 * (step + 1), early, W, later, window)

        @pl.when(jnp.logical_not(even))
        def _():
            early_ahead(V, S, R, coef_ref, early, W, later, window)


def last_kernel(step, window, V0, S0, R0, coef_ref, force, surface, msg, missing, v0, s0, r0, V, S, R, *rest):
    *results, G, sems = rest
    even, _, _ = place()
    here = force.at[step]

    @pl.when(even)
    def _():
        behind_bond(V, S, R, coef_ref, here, surface, msg, missing, G, step, window)
        write_out(V, S, R, results, sems, 0)

    @pl.when(jnp.logical_not(even))
    def _():
        ahead_bond(V, S, R, coef_ref, here, surface, msg, missing, G, step, window)
        write_out(V, S, R, results, sems, 1)


ENTRY_ROW, TRUCK_ROW = 36, 40
GROUP = 8


def pack_kernel(
    record, loads_in, entries_in, cells_in, piers_in, own, loads, steps_table, piers, entries, cells, sems
):
    panel = record.shape[1]
    slots, lanes = loads.shape
    steps = entries.shape[0]
    pairs = [(record, own.at[:, pl.ds(0, panel)]), (loads_in, loads), (entries_in, entries), (cells_in, cells)]
    pairs.append((piers_in, piers))
    copies = [pltpu.make_async_copy(*pair, sems.at[i]) for i, pair in enumerate(pairs)]
    for copy in copies:
        copy.start()
    own[:, panel:] = jnp.zeros((own.shape[0], own.shape[1] - panel), jnp.float32)
    steps_table[...] = jnp.zeros(steps_table.shape, jnp.float32)
    for copy in copies:
        copy.wait()
    steps_table[0:steps, 0:slots] = entries[...].astype(jnp.float32)
    steps_table[8 : 8 + steps, 0:slots] = cells[...].astype(jnp.float32)
    blocks = [loads[8 * i : 8 * i + 8, :] for i in range(slots // 8)] + [steps_table[0:8, :]]
    for i, block in enumerate(blocks):
        own[0:8, panel + i * lanes : panel + (i + 1) * lanes] = block


def lane_blocks(table, width):
    return sum(lane_roll(table[s : s + 1, :], s * width) for s in range(STEPS))


def split_kernel(panel, slots, own, behind, cells, after_this, result, out, sems):
    del after_this
    tiles, _, lanes = out.shape
    pieces = panel // lanes
    third = pieces // 3
    cell_of = cells[...]
    me = lax.axis_index("line")
    group, mine = lax.div(me, tiles), lax.rem(me, tiles)
    piers = cell_of.shape[1]
    row = lax.broadcasted_iota(jnp.int32, (3 * tiles, lanes), 0)
    j = lax.rem(row, 3)
    first = (lax.div(row, 3) + group * tiles) * 2
    cell_x, cell_yz = first + jnp.where(j == 2, -1, j), first + j
    record = jnp.where(group == 0, own[:, :panel], behind[:, :panel])

    def hits(cell):
        return [jnp.where(cell == cell_of[0:1, p : p + 1], 1.0, 0.0).astype(jnp.float32) for p in range(piers)]

    hit_x, hit_yz = hits(cell_x), hits(cell_yz)

    def share(m):
        hit = hit_x if m < third else hit_yz
        return sum(hit[p] * record[p : p + 1, m * lanes : (m + 1) * lanes] for p in range(piers))

    parts = [share(m) for m in range(pieces)]

    def trucks(source):
        blocks = [source[0:8, panel + i * lanes : panel + (i + 1) * lanes] for i in range(slots // 8 + 1)]
        return blocks[:-1], lane_blocks(blocks[-1], slots)

    copies = []
    own_rows, own_entry = trucks(own)
    far_rows, far_entry = trucks(behind)
    for tile in range(tiles):
        these = slice(3 * tile, 3 * tile + 3)
        for m in range(pieces):
            out[tile, 3 * m : 3 * m + 3, :] = parts[m][these, :]
        passed = mine < tile
        out[tile, ENTRY_ROW : ENTRY_ROW + 1, :] = jnp.where(passed, own_entry, far_entry)
        for i in range(slots // 8):
            at = TRUCK_ROW + 8 * i
            out[tile, at : at + 8, :] = jnp.where(passed, own_rows[i], far_rows[i])
        copies.append(pltpu.make_async_copy(out.at[tile], result.at[tile], sems.at[tile]))
        copies[-1].start()
    for copy in copies:
        copy.wait()


def prepare_kernel(parts, loads, steps_table, force, surface, table, rows_out):
    steps, comps, width = force.shape[:3]
    lanes = parts.shape[2]
    force[...] = jnp.zeros(force.shape, jnp.float32)
    per = ENTRY_ROW // (comps * width)
    lane = lax.broadcasted_iota(jnp.int32, (per, lanes), 1)
    scale = jnp.where(lane < FZ, DT, 0.0).astype(jnp.float32)
    for s in range(steps):
        for comp in range(comps):
            for cell in range(width):
                panel = parts[s, pl.ds(comp * per * width + cell, per, stride=width), :]
                force[s, comp, cell, pl.ds(4, per, stride=2), :] = scale * panel
                force[s, comp, cell, pl.ds(5, per, stride=2), :] = scale * lane_roll(panel, FZ)
    surface_loads(SOON, parts, loads, steps_table, surface, table, rows_out)


def surface_kernel(parts, loads, steps_table, surface, table, rows_out):
    surface_loads(STEPS, parts, loads, steps_table, surface, table, rows_out)


def surface_loads(steps, parts, loads, steps_table, surface, table, rows_out):
    slots = loads.shape[0]
    tiles = parts.shape[0]
    mine = lax.rem(lax.axis_index("line"), tiles)
    table[...] = jnp.zeros(table.shape, jnp.float32)
    table[0:1, :] = lane_blocks(steps_table[0:8, :], slots)
    table[steps + 1 : steps + 2, :] = lane_blocks(steps_table[8:16, :], slots)
    rows = [loads[...]]
    for k in range(1, steps + 1):
        source = lax.rem(mine + (tiles - k), tiles)
        rows.append(parts[source, TRUCK_ROW : TRUCK_ROW + slots, :])
        table[k : k + 1, :] = parts[source, ENTRY_ROW : ENTRY_ROW + 1, :]
    columns = table[...].T
    rows_out[...] = jnp.zeros(rows_out.shape, jnp.float32)
    for s in range(steps):
        block = slice(s * slots, (s + 1) * slots)
        moved = []
        for k in range(steps - s):
            entry = jnp.broadcast_to(columns[block, k : k + 1], rows[k].shape)
            new = rows[k]
            for slot in range(slots):
                new = jnp.where(entry == float(slot), rows[k + 1][slot : slot + 1, :], new)
            moved.append(new)
        rows = moved
        cell = jnp.broadcast_to(columns[block, steps + 1 : steps + 2], rows[0].shape)
        for c in range(2):
            load = jnp.sum(jnp.where(cell == float(c), rows[0], 0.0), axis=0, keepdims=True)
            rows_out[2 * s + c : 2 * s + c + 1, :] = load
    surface[...] = rows_out[...].T


def in_vmem(x):
    return pltpu.with_memory_space_constraint(x, pltpu.VMEM)


WHOLE = pl.BlockSpec(memory_space=pltpu.VMEM)
SCALARS = pl.BlockSpec(memory_space=pltpu.SMEM)
ANYWHERE = pl.BlockSpec(memory_space=pl.ANY)


def call(kernel, ins, specs, outs, out_specs, scratch=(), aliases=None, name=None, cost=1):
    return pl.pallas_call(
        kernel,
        out_shape=outs,
        in_specs=specs,
        out_specs=out_specs,
        scratch_shapes=list(scratch),
        input_output_aliases=aliases or {},
        compiler_params=pltpu.CompilerParams(vmem_limit_bytes=VMEM_LIMIT),
        cost_estimate=pl.CostEstimate(flops=cost, bytes_accessed=cost, transcendentals=0),
        name=name,
    )(*ins)


def body(
    velocity, stress, memory, truck_loads, pier_panels,
    lame_lambda, lame_mu, buoyancy, relax_rate, defect_mu, layer,
    truck_entry, truck_cell, pier_cell,
):
    tiles = lax.axis_size("line")
    width_x, across, depth = velocity.shape[1:]
    slots = truck_loads.shape[0]
    window = (across - FY) // 2 - 4
    f32 = jnp.float32

    near = [(i, i ^ 1) for i in range(tiles) if (i ^ 1) < tiles]
    far = [(i, i + 1) for i in range(1, tiles - 1, 2)] + [(i + 1, i) for i in range(1, tiles - 1, 2)]

    padded = across + 2 * PAD
    v_type = pltpu.VMEM((3, width_x, padded, depth), f32)
    s_type = pltpu.VMEM((6, width_x, padded, depth), f32)
    r_type = pltpu.VMEM((6, width_x, across, depth), f32)
    c_type = pltpu.VMEM((N_COEF, depth), f32)
    m_type = pltpu.VMEM((3, across, depth), f32)
    ghost = pltpu.VMEM((2, across, depth), f32)
    work = pltpu.VMEM((2, padded, depth), f32)

    def ahead_by(x, distance):
        return lax.ppermute(x, "line", [(i, i + distance) for i in range(tiles - distance)])

    def in_hbm(*arrays):
        return tuple(pltpu.with_memory_space_constraint(x, pltpu.HBM) for x in arrays)

    dma = pltpu.SemaphoreType.DMA
    piers, panel = pier_panels.shape[1:]
    own, loads, steps_table, pier_row = call(
        pack_kernel,
        in_hbm(pier_panels[0], truck_loads, truck_entry, truck_cell, pier_cell[None, :]),
        (ANYWHERE,) * 5,
        (
            pltpu.VMEM((piers, panel + (slots // 8 + 1) * depth), f32),
            pltpu.VMEM((slots, depth), f32),
            pltpu.VMEM((16, depth), f32),
            pltpu.VMEM((1, piers), jnp.int32),
        ),
        (WHOLE,) * 4,
        scratch=(pltpu.VMEM(truck_entry.shape, jnp.int32), pltpu.VMEM(truck_cell.shape, jnp.int32), dma((5,))),
        name="pack",
    )
    behind = ahead_by(own, GROUP)
    reach = 2 * GROUP
    index = lax.axis_index("line")
    while reach < tiles:
        record = jnp.where(index < GROUP, own, behind)[:, :panel]
        record = jnp.where(index < reach, record, ahead_by(record, reach))
        behind = jnp.concatenate([record, behind[:, panel:]], axis=1)
        reach *= 2
    tables = (lame_lambda, lame_mu, buoyancy, relax_rate, defect_mu)
    V, S, R, coef, msg_near, msg_far = call(
        start_kernel,
        in_hbm(velocity, stress, memory, layer[None, :], *tables) + (steps_table,),
        (ANYWHERE,) * 10,
        (v_type, s_type, r_type, c_type, m_type, m_type),
        (WHOLE,) * 6,
        scratch=(
            pltpu.VMEM((1, depth), jnp.int32), *(pltpu.SMEM(table.shape, f32) for table in tables), dma((21,)),
        ),
        name="start",
        cost=8 * 1024 * 1024,
    )
    msg_far = lax.ppermute(msg_far, "line", far)
    msg_near = lax.ppermute(msg_near, "line", near)
    parts = call(
        functools.partial(split_kernel, panel, slots),
        (own, behind, in_vmem(pier_row), coef),
        (WHOLE,) * 3 + (ANYWHERE,),
        jax.ShapeDtypeStruct((GROUP, TRUCK_ROW + slots, depth), f32),
        ANYWHERE,
        scratch=(pltpu.VMEM((GROUP, TRUCK_ROW + slots, depth), f32), dma((GROUP,))),
        name="split",
    )
    groups = [list(range(at, at + GROUP)) for at in range(0, tiles, GROUP)]
    parts = lax.all_to_all(parts, "line", 0, 0, axis_index_groups=groups, tiled=True)
    square = pltpu.VMEM((across, depth), f32)
    turned = (pltpu.VMEM((depth, depth), f32), pltpu.VMEM((depth, across), f32))
    ins = (parts, in_vmem(loads), in_vmem(steps_table))
    force, surface = call(
        prepare_kernel,
        ins,
        (WHOLE,) * 3,
        (pltpu.VMEM((STEPS, 3, 3, 16, depth), f32), square),
        (WHOLE,) * 2,
        scratch=turned,
        name="prepare",
    )
    later = call(surface_kernel, ins, (WHOLE,) * 3, square, WHOLE, scratch=turned, name="surface")
    V, early = call(
        functools.partial(first_kernel, window),
        tuple(in_vmem(x) for x in (V, S, R, coef, force, surface)),
        (WHOLE,) * 6,
        (v_type, m_type),
        (WHOLE,) * 2,
        scratch=(work,),
        aliases={0: 0},
        name="first",
    )
    early = lax.ppermute(early, "line", far)
    state = (v_type, s_type, r_type)
    results = tuple(jax.ShapeDtypeStruct(x.shape, f32) for x in (velocity, stress, memory))
    same = {0: 0, 1: 1, 2: 2}
    missing = None
    for step in range(STEPS):
        more = step < STEPS - 1
        ins = tuple(in_vmem(x) for x in (V, S, R, coef, force, surface, msg_near))
        outs = state + ((m_type,) if more else results)
        V, S, R, *msg = call(
            functools.partial(near_kernel, step, window),
            ins,
            (WHOLE,) * len(ins),
            outs,
            (WHOLE,) * 4 if more else (WHOLE,) * 3 + (ANYWHERE,) * 3,
            scratch=(ghost,) if more else (dma((3,)), ghost),
            aliases=same,
            name="near" + str(step),
        )
        if more:
            msg_near = lax.ppermute(msg[0], "line", near)
        if step == SOON - 1:
            surface = later
        ins = (V, S, R, coef, force, surface, msg_far) + ((missing,) if step else ())
        ins = tuple(in_vmem(x) for x in ins)
        if more:
            outs = state + (m_type,) + ((m_type,) if step < STEPS - 2 else ())
            V, S, R, missing, *msg = call(
                functools.partial(far_kernel, step, window),
                ins,
                (WHOLE,) * len(ins),
                outs,
                (WHOLE,) * len(outs),
                scratch=(ghost, work),
                aliases=same,
                name="far" + str(step),
            )
            msg_far = early
            if msg:
                early = lax.ppermute(msg[0], "line", far)
    ends = call(
        functools.partial(last_kernel, STEPS - 1, window),
        ins + tuple(msg),
        (WHOLE,) * 8 + (ANYWHERE,) * 3,
        state + results,
        (WHOLE,) * 3 + (ANYWHERE,) * 3,
        scratch=(ghost, dma((3,))),
        aliases={**same, 8: 3, 9: 4, 10: 5},
        name="last",
    )
    return ends[3:]


def solution(mesh):
    placed = (
        P(None, ("runs", "line"), None, None),
        P(None, ("runs", "line"), None, None),
        P(None, ("runs", "line"), None, None),
        P(("runs", "line"), None),
        P("line", "runs", None),
        P(),
        P(),
        P(),
        P(),
        P(),
        P(),
        P(None, ("runs", "line")),
        P(None, ("runs", "line")),
        P(),
    )
    return jax.shard_map(
        body,
        mesh=mesh,
        in_specs=placed,
        out_specs=(
            P(None, ("runs", "line"), None, None),
            P(None, ("runs", "line"), None, None),
            P(None, ("runs", "line"), None, None),
        ),
        check_vma=False,
    )
```

```python
import functools

import jax
import jax.numpy as jnp
import numpy as np
from jax import lax
from jax.experimental import pallas as pl
from jax.experimental.pallas import tpu as pltpu
from jax.sharding import PartitionSpec as P

STEPS = 6
FY = 8
FZ = 64
DT = 0.25
PAD = 8
ROWS = 16
VMEM_LIMIT = 32 * 1024 * 1024

C_B, C_B0, C_B1, C_M0, C_M1, C_LAM, C_MU2, C_MU, C_K1, C_K2, C_K2H, C_L0 = range(12)
N_COEF = 16

VX, VY, VZ = range(3)
XX, YY, ZZ, XY, XZ, YZ = range(6)


def lane_roll(x, shift):
    return pltpu.roll(x, shift % x.shape[-1], x.ndim - 1)


def before(x):
    return lane_roll(x, 1)


def after(x):
    return lane_roll(x, -1)


def over_rows(count, work, first=0):
    def step(i, carry):
        work(pl.multiple_of(first + i * ROWS, ROWS))
        return carry

    lax.fori_loop(0, count // ROWS, step, 0, unroll=count // ROWS)


def coefs(coef_ref, ids):
    return [coef_ref[i : i + 1, :] for i in ids]


def place():
    index = lax.axis_index("line")
    return lax.rem(index, 2) == 0, index > 0, index < lax.axis_size("line") - 1


def spans(r):
    return pl.ds(PAD + r, ROWS), pl.ds(PAD + r - 1, ROWS), pl.ds(PAD + r + 1, ROWS), pl.ds(r, ROWS)


def zero_edges(ref):
    across = ref.shape[-2] - 2 * PAD
    edge = jnp.zeros((PAD, ref.shape[-1]), jnp.float32)
    for where in np.ndindex(*ref.shape[:-2]):
        ref[(*where, pl.ds(0, PAD))] = edge
        ref[(*where, pl.ds(PAD + across, PAD))] = edge


class Halves:
    def __init__(self, *refs):
        self.refs, self.half, self.rows = refs, 0, refs[0].shape[1]

    def at(self, out):
        return pl.ds(out.start - self.half * self.rows, out.size)

    def __getitem__(self, at):
        return self.refs[self.half][at[0], self.at(at[1])]

    def __setitem__(self, at, value):
        self.refs[self.half][at[0], self.at(at[1])] = value

    def add_force(self, plane, force, which, first_row):
        upper, lower = self.refs
        above = self.rows - first_row
        upper[plane, pl.ds(first_row, above)] = upper[plane, pl.ds(first_row, above)] + force[which][:above]
        lower[plane, pl.ds(0, 16 - above)] = lower[plane, pl.ds(0, 16 - above)] + force[which][above:]


def over_message(count, work, msg):
    if not isinstance(msg, Halves):
        over_rows(count, work)
        return
    for half in range(2):
        msg.half = half
        over_rows(msg.rows, work, half * msg.rows)


def add_force(ref, index, force, which, first_row):
    if isinstance(ref, Halves):
        ref.add_force(*index, force, which, first_row)
        return
    rows = pl.ds(first_row, 16)
    ref[(*index, rows)] = ref[(*index, rows)] + force[which]


def pre_ahead(V, S, coef_ref, msg, force, window):
    b, b0 = coefs(coef_ref, (C_B, C_B0))

    def work(r):
        here, up, _, out = spans(r)
        sxy, sxz = S[XY, 1, here], S[XZ, 1, here]
        px = V[VX, 1, here] + b * (sxy - S[XY, 1, up] + sxz - S[XX, 1, here]) - b0 * before(sxz)
        V[VX, 1, here] = px
        if msg is not None:
            msg[0, out] = sxy
            msg[1, out] = sxz
            msg[2, out] = px

    over_message(V.shape[2] - 2 * PAD, work, msg)
    if force is not None:
        add_force(V, (VX, 1), force, (VX, 1), PAD + window)
        if msg is not None:
            add_force(msg, (2,), force, (VX, 1), window)


def pre_behind(V, S, coef_ref, msg, force, window):
    b, b0, b1 = coefs(coef_ref, (C_B, C_B0, C_B1))

    def work(r):
        here, up, down, out = spans(r)
        syz, szz = S[YZ, 0, here], S[ZZ, 0, here]
        qy = V[VY, 0, here] + b * (S[XY, 0, here] + S[YY, 0, down] - S[YY, 0, here] + syz) - b0 * before(syz)
        qz = V[VZ, 0, here] + b * (S[XZ, 0, here] + syz - S[YZ, 0, up] - szz) + b1 * after(szz)
        V[VY, 0, here] = qy
        V[VZ, 0, here] = qz
        if msg is not None:
            msg[0, out] = S[XX, 0, here]
            msg[1, out] = qy
            msg[2, out] = qz

    over_message(V.shape[2] - 2 * PAD, work, msg)
    if force is not None:
        add_force(V, (VY, 0), force, (VY, 0), PAD + window)
        add_force(V, (VZ, 0), force, (VZ, 0), PAD + window)
        if msg is not None:
            add_force(msg, (1,), force, (VY, 0), window)
            add_force(msg, (2,), force, (VZ, 0), window)


def inner(V, S, coef_ref, force, window):
    b, b0, b1 = coefs(coef_ref, (C_B, C_B0, C_B1))

    def work(r):
        here, up, down, _ = spans(r)
        sxy, sxz = S[XY, 0, here], S[XZ, 0, here]
        V[VX, 0, here] = (
            V[VX, 0, here]
            + b * (S[XX, 1, here] - S[XX, 0, here] + sxy - S[XY, 0, up] + sxz)
            - b0 * before(sxz)
        )
        syz, szz = S[YZ, 1, here], S[ZZ, 1, here]
        V[VY, 1, here] = (
            V[VY, 1, here]
            + b * (S[XY, 1, here] - sxy + S[YY, 1, down] - S[YY, 1, here] + syz)
            - b0 * before(syz)
        )
        V[VZ, 1, here] = (
            V[VZ, 1, here]
            + b * (S[XZ, 1, here] - sxz + syz - S[YZ, 1, up] - szz)
            + b1 * after(szz)
        )

    over_rows(V.shape[2] - 2 * PAD, work)
    if force is not None:
        add_force(V, (VX, 0), force, (VX, 0), PAD + window)
        add_force(V, (VY, 1), force, (VY, 1), PAD + window)
        add_force(V, (VZ, 1), force, (VZ, 1), PAD + window)


def post(V, S, R, coef_ref, surface, cell, column, behind_x, ahead_y, ahead_z):
    m0, m1, lam, mu2, mu, k1, k2, k2h, l0 = coefs(
        coef_ref, (C_M0, C_M1, C_LAM, C_MU2, C_MU, C_K1, C_K2, C_K2H, C_L0)
    )

    def work(r):
        here, up, down, out = spans(r)
        vx, vy, vz = V[VX, cell, here], V[VY, cell, here], V[VZ, cell, here]
        exx = vx - behind_x(r)
        eyy = vy - V[VY, cell, up]
        ezz = vz - m0 * before(vz)
        exy = V[VX, cell, down] - vx + (ahead_y(r) - vy)
        exz = m1 * after(vx) - vx + (ahead_z(r) - vz)
        eyz = m1 * after(vy) - vy + (V[VZ, cell, down] - vz)
        volume = lam * (exx + eyy + ezz)
        for comp, e in ((XX, exx), (YY, eyy), (ZZ, ezz)):
            old = R[comp, cell, out]
            new = S[comp, cell, here] + (volume + mu2 * e) + DT * old
            if comp == ZZ:
                new = new + l0 * lane_roll(surface[out, :], -column)
            S[comp, cell, here] = new
            R[comp, cell, out] = k1 * old - k2 * e
        for comp, e in ((XY, exy), (XZ, exz), (YZ, eyz)):
            old = R[comp, cell, out]
            S[comp, cell, here] = S[comp, cell, here] + mu * e + DT * old
            R[comp, cell, out] = k1 * old - k2h * e

    over_rows(R.shape[2], work)


def response_behind(V, S, coef_ref, D, W):
    b, b0, b1, m0, m1, lam, mu2, mu = coefs(coef_ref, (C_B, C_B0, C_B1, C_M0, C_M1, C_LAM, C_MU2, C_MU))

    def work(r):
        here, up, down, out = spans(r)
        sxy = S[XY, 1, here]
        vy, vz = -b * sxy, -b * S[XZ, 1, here]
        exx = -V[VX, 1, here]
        eyy = b * (S[XY, 1, up] - sxy)
        ezz = vz - m0 * before(vz)
        volume = lam * (exx + eyy + ezz)
        dyy, dzz = volume + mu2 * eyy, volume + mu2 * ezz
        dyz = mu * (m1 * after(vy) - vy - b * S[XZ, 1, down] - vz)
        W[0, here] = dyy
        W[1, here] = dyz
        D[0, out] = volume + mu2 * exx
        D[1, out] = vy + b * (dyz - mu * vy - dyy) - b0 * before(dyz)
        D[2, out] = vz + b * (dyz - mu * vz - dzz) + b1 * after(dzz)

    over_rows(D.shape[1], work)

    def rest(r):
        _, up, down, out = spans(r)
        D[1, out] = D[1, out] + b * W[0, down]
        D[2, out] = D[2, out] - b * W[1, up]

    over_rows(D.shape[1], rest)


def response_ahead(V, S, coef_ref, D, W):
    b, b0, m1, lam, mu2, mu = coefs(coef_ref, (C_B, C_B0, C_M1, C_LAM, C_MU2, C_MU))

    def work(r):
        here, _, down, out = spans(r)
        vx = b * S[XX, 0, here]
        dxy = mu * (b * S[XX, 0, down] - vx + V[VY, 0, here])
        dxz = mu * (m1 * after(vx) - vx + V[VZ, 0, here])
        W[0, here] = dxy
        D[0, out] = dxy
        D[1, out] = dxz
        D[2, out] = vx + b * (dxy + dxz - (lam + mu2) * vx) - b0 * before(dxz)

    over_rows(D.shape[1], work)

    def rest(r):
        _, up, _, out = spans(r)
        D[2, out] = D[2, out] - b * W[0, up]

    over_rows(D.shape[1], rest)


def early_ahead(V, S, R, coef_ref, msg, W, force, window):
    b, b0, m0, m1, lam, mu2, mu = coefs(coef_ref, (C_B, C_B0, C_M0, C_M1, C_LAM, C_MU2, C_MU))

    def work(r):
        here, up, down, out = spans(r)
        vx, vy, vz = V[VX, 1, here], V[VY, 1, here], V[VZ, 1, here]
        exx = vx - V[VX, 0, here]
        volume = lam * (exx + (vy - V[VY, 1, up]) + (vz - m0 * before(vz)))
        sxx = S[XX, 1, here] + (volume + mu2 * exx) + DT * R[XX, 1, out]
        sxy = S[XY, 1, here] + mu * (V[VX, 1, down] - vx - vy) + DT * R[XY, 1, out]
        sxz = S[XZ, 1, here] + mu * (m1 * after(vx) - vx - vz) + DT * R[XZ, 1, out]
        W[0, here] = sxy
        msg[0, out] = sxy
        msg[1, out] = sxz
        msg[2, out] = vx + b * (sxy + sxz - sxx) - b0 * before(sxz)

    over_rows(msg.shape[1], work)

    def rest(r):
        _, up, _, out = spans(r)
        msg[2, out] = msg[2, out] - b * W[0, up]

    over_rows(msg.shape[1], rest)
    if force is not None:
        add_force(msg, (2,), force, (VX, 1), window)


def early_behind(V, S, R, coef_ref, surface, column, msg, W, force, window):
    b, b0, b1, m0, m1, lam, mu2, mu, l0 = coefs(
        coef_ref, (C_B, C_B0, C_B1, C_M0, C_M1, C_LAM, C_MU2, C_MU, C_L0)
    )

    def work(r):
        here, up, down, out = spans(r)
        vx, vy, vz = V[VX, 0, here], V[VY, 0, here], V[VZ, 0, here]
        eyy = vy - V[VY, 0, up]
        ezz = vz - m0 * before(vz)
        volume = lam * (vx + eyy + ezz)
        sxx = S[XX, 0, here] + (volume + mu2 * vx) + DT * R[XX, 0, out]
        syy = S[YY, 0, here] + (volume + mu2 * eyy) + DT * R[YY, 0, out]
        szz = S[ZZ, 0, here] + (volume + mu2 * ezz) + DT * R[ZZ, 0, out]
        if surface is not None:
            szz = szz + l0 * lane_roll(surface[out, :], -column)
        sxy = S[XY, 0, here] + mu * (V[VX, 0, down] - vx + (V[VY, 1, here] - vy)) + DT * R[XY, 0, out]
        sxz = S[XZ, 0, here] + mu * (m1 * after(vx) - vx + (V[VZ, 1, here] - vz)) + DT * R[XZ, 0, out]
        syz = S[YZ, 0, here] + mu * (m1 * after(vy) - vy + (V[VZ, 0, down] - vz)) + DT * R[YZ, 0, out]
        W[0, here] = syy
        W[1, here] = syz
        msg[0, out] = sxx
        msg[1, out] = vy + b * (sxy - syy + syz) - b0 * before(syz)
        msg[2, out] = vz + b * (sxz + syz - szz) + b1 * after(szz)

    over_rows(msg.shape[1], work)

    def rest(r):
        _, up, down, out = spans(r)
        msg[1, out] = msg[1, out] + b * W[0, down]
        msg[2, out] = msg[2, out] - b * W[1, up]

    over_rows(msg.shape[1], rest)
    if force is not None:
        add_force(msg, (1,), force, (VY, 0), window)
        add_force(msg, (2,), force, (VZ, 0), window)


def ahead_bond(V, S, R, coef_ref, force, surface, msg, missing, G, step, window, unforced=0, respond=None):
    (b,) = coefs(coef_ref, (C_B,))
    _, _, has_ahead = place()
    keep = jnp.where(has_ahead, 1.0, 0.0).astype(jnp.float32)

    def got(i, out):
        return msg[i, out] if missing is None else msg[i, out] + missing[i, out]

    def work(r):
        here, _, _, out = spans(r)
        V[VX, 1, here] = V[VX, 1, here] + (keep * b) * got(0, out)
        G[0, out] = keep * (got(1, out) - b * S[XY, 1, here])
        G[1, out] = keep * (got(2, out) - b * S[XZ, 1, here])

    over_message(R.shape[2], work, msg)
    if step < unforced:
        add_force(G, (0,), force, (VY, 2), window)
        add_force(G, (1,), force, (VZ, 2), window)
    if respond is not None:
        respond()
    post(
        V, S, R, coef_ref, surface, 1, 2 * step + 1,
        lambda r: V[VX, 0, pl.ds(PAD + r, ROWS)],
        lambda r: G[0, pl.ds(r, ROWS)],
        lambda r: G[1, pl.ds(r, ROWS)],
    )


def behind_bond(V, S, R, coef_ref, force, surface, msg, missing, G, step, window, unforced=0, respond=None):
    (b,) = coefs(coef_ref, (C_B,))
    _, has_behind, _ = place()
    keep = jnp.where(has_behind, 1.0, 0.0).astype(jnp.float32)

    def got(i, out):
        return msg[i, out] if missing is None else msg[i, out] + missing[i, out]

    def work(r):
        here, _, _, out = spans(r)
        V[VY, 0, here] = V[VY, 0, here] - (keep * b) * got(0, out)
        V[VZ, 0, here] = V[VZ, 0, here] - (keep * b) * got(1, out)
        G[0, out] = keep * (got(2, out) + b * S[XX, 0, here])

    over_message(R.shape[2], work, msg)
    if step < unforced:
        add_force(G, (0,), force, (VX, 2), window)
    if respond is not None:
        respond()
    post(
        V, S, R, coef_ref, surface, 0, 2 * step,
        lambda r: G[0, pl.ds(r, ROWS)],
        lambda r: V[VY, 1, pl.ds(PAD + r, ROWS)],
        lambda r: V[VZ, 1, pl.ds(PAD + r, ROWS)],
    )


def start_kernel(
    velocity, stress, memory, layer_in, lam_in, mu_in, buoy_in, rate_in, defect_in, after_this,
    V, S, R, coef_ref, near_upper, near_lower, msg_far, layer_ref, lam, mu, buoy, rate, defect, sems,
):
    del after_this
    msg_near = Halves(near_upper, near_lower)
    across = velocity.shape[2]
    inside = pl.ds(PAD, across)
    pairs = [
        (layer_in, layer_ref), (lam_in, lam), (mu_in, mu), (buoy_in, buoy), (rate_in, rate), (defect_in, defect),
    ]
    pairs += [(stress.at[i], S.at[i, :, inside]) for i in range(6)]
    pairs += [(velocity.at[i], V.at[i, :, inside]) for i in range(3)]
    pairs += [(memory.at[i], R.at[i]) for i in range(6)]
    copies = [pltpu.make_async_copy(*pair, sems.at[i]) for i, pair in enumerate(pairs)]
    for copy in copies:
        copy.start()
    zero_edges(V)
    zero_edges(S)
    for copy in copies[:6]:
        copy.wait()
    layer = layer_ref[...]

    def per_depth(table):
        row = jnp.zeros(layer.shape, jnp.float32)
        for level in range(table.shape[0]):
            row = jnp.where(layer == level, table[level], row)
        return row

    lane = lax.broadcasted_iota(jnp.int32, layer.shape, 1)
    not_first = jnp.where(lane > 0, 1.0, 0.0).astype(jnp.float32)
    not_last = jnp.where(lane < layer.shape[1] - 1, 1.0, 0.0).astype(jnp.float32)
    b = DT * per_depth(buoy)
    two_mu = (2.0 * DT) * per_depth(mu)
    decay = DT * per_depth(rate)
    drop = 2.0 * decay * per_depth(defect)
    for row, value in (
        (C_B, b),
        (C_B0, b * not_first),
        (C_B1, b * not_last),
        (C_M0, not_first),
        (C_M1, not_last),
        (C_LAM, DT * per_depth(lam)),
        (C_MU2, two_mu),
        (C_MU, 0.5 * two_mu),
        (C_K1, 1.0 - decay),
        (C_K2, drop),
        (C_K2H, 0.5 * drop),
        (C_L0, DT * (1.0 - not_first)),
    ):
        coef_ref[row : row + 1, :] = value
    coef_ref[12:16, :] = jnp.zeros((4, layer.shape[1]), jnp.float32)
    for copy in copies[6:15]:
        copy.wait()
    even, _, _ = place()

    @pl.when(even)
    def _():
        pre_ahead(V, S, coef_ref, msg_near, None, 0)
        pre_behind(V, S, coef_ref, msg_far, None, 0)

    @pl.when(jnp.logical_not(even))
    def _():
        pre_behind(V, S, coef_ref, msg_near, None, 0)
        pre_ahead(V, S, coef_ref, msg_far, None, 0)

    for copy in copies[15:]:
        copy.wait()


def first_kernel(window, V0, S, R, coef_ref, force, surface, V, msg, W):
    even, _, _ = place()
    zero_edges(W)
    now, then = force.at[0], force.at[1]
    add_force(V, (VX, 1), now, (VX, 1), PAD + window)
    add_force(V, (VY, 0), now, (VY, 0), PAD + window)
    add_force(V, (VZ, 0), now, (VZ, 0), PAD + window)
    inner(V, S, coef_ref, now, window)

    @pl.when(even)
    def _():
        early_behind(V, S, R, coef_ref, surface, 0, msg, W, then, window)

    @pl.when(jnp.logical_not(even))
    def _():
        early_ahead(V, S, R, coef_ref, msg, W, then, window)


def results_out(V, S, R, results, sems, cell):
    inside = pl.ds(PAD, R.shape[2])
    pairs = [(V.at[:, cell, inside], results[0]), (S.at[:, cell, inside], results[1]), (R.at[:, cell], results[2])]
    return [
        pltpu.make_async_copy(source, result.at[:, cell], sems.at[i]) for i, (source, result) in enumerate(pairs)
    ]


def start_all(copies):
    for copy in copies:
        copy.start()


def wait_all(copies):
    for copy in copies:
        copy.wait()


def near_kernel(step, window, V0, S0, R0, coef_ref, force, surface, upper, lower, V, S, R, *rest):
    G = rest[-1]
    msg = Halves(upper, lower)
    even, _, _ = place()
    more = step < STEPS - 1
    send = Halves(*rest[:2]) if more else None

    @pl.when(even)
    def _():
        ahead_bond(V, S, R, coef_ref, force.at[step], surface, msg, None, G, step, window, 1)
        if more:
            pre_ahead(V, S, coef_ref, send, force.at[step + 1], window)
        else:
            copies = results_out(V, S, R, rest[:3], rest[-2], 1)
            start_all(copies)
            wait_all(copies)

    @pl.when(jnp.logical_not(even))
    def _():
        behind_bond(V, S, R, coef_ref, force.at[step], surface, msg, None, G, step, window, 1)
        if more:
            pre_behind(V, S, coef_ref, send, force.at[step + 1], window)
        else:
            copies = results_out(V, S, R, rest[:3], rest[-2], 0)
            start_all(copies)
            wait_all(copies)


def far_kernel(step, window, V0, S0, R0, coef_ref, force, surface, msg, *rest):
    rest = list(rest)
    missing = rest.pop(0) if step > 0 else None
    V, S, R, D = rest[:4]
    G, W = rest[-2:]
    early = rest[4] if step < STEPS - 2 else None
    even, _, _ = place()
    zero_edges(W)
    here, then = force.at[step], force.at[step + 1]

    @pl.when(even)
    def _():
        behind_bond(
            V, S, R, coef_ref, here, surface, msg, missing, G, step, window, 1,
            lambda: response_ahead(V, S, coef_ref, D, W),
        )
        pre_behind(V, S, coef_ref, None, then, window)

    @pl.when(jnp.logical_not(even))
    def _():
        ahead_bond(
            V, S, R, coef_ref, here, surface, msg, missing, G, step, window, 1,
            lambda: response_behind(V, S, coef_ref, D, W),
        )
        pre_ahead(V, S, coef_ref, None, then, window)

    inner(V, S, coef_ref, then, window)
    if early is not None:
        later = force.at[step + 2]

        @pl.when(even)
        def _():
            early_behind(V, S, R, coef_ref, surface, 2 * (step + 1), early, W, later, window)

        @pl.when(jnp.logical_not(even))
        def _():
            early_ahead(V, S, R, coef_ref, early, W, later, window)


def last_kernel(step, window, V0, S0, R0, coef_ref, force, surface, msg, missing, v0, s0, r0, V, S, R, *rest):
    *results, G, sems = rest
    even, _, _ = place()
    here = force.at[step]

    @pl.when(even)
    def _():
        copies = results_out(V, S, R, results, sems, 0)
        behind_bond(
            V, S, R, coef_ref, here, surface, msg, missing, G, step, window, 0, lambda: start_all(copies[:1])
        )
        start_all(copies[1:])
        wait_all(copies)

    @pl.when(jnp.logical_not(even))
    def _():
        copies = results_out(V, S, R, results, sems, 1)
        ahead_bond(
            V, S, R, coef_ref, here, surface, msg, missing, G, step, window, 0, lambda: start_all(copies[:1])
        )
        start_all(copies[1:])
        wait_all(copies)


ENTRY_ROW, TRUCK_ROW = 36, 40
GROUP = 8


def pack_kernel(
    record, loads_in, entries_in, cells_in, piers_in, own, loads, steps_table, piers, entries, cells, sems
):
    panel = record.shape[1]
    slots, lanes = loads.shape
    steps = entries.shape[0]
    pairs = [(record, own.at[:, pl.ds(0, panel)]), (loads_in, loads), (entries_in, entries), (cells_in, cells)]
    pairs.append((piers_in, piers))
    copies = [pltpu.make_async_copy(*pair, sems.at[i]) for i, pair in enumerate(pairs)]
    for copy in copies:
        copy.start()
    own[:, panel:] = jnp.zeros((own.shape[0], own.shape[1] - panel), jnp.float32)
    steps_table[...] = jnp.zeros(steps_table.shape, jnp.float32)
    for copy in copies:
        copy.wait()
    steps_table[0:steps, 0:slots] = entries[...].astype(jnp.float32)
    steps_table[8 : 8 + steps, 0:slots] = cells[...].astype(jnp.float32)
    blocks = [loads[8 * i : 8 * i + 8, :] for i in range(slots // 8)] + [steps_table[0:8, :]]
    for i, block in enumerate(blocks):
        own[0:8, panel + i * lanes : panel + (i + 1) * lanes] = block


def lane_blocks(table, width):
    return sum(lane_roll(table[s : s + 1, :], s * width) for s in range(STEPS))


def split_kernel(panel, slots, own, behind, cells, after_this, out):
    del after_this
    tiles, _, lanes = out.shape
    pieces = panel // lanes
    third = pieces // 3
    cell_of = cells[...]
    me = lax.axis_index("line")
    group, mine = lax.div(me, tiles), lax.rem(me, tiles)
    piers = cell_of.shape[1]
    row = lax.broadcasted_iota(jnp.int32, (3 * tiles, lanes), 0)
    j = lax.rem(row, 3)
    first = (lax.div(row, 3) + group * tiles) * 2
    cell_x, cell_yz = first + jnp.where(j == 2, -1, j), first + j
    record = jnp.where(group == 0, own[:, :panel], behind[:, :panel])

    def hits(cell):
        return [jnp.where(cell == cell_of[0:1, p : p + 1], 1.0, 0.0).astype(jnp.float32) for p in range(piers)]

    hit_x, hit_yz = hits(cell_x), hits(cell_yz)

    def share(m):
        hit = hit_x if m < third else hit_yz
        return sum(hit[p] * record[p : p + 1, m * lanes : (m + 1) * lanes] for p in range(piers))

    parts = [share(m) for m in range(pieces)]

    def trucks(source):
        blocks = [source[0:8, panel + i * lanes : panel + (i + 1) * lanes] for i in range(slots // 8 + 1)]
        return blocks[:-1], lane_blocks(blocks[-1], slots)

    own_rows, own_entry = trucks(own)
    far_rows, far_entry = trucks(behind)
    for tile in range(tiles):
        these = slice(3 * tile, 3 * tile + 3)
        for m in range(pieces):
            out[tile, 3 * m : 3 * m + 3, :] = parts[m][these, :]
        passed = mine < tile
        out[tile, ENTRY_ROW : ENTRY_ROW + 1, :] = jnp.where(passed, own_entry, far_entry)
        for i in range(slots // 8):
            at = TRUCK_ROW + 8 * i
            out[tile, at : at + 8, :] = jnp.where(passed, own_rows[i], far_rows[i])


def prepare_kernel(parts, loads, steps_table, force, surface, table, rows_out):
    steps, comps, width = force.shape[:3]
    lanes = parts.shape[2]
    force[...] = jnp.zeros(force.shape, jnp.float32)
    per = ENTRY_ROW // (comps * width)
    lane = lax.broadcasted_iota(jnp.int32, (per, lanes), 1)
    scale = jnp.where(lane < FZ, DT, 0.0).astype(jnp.float32)
    for s in range(steps):
        for comp in range(comps):
            for cell in range(width):
                panel = parts[s, pl.ds(comp * per * width + cell, per, stride=width), :]
                force[s, comp, cell, pl.ds(4, per, stride=2), :] = scale * panel
                force[s, comp, cell, pl.ds(5, per, stride=2), :] = scale * lane_roll(panel, FZ)
    surface_loads(1, parts, loads, steps_table, surface, table, rows_out)


def surface_kernel(parts, loads, steps_table, surface, table, rows_out):
    surface_loads(STEPS, parts, loads, steps_table, surface, table, rows_out)


def surface_loads(steps, parts, loads, steps_table, surface, table, rows_out):
    slots = loads.shape[0]
    tiles = parts.shape[0]
    mine = lax.rem(lax.axis_index("line"), tiles)
    table[...] = jnp.zeros(table.shape, jnp.float32)
    table[0:1, :] = lane_blocks(steps_table[0:8, :], slots)
    table[steps + 1 : steps + 2, :] = lane_blocks(steps_table[8:16, :], slots)
    rows = [loads[...]]
    for k in range(1, steps + 1):
        source = lax.rem(mine + (tiles - k), tiles)
        rows.append(parts[source, TRUCK_ROW : TRUCK_ROW + slots, :])
        table[k : k + 1, :] = parts[source, ENTRY_ROW : ENTRY_ROW + 1, :]
    columns = table[...].T
    rows_out[...] = jnp.zeros(rows_out.shape, jnp.float32)
    for s in range(steps):
        block = slice(s * slots, (s + 1) * slots)
        moved = []
        for k in range(steps - s):
            entry = jnp.broadcast_to(columns[block, k : k + 1], rows[k].shape)
            new = rows[k]
            for slot in range(slots):
                new = jnp.where(entry == float(slot), rows[k + 1][slot : slot + 1, :], new)
            moved.append(new)
        rows = moved
        cell = jnp.broadcast_to(columns[block, steps + 1 : steps + 2], rows[0].shape)
        for c in range(2):
            load = jnp.sum(jnp.where(cell == float(c), rows[0], 0.0), axis=0, keepdims=True)
            rows_out[2 * s + c : 2 * s + c + 1, :] = load
    surface[...] = rows_out[...].T


def in_vmem(x):
    return pltpu.with_memory_space_constraint(x, pltpu.VMEM)


WHOLE = pl.BlockSpec(memory_space=pltpu.VMEM)
SCALARS = pl.BlockSpec(memory_space=pltpu.SMEM)
ANYWHERE = pl.BlockSpec(memory_space=pl.ANY)


def call(kernel, ins, specs, outs, out_specs, scratch=(), aliases=None, name=None, cost=1):
    return pl.pallas_call(
        kernel,
        out_shape=outs,
        in_specs=specs,
        out_specs=out_specs,
        scratch_shapes=list(scratch),
        input_output_aliases=aliases or {},
        compiler_params=pltpu.CompilerParams(vmem_limit_bytes=VMEM_LIMIT),
        cost_estimate=pl.CostEstimate(flops=cost, bytes_accessed=cost, transcendentals=0),
        name=name,
    )(*ins)


def body(
    velocity, stress, memory, truck_loads, pier_panels,
    lame_lambda, lame_mu, buoyancy, relax_rate, defect_mu, layer,
    truck_entry, truck_cell, pier_cell,
):
    tiles = lax.axis_size("line")
    width_x, across, depth = velocity.shape[1:]
    slots = truck_loads.shape[0]
    window = (across - FY) // 2 - 4
    f32 = jnp.float32

    near = [(i, i ^ 1) for i in range(tiles) if (i ^ 1) < tiles]
    far = [(i, i + 1) for i in range(1, tiles - 1, 2)] + [(i + 1, i) for i in range(1, tiles - 1, 2)]

    padded = across + 2 * PAD
    v_type = pltpu.VMEM((3, width_x, padded, depth), f32)
    s_type = pltpu.VMEM((6, width_x, padded, depth), f32)
    r_type = pltpu.VMEM((6, width_x, across, depth), f32)
    c_type = pltpu.VMEM((N_COEF, depth), f32)
    m_type = pltpu.VMEM((3, across, depth), f32)
    planes = (pltpu.VMEM((3, across // 2, depth), f32),) * 2
    ghost = pltpu.VMEM((2, across, depth), f32)
    work = pltpu.VMEM((2, padded, depth), f32)

    def ahead_by(x, distance):
        return lax.ppermute(x, "line", [(i, i + distance) for i in range(tiles - distance)])

    def in_hbm(*arrays):
        return tuple(pltpu.with_memory_space_constraint(x, pltpu.HBM) for x in arrays)

    dma = pltpu.SemaphoreType.DMA
    piers, panel = pier_panels.shape[1:]
    own, loads, steps_table, pier_row = call(
        pack_kernel,
        in_hbm(pier_panels[0], truck_loads, truck_entry, truck_cell, pier_cell[None, :]),
        (ANYWHERE,) * 5,
        (
            pltpu.VMEM((piers, panel + (slots // 8 + 1) * depth), f32),
            pltpu.VMEM((slots, depth), f32),
            pltpu.VMEM((16, depth), f32),
            pltpu.VMEM((1, piers), jnp.int32),
        ),
        (WHOLE,) * 4,
        scratch=(pltpu.VMEM(truck_entry.shape, jnp.int32), pltpu.VMEM(truck_cell.shape, jnp.int32), dma((5,))),
        name="pack",
    )
    behind = ahead_by(own, GROUP)
    reach = 2 * GROUP
    index = lax.axis_index("line")
    while reach < tiles:
        record = jnp.where(index < GROUP, own, behind)[:, :panel]
        record = jnp.where(index < reach, record, ahead_by(record, reach))
        behind = jnp.concatenate([record, behind[:, panel:]], axis=1)
        reach *= 2
    tables = (lame_lambda, lame_mu, buoyancy, relax_rate, defect_mu)
    V, S, R, coef, *msg_near, msg_far = call(
        start_kernel,
        in_hbm(velocity, stress, memory, layer[None, :], *tables) + (steps_table,),
        (ANYWHERE,) * 10,
        (v_type, s_type, r_type, c_type, *planes, m_type),
        (WHOLE,) * 7,
        scratch=(
            pltpu.VMEM((1, depth), jnp.int32), *(pltpu.SMEM(table.shape, f32) for table in tables), dma((21,)),
        ),
        name="start",
        cost=8 * 1024 * 1024,
    )
    msg_far = lax.ppermute(msg_far, "line", far)
    msg_near = [lax.ppermute(plane, "line", near) for plane in msg_near]
    parts = call(
        functools.partial(split_kernel, panel, slots),
        (own, behind, in_vmem(pier_row), coef),
        (WHOLE,) * 3 + (ANYWHERE,),
        pltpu.VMEM((GROUP, TRUCK_ROW + slots, depth), f32),
        WHOLE,
        name="split",
    )
    groups = [list(range(at, at + GROUP)) for at in range(0, tiles, GROUP)]
    parts = lax.all_to_all(parts, "line", 0, 0, axis_index_groups=groups, tiled=True)
    square = pltpu.VMEM((across, depth), f32)
    turned = (pltpu.VMEM((depth, depth), f32), pltpu.VMEM((depth, across), f32))
    ins = (parts, in_vmem(loads), in_vmem(steps_table))
    force, surface = call(
        prepare_kernel,
        ins,
        (WHOLE,) * 3,
        (pltpu.VMEM((STEPS, 3, 3, 16, depth), f32), square),
        (WHOLE,) * 2,
        scratch=turned,
        name="prepare",
    )
    later = call(surface_kernel, ins, (WHOLE,) * 3, square, WHOLE, scratch=turned, name="surface")
    V, early = call(
        functools.partial(first_kernel, window),
        tuple(in_vmem(x) for x in (V, S, R, coef, force, surface)),
        (WHOLE,) * 6,
        (v_type, m_type),
        (WHOLE,) * 2,
        scratch=(work,),
        aliases={0: 0},
        name="first",
    )
    early = lax.ppermute(early, "line", far)
    state = (v_type, s_type, r_type)
    results = tuple(jax.ShapeDtypeStruct(x.shape, f32) for x in (velocity, stress, memory))
    same = {0: 0, 1: 1, 2: 2}
    missing = None
    for step in range(STEPS):
        more = step < STEPS - 1
        ins = tuple(in_vmem(x) for x in (V, S, R, coef, force, surface, *msg_near))
        outs = state + (planes if more else results)
        V, S, R, *msg = call(
            functools.partial(near_kernel, step, window),
            ins,
            (WHOLE,) * len(ins),
            outs,
            (WHOLE,) * 5 if more else (WHOLE,) * 3 + (ANYWHERE,) * 3,
            scratch=(ghost,) if more else (dma((3,)), ghost),
            aliases=same,
            name="near" + str(step),
        )
        if more:
            msg_near = [lax.ppermute(plane, "line", near) for plane in msg]
        if step == 0:
            surface = later
        ins = (V, S, R, coef, force, surface, msg_far) + ((missing,) if step else ())
        ins = tuple(in_vmem(x) for x in ins)
        if more:
            outs = state + (m_type,) + ((m_type,) if step < STEPS - 2 else ())
            V, S, R, missing, *msg = call(
                functools.partial(far_kernel, step, window),
                ins,
                (WHOLE,) * len(ins),
                outs,
                (WHOLE,) * len(outs),
                scratch=(ghost, work),
                aliases=same,
                name="far" + str(step),
            )
            msg_far = early
            if msg:
                early = lax.ppermute(msg[0], "line", far)
    ends = call(
        functools.partial(last_kernel, STEPS - 1, window),
        ins + tuple(msg),
        (WHOLE,) * 8 + (ANYWHERE,) * 3,
        state + results,
        (WHOLE,) * 3 + (ANYWHERE,) * 3,
        scratch=(ghost, dma((3,))),
        aliases={**same, 8: 3, 9: 4, 10: 5},
        name="last",
    )
    return ends[3:]


def solution(mesh):
    placed = (
        P(None, ("runs", "line"), None, None),
        P(None, ("runs", "line"), None, None),
        P(None, ("runs", "line"), None, None),
        P(("runs", "line"), None),
        P("line", "runs", None),
        P(),
        P(),
        P(),
        P(),
        P(),
        P(),
        P(None, ("runs", "line")),
        P(None, ("runs", "line")),
        P(),
    )
    return jax.shard_map(
        body,
        mesh=mesh,
        in_specs=placed,
        out_specs=(
            P(None, ("runs", "line"), None, None),
            P(None, ("runs", "line"), None, None),
            P(None, ("runs", "line"), None, None),
        ),
        check_vma=False,
    )
```

```python
import functools

import jax
import jax.numpy as jnp
import numpy as np
from jax import lax
from jax.experimental import pallas as pl
from jax.experimental.pallas import tpu as pltpu
from jax.sharding import PartitionSpec as P

STEPS = 6
SOON = 3
FY = 8
FZ = 64
DT = 0.25
PAD = 8
ROWS = 16
VMEM_LIMIT = 32 * 1024 * 1024

C_B, C_B0, C_B1, C_M0, C_M1, C_LAM, C_MU2, C_MU, C_K1, C_K2, C_K2H, C_L0 = range(12)
N_COEF = 16

VX, VY, VZ = range(3)
XX, YY, ZZ, XY, XZ, YZ = range(6)


def lane_roll(x, shift):
    return pltpu.roll(x, shift % x.shape[-1], x.ndim - 1)


def before(x):
    return lane_roll(x, 1)


def after(x):
    return lane_roll(x, -1)


def over_rows(count, work, first=0):
    def step(i, carry):
        work(pl.multiple_of(first + i * ROWS, ROWS))
        return carry

    lax.fori_loop(0, count // ROWS, step, 0, unroll=count // ROWS)


def coefs(coef_ref, ids):
    return [coef_ref[i : i + 1, :] for i in ids]


def place():
    index = lax.axis_index("line")
    return lax.rem(index, 2) == 0, index > 0, index < lax.axis_size("line") - 1


def spans(r):
    return pl.ds(PAD + r, ROWS), pl.ds(PAD + r - 1, ROWS), pl.ds(PAD + r + 1, ROWS), pl.ds(r, ROWS)


def zero_edges(ref):
    across = ref.shape[-2] - 2 * PAD
    edge = jnp.zeros((PAD, ref.shape[-1]), jnp.float32)
    for where in np.ndindex(*ref.shape[:-2]):
        ref[(*where, pl.ds(0, PAD))] = edge
        ref[(*where, pl.ds(PAD + across, PAD))] = edge


class Halves:
    def __init__(self, *refs):
        self.refs, self.half, self.rows = refs, 0, refs[0].shape[1]

    def at(self, out):
        return pl.ds(out.start - self.half * self.rows, out.size)

    def __getitem__(self, at):
        return self.refs[self.half][at[0], self.at(at[1])]

    def __setitem__(self, at, value):
        self.refs[self.half][at[0], self.at(at[1])] = value

    def add_force(self, plane, force, which, first_row):
        upper, lower = self.refs
        above = self.rows - first_row
        upper[plane, pl.ds(first_row, above)] = upper[plane, pl.ds(first_row, above)] + force[which][:above]
        lower[plane, pl.ds(0, 16 - above)] = lower[plane, pl.ds(0, 16 - above)] + force[which][above:]


def over_message(count, work, msg):
    if not isinstance(msg, Halves):
        over_rows(count, work)
        return
    for half in range(2):
        msg.half = half
        over_rows(msg.rows, work, half * msg.rows)


def add_force(ref, index, force, which, first_row):
    if isinstance(ref, Halves):
        ref.add_force(*index, force, which, first_row)
        return
    rows = pl.ds(first_row, 16)
    ref[(*index, rows)] = ref[(*index, rows)] + force[which]


def pre_ahead(V, S, coef_ref, msg, force, window):
    b, b0 = coefs(coef_ref, (C_B, C_B0))

    def work(r):
        here, up, _, out = spans(r)
        sxy, sxz = S[XY, 1, here], S[XZ, 1, here]
        px = V[VX, 1, here] + b * (sxy - S[XY, 1, up] + sxz - S[XX, 1, here]) - b0 * before(sxz)
        V[VX, 1, here] = px
        if msg is not None:
            msg[0, out] = sxy
            msg[1, out] = sxz
            msg[2, out] = px

    over_message(V.shape[2] - 2 * PAD, work, msg)
    if force is not None:
        add_force(V, (VX, 1), force, (VX, 1), PAD + window)
        if msg is not None:
            add_force(msg, (2,), force, (VX, 1), window)


def pre_behind(V, S, coef_ref, msg, force, window):
    b, b0, b1 = coefs(coef_ref, (C_B, C_B0, C_B1))

    def work(r):
        here, up, down, out = spans(r)
        syz, szz = S[YZ, 0, here], S[ZZ, 0, here]
        qy = V[VY, 0, here] + b * (S[XY, 0, here] + S[YY, 0, down] - S[YY, 0, here] + syz) - b0 * before(syz)
        qz = V[VZ, 0, here] + b * (S[XZ, 0, here] + syz - S[YZ, 0, up] - szz) + b1 * after(szz)
        V[VY, 0, here] = qy
        V[VZ, 0, here] = qz
        if msg is not None:
            msg[0, out] = S[XX, 0, here]
            msg[1, out] = qy
            msg[2, out] = qz

    over_message(V.shape[2] - 2 * PAD, work, msg)
    if force is not None:
        add_force(V, (VY, 0), force, (VY, 0), PAD + window)
        add_force(V, (VZ, 0), force, (VZ, 0), PAD + window)
        if msg is not None:
            add_force(msg, (1,), force, (VY, 0), window)
            add_force(msg, (2,), force, (VZ, 0), window)


def inner(V, S, coef_ref, force, window):
    b, b0, b1 = coefs(coef_ref, (C_B, C_B0, C_B1))

    def work(r):
        here, up, down, _ = spans(r)
        sxy, sxz = S[XY, 0, here], S[XZ, 0, here]
        V[VX, 0, here] = (
            V[VX, 0, here]
            + b * (S[XX, 1, here] - S[XX, 0, here] + sxy - S[XY, 0, up] + sxz)
            - b0 * before(sxz)
        )
        syz, szz = S[YZ, 1, here], S[ZZ, 1, here]
        V[VY, 1, here] = (
            V[VY, 1, here]
            + b * (S[XY, 1, here] - sxy + S[YY, 1, down] - S[YY, 1, here] + syz)
            - b0 * before(syz)
        )
        V[VZ, 1, here] = (
            V[VZ, 1, here]
            + b * (S[XZ, 1, here] - sxz + syz - S[YZ, 1, up] - szz)
            + b1 * after(szz)
        )

    over_rows(V.shape[2] - 2 * PAD, work)
    if force is not None:
        add_force(V, (VX, 0), force, (VX, 0), PAD + window)
        add_force(V, (VY, 1), force, (VY, 1), PAD + window)
        add_force(V, (VZ, 1), force, (VZ, 1), PAD + window)


def post(V, S, R, coef_ref, surface, cell, column, behind_x, ahead_y, ahead_z):
    m0, m1, lam, mu2, mu, k1, k2, k2h, l0 = coefs(
        coef_ref, (C_M0, C_M1, C_LAM, C_MU2, C_MU, C_K1, C_K2, C_K2H, C_L0)
    )

    def work(r):
        here, up, down, out = spans(r)
        vx, vy, vz = V[VX, cell, here], V[VY, cell, here], V[VZ, cell, here]
        exx = vx - behind_x(r)
        eyy = vy - V[VY, cell, up]
        ezz = vz - m0 * before(vz)
        exy = V[VX, cell, down] - vx + (ahead_y(r) - vy)
        exz = m1 * after(vx) - vx + (ahead_z(r) - vz)
        eyz = m1 * after(vy) - vy + (V[VZ, cell, down] - vz)
        volume = lam * (exx + eyy + ezz)
        for comp, e in ((XX, exx), (YY, eyy), (ZZ, ezz)):
            old = R[comp, cell, out]
            new = S[comp, cell, here] + (volume + mu2 * e) + DT * old
            if comp == ZZ:
                new = new + l0 * lane_roll(surface[out, :], -column)
            S[comp, cell, here] = new
            R[comp, cell, out] = k1 * old - k2 * e
        for comp, e in ((XY, exy), (XZ, exz), (YZ, eyz)):
            old = R[comp, cell, out]
            S[comp, cell, here] = S[comp, cell, here] + mu * e + DT * old
            R[comp, cell, out] = k1 * old - k2h * e

    over_rows(R.shape[2], work)


def response_behind(V, S, coef_ref, D, W):
    b, b0, b1, m0, m1, lam, mu2, mu = coefs(coef_ref, (C_B, C_B0, C_B1, C_M0, C_M1, C_LAM, C_MU2, C_MU))

    def work(r):
        here, up, down, out = spans(r)
        sxy = S[XY, 1, here]
        vy, vz = -b * sxy, -b * S[XZ, 1, here]
        exx = -V[VX, 1, here]
        eyy = b * (S[XY, 1, up] - sxy)
        ezz = vz - m0 * before(vz)
        volume = lam * (exx + eyy + ezz)
        dyy, dzz = volume + mu2 * eyy, volume + mu2 * ezz
        dyz = mu * (m1 * after(vy) - vy - b * S[XZ, 1, down] - vz)
        W[0, here] = dyy
        W[1, here] = dyz
        D[0, out] = volume + mu2 * exx
        D[1, out] = vy + b * (dyz - mu * vy - dyy) - b0 * before(dyz)
        D[2, out] = vz + b * (dyz - mu * vz - dzz) + b1 * after(dzz)

    over_rows(D.shape[1], work)

    def rest(r):
        _, up, down, out = spans(r)
        D[1, out] = D[1, out] + b * W[0, down]
        D[2, out] = D[2, out] - b * W[1, up]

    over_rows(D.shape[1], rest)


def response_ahead(V, S, coef_ref, D, W):
    b, b0, m1, lam, mu2, mu = coefs(coef_ref, (C_B, C_B0, C_M1, C_LAM, C_MU2, C_MU))

    def work(r):
        here, _, down, out = spans(r)
        vx = b * S[XX, 0, here]
        dxy = mu * (b * S[XX, 0, down] - vx + V[VY, 0, here])
        dxz = mu * (m1 * after(vx) - vx + V[VZ, 0, here])
        W[0, here] = dxy
        D[0, out] = dxy
        D[1, out] = dxz
        D[2, out] = vx + b * (dxy + dxz - (lam + mu2) * vx) - b0 * before(dxz)

    over_rows(D.shape[1], work)

    def rest(r):
        _, up, _, out = spans(r)
        D[2, out] = D[2, out] - b * W[0, up]

    over_rows(D.shape[1], rest)


def early_ahead(V, S, R, coef_ref, msg, W, force, window):
    b, b0, m0, m1, lam, mu2, mu = coefs(coef_ref, (C_B, C_B0, C_M0, C_M1, C_LAM, C_MU2, C_MU))

    def work(r):
        here, up, down, out = spans(r)
        vx, vy, vz = V[VX, 1, here], V[VY, 1, here], V[VZ, 1, here]
        exx = vx - V[VX, 0, here]
        volume = lam * (exx + (vy - V[VY, 1, up]) + (vz - m0 * before(vz)))
        sxx = S[XX, 1, here] + (volume + mu2 * exx) + DT * R[XX, 1, out]
        sxy = S[XY, 1, here] + mu * (V[VX, 1, down] - vx - vy) + DT * R[XY, 1, out]
        sxz = S[XZ, 1, here] + mu * (m1 * after(vx) - vx - vz) + DT * R[XZ, 1, out]
        W[0, here] = sxy
        msg[0, out] = sxy
        msg[1, out] = sxz
        msg[2, out] = vx + b * (sxy + sxz - sxx) - b0 * before(sxz)

    over_rows(msg.shape[1], work)

    def rest(r):
        _, up, _, out = spans(r)
        msg[2, out] = msg[2, out] - b * W[0, up]

    over_rows(msg.shape[1], rest)
    if force is not None:
        add_force(msg, (2,), force, (VX, 1), window)


def early_behind(V, S, R, coef_ref, surface, column, msg, W, force, window):
    b, b0, b1, m0, m1, lam, mu2, mu, l0 = coefs(
        coef_ref, (C_B, C_B0, C_B1, C_M0, C_M1, C_LAM, C_MU2, C_MU, C_L0)
    )

    def work(r):
        here, up, down, out = spans(r)
        vx, vy, vz = V[VX, 0, here], V[VY, 0, here], V[VZ, 0, here]
        eyy = vy - V[VY, 0, up]
        ezz = vz - m0 * before(vz)
        volume = lam * (vx + eyy + ezz)
        sxx = S[XX, 0, here] + (volume + mu2 * vx) + DT * R[XX, 0, out]
        syy = S[YY, 0, here] + (volume + mu2 * eyy) + DT * R[YY, 0, out]
        szz = S[ZZ, 0, here] + (volume + mu2 * ezz) + DT * R[ZZ, 0, out]
        if surface is not None:
            szz = szz + l0 * lane_roll(surface[out, :], -column)
        sxy = S[XY, 0, here] + mu * (V[VX, 0, down] - vx + (V[VY, 1, here] - vy)) + DT * R[XY, 0, out]
        sxz = S[XZ, 0, here] + mu * (m1 * after(vx) - vx + (V[VZ, 1, here] - vz)) + DT * R[XZ, 0, out]
        syz = S[YZ, 0, here] + mu * (m1 * after(vy) - vy + (V[VZ, 0, down] - vz)) + DT * R[YZ, 0, out]
        W[0, here] = syy
        W[1, here] = syz
        msg[0, out] = sxx
        msg[1, out] = vy + b * (sxy - syy + syz) - b0 * before(syz)
        msg[2, out] = vz + b * (sxz + syz - szz) + b1 * after(szz)

    over_rows(msg.shape[1], work)

    def rest(r):
        _, up, down, out = spans(r)
        msg[1, out] = msg[1, out] + b * W[0, down]
        msg[2, out] = msg[2, out] - b * W[1, up]

    over_rows(msg.shape[1], rest)
    if force is not None:
        add_force(msg, (1,), force, (VY, 0), window)
        add_force(msg, (2,), force, (VZ, 0), window)


def ahead_bond(V, S, R, coef_ref, force, surface, msg, missing, G, step, window, unforced=0, respond=None):
    (b,) = coefs(coef_ref, (C_B,))
    _, _, has_ahead = place()
    keep = jnp.where(has_ahead, 1.0, 0.0).astype(jnp.float32)

    def got(i, out):
        return msg[i, out] if missing is None else msg[i, out] + missing[i, out]

    def work(r):
        here, _, _, out = spans(r)
        V[VX, 1, here] = V[VX, 1, here] + (keep * b) * got(0, out)
        G[0, out] = keep * (got(1, out) - b * S[XY, 1, here])
        G[1, out] = keep * (got(2, out) - b * S[XZ, 1, here])

    over_message(R.shape[2], work, msg)
    if step < unforced:
        add_force(G, (0,), force, (VY, 2), window)
        add_force(G, (1,), force, (VZ, 2), window)
    if respond is not None:
        respond()
    post(
        V, S, R, coef_ref, surface, 1, 2 * step + 1,
        lambda r: V[VX, 0, pl.ds(PAD + r, ROWS)],
        lambda r: G[0, pl.ds(r, ROWS)],
        lambda r: G[1, pl.ds(r, ROWS)],
    )


def behind_bond(V, S, R, coef_ref, force, surface, msg, missing, G, step, window, unforced=0, respond=None):
    (b,) = coefs(coef_ref, (C_B,))
    _, has_behind, _ = place()
    keep = jnp.where(has_behind, 1.0, 0.0).astype(jnp.float32)

    def got(i, out):
        return msg[i, out] if missing is None else msg[i, out] + missing[i, out]

    def work(r):
        here, _, _, out = spans(r)
        V[VY, 0, here] = V[VY, 0, here] - (keep * b) * got(0, out)
        V[VZ, 0, here] = V[VZ, 0, here] - (keep * b) * got(1, out)
        G[0, out] = keep * (got(2, out) + b * S[XX, 0, here])

    over_message(R.shape[2], work, msg)
    if step < unforced:
        add_force(G, (0,), force, (VX, 2), window)
    if respond is not None:
        respond()
    post(
        V, S, R, coef_ref, surface, 0, 2 * step,
        lambda r: G[0, pl.ds(r, ROWS)],
        lambda r: V[VY, 1, pl.ds(PAD + r, ROWS)],
        lambda r: V[VZ, 1, pl.ds(PAD + r, ROWS)],
    )


def start_kernel(
    velocity, stress, memory, layer_in, lam_in, mu_in, buoy_in, rate_in, defect_in, after_this,
    V, S, R, coef_ref, near_upper, near_lower, msg_far, layer_ref, lam, mu, buoy, rate, defect, sems,
):
    del after_this
    msg_near = Halves(near_upper, near_lower)
    across = velocity.shape[2]
    inside = pl.ds(PAD, across)
    pairs = [
        (layer_in, layer_ref), (lam_in, lam), (mu_in, mu), (buoy_in, buoy), (rate_in, rate), (defect_in, defect),
    ]
    pairs += [(stress.at[i], S.at[i, :, inside]) for i in range(6)]
    pairs += [(velocity.at[i], V.at[i, :, inside]) for i in range(3)]
    pairs += [(memory.at[i], R.at[i]) for i in range(6)]
    copies = [pltpu.make_async_copy(*pair, sems.at[i]) for i, pair in enumerate(pairs)]
    for copy in copies:
        copy.start()
    zero_edges(V)
    zero_edges(S)
    for copy in copies[:6]:
        copy.wait()
    layer = layer_ref[...]

    def per_depth(table):
        row = jnp.zeros(layer.shape, jnp.float32)
        for level in range(table.shape[0]):
            row = jnp.where(layer == level, table[level], row)
        return row

    lane = lax.broadcasted_iota(jnp.int32, layer.shape, 1)
    not_first = jnp.where(lane > 0, 1.0, 0.0).astype(jnp.float32)
    not_last = jnp.where(lane < layer.shape[1] - 1, 1.0, 0.0).astype(jnp.float32)
    b = DT * per_depth(buoy)
    two_mu = (2.0 * DT) * per_depth(mu)
    decay = DT * per_depth(rate)
    drop = 2.0 * decay * per_depth(defect)
    for row, value in (
        (C_B, b),
        (C_B0, b * not_first),
        (C_B1, b * not_last),
        (C_M0, not_first),
        (C_M1, not_last),
        (C_LAM, DT * per_depth(lam)),
        (C_MU2, two_mu),
        (C_MU, 0.5 * two_mu),
        (C_K1, 1.0 - decay),
        (C_K2, drop),
        (C_K2H, 0.5 * drop),
        (C_L0, DT * (1.0 - not_first)),
    ):
        coef_ref[row : row + 1, :] = value
    coef_ref[12:16, :] = jnp.zeros((4, layer.shape[1]), jnp.float32)
    for copy in copies[6:15]:
        copy.wait()
    even, _, _ = place()

    @pl.when(even)
    def _():
        pre_ahead(V, S, coef_ref, msg_near, None, 0)
        pre_behind(V, S, coef_ref, msg_far, None, 0)

    @pl.when(jnp.logical_not(even))
    def _():
        pre_behind(V, S, coef_ref, msg_near, None, 0)
        pre_ahead(V, S, coef_ref, msg_far, None, 0)

    for copy in copies[15:]:
        copy.wait()


def first_kernel(window, V0, S, R, coef_ref, force, surface, V, msg, W):
    even, _, _ = place()
    zero_edges(W)
    now, then = force.at[0], force.at[1]
    add_force(V, (VX, 1), now, (VX, 1), PAD + window)
    add_force(V, (VY, 0), now, (VY, 0), PAD + window)
    add_force(V, (VZ, 0), now, (VZ, 0), PAD + window)
    inner(V, S, coef_ref, now, window)

    @pl.when(even)
    def _():
        early_behind(V, S, R, coef_ref, surface, 0, msg, W, then, window)

    @pl.when(jnp.logical_not(even))
    def _():
        early_ahead(V, S, R, coef_ref, msg, W, then, window)


def results_out(V, S, R, results, sems, cell):
    inside = pl.ds(PAD, R.shape[2])
    pairs = [(V.at[:, cell, inside], results[0]), (S.at[:, cell, inside], results[1]), (R.at[:, cell], results[2])]
    return [
        pltpu.make_async_copy(source, result.at[:, cell], sems.at[i]) for i, (source, result) in enumerate(pairs)
    ]


def start_all(copies):
    for copy in copies:
        copy.start()


def wait_all(copies):
    for copy in copies:
        copy.wait()


def near_kernel(step, window, V0, S0, R0, coef_ref, force, surface, upper, lower, V, S, R, *rest):
    G = rest[-1]
    msg = Halves(upper, lower)
    even, _, _ = place()
    more = step < STEPS - 1
    send = Halves(*rest[:2]) if more else None

    @pl.when(even)
    def _():
        ahead_bond(V, S, R, coef_ref, force.at[step], surface, msg, None, G, step, window, 1)
        if more:
            pre_ahead(V, S, coef_ref, send, force.at[step + 1], window)
        else:
            copies = results_out(V, S, R, rest[:3], rest[-2], 1)
            start_all(copies)
            wait_all(copies)

    @pl.when(jnp.logical_not(even))
    def _():
        behind_bond(V, S, R, coef_ref, force.at[step], surface, msg, None, G, step, window, 1)
        if more:
            pre_behind(V, S, coef_ref, send, force.at[step + 1], window)
        else:
            copies = results_out(V, S, R, rest[:3], rest[-2], 0)
            start_all(copies)
            wait_all(copies)


def far_kernel(step, window, V0, S0, R0, coef_ref, force, surface, msg, *rest):
    rest = list(rest)
    missing = rest.pop(0) if step > 0 else None
    V, S, R, D = rest[:4]
    G, W = rest[-2:]
    early = rest[4] if step < STEPS - 2 else None
    even, _, _ = place()
    zero_edges(W)
    here, then = force.at[step], force.at[step + 1]

    @pl.when(even)
    def _():
        behind_bond(
            V, S, R, coef_ref, here, surface, msg, missing, G, step, window, 1,
            lambda: response_ahead(V, S, coef_ref, D, W),
        )
        pre_behind(V, S, coef_ref, None, then, window)

    @pl.when(jnp.logical_not(even))
    def _():
        ahead_bond(
            V, S, R, coef_ref, here, surface, msg, missing, G, step, window, 1,
            lambda: response_behind(V, S, coef_ref, D, W),
        )
        pre_ahead(V, S, coef_ref, None, then, window)

    inner(V, S, coef_ref, then, window)
    if early is not None:
        later = force.at[step + 2]

        @pl.when(even)
        def _():
            early_behind(V, S, R, coef_ref, surface, 2 * (step + 1), early, W, later, window)

        @pl.when(jnp.logical_not(even))
        def _():
            early_ahead(V, S, R, coef_ref, early, W, later, window)


def last_kernel(step, window, V0, S0, R0, coef_ref, force, surface, msg, missing, v0, s0, r0, V, S, R, *rest):
    *results, G, sems = rest
    even, _, _ = place()
    here = force.at[step]

    @pl.when(even)
    def _():
        copies = results_out(V, S, R, results, sems, 0)
        behind_bond(
            V, S, R, coef_ref, here, surface, msg, missing, G, step, window, 0, lambda: start_all(copies[:1])
        )
        start_all(copies[1:])
        wait_all(copies)

    @pl.when(jnp.logical_not(even))
    def _():
        copies = results_out(V, S, R, results, sems, 1)
        ahead_bond(
            V, S, R, coef_ref, here, surface, msg, missing, G, step, window, 0, lambda: start_all(copies[:1])
        )
        start_all(copies[1:])
        wait_all(copies)


ENTRY_ROW, TRUCK_ROW = 36, 40
GROUP = 8


def pack_kernel(
    record, loads_in, entries_in, cells_in, piers_in, own, loads, steps_table, piers, entries, cells, sems
):
    panel = record.shape[1]
    slots, lanes = loads.shape
    steps = entries.shape[0]
    pairs = [(record, own.at[:, pl.ds(0, panel)]), (loads_in, loads), (entries_in, entries), (cells_in, cells)]
    pairs.append((piers_in, piers))
    copies = [pltpu.make_async_copy(*pair, sems.at[i]) for i, pair in enumerate(pairs)]
    for copy in copies:
        copy.start()
    own[:, panel:] = jnp.zeros((own.shape[0], own.shape[1] - panel), jnp.float32)
    steps_table[...] = jnp.zeros(steps_table.shape, jnp.float32)
    for copy in copies:
        copy.wait()
    steps_table[0:steps, 0:slots] = entries[...].astype(jnp.float32)
    steps_table[8 : 8 + steps, 0:slots] = cells[...].astype(jnp.float32)
    blocks = [loads[8 * i : 8 * i + 8, :] for i in range(slots // 8)] + [steps_table[0:8, :]]
    for i, block in enumerate(blocks):
        own[0:8, panel + i * lanes : panel + (i + 1) * lanes] = block


def lane_blocks(table, width):
    return sum(lane_roll(table[s : s + 1, :], s * width) for s in range(STEPS))


def split_kernel(panel, slots, own, behind, cells, after_this, out):
    del after_this
    tiles, _, lanes = out.shape
    pieces = panel // lanes
    third = pieces // 3
    cell_of = cells[...]
    me = lax.axis_index("line")
    group, mine = lax.div(me, tiles), lax.rem(me, tiles)
    piers = cell_of.shape[1]
    row = lax.broadcasted_iota(jnp.int32, (3 * tiles, lanes), 0)
    j = lax.rem(row, 3)
    first = (lax.div(row, 3) + group * tiles) * 2
    cell_x, cell_yz = first + jnp.where(j == 2, -1, j), first + j
    record = jnp.where(group == 0, own[:, :panel], behind[:, :panel])

    def hits(cell):
        return [jnp.where(cell == cell_of[0:1, p : p + 1], 1.0, 0.0).astype(jnp.float32) for p in range(piers)]

    hit_x, hit_yz = hits(cell_x), hits(cell_yz)

    def share(m):
        hit = hit_x if m < third else hit_yz
        return sum(hit[p] * record[p : p + 1, m * lanes : (m + 1) * lanes] for p in range(piers))

    parts = [share(m) for m in range(pieces)]

    def trucks(source):
        blocks = [source[0:8, panel + i * lanes : panel + (i + 1) * lanes] for i in range(slots // 8 + 1)]
        return blocks[:-1], lane_blocks(blocks[-1], slots)

    own_rows, own_entry = trucks(own)
    far_rows, far_entry = trucks(behind)
    for tile in range(tiles):
        these = slice(3 * tile, 3 * tile + 3)
        for m in range(pieces):
            out[tile, 3 * m : 3 * m + 3, :] = parts[m][these, :]
        passed = mine < tile
        out[tile, ENTRY_ROW : ENTRY_ROW + 1, :] = jnp.where(passed, own_entry, far_entry)
        for i in range(slots // 8):
            at = TRUCK_ROW + 8 * i
            out[tile, at : at + 8, :] = jnp.where(passed, own_rows[i], far_rows[i])


def prepare_kernel(parts, loads, steps_table, force, surface, table, rows_out):
    steps, comps, width = force.shape[:3]
    lanes = parts.shape[2]
    force[...] = jnp.zeros(force.shape, jnp.float32)
    per = ENTRY_ROW // (comps * width)
    lane = lax.broadcasted_iota(jnp.int32, (per, lanes), 1)
    scale = jnp.where(lane < FZ, DT, 0.0).astype(jnp.float32)
    for s in range(steps):
        for comp in range(comps):
            for cell in range(width):
                panel = parts[s, pl.ds(comp * per * width + cell, per, stride=width), :]
                force[s, comp, cell, pl.ds(4, per, stride=2), :] = scale * panel
                force[s, comp, cell, pl.ds(5, per, stride=2), :] = scale * lane_roll(panel, FZ)
    surface_loads(SOON, parts, loads, steps_table, surface, table, rows_out)


def surface_kernel(parts, loads, steps_table, surface, table, rows_out):
    surface_loads(STEPS, parts, loads, steps_table, surface, table, rows_out)


def surface_loads(steps, parts, loads, steps_table, surface, table, rows_out):
    slots = loads.shape[0]
    tiles = parts.shape[0]
    mine = lax.rem(lax.axis_index("line"), tiles)
    table[...] = jnp.zeros(table.shape, jnp.float32)
    table[0:1, :] = lane_blocks(steps_table[0:8, :], slots)
    table[steps + 1 : steps + 2, :] = lane_blocks(steps_table[8:16, :], slots)
    rows = [loads[...]]
    for k in range(1, steps + 1):
        source = lax.rem(mine + (tiles - k), tiles)
        rows.append(parts[source, TRUCK_ROW : TRUCK_ROW + slots, :])
        table[k : k + 1, :] = parts[source, ENTRY_ROW : ENTRY_ROW + 1, :]
    columns = table[...].T
    rows_out[...] = jnp.zeros(rows_out.shape, jnp.float32)
    for s in range(steps):
        block = slice(s * slots, (s + 1) * slots)
        moved = []
        for k in range(steps - s):
            entry = jnp.broadcast_to(columns[block, k : k + 1], rows[k].shape)
            new = rows[k]
            for slot in range(slots):
                new = jnp.where(entry == float(slot), rows[k + 1][slot : slot + 1, :], new)
            moved.append(new)
        rows = moved
        cell = jnp.broadcast_to(columns[block, steps + 1 : steps + 2], rows[0].shape)
        for c in range(2):
            load = jnp.sum(jnp.where(cell == float(c), rows[0], 0.0), axis=0, keepdims=True)
            rows_out[2 * s + c : 2 * s + c + 1, :] = load
    surface[...] = rows_out[...].T


def in_vmem(x):
    return pltpu.with_memory_space_constraint(x, pltpu.VMEM)


WHOLE = pl.BlockSpec(memory_space=pltpu.VMEM)
SCALARS = pl.BlockSpec(memory_space=pltpu.SMEM)
ANYWHERE = pl.BlockSpec(memory_space=pl.ANY)


def call(kernel, ins, specs, outs, out_specs, scratch=(), aliases=None, name=None, cost=1):
    return pl.pallas_call(
        kernel,
        out_shape=outs,
        in_specs=specs,
        out_specs=out_specs,
        scratch_shapes=list(scratch),
        input_output_aliases=aliases or {},
        compiler_params=pltpu.CompilerParams(vmem_limit_bytes=VMEM_LIMIT),
        cost_estimate=pl.CostEstimate(flops=cost, bytes_accessed=cost, transcendentals=0),
        name=name,
    )(*ins)


def body(
    velocity, stress, memory, truck_loads, pier_panels,
    lame_lambda, lame_mu, buoyancy, relax_rate, defect_mu, layer,
    truck_entry, truck_cell, pier_cell,
):
    tiles = lax.axis_size("line")
    width_x, across, depth = velocity.shape[1:]
    slots = truck_loads.shape[0]
    window = (across - FY) // 2 - 4
    f32 = jnp.float32

    near = [(i, i ^ 1) for i in range(tiles) if (i ^ 1) < tiles]
    far = [(i, i + 1) for i in range(1, tiles - 1, 2)] + [(i + 1, i) for i in range(1, tiles - 1, 2)]

    padded = across + 2 * PAD
    v_type = pltpu.VMEM((3, width_x, padded, depth), f32)
    s_type = pltpu.VMEM((6, width_x, padded, depth), f32)
    r_type = pltpu.VMEM((6, width_x, across, depth), f32)
    c_type = pltpu.VMEM((N_COEF, depth), f32)
    m_type = pltpu.VMEM((3, across, depth), f32)
    planes = (pltpu.VMEM((3, across // 2, depth), f32),) * 2
    ghost = pltpu.VMEM((2, across, depth), f32)
    work = pltpu.VMEM((2, padded, depth), f32)

    def ahead_by(x, distance):
        return lax.ppermute(x, "line", [(i, i + distance) for i in range(tiles - distance)])

    def in_hbm(*arrays):
        return tuple(pltpu.with_memory_space_constraint(x, pltpu.HBM) for x in arrays)

    dma = pltpu.SemaphoreType.DMA
    piers, panel = pier_panels.shape[1:]
    own, loads, steps_table, pier_row = call(
        pack_kernel,
        in_hbm(pier_panels[0], truck_loads, truck_entry, truck_cell, pier_cell[None, :]),
        (ANYWHERE,) * 5,
        (
            pltpu.VMEM((piers, panel + (slots // 8 + 1) * depth), f32),
            pltpu.VMEM((slots, depth), f32),
            pltpu.VMEM((16, depth), f32),
            pltpu.VMEM((1, piers), jnp.int32),
        ),
        (WHOLE,) * 4,
        scratch=(pltpu.VMEM(truck_entry.shape, jnp.int32), pltpu.VMEM(truck_cell.shape, jnp.int32), dma((5,))),
        name="pack",
    )
    behind = ahead_by(own, GROUP)
    reach = 2 * GROUP
    index = lax.axis_index("line")
    while reach < tiles:
        record = jnp.where(index < GROUP, own, behind)[:, :panel]
        record = jnp.where(index < reach, record, ahead_by(record, reach))
        behind = jnp.concatenate([record, behind[:, panel:]], axis=1)
        reach *= 2
    tables = (lame_lambda, lame_mu, buoyancy, relax_rate, defect_mu)
    V, S, R, coef, *msg_near, msg_far = call(
        start_kernel,
        in_hbm(velocity, stress, memory, layer[None, :], *tables) + (steps_table,),
        (ANYWHERE,) * 10,
        (v_type, s_type, r_type, c_type, *planes, m_type),
        (WHOLE,) * 7,
        scratch=(
            pltpu.VMEM((1, depth), jnp.int32), *(pltpu.SMEM(table.shape, f32) for table in tables), dma((21,)),
        ),
        name="start",
        cost=8 * 1024 * 1024,
    )
    msg_far = lax.ppermute(msg_far, "line", far)
    msg_near = [lax.ppermute(plane, "line", near) for plane in msg_near]
    parts = call(
        functools.partial(split_kernel, panel, slots),
        (own, behind, in_vmem(pier_row), coef),
        (WHOLE,) * 3 + (ANYWHERE,),
        pltpu.VMEM((GROUP, TRUCK_ROW + slots, depth), f32),
        WHOLE,
        name="split",
    )
    groups = [list(range(at, at + GROUP)) for at in range(0, tiles, GROUP)]
    parts = lax.all_to_all(parts, "line", 0, 0, axis_index_groups=groups, tiled=True)
    square = pltpu.VMEM((across, depth), f32)
    turned = (pltpu.VMEM((depth, depth), f32), pltpu.VMEM((depth, across), f32))
    ins = (parts, in_vmem(loads), in_vmem(steps_table))
    force, surface = call(
        prepare_kernel,
        ins,
        (WHOLE,) * 3,
        (pltpu.VMEM((STEPS, 3, 3, 16, depth), f32), square),
        (WHOLE,) * 2,
        scratch=turned,
        name="prepare",
    )
    later = call(surface_kernel, ins, (WHOLE,) * 3, square, WHOLE, scratch=turned, name="surface")
    V, early = call(
        functools.partial(first_kernel, window),
        tuple(in_vmem(x) for x in (V, S, R, coef, force, surface)),
        (WHOLE,) * 6,
        (v_type, m_type),
        (WHOLE,) * 2,
        scratch=(work,),
        aliases={0: 0},
        name="first",
    )
    early = lax.ppermute(early, "line", far)
    state = (v_type, s_type, r_type)
    results = tuple(jax.ShapeDtypeStruct(x.shape, f32) for x in (velocity, stress, memory))
    same = {0: 0, 1: 1, 2: 2}
    missing = None
    for step in range(STEPS):
        more = step < STEPS - 1
        ins = tuple(in_vmem(x) for x in (V, S, R, coef, force, surface, *msg_near))
        outs = state + (planes if more else results)
        V, S, R, *msg = call(
            functools.partial(near_kernel, step, window),
            ins,
            (WHOLE,) * len(ins),
            outs,
            (WHOLE,) * 5 if more else (WHOLE,) * 3 + (ANYWHERE,) * 3,
            scratch=(ghost,) if more else (dma((3,)), ghost),
            aliases=same,
            name="near" + str(step),
        )
        if more:
            msg_near = [lax.ppermute(plane, "line", near) for plane in msg]
        if step == SOON - 1:
            surface = later
        ins = (V, S, R, coef, force, surface, msg_far) + ((missing,) if step else ())
        ins = tuple(in_vmem(x) for x in ins)
        if more:
            outs = state + (m_type,) + ((m_type,) if step < STEPS - 2 else ())
            V, S, R, missing, *msg = call(
                functools.partial(far_kernel, step, window),
                ins,
                (WHOLE,) * len(ins),
                outs,
                (WHOLE,) * len(outs),
                scratch=(ghost, work),
                aliases=same,
                name="far" + str(step),
            )
            msg_far = early
            if msg:
                early = lax.ppermute(msg[0], "line", far)
    ends = call(
        functools.partial(last_kernel, STEPS - 1, window),
        ins + tuple(msg),
        (WHOLE,) * 8 + (ANYWHERE,) * 3,
        state + results,
        (WHOLE,) * 3 + (ANYWHERE,) * 3,
        scratch=(ghost, dma((3,))),
        aliases={**same, 8: 3, 9: 4, 10: 5},
        name="last",
    )
    return ends[3:]


def solution(mesh):
    placed = (
        P(None, ("runs", "line"), None, None),
        P(None, ("runs", "line"), None, None),
        P(None, ("runs", "line"), None, None),
        P(("runs", "line"), None),
        P("line", "runs", None),
        P(),
        P(),
        P(),
        P(),
        P(),
        P(),
        P(None, ("runs", "line")),
        P(None, ("runs", "line")),
        P(),
    )
    return jax.shard_map(
        body,
        mesh=mesh,
        in_specs=placed,
        out_specs=(
            P(None, ("runs", "line"), None, None),
            P(None, ("runs", "line"), None, None),
            P(None, ("runs", "line"), None, None),
        ),
        check_vma=False,
    )
```

```python
import functools

import jax
import jax.numpy as jnp
import numpy as np
from jax import lax
from jax.experimental import pallas as pl
from jax.experimental.pallas import tpu as pltpu
from jax.sharding import PartitionSpec as P

STEPS = 6
FY = 8
FZ = 64
DT = 0.25
PAD = 8
ROWS = 16
VMEM_LIMIT = 32 * 1024 * 1024

C_B, C_B0, C_B1, C_M0, C_M1, C_LAM, C_MU2, C_MU, C_K1, C_K2, C_K2H, C_L0 = range(12)
N_COEF = 16

VX, VY, VZ = range(3)
XX, YY, ZZ, XY, XZ, YZ = range(6)


def lane_roll(x, shift):
    return pltpu.roll(x, shift % x.shape[-1], x.ndim - 1)


def before(x):
    return lane_roll(x, 1)


def after(x):
    return lane_roll(x, -1)


def over_rows(count, work, first=0):
    def step(i, carry):
        work(pl.multiple_of(first + i * ROWS, ROWS))
        return carry

    lax.fori_loop(0, count // ROWS, step, 0, unroll=count // ROWS)


def coefs(coef_ref, ids):
    return [coef_ref[i : i + 1, :] for i in ids]


def place():
    index = lax.axis_index("line")
    return lax.rem(index, 2) == 0, index > 0, index < lax.axis_size("line") - 1


def spans(r):
    return pl.ds(PAD + r, ROWS), pl.ds(PAD + r - 1, ROWS), pl.ds(PAD + r + 1, ROWS), pl.ds(r, ROWS)


def zero_edges(ref):
    across = ref.shape[-2] - 2 * PAD
    edge = jnp.zeros((PAD, ref.shape[-1]), jnp.float32)
    for where in np.ndindex(*ref.shape[:-2]):
        ref[(*where, pl.ds(0, PAD))] = edge
        ref[(*where, pl.ds(PAD + across, PAD))] = edge


class Halves:
    def __init__(self, *refs):
        self.refs, self.half, self.rows = refs, 0, refs[0].shape[1]

    def at(self, out):
        return pl.ds(out.start - self.half * self.rows, out.size)

    def __getitem__(self, at):
        return self.refs[self.half][at[0], self.at(at[1])]

    def __setitem__(self, at, value):
        self.refs[self.half][at[0], self.at(at[1])] = value

    def add_force(self, plane, force, which, first_row):
        upper, lower = self.refs
        above = self.rows - first_row
        upper[plane, pl.ds(first_row, above)] = upper[plane, pl.ds(first_row, above)] + force[which][:above]
        lower[plane, pl.ds(0, 16 - above)] = lower[plane, pl.ds(0, 16 - above)] + force[which][above:]


def over_message(count, work, msg):
    if not isinstance(msg, Halves):
        over_rows(count, work)
        return
    for half in range(2):
        msg.half = half
        over_rows(msg.rows, work, half * msg.rows)


def add_force(ref, index, force, which, first_row):
    if isinstance(ref, Halves):
        ref.add_force(*index, force, which, first_row)
        return
    rows = pl.ds(first_row, 16)
    ref[(*index, rows)] = ref[(*index, rows)] + force[which]


def pre_ahead(V, S, coef_ref, msg, force, window):
    b, b0 = coefs(coef_ref, (C_B, C_B0))

    def work(r):
        here, up, _, out = spans(r)
        sxy, sxz = S[XY, 1, here], S[XZ, 1, here]
        px = V[VX, 1, here] + b * (sxy - S[XY, 1, up] + sxz - S[XX, 1, here]) - b0 * before(sxz)
        V[VX, 1, here] = px
        if msg is not None:
            msg[0, out] = sxy
            msg[1, out] = sxz
            msg[2, out] = px

    over_message(V.shape[2] - 2 * PAD, work, msg)
    if force is not None:
        add_force(V, (VX, 1), force, (VX, 1), PAD + window)
        if msg is not None:
            add_force(msg, (2,), force, (VX, 1), window)


def pre_behind(V, S, coef_ref, msg, force, window):
    b, b0, b1 = coefs(coef_ref, (C_B, C_B0, C_B1))

    def work(r):
        here, up, down, out = spans(r)
        syz, szz = S[YZ, 0, here], S[ZZ, 0, here]
        qy = V[VY, 0, here] + b * (S[XY, 0, here] + S[YY, 0, down] - S[YY, 0, here] + syz) - b0 * before(syz)
        qz = V[VZ, 0, here] + b * (S[XZ, 0, here] + syz - S[YZ, 0, up] - szz) + b1 * after(szz)
        V[VY, 0, here] = qy
        V[VZ, 0, here] = qz
        if msg is not None:
            msg[0, out] = S[XX, 0, here]
            msg[1, out] = qy
            msg[2, out] = qz

    over_message(V.shape[2] - 2 * PAD, work, msg)
    if force is not None:
        add_force(V, (VY, 0), force, (VY, 0), PAD + window)
        add_force(V, (VZ, 0), force, (VZ, 0), PAD + window)
        if msg is not None:
            add_force(msg, (1,), force, (VY, 0), window)
            add_force(msg, (2,), force, (VZ, 0), window)


def inner(V, S, coef_ref, force, window):
    b, b0, b1 = coefs(coef_ref, (C_B, C_B0, C_B1))

    def work(r):
        here, up, down, _ = spans(r)
        sxy, sxz = S[XY, 0, here], S[XZ, 0, here]
        V[VX, 0, here] = (
            V[VX, 0, here]
            + b * (S[XX, 1, here] - S[XX, 0, here] + sxy - S[XY, 0, up] + sxz)
            - b0 * before(sxz)
        )
        syz, szz = S[YZ, 1, here], S[ZZ, 1, here]
        V[VY, 1, here] = (
            V[VY, 1, here]
            + b * (S[XY, 1, here] - sxy + S[YY, 1, down] - S[YY, 1, here] + syz)
            - b0 * before(syz)
        )
        V[VZ, 1, here] = (
            V[VZ, 1, here]
            + b * (S[XZ, 1, here] - sxz + syz - S[YZ, 1, up] - szz)
            + b1 * after(szz)
        )

    over_rows(V.shape[2] - 2 * PAD, work)
    if force is not None:
        add_force(V, (VX, 0), force, (VX, 0), PAD + window)
        add_force(V, (VY, 1), force, (VY, 1), PAD + window)
        add_force(V, (VZ, 1), force, (VZ, 1), PAD + window)


def post(V, S, R, coef_ref, surface, cell, column, behind_x, ahead_y, ahead_z, done=None):
    m0, m1, lam, mu2, mu, k1, k2, k2h, l0 = coefs(
        coef_ref, (C_M0, C_M1, C_LAM, C_MU2, C_MU, C_K1, C_K2, C_K2H, C_L0)
    )

    def work(r):
        here, up, down, out = spans(r)
        vx, vy, vz = V[VX, cell, here], V[VY, cell, here], V[VZ, cell, here]
        exx = vx - behind_x(r)
        eyy = vy - V[VY, cell, up]
        ezz = vz - m0 * before(vz)
        exy = V[VX, cell, down] - vx + (ahead_y(r) - vy)
        exz = m1 * after(vx) - vx + (ahead_z(r) - vz)
        eyz = m1 * after(vy) - vy + (V[VZ, cell, down] - vz)
        volume = lam * (exx + eyy + ezz)
        for comp, e in ((XX, exx), (YY, eyy), (ZZ, ezz)):
            old = R[comp, cell, out]
            new = S[comp, cell, here] + (volume + mu2 * e) + DT * old
            if comp == ZZ:
                new = new + l0 * lane_roll(surface[out, :], -column)
            S[comp, cell, here] = new
            R[comp, cell, out] = k1 * old - k2 * e
        for comp, e in ((XY, exy), (XZ, exz), (YZ, eyz)):
            old = R[comp, cell, out]
            S[comp, cell, here] = S[comp, cell, here] + mu * e + DT * old
            R[comp, cell, out] = k1 * old - k2h * e

    if done is None:
        over_rows(R.shape[2], work)
        return
    half = R.shape[2] // 2
    for first in (0, half):
        over_rows(half, work, first)
        done(first, half)


def response_behind(V, S, coef_ref, D, W):
    b, b0, b1, m0, m1, lam, mu2, mu = coefs(coef_ref, (C_B, C_B0, C_B1, C_M0, C_M1, C_LAM, C_MU2, C_MU))

    def work(r):
        here, up, down, out = spans(r)
        sxy = S[XY, 1, here]
        vy, vz = -b * sxy, -b * S[XZ, 1, here]
        exx = -V[VX, 1, here]
        eyy = b * (S[XY, 1, up] - sxy)
        ezz = vz - m0 * before(vz)
        volume = lam * (exx + eyy + ezz)
        dyy, dzz = volume + mu2 * eyy, volume + mu2 * ezz
        dyz = mu * (m1 * after(vy) - vy - b * S[XZ, 1, down] - vz)
        W[0, here] = dyy
        W[1, here] = dyz
        D[0, out] = volume + mu2 * exx
        D[1, out] = vy + b * (dyz - mu * vy - dyy) - b0 * before(dyz)
        D[2, out] = vz + b * (dyz - mu * vz - dzz) + b1 * after(dzz)

    over_rows(D.shape[1], work)

    def rest(r):
        _, up, down, out = spans(r)
        D[1, out] = D[1, out] + b * W[0, down]
        D[2, out] = D[2, out] - b * W[1, up]

    over_rows(D.shape[1], rest)


def response_ahead(V, S, coef_ref, D, W):
    b, b0, m1, lam, mu2, mu = coefs(coef_ref, (C_B, C_B0, C_M1, C_LAM, C_MU2, C_MU))

    def work(r):
        here, _, down, out = spans(r)
        vx = b * S[XX, 0, here]
        dxy = mu * (b * S[XX, 0, down] - vx + V[VY, 0, here])
        dxz = mu * (m1 * after(vx) - vx + V[VZ, 0, here])
        W[0, here] = dxy
        D[0, out] = dxy
        D[1, out] = dxz
        D[2, out] = vx + b * (dxy + dxz - (lam + mu2) * vx) - b0 * before(dxz)

    over_rows(D.shape[1], work)

    def rest(r):
        _, up, _, out = spans(r)
        D[2, out] = D[2, out] - b * W[0, up]

    over_rows(D.shape[1], rest)


def early_ahead(V, S, R, coef_ref, msg, W, force, window):
    b, b0, m0, m1, lam, mu2, mu = coefs(coef_ref, (C_B, C_B0, C_M0, C_M1, C_LAM, C_MU2, C_MU))

    def work(r):
        here, up, down, out = spans(r)
        vx, vy, vz = V[VX, 1, here], V[VY, 1, here], V[VZ, 1, here]
        exx = vx - V[VX, 0, here]
        volume = lam * (exx + (vy - V[VY, 1, up]) + (vz - m0 * before(vz)))
        sxx = S[XX, 1, here] + (volume + mu2 * exx) + DT * R[XX, 1, out]
        sxy = S[XY, 1, here] + mu * (V[VX, 1, down] - vx - vy) + DT * R[XY, 1, out]
        sxz = S[XZ, 1, here] + mu * (m1 * after(vx) - vx - vz) + DT * R[XZ, 1, out]
        W[0, here] = sxy
        msg[0, out] = sxy
        msg[1, out] = sxz
        msg[2, out] = vx + b * (sxy + sxz - sxx) - b0 * before(sxz)

    over_rows(msg.shape[1], work)

    def rest(r):
        _, up, _, out = spans(r)
        msg[2, out] = msg[2, out] - b * W[0, up]

    over_rows(msg.shape[1], rest)
    if force is not None:
        add_force(msg, (2,), force, (VX, 1), window)


def early_behind(V, S, R, coef_ref, surface, column, msg, W, force, window):
    b, b0, b1, m0, m1, lam, mu2, mu, l0 = coefs(
        coef_ref, (C_B, C_B0, C_B1, C_M0, C_M1, C_LAM, C_MU2, C_MU, C_L0)
    )

    def work(r):
        here, up, down, out = spans(r)
        vx, vy, vz = V[VX, 0, here], V[VY, 0, here], V[VZ, 0, here]
        eyy = vy - V[VY, 0, up]
        ezz = vz - m0 * before(vz)
        volume = lam * (vx + eyy + ezz)
        sxx = S[XX, 0, here] + (volume + mu2 * vx) + DT * R[XX, 0, out]
        syy = S[YY, 0, here] + (volume + mu2 * eyy) + DT * R[YY, 0, out]
        szz = S[ZZ, 0, here] + (volume + mu2 * ezz) + DT * R[ZZ, 0, out]
        if surface is not None:
            szz = szz + l0 * lane_roll(surface[out, :], -column)
        sxy = S[XY, 0, here] + mu * (V[VX, 0, down] - vx + (V[VY, 1, here] - vy)) + DT * R[XY, 0, out]
        sxz = S[XZ, 0, here] + mu * (m1 * after(vx) - vx + (V[VZ, 1, here] - vz)) + DT * R[XZ, 0, out]
        syz = S[YZ, 0, here] + mu * (m1 * after(vy) - vy + (V[VZ, 0, down] - vz)) + DT * R[YZ, 0, out]
        W[0, here] = syy
        W[1, here] = syz
        msg[0, out] = sxx
        msg[1, out] = vy + b * (sxy - syy + syz) - b0 * before(syz)
        msg[2, out] = vz + b * (sxz + syz - szz) + b1 * after(szz)

    over_rows(msg.shape[1], work)

    def rest(r):
        _, up, down, out = spans(r)
        msg[1, out] = msg[1, out] + b * W[0, down]
        msg[2, out] = msg[2, out] - b * W[1, up]

    over_rows(msg.shape[1], rest)
    if force is not None:
        add_force(msg, (1,), force, (VY, 0), window)
        add_force(msg, (2,), force, (VZ, 0), window)


def ahead_bond(V, S, R, coef_ref, force, surface, msg, missing, G, step, window, unforced=0, respond=None, done=None):
    (b,) = coefs(coef_ref, (C_B,))
    _, _, has_ahead = place()
    keep = jnp.where(has_ahead, 1.0, 0.0).astype(jnp.float32)

    def got(i, out):
        return msg[i, out] if missing is None else msg[i, out] + missing[i, out]

    def work(r):
        here, _, _, out = spans(r)
        V[VX, 1, here] = V[VX, 1, here] + (keep * b) * got(0, out)
        G[0, out] = keep * (got(1, out) - b * S[XY, 1, here])
        G[1, out] = keep * (got(2, out) - b * S[XZ, 1, here])

    over_message(R.shape[2], work, msg)
    if step < unforced:
        add_force(G, (0,), force, (VY, 2), window)
        add_force(G, (1,), force, (VZ, 2), window)
    if respond is not None:
        respond()
    post(
        V, S, R, coef_ref, surface, 1, 2 * step + 1,
        lambda r: V[VX, 0, pl.ds(PAD + r, ROWS)],
        lambda r: G[0, pl.ds(r, ROWS)],
        lambda r: G[1, pl.ds(r, ROWS)],
        done,
    )


def behind_bond(V, S, R, coef_ref, force, surface, msg, missing, G, step, window, unforced=0, respond=None, done=None):
    (b,) = coefs(coef_ref, (C_B,))
    _, has_behind, _ = place()
    keep = jnp.where(has_behind, 1.0, 0.0).astype(jnp.float32)

    def got(i, out):
        return msg[i, out] if missing is None else msg[i, out] + missing[i, out]

    def work(r):
        here, _, _, out = spans(r)
        V[VY, 0, here] = V[VY, 0, here] - (keep * b) * got(0, out)
        V[VZ, 0, here] = V[VZ, 0, here] - (keep * b) * got(1, out)
        G[0, out] = keep * (got(2, out) + b * S[XX, 0, here])

    over_message(R.shape[2], work, msg)
    if step < unforced:
        add_force(G, (0,), force, (VX, 2), window)
    if respond is not None:
        respond()
    post(
        V, S, R, coef_ref, surface, 0, 2 * step,
        lambda r: G[0, pl.ds(r, ROWS)],
        lambda r: V[VY, 1, pl.ds(PAD + r, ROWS)],
        lambda r: V[VZ, 1, pl.ds(PAD + r, ROWS)],
        done,
    )


def start_kernel(
    velocity, stress, memory, layer_in, lam_in, mu_in, buoy_in, rate_in, defect_in, after_this,
    V, S, R, coef_ref, near_upper, near_lower, msg_far, layer_ref, lam, mu, buoy, rate, defect, sems,
):
    del after_this
    msg_near = Halves(near_upper, near_lower)
    across = velocity.shape[2]
    inside = pl.ds(PAD, across)
    pairs = [
        (layer_in, layer_ref), (lam_in, lam), (mu_in, mu), (buoy_in, buoy), (rate_in, rate), (defect_in, defect),
    ]
    pairs += [(stress.at[i], S.at[i, :, inside]) for i in range(6)]
    pairs += [(velocity.at[i], V.at[i, :, inside]) for i in range(3)]
    pairs += [(memory.at[i], R.at[i]) for i in range(6)]
    copies = [pltpu.make_async_copy(*pair, sems.at[i]) for i, pair in enumerate(pairs)]
    for copy in copies:
        copy.start()
    zero_edges(V)
    zero_edges(S)
    for copy in copies[:6]:
        copy.wait()
    layer = layer_ref[...]

    def per_depth(table):
        row = jnp.zeros(layer.shape, jnp.float32)
        for level in range(table.shape[0]):
            row = jnp.where(layer == level, table[level], row)
        return row

    lane = lax.broadcasted_iota(jnp.int32, layer.shape, 1)
    not_first = jnp.where(lane > 0, 1.0, 0.0).astype(jnp.float32)
    not_last = jnp.where(lane < layer.shape[1] - 1, 1.0, 0.0).astype(jnp.float32)
    b = DT * per_depth(buoy)
    two_mu = (2.0 * DT) * per_depth(mu)
    decay = DT * per_depth(rate)
    drop = 2.0 * decay * per_depth(defect)
    for row, value in (
        (C_B, b),
        (C_B0, b * not_first),
        (C_B1, b * not_last),
        (C_M0, not_first),
        (C_M1, not_last),
        (C_LAM, DT * per_depth(lam)),
        (C_MU2, two_mu),
        (C_MU, 0.5 * two_mu),
        (C_K1, 1.0 - decay),
        (C_K2, drop),
        (C_K2H, 0.5 * drop),
        (C_L0, DT * (1.0 - not_first)),
    ):
        coef_ref[row : row + 1, :] = value
    coef_ref[12:16, :] = jnp.zeros((4, layer.shape[1]), jnp.float32)
    for copy in copies[6:15]:
        copy.wait()
    even, _, _ = place()

    @pl.when(even)
    def _():
        pre_ahead(V, S, coef_ref, msg_near, None, 0)
        pre_behind(V, S, coef_ref, msg_far, None, 0)

    @pl.when(jnp.logical_not(even))
    def _():
        pre_behind(V, S, coef_ref, msg_near, None, 0)
        pre_ahead(V, S, coef_ref, msg_far, None, 0)

    for copy in copies[15:]:
        copy.wait()


def first_kernel(window, V0, S, R, coef_ref, force, surface, V, msg, W):
    even, _, _ = place()
    zero_edges(W)
    now, then = force.at[0], force.at[1]
    add_force(V, (VX, 1), now, (VX, 1), PAD + window)
    add_force(V, (VY, 0), now, (VY, 0), PAD + window)
    add_force(V, (VZ, 0), now, (VZ, 0), PAD + window)
    inner(V, S, coef_ref, now, window)

    @pl.when(even)
    def _():
        early_behind(V, S, R, coef_ref, surface, 0, msg, W, then, window)

    @pl.when(jnp.logical_not(even))
    def _():
        early_ahead(V, S, R, coef_ref, msg, W, then, window)


def results_out(V, S, R, results, sems, cell):
    inside = pl.ds(PAD, R.shape[2])
    pairs = [(V.at[:, cell, inside], results[0]), (S.at[:, cell, inside], results[1]), (R.at[:, cell], results[2])]
    return [
        pltpu.make_async_copy(source, result.at[:, cell], sems.at[i]) for i, (source, result) in enumerate(pairs)
    ]


def start_all(copies):
    for copy in copies:
        copy.start()


def wait_all(copies):
    for copy in copies:
        copy.wait()


def near_kernel(step, window, V0, S0, R0, coef_ref, force, surface, upper, lower, V, S, R, *rest):
    G = rest[-1]
    msg = Halves(upper, lower)
    even, _, _ = place()
    more = step < STEPS - 1
    send = Halves(*rest[:2]) if more else None

    @pl.when(even)
    def _():
        ahead_bond(V, S, R, coef_ref, force.at[step], surface, msg, None, G, step, window, 1)
        if more:
            pre_ahead(V, S, coef_ref, send, force.at[step + 1], window)
        else:
            copies = results_out(V, S, R, rest[:3], rest[-2], 1)
            start_all(copies)
            wait_all(copies)

    @pl.when(jnp.logical_not(even))
    def _():
        behind_bond(V, S, R, coef_ref, force.at[step], surface, msg, None, G, step, window, 1)
        if more:
            pre_behind(V, S, coef_ref, send, force.at[step + 1], window)
        else:
            copies = results_out(V, S, R, rest[:3], rest[-2], 0)
            start_all(copies)
            wait_all(copies)


def far_kernel(step, window, V0, S0, R0, coef_ref, force, surface, msg, *rest):
    rest = list(rest)
    missing = rest.pop(0) if step > 0 else None
    V, S, R, D = rest[:4]
    G, W = rest[-2:]
    early = rest[4] if step < STEPS - 2 else None
    even, _, _ = place()
    zero_edges(W)
    here, then = force.at[step], force.at[step + 1]

    @pl.when(even)
    def _():
        behind_bond(
            V, S, R, coef_ref, here, surface, msg, missing, G, step, window, 1,
            lambda: response_ahead(V, S, coef_ref, D, W),
        )
        pre_behind(V, S, coef_ref, None, then, window)

    @pl.when(jnp.logical_not(even))
    def _():
        ahead_bond(
            V, S, R, coef_ref, here, surface, msg, missing, G, step, window, 1,
            lambda: response_behind(V, S, coef_ref, D, W),
        )
        pre_ahead(V, S, coef_ref, None, then, window)

    inner(V, S, coef_ref, then, window)
    if early is not None:
        later = force.at[step + 2]

        @pl.when(even)
        def _():
            early_behind(V, S, R, coef_ref, surface, 2 * (step + 1), early, W, later, window)

        @pl.when(jnp.logical_not(even))
        def _():
            early_ahead(V, S, R, coef_ref, early, W, later, window)


def last_kernel(step, window, V0, S0, R0, coef_ref, force, surface, msg, missing, v0, s0, r0, V, S, R, *rest):
    *results, G, sems = rest
    even, _, _ = place()
    here = force.at[step]

    def finish(cell, bond):
        copies = []

        def send(source, result):
            copies.append(pltpu.make_async_copy(source, result, sems.at[len(copies)]))
            copies[-1].start()

        def velocities():
            send(V.at[:, cell, pl.ds(PAD, R.shape[2])], results[0].at[:, cell])

        def done(first, count):
            out = pl.ds(first, count)
            send(S.at[:, cell, pl.ds(PAD + first, count)], results[1].at[:, cell, out])
            send(R.at[:, cell, out], results[2].at[:, cell, out])

        bond(V, S, R, coef_ref, here, surface, msg, missing, G, step, window, 0, velocities, done)
        wait_all(copies)

    @pl.when(even)
    def _():
        finish(0, behind_bond)

    @pl.when(jnp.logical_not(even))
    def _():
        finish(1, ahead_bond)


ENTRY_ROW, TRUCK_ROW = 36, 40
GROUP = 8


def pack_kernel(
    record, loads_in, entries_in, cells_in, piers_in, own, loads, steps_table, piers, entries, cells, sems
):
    panel = record.shape[1]
    slots, lanes = loads.shape
    steps = entries.shape[0]
    pairs = [(record, own.at[:, pl.ds(0, panel)]), (loads_in, loads), (entries_in, entries), (cells_in, cells)]
    pairs.append((piers_in, piers))
    copies = [pltpu.make_async_copy(*pair, sems.at[i]) for i, pair in enumerate(pairs)]
    for copy in copies:
        copy.start()
    own[:, panel:] = jnp.zeros((own.shape[0], own.shape[1] - panel), jnp.float32)
    steps_table[...] = jnp.zeros(steps_table.shape, jnp.float32)
    for copy in copies:
        copy.wait()
    steps_table[0:steps, 0:slots] = entries[...].astype(jnp.float32)
    steps_table[8 : 8 + steps, 0:slots] = cells[...].astype(jnp.float32)
    blocks = [loads[8 * i : 8 * i + 8, :] for i in range(slots // 8)] + [steps_table[0:8, :]]
    for i, block in enumerate(blocks):
        own[0:8, panel + i * lanes : panel + (i + 1) * lanes] = block


def lane_blocks(table, width):
    return sum(lane_roll(table[s : s + 1, :], s * width) for s in range(STEPS))


def split_kernel(panel, slots, own, behind, cells, after_this, out):
    del after_this
    tiles, _, lanes = out.shape
    pieces = panel // lanes
    third = pieces // 3
    cell_of = cells[...]
    me = lax.axis_index("line")
    group, mine = lax.div(me, tiles), lax.rem(me, tiles)
    piers = cell_of.shape[1]
    row = lax.broadcasted_iota(jnp.int32, (3 * tiles, lanes), 0)
    j = lax.rem(row, 3)
    first = (lax.div(row, 3) + group * tiles) * 2
    cell_x, cell_yz = first + jnp.where(j == 2, -1, j), first + j
    record = jnp.where(group == 0, own[:, :panel], behind[:, :panel])

    def hits(cell):
        return [jnp.where(cell == cell_of[0:1, p : p + 1], 1.0, 0.0).astype(jnp.float32) for p in range(piers)]

    hit_x, hit_yz = hits(cell_x), hits(cell_yz)

    def share(m):
        hit = hit_x if m < third else hit_yz
        return sum(hit[p] * record[p : p + 1, m * lanes : (m + 1) * lanes] for p in range(piers))

    parts = [share(m) for m in range(pieces)]

    def trucks(source):
        blocks = [source[0:8, panel + i * lanes : panel + (i + 1) * lanes] for i in range(slots // 8 + 1)]
        return blocks[:-1], lane_blocks(blocks[-1], slots)

    own_rows, own_entry = trucks(own)
    far_rows, far_entry = trucks(behind)
    for tile in range(tiles):
        these = slice(3 * tile, 3 * tile + 3)
        for m in range(pieces):
            out[tile, 3 * m : 3 * m + 3, :] = parts[m][these, :]
        passed = mine < tile
        out[tile, ENTRY_ROW : ENTRY_ROW + 1, :] = jnp.where(passed, own_entry, far_entry)
        for i in range(slots // 8):
            at = TRUCK_ROW + 8 * i
            out[tile, at : at + 8, :] = jnp.where(passed, own_rows[i], far_rows[i])


def prepare_kernel(parts, loads, steps_table, force, surface, table, rows_out):
    steps, comps, width = force.shape[:3]
    lanes = parts.shape[2]
    force[...] = jnp.zeros(force.shape, jnp.float32)
    per = ENTRY_ROW // (comps * width)
    lane = lax.broadcasted_iota(jnp.int32, (per, lanes), 1)
    scale = jnp.where(lane < FZ, DT, 0.0).astype(jnp.float32)
    for s in range(steps):
        for comp in range(comps):
            for cell in range(width):
                panel = parts[s, pl.ds(comp * per * width + cell, per, stride=width), :]
                force[s, comp, cell, pl.ds(4, per, stride=2), :] = scale * panel
                force[s, comp, cell, pl.ds(5, per, stride=2), :] = scale * lane_roll(panel, FZ)
    surface_loads(1, parts, loads, steps_table, surface, table, rows_out)


def surface_kernel(parts, loads, steps_table, surface, table, rows_out):
    surface_loads(STEPS, parts, loads, steps_table, surface, table, rows_out)


def surface_loads(steps, parts, loads, steps_table, surface, table, rows_out):
    slots = loads.shape[0]
    tiles = parts.shape[0]
    mine = lax.rem(lax.axis_index("line"), tiles)
    table[...] = jnp.zeros(table.shape, jnp.float32)
    table[0:1, :] = lane_blocks(steps_table[0:8, :], slots)
    table[steps + 1 : steps + 2, :] = lane_blocks(steps_table[8:16, :], slots)
    rows = [loads[...]]
    for k in range(1, steps + 1):
        source = lax.rem(mine + (tiles - k), tiles)
        rows.append(parts[source, TRUCK_ROW : TRUCK_ROW + slots, :])
        table[k : k + 1, :] = parts[source, ENTRY_ROW : ENTRY_ROW + 1, :]
    columns = table[...].T
    rows_out[...] = jnp.zeros(rows_out.shape, jnp.float32)
    for s in range(steps):
        block = slice(s * slots, (s + 1) * slots)
        moved = []
        for k in range(steps - s):
            entry = jnp.broadcast_to(columns[block, k : k + 1], rows[k].shape)
            new = rows[k]
            for slot in range(slots):
                new = jnp.where(entry == float(slot), rows[k + 1][slot : slot + 1, :], new)
            moved.append(new)
        rows = moved
        cell = jnp.broadcast_to(columns[block, steps + 1 : steps + 2], rows[0].shape)
        for c in range(2):
            load = jnp.sum(jnp.where(cell == float(c), rows[0], 0.0), axis=0, keepdims=True)
            rows_out[2 * s + c : 2 * s + c + 1, :] = load
    surface[...] = rows_out[...].T


def in_vmem(x):
    return pltpu.with_memory_space_constraint(x, pltpu.VMEM)


WHOLE = pl.BlockSpec(memory_space=pltpu.VMEM)
SCALARS = pl.BlockSpec(memory_space=pltpu.SMEM)
ANYWHERE = pl.BlockSpec(memory_space=pl.ANY)


def call(kernel, ins, specs, outs, out_specs, scratch=(), aliases=None, name=None, cost=1):
    return pl.pallas_call(
        kernel,
        out_shape=outs,
        in_specs=specs,
        out_specs=out_specs,
        scratch_shapes=list(scratch),
        input_output_aliases=aliases or {},
        compiler_params=pltpu.CompilerParams(vmem_limit_bytes=VMEM_LIMIT),
        cost_estimate=pl.CostEstimate(flops=cost, bytes_accessed=cost, transcendentals=0),
        name=name,
    )(*ins)


def body(
    velocity, stress, memory, truck_loads, pier_panels,
    lame_lambda, lame_mu, buoyancy, relax_rate, defect_mu, layer,
    truck_entry, truck_cell, pier_cell,
):
    tiles = lax.axis_size("line")
    width_x, across, depth = velocity.shape[1:]
    slots = truck_loads.shape[0]
    window = (across - FY) // 2 - 4
    f32 = jnp.float32

    near = [(i, i ^ 1) for i in range(tiles) if (i ^ 1) < tiles]
    far = [(i, i + 1) for i in range(1, tiles - 1, 2)] + [(i + 1, i) for i in range(1, tiles - 1, 2)]

    padded = across + 2 * PAD
    v_type = pltpu.VMEM((3, width_x, padded, depth), f32)
    s_type = pltpu.VMEM((6, width_x, padded, depth), f32)
    r_type = pltpu.VMEM((6, width_x, across, depth), f32)
    c_type = pltpu.VMEM((N_COEF, depth), f32)
    m_type = pltpu.VMEM((3, across, depth), f32)
    planes = (pltpu.VMEM((3, across // 2, depth), f32),) * 2
    ghost = pltpu.VMEM((2, across, depth), f32)
    work = pltpu.VMEM((2, padded, depth), f32)

    def ahead_by(x, distance):
        return lax.ppermute(x, "line", [(i, i + distance) for i in range(tiles - distance)])

    def in_hbm(*arrays):
        return tuple(pltpu.with_memory_space_constraint(x, pltpu.HBM) for x in arrays)

    dma = pltpu.SemaphoreType.DMA
    piers, panel = pier_panels.shape[1:]
    own, loads, steps_table, pier_row = call(
        pack_kernel,
        in_hbm(pier_panels[0], truck_loads, truck_entry, truck_cell, pier_cell[None, :]),
        (ANYWHERE,) * 5,
        (
            pltpu.VMEM((piers, panel + (slots // 8 + 1) * depth), f32),
            pltpu.VMEM((slots, depth), f32),
            pltpu.VMEM((16, depth), f32),
            pltpu.VMEM((1, piers), jnp.int32),
        ),
        (WHOLE,) * 4,
        scratch=(pltpu.VMEM(truck_entry.shape, jnp.int32), pltpu.VMEM(truck_cell.shape, jnp.int32), dma((5,))),
        name="pack",
    )
    behind = ahead_by(own, GROUP)
    reach = 2 * GROUP
    index = lax.axis_index("line")
    while reach < tiles:
        record = jnp.where(index < GROUP, own, behind)[:, :panel]
        record = jnp.where(index < reach, record, ahead_by(record, reach))
        behind = jnp.concatenate([record, behind[:, panel:]], axis=1)
        reach *= 2
    tables = (lame_lambda, lame_mu, buoyancy, relax_rate, defect_mu)
    V, S, R, coef, *msg_near, msg_far = call(
        start_kernel,
        in_hbm(velocity, stress, memory, layer[None, :], *tables) + (steps_table,),
        (ANYWHERE,) * 10,
        (v_type, s_type, r_type, c_type, *planes, m_type),
        (WHOLE,) * 7,
        scratch=(
            pltpu.VMEM((1, depth), jnp.int32), *(pltpu.SMEM(table.shape, f32) for table in tables), dma((21,)),
        ),
        name="start",
        cost=8 * 1024 * 1024,
    )
    msg_far = lax.ppermute(msg_far, "line", far)
    msg_near = [lax.ppermute(plane, "line", near) for plane in msg_near]
    parts = call(
        functools.partial(split_kernel, panel, slots),
        (own, behind, in_vmem(pier_row), coef),
        (WHOLE,) * 3 + (ANYWHERE,),
        pltpu.VMEM((GROUP, TRUCK_ROW + slots, depth), f32),
        WHOLE,
        name="split",
    )
    groups = [list(range(at, at + GROUP)) for at in range(0, tiles, GROUP)]
    parts = lax.all_to_all(parts, "line", 0, 0, axis_index_groups=groups, tiled=True)
    square = pltpu.VMEM((across, depth), f32)
    turned = (pltpu.VMEM((depth, depth), f32), pltpu.VMEM((depth, across), f32))
    ins = (parts, in_vmem(loads), in_vmem(steps_table))
    force, surface = call(
        prepare_kernel,
        ins,
        (WHOLE,) * 3,
        (pltpu.VMEM((STEPS, 3, 3, 16, depth), f32), square),
        (WHOLE,) * 2,
        scratch=turned,
        name="prepare",
    )
    later = call(surface_kernel, ins, (WHOLE,) * 3, square, WHOLE, scratch=turned, name="surface")
    V, early = call(
        functools.partial(first_kernel, window),
        tuple(in_vmem(x) for x in (V, S, R, coef, force, surface)),
        (WHOLE,) * 6,
        (v_type, m_type),
        (WHOLE,) * 2,
        scratch=(work,),
        aliases={0: 0},
        name="first",
    )
    early = lax.ppermute(early, "line", far)
    state = (v_type, s_type, r_type)
    results = tuple(jax.ShapeDtypeStruct(x.shape, f32) for x in (velocity, stress, memory))
    same = {0: 0, 1: 1, 2: 2}
    missing = None
    for step in range(STEPS):
        more = step < STEPS - 1
        ins = tuple(in_vmem(x) for x in (V, S, R, coef, force, surface, *msg_near))
        outs = state + (planes if more else results)
        V, S, R, *msg = call(
            functools.partial(near_kernel, step, window),
            ins,
            (WHOLE,) * len(ins),
            outs,
            (WHOLE,) * 5 if more else (WHOLE,) * 3 + (ANYWHERE,) * 3,
            scratch=(ghost,) if more else (dma((3,)), ghost),
            aliases=same,
            name="near" + str(step),
        )
        if more:
            msg_near = [lax.ppermute(plane, "line", near) for plane in msg]
        if step == 0:
            surface = later
        ins = (V, S, R, coef, force, surface, msg_far) + ((missing,) if step else ())
        ins = tuple(in_vmem(x) for x in ins)
        if more:
            outs = state + (m_type,) + ((m_type,) if step < STEPS - 2 else ())
            V, S, R, missing, *msg = call(
                functools.partial(far_kernel, step, window),
                ins,
                (WHOLE,) * len(ins),
                outs,
                (WHOLE,) * len(outs),
                scratch=(ghost, work),
                aliases=same,
                name="far" + str(step),
            )
            msg_far = early
            if msg:
                early = lax.ppermute(msg[0], "line", far)
    ends = call(
        functools.partial(last_kernel, STEPS - 1, window),
        ins + tuple(msg),
        (WHOLE,) * 8 + (ANYWHERE,) * 3,
        state + results,
        (WHOLE,) * 3 + (ANYWHERE,) * 3,
        scratch=(ghost, dma((5,))),
        aliases={**same, 8: 3, 9: 4, 10: 5},
        name="last",
    )
    return ends[3:]


def solution(mesh):
    placed = (
        P(None, ("runs", "line"), None, None),
        P(None, ("runs", "line"), None, None),
        P(None, ("runs", "line"), None, None),
        P(("runs", "line"), None),
        P("line", "runs", None),
        P(),
        P(),
        P(),
        P(),
        P(),
        P(),
        P(None, ("runs", "line")),
        P(None, ("runs", "line")),
        P(),
    )
    return jax.shard_map(
        body,
        mesh=mesh,
        in_specs=placed,
        out_specs=(
            P(None, ("runs", "line"), None, None),
            P(None, ("runs", "line"), None, None),
            P(None, ("runs", "line"), None, None),
        ),
        check_vma=False,
    )
```

```python
import functools

import jax
import jax.numpy as jnp
import numpy as np
from jax import lax
from jax.experimental import pallas as pl
from jax.experimental.pallas import tpu as pltpu
from jax.sharding import PartitionSpec as P

STEPS = 6
FY = 8
FZ = 64
DT = 0.25
PAD = 8
ROWS = 16
VMEM_LIMIT = 32 * 1024 * 1024

C_B, C_B0, C_B1, C_M0, C_M1, C_LAM, C_MU2, C_MU, C_K1, C_K2, C_K2H, C_L0 = range(12)
N_COEF = 16

VX, VY, VZ = range(3)
XX, YY, ZZ, XY, XZ, YZ = range(6)


def lane_roll(x, shift):
    return pltpu.roll(x, shift % x.shape[-1], x.ndim - 1)


def before(x):
    return lane_roll(x, 1)


def after(x):
    return lane_roll(x, -1)


def over_rows(count, work, first=0):
    def step(i, carry):
        work(pl.multiple_of(first + i * ROWS, ROWS))
        return carry

    lax.fori_loop(0, count // ROWS, step, 0, unroll=count // ROWS)


def coefs(coef_ref, ids):
    return [coef_ref[i : i + 1, :] for i in ids]


def place():
    index = lax.axis_index("line")
    return lax.rem(index, 2) == 0, index > 0, index < lax.axis_size("line") - 1


def spans(r):
    return pl.ds(PAD + r, ROWS), pl.ds(PAD + r - 1, ROWS), pl.ds(PAD + r + 1, ROWS), pl.ds(r, ROWS)


def zero_edges(ref):
    across = ref.shape[-2] - 2 * PAD
    edge = jnp.zeros((PAD, ref.shape[-1]), jnp.float32)
    for where in np.ndindex(*ref.shape[:-2]):
        ref[(*where, pl.ds(0, PAD))] = edge
        ref[(*where, pl.ds(PAD + across, PAD))] = edge


class Halves:
    def __init__(self, *refs):
        self.refs, self.half, self.rows = refs, 0, refs[0].shape[1]

    def at(self, out):
        return pl.ds(out.start - self.half * self.rows, out.size)

    def __getitem__(self, at):
        return self.refs[self.half][at[0], self.at(at[1])]

    def __setitem__(self, at, value):
        self.refs[self.half][at[0], self.at(at[1])] = value

    def add_force(self, plane, force, which, first_row):
        upper, lower = self.refs
        above = self.rows - first_row
        upper[plane, pl.ds(first_row, above)] = upper[plane, pl.ds(first_row, above)] + force[which][:above]
        lower[plane, pl.ds(0, 16 - above)] = lower[plane, pl.ds(0, 16 - above)] + force[which][above:]


def over_message(count, work, msg):
    if not isinstance(msg, Halves):
        over_rows(count, work)
        return
    for half in range(2):
        msg.half = half
        over_rows(msg.rows, work, half * msg.rows)


def add_force(ref, index, force, which, first_row):
    if isinstance(ref, Halves):
        ref.add_force(*index, force, which, first_row)
        return
    rows = pl.ds(first_row, 16)
    ref[(*index, rows)] = ref[(*index, rows)] + force[which]


def pre_ahead(V, S, coef_ref, msg, force, window):
    b, b0 = coefs(coef_ref, (C_B, C_B0))

    def work(r):
        here, up, _, out = spans(r)
        sxy, sxz = S[XY, 1, here], S[XZ, 1, here]
        px = V[VX, 1, here] + b * (sxy - S[XY, 1, up] + sxz - S[XX, 1, here]) - b0 * before(sxz)
        V[VX, 1, here] = px
        if msg is not None:
            msg[0, out] = sxy
            msg[1, out] = sxz
            msg[2, out] = px

    over_message(V.shape[2] - 2 * PAD, work, msg)
    if force is not None:
        add_force(V, (VX, 1), force, (VX, 1), PAD + window)
        if msg is not None:
            add_force(msg, (2,), force, (VX, 1), window)


def pre_behind(V, S, coef_ref, msg, force, window):
    b, b0, b1 = coefs(coef_ref, (C_B, C_B0, C_B1))

    def work(r):
        here, up, down, out = spans(r)
        syz, szz = S[YZ, 0, here], S[ZZ, 0, here]
        qy = V[VY, 0, here] + b * (S[XY, 0, here] + S[YY, 0, down] - S[YY, 0, here] + syz) - b0 * before(syz)
        qz = V[VZ, 0, here] + b * (S[XZ, 0, here] + syz - S[YZ, 0, up] - szz) + b1 * after(szz)
        V[VY, 0, here] = qy
        V[VZ, 0, here] = qz
        if msg is not None:
            msg[0, out] = S[XX, 0, here]
            msg[1, out] = qy
            msg[2, out] = qz

    over_message(V.shape[2] - 2 * PAD, work, msg)
    if force is not None:
        add_force(V, (VY, 0), force, (VY, 0), PAD + window)
        add_force(V, (VZ, 0), force, (VZ, 0), PAD + window)
        if msg is not None:
            add_force(msg, (1,), force, (VY, 0), window)
            add_force(msg, (2,), force, (VZ, 0), window)


def inner(V, S, coef_ref, force, window):
    b, b0, b1 = coefs(coef_ref, (C_B, C_B0, C_B1))

    def work(r):
        here, up, down, _ = spans(r)
        sxy, sxz = S[XY, 0, here], S[XZ, 0, here]
        V[VX, 0, here] = (
            V[VX, 0, here]
            + b * (S[XX, 1, here] - S[XX, 0, here] + sxy - S[XY, 0, up] + sxz)
            - b0 * before(sxz)
        )
        syz, szz = S[YZ, 1, here], S[ZZ, 1, here]
        V[VY, 1, here] = (
            V[VY, 1, here]
            + b * (S[XY, 1, here] - sxy + S[YY, 1, down] - S[YY, 1, here] + syz)
            - b0 * before(syz)
        )
        V[VZ, 1, here] = (
            V[VZ, 1, here]
            + b * (S[XZ, 1, here] - sxz + syz - S[YZ, 1, up] - szz)
            + b1 * after(szz)
        )

    over_rows(V.shape[2] - 2 * PAD, work)
    if force is not None:
        add_force(V, (VX, 0), force, (VX, 0), PAD + window)
        add_force(V, (VY, 1), force, (VY, 1), PAD + window)
        add_force(V, (VZ, 1), force, (VZ, 1), PAD + window)


def post(V, S, R, coef_ref, surface, cell, column, behind_x, ahead_y, ahead_z):
    m0, m1, lam, mu2, mu, k1, k2, k2h, l0 = coefs(
        coef_ref, (C_M0, C_M1, C_LAM, C_MU2, C_MU, C_K1, C_K2, C_K2H, C_L0)
    )

    def work(r):
        here, up, down, out = spans(r)
        vx, vy, vz = V[VX, cell, here], V[VY, cell, here], V[VZ, cell, here]
        exx = vx - behind_x(r)
        eyy = vy - V[VY, cell, up]
        ezz = vz - m0 * before(vz)
        exy = V[VX, cell, down] - vx + (ahead_y(r) - vy)
        exz = m1 * after(vx) - vx + (ahead_z(r) - vz)
        eyz = m1 * after(vy) - vy + (V[VZ, cell, down] - vz)
        volume = lam * (exx + eyy + ezz)
        for comp, e in ((XX, exx), (YY, eyy), (ZZ, ezz)):
            old = R[comp, cell, out]
            new = S[comp, cell, here] + (volume + mu2 * e) + DT * old
            if comp == ZZ:
                new = new + l0 * lane_roll(surface[out, :], -column)
            S[comp, cell, here] = new
            R[comp, cell, out] = k1 * old - k2 * e
        for comp, e in ((XY, exy), (XZ, exz), (YZ, eyz)):
            old = R[comp, cell, out]
            S[comp, cell, here] = S[comp, cell, here] + mu * e + DT * old
            R[comp, cell, out] = k1 * old - k2h * e

    over_rows(R.shape[2], work)


def response_behind(V, S, coef_ref, D, W):
    b, b0, b1, m0, m1, lam, mu2, mu = coefs(coef_ref, (C_B, C_B0, C_B1, C_M0, C_M1, C_LAM, C_MU2, C_MU))

    def work(r):
        here, up, down, out = spans(r)
        sxy = S[XY, 1, here]
        vy, vz = -b * sxy, -b * S[XZ, 1, here]
        exx = -V[VX, 1, here]
        eyy = b * (S[XY, 1, up] - sxy)
        ezz = vz - m0 * before(vz)
        volume = lam * (exx + eyy + ezz)
        dyy, dzz = volume + mu2 * eyy, volume + mu2 * ezz
        dyz = mu * (m1 * after(vy) - vy - b * S[XZ, 1, down] - vz)
        W[0, here] = dyy
        W[1, here] = dyz
        D[0, out] = volume + mu2 * exx
        D[1, out] = vy + b * (dyz - mu * vy - dyy) - b0 * before(dyz)
        D[2, out] = vz + b * (dyz - mu * vz - dzz) + b1 * after(dzz)

    over_rows(D.shape[1], work)

    def rest(r):
        _, up, down, out = spans(r)
        D[1, out] = D[1, out] + b * W[0, down]
        D[2, out] = D[2, out] - b * W[1, up]

    over_rows(D.shape[1], rest)


def response_ahead(V, S, coef_ref, D, W):
    b, b0, m1, lam, mu2, mu = coefs(coef_ref, (C_B, C_B0, C_M1, C_LAM, C_MU2, C_MU))

    def work(r):
        here, _, down, out = spans(r)
        vx = b * S[XX, 0, here]
        dxy = mu * (b * S[XX, 0, down] - vx + V[VY, 0, here])
        dxz = mu * (m1 * after(vx) - vx + V[VZ, 0, here])
        W[0, here] = dxy
        D[0, out] = dxy
        D[1, out] = dxz
        D[2, out] = vx + b * (dxy + dxz - (lam + mu2) * vx) - b0 * before(dxz)

    over_rows(D.shape[1], work)

    def rest(r):
        _, up, _, out = spans(r)
        D[2, out] = D[2, out] - b * W[0, up]

    over_rows(D.shape[1], rest)


def early_ahead(V, S, R, coef_ref, msg, W, force, window):
    b, b0, m0, m1, lam, mu2, mu = coefs(coef_ref, (C_B, C_B0, C_M0, C_M1, C_LAM, C_MU2, C_MU))

    def work(r):
        here, up, down, out = spans(r)
        vx, vy, vz = V[VX, 1, here], V[VY, 1, here], V[VZ, 1, here]
        exx = vx - V[VX, 0, here]
        volume = lam * (exx + (vy - V[VY, 1, up]) + (vz - m0 * before(vz)))
        sxx = S[XX, 1, here] + (volume + mu2 * exx) + DT * R[XX, 1, out]
        sxy = S[XY, 1, here] + mu * (V[VX, 1, down] - vx - vy) + DT * R[XY, 1, out]
        sxz = S[XZ, 1, here] + mu * (m1 * after(vx) - vx - vz) + DT * R[XZ, 1, out]
        W[0, here] = sxy
        msg[0, out] = sxy
        msg[1, out] = sxz
        msg[2, out] = vx + b * (sxy + sxz - sxx) - b0 * before(sxz)

    over_rows(msg.shape[1], work)

    def rest(r):
        _, up, _, out = spans(r)
        msg[2, out] = msg[2, out] - b * W[0, up]

    over_rows(msg.shape[1], rest)
    if force is not None:
        add_force(msg, (2,), force, (VX, 1), window)


def early_behind(V, S, R, coef_ref, surface, column, msg, W, force, window):
    b, b0, b1, m0, m1, lam, mu2, mu, l0 = coefs(
        coef_ref, (C_B, C_B0, C_B1, C_M0, C_M1, C_LAM, C_MU2, C_MU, C_L0)
    )

    def work(r):
        here, up, down, out = spans(r)
        vx, vy, vz = V[VX, 0, here], V[VY, 0, here], V[VZ, 0, here]
        eyy = vy - V[VY, 0, up]
        ezz = vz - m0 * before(vz)
        volume = lam * (vx + eyy + ezz)
        sxx = S[XX, 0, here] + (volume + mu2 * vx) + DT * R[XX, 0, out]
        syy = S[YY, 0, here] + (volume + mu2 * eyy) + DT * R[YY, 0, out]
        szz = S[ZZ, 0, here] + (volume + mu2 * ezz) + DT * R[ZZ, 0, out]
        if surface is not None:
            szz = szz + l0 * lane_roll(surface[out, :], -column)
        sxy = S[XY, 0, here] + mu * (V[VX, 0, down] - vx + (V[VY, 1, here] - vy)) + DT * R[XY, 0, out]
        sxz = S[XZ, 0, here] + mu * (m1 * after(vx) - vx + (V[VZ, 1, here] - vz)) + DT * R[XZ, 0, out]
        syz = S[YZ, 0, here] + mu * (m1 * after(vy) - vy + (V[VZ, 0, down] - vz)) + DT * R[YZ, 0, out]
        W[0, here] = syy
        W[1, here] = syz
        msg[0, out] = sxx
        msg[1, out] = vy + b * (sxy - syy + syz) - b0 * before(syz)
        msg[2, out] = vz + b * (sxz + syz - szz) + b1 * after(szz)

    over_rows(msg.shape[1], work)

    def rest(r):
        _, up, down, out = spans(r)
        msg[1, out] = msg[1, out] + b * W[0, down]
        msg[2, out] = msg[2, out] - b * W[1, up]

    over_rows(msg.shape[1], rest)
    if force is not None:
        add_force(msg, (1,), force, (VY, 0), window)
        add_force(msg, (2,), force, (VZ, 0), window)


def ahead_bond(V, S, R, coef_ref, force, surface, msg, missing, G, step, window, unforced=0, respond=None):
    (b,) = coefs(coef_ref, (C_B,))
    _, _, has_ahead = place()
    keep = jnp.where(has_ahead, 1.0, 0.0).astype(jnp.float32)

    def got(i, out):
        return msg[i, out] if missing is None else msg[i, out] + missing[i, out]

    def work(r):
        here, _, _, out = spans(r)
        V[VX, 1, here] = V[VX, 1, here] + (keep * b) * got(0, out)
        G[0, out] = keep * (got(1, out) - b * S[XY, 1, here])
        G[1, out] = keep * (got(2, out) - b * S[XZ, 1, here])

    over_message(R.shape[2], work, msg)
    if step < unforced:
        add_force(G, (0,), force, (VY, 2), window)
        add_force(G, (1,), force, (VZ, 2), window)
    if respond is not None:
        respond()
    post(
        V, S, R, coef_ref, surface, 1, 2 * step + 1,
        lambda r: V[VX, 0, pl.ds(PAD + r, ROWS)],
        lambda r: G[0, pl.ds(r, ROWS)],
        lambda r: G[1, pl.ds(r, ROWS)],
    )


def behind_bond(V, S, R, coef_ref, force, surface, msg, missing, G, step, window, unforced=0, respond=None):
    (b,) = coefs(coef_ref, (C_B,))
    _, has_behind, _ = place()
    keep = jnp.where(has_behind, 1.0, 0.0).astype(jnp.float32)

    def got(i, out):
        return msg[i, out] if missing is None else msg[i, out] + missing[i, out]

    def work(r):
        here, _, _, out = spans(r)
        V[VY, 0, here] = V[VY, 0, here] - (keep * b) * got(0, out)
        V[VZ, 0, here] = V[VZ, 0, here] - (keep * b) * got(1, out)
        G[0, out] = keep * (got(2, out) + b * S[XX, 0, here])

    over_message(R.shape[2], work, msg)
    if step < unforced:
        add_force(G, (0,), force, (VX, 2), window)
    if respond is not None:
        respond()
    post(
        V, S, R, coef_ref, surface, 0, 2 * step,
        lambda r: G[0, pl.ds(r, ROWS)],
        lambda r: V[VY, 1, pl.ds(PAD + r, ROWS)],
        lambda r: V[VZ, 1, pl.ds(PAD + r, ROWS)],
    )


def start_kernel(
    velocity, stress, memory, layer_in, lam_in, mu_in, buoy_in, rate_in, defect_in, after_this,
    V, S, R, coef_ref, near_upper, near_lower, msg_far, layer_ref, lam, mu, buoy, rate, defect, sems,
):
    del after_this
    msg_near = Halves(near_upper, near_lower)
    across = velocity.shape[2]
    inside = pl.ds(PAD, across)
    pairs = [
        (layer_in, layer_ref), (lam_in, lam), (mu_in, mu), (buoy_in, buoy), (rate_in, rate), (defect_in, defect),
    ]
    pairs += [(stress.at[i], S.at[i, :, inside]) for i in range(6)]
    pairs += [(velocity.at[i], V.at[i, :, inside]) for i in range(3)]
    pairs += [(memory.at[i], R.at[i]) for i in range(6)]
    copies = [pltpu.make_async_copy(*pair, sems.at[i]) for i, pair in enumerate(pairs)]
    for copy in copies:
        copy.start()
    zero_edges(V)
    zero_edges(S)
    for copy in copies[:6]:
        copy.wait()
    layer = layer_ref[...]

    def per_depth(table):
        row = jnp.zeros(layer.shape, jnp.float32)
        for level in range(table.shape[0]):
            row = jnp.where(layer == level, table[level], row)
        return row

    lane = lax.broadcasted_iota(jnp.int32, layer.shape, 1)
    not_first = jnp.where(lane > 0, 1.0, 0.0).astype(jnp.float32)
    not_last = jnp.where(lane < layer.shape[1] - 1, 1.0, 0.0).astype(jnp.float32)
    b = DT * per_depth(buoy)
    two_mu = (2.0 * DT) * per_depth(mu)
    decay = DT * per_depth(rate)
    drop = 2.0 * decay * per_depth(defect)
    for row, value in (
        (C_B, b),
        (C_B0, b * not_first),
        (C_B1, b * not_last),
        (C_M0, not_first),
        (C_M1, not_last),
        (C_LAM, DT * per_depth(lam)),
        (C_MU2, two_mu),
        (C_MU, 0.5 * two_mu),
        (C_K1, 1.0 - decay),
        (C_K2, drop),
        (C_K2H, 0.5 * drop),
        (C_L0, DT * (1.0 - not_first)),
    ):
        coef_ref[row : row + 1, :] = value
    coef_ref[12:16, :] = jnp.zeros((4, layer.shape[1]), jnp.float32)
    for copy in copies[6:15]:
        copy.wait()
    even, _, _ = place()

    @pl.when(even)
    def _():
        pre_ahead(V, S, coef_ref, msg_near, None, 0)
        pre_behind(V, S, coef_ref, msg_far, None, 0)

    @pl.when(jnp.logical_not(even))
    def _():
        pre_behind(V, S, coef_ref, msg_near, None, 0)
        pre_ahead(V, S, coef_ref, msg_far, None, 0)

    for copy in copies[15:]:
        copy.wait()


def first_kernel(window, V0, S, R, coef_ref, force, surface, V, msg, W):
    even, _, _ = place()
    zero_edges(W)
    now, then = force.at[0], force.at[1]
    add_force(V, (VX, 1), now, (VX, 1), PAD + window)
    add_force(V, (VY, 0), now, (VY, 0), PAD + window)
    add_force(V, (VZ, 0), now, (VZ, 0), PAD + window)
    inner(V, S, coef_ref, now, window)

    @pl.when(even)
    def _():
        early_behind(V, S, R, coef_ref, surface, 0, msg, W, then, window)

    @pl.when(jnp.logical_not(even))
    def _():
        early_ahead(V, S, R, coef_ref, msg, W, then, window)


def results_out(V, S, R, results, sems, cell):
    inside = pl.ds(PAD, R.shape[2])
    pairs = [(V.at[:, cell, inside], results[0]), (S.at[:, cell, inside], results[1]), (R.at[:, cell], results[2])]
    return [
        pltpu.make_async_copy(source, result.at[:, cell], sems.at[i]) for i, (source, result) in enumerate(pairs)
    ]


def start_all(copies):
    for copy in copies:
        copy.start()


def wait_all(copies):
    for copy in copies:
        copy.wait()


def near_kernel(step, window, V0, S0, R0, coef_ref, force, surface, upper, lower, V, S, R, *rest):
    G = rest[-1]
    msg = Halves(upper, lower)
    even, _, _ = place()
    more = step < STEPS - 1
    send = Halves(*rest[:2]) if more else None

    @pl.when(even)
    def _():
        ahead_bond(V, S, R, coef_ref, force.at[step], surface, msg, None, G, step, window, 1)
        if more:
            pre_ahead(V, S, coef_ref, send, force.at[step + 1], window)
        else:
            copies = results_out(V, S, R, rest[:3], rest[-2], 1)
            start_all(copies)
            wait_all(copies)

    @pl.when(jnp.logical_not(even))
    def _():
        behind_bond(V, S, R, coef_ref, force.at[step], surface, msg, None, G, step, window, 1)
        if more:
            pre_behind(V, S, coef_ref, send, force.at[step + 1], window)
        else:
            copies = results_out(V, S, R, rest[:3], rest[-2], 0)
            start_all(copies)
            wait_all(copies)


def far_kernel(step, window, V0, S0, R0, coef_ref, force, surface, msg, *rest):
    rest = list(rest)
    missing = rest.pop(0) if step > 0 else None
    V, S, R, D = rest[:4]
    G, W = rest[-2:]
    early = rest[4] if step < STEPS - 2 else None
    even, _, _ = place()
    zero_edges(W)
    here, then = force.at[step], force.at[step + 1]

    @pl.when(even)
    def _():
        behind_bond(
            V, S, R, coef_ref, here, surface, msg, missing, G, step, window, 1,
            lambda: response_ahead(V, S, coef_ref, D, W),
        )
        pre_behind(V, S, coef_ref, None, then, window)

    @pl.when(jnp.logical_not(even))
    def _():
        ahead_bond(
            V, S, R, coef_ref, here, surface, msg, missing, G, step, window, 1,
            lambda: response_behind(V, S, coef_ref, D, W),
        )
        pre_ahead(V, S, coef_ref, None, then, window)

    inner(V, S, coef_ref, then, window)
    if early is not None:
        later = force.at[step + 2]

        @pl.when(even)
        def _():
            early_behind(V, S, R, coef_ref, surface, 2 * (step + 1), early, W, later, window)

        @pl.when(jnp.logical_not(even))
        def _():
            early_ahead(V, S, R, coef_ref, early, W, later, window)


def last_kernel(step, window, V0, S0, R0, coef_ref, force, surface, msg, missing, v0, s0, r0, V, S, R, *rest):
    *results, G, sems = rest
    even, _, _ = place()
    here = force.at[step]

    @pl.when(even)
    def _():
        copies = results_out(V, S, R, results, sems, 0)
        behind_bond(
            V, S, R, coef_ref, here, surface, msg, missing, G, step, window, 0, lambda: start_all(copies[:1])
        )
        start_all(copies[1:])
        wait_all(copies)

    @pl.when(jnp.logical_not(even))
    def _():
        copies = results_out(V, S, R, results, sems, 1)
        ahead_bond(
            V, S, R, coef_ref, here, surface, msg, missing, G, step, window, 0, lambda: start_all(copies[:1])
        )
        start_all(copies[1:])
        wait_all(copies)


ENTRY_ROW, TRUCK_ROW = 36, 40
GROUP = 8


def pack_kernel(
    record, loads_in, entries_in, cells_in, piers_in, own, loads, steps_table, piers, entries, cells, sems
):
    panel = record.shape[1]
    slots, lanes = loads.shape
    steps = entries.shape[0]
    pairs = [(record, own.at[:, pl.ds(0, panel)]), (loads_in, loads), (entries_in, entries), (cells_in, cells)]
    pairs.append((piers_in, piers))
    copies = [pltpu.make_async_copy(*pair, sems.at[i]) for i, pair in enumerate(pairs)]
    for copy in copies:
        copy.start()
    own[:, panel:] = jnp.zeros((own.shape[0], own.shape[1] - panel), jnp.float32)
    steps_table[...] = jnp.zeros(steps_table.shape, jnp.float32)
    for copy in copies:
        copy.wait()
    steps_table[0:steps, 0:slots] = entries[...].astype(jnp.float32)
    steps_table[8 : 8 + steps, 0:slots] = cells[...].astype(jnp.float32)
    blocks = [loads[8 * i : 8 * i + 8, :] for i in range(slots // 8)] + [steps_table[0:8, :]]
    for i, block in enumerate(blocks):
        own[0:8, panel + i * lanes : panel + (i + 1) * lanes] = block


def lane_blocks(table, width):
    return sum(lane_roll(table[s : s + 1, :], s * width) for s in range(STEPS))


def split_kernel(panel, slots, own, behind, cells, after_this, out):
    del after_this
    tiles, _, lanes = out.shape
    pieces = panel // lanes
    third = pieces // 3
    cell_of = cells[...]
    me = lax.axis_index("line")
    group, mine = lax.div(me, tiles), lax.rem(me, tiles)
    piers = cell_of.shape[1]
    row = lax.broadcasted_iota(jnp.int32, (3 * tiles, lanes), 0)
    j = lax.rem(row, 3)
    first = (lax.div(row, 3) + group * tiles) * 2
    cell_x, cell_yz = first + jnp.where(j == 2, -1, j), first + j
    record = jnp.where(group == 0, own[:, :panel], behind[:, :panel])

    def hits(cell):
        return [jnp.where(cell == cell_of[0:1, p : p + 1], 1.0, 0.0).astype(jnp.float32) for p in range(piers)]

    hit_x, hit_yz = hits(cell_x), hits(cell_yz)

    def share(m):
        hit = hit_x if m < third else hit_yz
        return sum(hit[p] * record[p : p + 1, m * lanes : (m + 1) * lanes] for p in range(piers))

    parts = [share(m) for m in range(pieces)]

    def trucks(source):
        blocks = [source[0:8, panel + i * lanes : panel + (i + 1) * lanes] for i in range(slots // 8 + 1)]
        return blocks[:-1], lane_blocks(blocks[-1], slots)

    own_rows, own_entry = trucks(own)
    far_rows, far_entry = trucks(behind)
    for tile in range(tiles):
        these = slice(3 * tile, 3 * tile + 3)
        for m in range(pieces):
            out[tile, 3 * m : 3 * m + 3, :] = parts[m][these, :]
        passed = mine < tile
        out[tile, ENTRY_ROW : ENTRY_ROW + 1, :] = jnp.where(passed, own_entry, far_entry)
        for i in range(slots // 8):
            at = TRUCK_ROW + 8 * i
            out[tile, at : at + 8, :] = jnp.where(passed, own_rows[i], far_rows[i])


def prepare_kernel(parts, loads, steps_table, force, surface, table, rows_out):
    steps, comps, width = force.shape[:3]
    lanes = parts.shape[2]
    force[...] = jnp.zeros(force.shape, jnp.float32)
    per = ENTRY_ROW // (comps * width)
    lane = lax.broadcasted_iota(jnp.int32, (per, lanes), 1)
    scale = jnp.where(lane < FZ, DT, 0.0).astype(jnp.float32)
    for s in range(steps):
        for comp in range(comps):
            for cell in range(width):
                panel = parts[s, pl.ds(comp * per * width + cell, per, stride=width), :]
                force[s, comp, cell, pl.ds(4, per, stride=2), :] = scale * panel
                force[s, comp, cell, pl.ds(5, per, stride=2), :] = scale * lane_roll(panel, FZ)
    surface_loads(1, parts, loads, steps_table, surface, table, rows_out)


def opening_kernel(
    window, parts, loads, steps_table, V0, S, R, coef_ref, force, surface, V, msg, table, rows_out, W
):
    prepare_kernel(parts, loads, steps_table, force, surface, table, rows_out)
    first_kernel(window, V0, S, R, coef_ref, force, surface, V, msg, W)


def surface_kernel(parts, loads, steps_table, surface, table, rows_out):
    surface_loads(STEPS, parts, loads, steps_table, surface, table, rows_out)


def surface_loads(steps, parts, loads, steps_table, surface, table, rows_out):
    slots = loads.shape[0]
    tiles = parts.shape[0]
    mine = lax.rem(lax.axis_index("line"), tiles)
    table[...] = jnp.zeros(table.shape, jnp.float32)
    table[0:1, :] = lane_blocks(steps_table[0:8, :], slots)
    table[steps + 1 : steps + 2, :] = lane_blocks(steps_table[8:16, :], slots)
    rows = [loads[...]]
    for k in range(1, steps + 1):
        source = lax.rem(mine + (tiles - k), tiles)
        rows.append(parts[source, TRUCK_ROW : TRUCK_ROW + slots, :])
        table[k : k + 1, :] = parts[source, ENTRY_ROW : ENTRY_ROW + 1, :]
    columns = table[...].T
    rows_out[...] = jnp.zeros(rows_out.shape, jnp.float32)
    for s in range(steps):
        block = slice(s * slots, (s + 1) * slots)
        moved = []
        for k in range(steps - s):
            entry = jnp.broadcast_to(columns[block, k : k + 1], rows[k].shape)
            new = rows[k]
            for slot in range(slots):
                new = jnp.where(entry == float(slot), rows[k + 1][slot : slot + 1, :], new)
            moved.append(new)
        rows = moved
        cell = jnp.broadcast_to(columns[block, steps + 1 : steps + 2], rows[0].shape)
        for c in range(2):
            load = jnp.sum(jnp.where(cell == float(c), rows[0], 0.0), axis=0, keepdims=True)
            rows_out[2 * s + c : 2 * s + c + 1, :] = load
    surface[...] = rows_out[...].T


def in_vmem(x):
    return pltpu.with_memory_space_constraint(x, pltpu.VMEM)


WHOLE = pl.BlockSpec(memory_space=pltpu.VMEM)
SCALARS = pl.BlockSpec(memory_space=pltpu.SMEM)
ANYWHERE = pl.BlockSpec(memory_space=pl.ANY)


def call(kernel, ins, specs, outs, out_specs, scratch=(), aliases=None, name=None, cost=1):
    return pl.pallas_call(
        kernel,
        out_shape=outs,
        in_specs=specs,
        out_specs=out_specs,
        scratch_shapes=list(scratch),
        input_output_aliases=aliases or {},
        compiler_params=pltpu.CompilerParams(vmem_limit_bytes=VMEM_LIMIT),
        cost_estimate=pl.CostEstimate(flops=cost, bytes_accessed=cost, transcendentals=0),
        name=name,
    )(*ins)


def body(
    velocity, stress, memory, truck_loads, pier_panels,
    lame_lambda, lame_mu, buoyancy, relax_rate, defect_mu, layer,
    truck_entry, truck_cell, pier_cell,
):
    tiles = lax.axis_size("line")
    width_x, across, depth = velocity.shape[1:]
    slots = truck_loads.shape[0]
    window = (across - FY) // 2 - 4
    f32 = jnp.float32

    near = [(i, i ^ 1) for i in range(tiles) if (i ^ 1) < tiles]
    far = [(i, i + 1) for i in range(1, tiles - 1, 2)] + [(i + 1, i) for i in range(1, tiles - 1, 2)]

    padded = across + 2 * PAD
    v_type = pltpu.VMEM((3, width_x, padded, depth), f32)
    s_type = pltpu.VMEM((6, width_x, padded, depth), f32)
    r_type = pltpu.VMEM((6, width_x, across, depth), f32)
    c_type = pltpu.VMEM((N_COEF, depth), f32)
    m_type = pltpu.VMEM((3, across, depth), f32)
    planes = (pltpu.VMEM((3, across // 2, depth), f32),) * 2
    ghost = pltpu.VMEM((2, across, depth), f32)
    work = pltpu.VMEM((2, padded, depth), f32)

    def ahead_by(x, distance):
        return lax.ppermute(x, "line", [(i, i + distance) for i in range(tiles - distance)])

    def in_hbm(*arrays):
        return tuple(pltpu.with_memory_space_constraint(x, pltpu.HBM) for x in arrays)

    dma = pltpu.SemaphoreType.DMA
    piers, panel = pier_panels.shape[1:]
    own, loads, steps_table, pier_row = call(
        pack_kernel,
        in_hbm(pier_panels[0], truck_loads, truck_entry, truck_cell, pier_cell[None, :]),
        (ANYWHERE,) * 5,
        (
            pltpu.VMEM((piers, panel + (slots // 8 + 1) * depth), f32),
            pltpu.VMEM((slots, depth), f32),
            pltpu.VMEM((16, depth), f32),
            pltpu.VMEM((1, piers), jnp.int32),
        ),
        (WHOLE,) * 4,
        scratch=(pltpu.VMEM(truck_entry.shape, jnp.int32), pltpu.VMEM(truck_cell.shape, jnp.int32), dma((5,))),
        name="pack",
    )
    behind = ahead_by(own, GROUP)
    reach = 2 * GROUP
    index = lax.axis_index("line")
    while reach < tiles:
        record = jnp.where(index < GROUP, own, behind)[:, :panel]
        record = jnp.where(index < reach, record, ahead_by(record, reach))
        behind = jnp.concatenate([record, behind[:, panel:]], axis=1)
        reach *= 2
    tables = (lame_lambda, lame_mu, buoyancy, relax_rate, defect_mu)
    V, S, R, coef, *msg_near, msg_far = call(
        start_kernel,
        in_hbm(velocity, stress, memory, layer[None, :], *tables) + (steps_table,),
        (ANYWHERE,) * 10,
        (v_type, s_type, r_type, c_type, *planes, m_type),
        (WHOLE,) * 7,
        scratch=(
            pltpu.VMEM((1, depth), jnp.int32), *(pltpu.SMEM(table.shape, f32) for table in tables), dma((21,)),
        ),
        name="start",
        cost=8 * 1024 * 1024,
    )
    msg_far = lax.ppermute(msg_far, "line", far)
    msg_near = [lax.ppermute(plane, "line", near) for plane in msg_near]
    parts = call(
        functools.partial(split_kernel, panel, slots),
        (own, behind, in_vmem(pier_row), coef),
        (WHOLE,) * 3 + (ANYWHERE,),
        pltpu.VMEM((GROUP, TRUCK_ROW + slots, depth), f32),
        WHOLE,
        name="split",
    )
    groups = [list(range(at, at + GROUP)) for at in range(0, tiles, GROUP)]
    parts = lax.all_to_all(parts, "line", 0, 0, axis_index_groups=groups, tiled=True)
    square = pltpu.VMEM((across, depth), f32)
    turned = (pltpu.VMEM((depth, depth), f32), pltpu.VMEM((depth, across), f32))
    ins = (parts, in_vmem(loads), in_vmem(steps_table))
    later = call(surface_kernel, ins, (WHOLE,) * 3, square, WHOLE, scratch=turned, name="surface")
    force, surface, V, early = call(
        functools.partial(opening_kernel, window),
        ins + tuple(in_vmem(x) for x in (V, S, R, coef)),
        (WHOLE,) * 7,
        (pltpu.VMEM((STEPS, 3, 3, 16, depth), f32), square, v_type, m_type),
        (WHOLE,) * 4,
        scratch=(*turned, work),
        aliases={3: 2},
        name="opening",
    )
    early = lax.ppermute(early, "line", far)
    state = (v_type, s_type, r_type)
    results = tuple(jax.ShapeDtypeStruct(x.shape, f32) for x in (velocity, stress, memory))
    same = {0: 0, 1: 1, 2: 2}
    missing = None
    for step in range(STEPS):
        more = step < STEPS - 1
        ins = tuple(in_vmem(x) for x in (V, S, R, coef, force, surface, *msg_near))
        outs = state + (planes if more else results)
        V, S, R, *msg = call(
            functools.partial(near_kernel, step, window),
            ins,
            (WHOLE,) * len(ins),
            outs,
            (WHOLE,) * 5 if more else (WHOLE,) * 3 + (ANYWHERE,) * 3,
            scratch=(ghost,) if more else (dma((3,)), ghost),
            aliases=same,
            name="near" + str(step),
        )
        if more:
            msg_near = [lax.ppermute(plane, "line", near) for plane in msg]
        if step == 0:
            surface = later
        ins = (V, S, R, coef, force, surface, msg_far) + ((missing,) if step else ())
        ins = tuple(in_vmem(x) for x in ins)
        if more:
            outs = state + (m_type,) + ((m_type,) if step < STEPS - 2 else ())
            V, S, R, missing, *msg = call(
                functools.partial(far_kernel, step, window),
                ins,
                (WHOLE,) * len(ins),
                outs,
                (WHOLE,) * len(outs),
                scratch=(ghost, work),
                aliases=same,
                name="far" + str(step),
            )
            msg_far = early
            if msg:
                early = lax.ppermute(msg[0], "line", far)
    ends = call(
        functools.partial(last_kernel, STEPS - 1, window),
        ins + tuple(msg),
        (WHOLE,) * 8 + (ANYWHERE,) * 3,
        state + results,
        (WHOLE,) * 3 + (ANYWHERE,) * 3,
        scratch=(ghost, dma((3,))),
        aliases={**same, 8: 3, 9: 4, 10: 5},
        name="last",
    )
    return ends[3:]


def solution(mesh):
    placed = (
        P(None, ("runs", "line"), None, None),
        P(None, ("runs", "line"), None, None),
        P(None, ("runs", "line"), None, None),
        P(("runs", "line"), None),
        P("line", "runs", None),
        P(),
        P(),
        P(),
        P(),
        P(),
        P(),
        P(None, ("runs", "line")),
        P(None, ("runs", "line")),
        P(),
    )
    return jax.shard_map(
        body,
        mesh=mesh,
        in_specs=placed,
        out_specs=(
            P(None, ("runs", "line"), None, None),
            P(None, ("runs", "line"), None, None),
            P(None, ("runs", "line"), None, None),
        ),
        check_vma=False,
    )
```
